32 devices in a mesh: seq: 4 (over y, x), dp: 8 (over z, core).
Axes of the slice: x: 2, y: 2, z: 4, core: 2. Of those that a mesh axis runs over, the one named last changes fastest.
Arguments:
- tokens: bfloat16 [8, 1536, 2048], P('dp', 'seq'), may hold values from -6 to 6
- seq_lengths: int32 [8, 4], P('dp'), may hold values from 1 to 768, 1536 in all within a row
- out_grad: bfloat16 [8, 1536, 2048], P('dp', 'seq'), may hold values from -6 to 6
- w_receptance: bfloat16 [2048, 2048], P(('seq', 'dp')), may hold values from -0.125 to 0.125
- w_key: bfloat16 [2048, 2048], P(('seq', 'dp')), may hold values from -0.125 to 0.125
- w_value: bfloat16 [2048, 2048], P(('seq', 'dp')), may hold values from -0.125 to 0.125
- w_gate: bfloat16 [2048, 2048], P(('seq', 'dp')), may hold values from -0.125 to 0.125
- w_output: bfloat16 [2048, 2048], P(('seq', 'dp')), may hold values from -0.25 to 0.25
- ffn_key: bfloat16 [2048, 7168], P(('seq', 'dp')), may hold values from -0.125 to 0.125
- ffn_receptance: bfloat16 [2048, 2048], P(('seq', 'dp')), may hold values from -0.125 to 0.125
- ffn_value: bfloat16 [7168, 2048], P(('seq', 'dp')), may hold values from -0.0625 to 0.0625
- vectors: bfloat16 [14, 2048], P(None, ('seq', 'dp')), as said below
Outputs:
- out: bfloat16 [8, 1536, 2048], P('dp', 'seq')
- tokens_grad: float32 [8, 1536, 2048], P('dp', 'seq')
- w_receptance_grad: float32 [2048, 2048], P(('seq', 'dp'))
- w_key_grad: float32 [2048, 2048], P(('seq', 'dp'))
- w_value_grad: float32 [2048, 2048], P(('seq', 'dp'))
- w_gate_grad: float32 [2048, 2048], P(('seq', 'dp'))
- w_output_grad: float32 [2048, 2048], P(('seq', 'dp'))
- ffn_key_grad: float32 [2048, 7168], P(('seq', 'dp'))
- ffn_receptance_grad: float32 [2048, 2048], P(('seq', 'dp'))
- ffn_value_grad: float32 [7168, 2048], P(('seq', 'dp'))
- vectors_grad: float32 [14, 2048], P(None, ('seq', 'dp'))
The draws below stay inside these ranges and needn't reach their ends.
Inputs may be any that keep to these rules, and one draw needn't show every extreme that they name: `seq_lengths`: row g lists in order the lengths of the 4 sequences that fill group g's 1536 tokens; they sum to 1536 and the longest of each row has exactly 768 tokens. `vectors`: rows 0, 8, 10 lie in 0.5 to 1.5, rows 1, 9, 11 in -0.5 to 0.5, mixes in 0 to 1, decay parameters in -9.3 to -2.9, bonus in -1 to 1.
All inputs are finite; a program needn't handle non-finite values.
Results may differ from the reference program's by a relative error of at most 0.019.
Values may be sent and summed in bfloat16 or wider, within the bound.
No kernel may reach another device: no remote copies, remote signals or barrier semaphores. Data moves between devices by JAX's collectives and lax.ppermute only.
A program may use at most 448 MiB of HBM per device.

```python
import math
from functools import partial
import jax
import jax.numpy as jnp
import numpy as np
from jax import lax

D = 2048
FF = 7168
ATTENDER_WIDTH = 64
HEADS = 32
SPAN = 64
TOK_DEV = 384
SEQS = 4
VECS = 14
GROUP_TOK = 1536
GROUPS = 8
N_SEQ = 4


def draw_vectors(key, part):
    lower = jnp.array([0.5, -0.5, 0.0, 0.0, 0.0, 0.0, -9.3, -1.0, 0.5, -0.5, 0.5, -0.5, 0.0, 0.0], jnp.float32)
    upper = jnp.array([1.5, 0.5, 1.0, 1.0, 1.0, 1.0, -2.9, 1.0, 1.5, 0.5, 1.5, 0.5, 1.0, 1.0], jnp.float32)
    uniform_part = jax.random.uniform(jax.random.fold_in(key, 11), (VECS, D), jnp.float32)
    return (lower[:, None] + (upper - lower)[:, None] * uniform_part).astype(jnp.bfloat16)


def block_levels(key, shape, cuts, low, high):
    loudness, own = 1.0, jax.random.fold_in(key, 6)
    for position, shards_of in cuts:
        heights = jnp.exp(jax.random.uniform(jax.random.fold_in(own, position), (shards_of,), jnp.float32, low / len(cuts), high / len(cuts)))
        loudness = loudness * jnp.repeat(heights, shape[position] // shards_of).reshape([-1 if axis == position else 1 for axis in range(len(shape))])
    return loudness


def profile(number_of, total, limit, lean):
    portions = [(1 << 20) // math.isqrt(standing ** lean) + 1 for standing in range(2, number_of + 1)]
    surplus, holding = total - limit - (number_of - 1), [1] * (number_of - 1)
    while surplus > 0:
        movable = [i for i in range(number_of - 1) if holding[i] < limit]
        pool, left = sum([portions[i] for i in movable]), surplus
        for i in movable:
            more = min(limit - holding[i], max(1, left * portions[i] // pool), surplus)
            holding[i] = holding[i] + more
            surplus = surplus - more
    return np.array([limit] + holding)


def ragged_sizes(rng, amount, total, bound, lean):
    if amount == 2:
        one = jax.random.randint(rng, (), max(1, total - bound), min(bound, total - 1) + 1)
        return jnp.stack([one, total - one])
    sizes = jnp.asarray(profile(amount, total, bound, lean), jnp.int32)
    pairs = (amount - 1) // 2
    donor, receiver = sizes[1:1 + 2 * pairs:2], sizes[2:2 + 2 * pairs:2]
    room = jnp.minimum(donor - 1, bound - receiver)
    moved = jax.random.randint(jax.random.fold_in(rng, 1), (pairs,), 0, 1 << 20) % (room + 1)
    sizes = sizes.at[1:1 + 2 * pairs:2].set(donor - moved).at[2:2 + 2 * pairs:2].set(receiver + moved)
    return sizes[jax.random.permutation(jax.random.fold_in(rng, 2), amount)]


def normal_values(stream_key, extent, deviation, limit, shards=(), kind=jnp.bfloat16):
    factor_of = block_levels(stream_key, extent, shards, -0.22, 0.18) if shards else 1.0
    values = jax.random.normal(stream_key, extent, jnp.float32) * deviation * factor_of
    return jnp.minimum(jnp.maximum(values, -limit), limit).astype(kind)


def setup_inputs(seed: int = 0) -> dict:
    streams_of = jax.random.split(jax.random.key(seed), 13)
    tokens = normal_values(streams_of[0], (GROUPS, GROUP_TOK, D), 1.0, 6.0, ((0, 8), (1, 4)))
    seq_lengths = jax.vmap(lambda own: ragged_sizes(own, SEQS, TOK_DEV * N_SEQ, TOK_DEV * N_SEQ // 2, 2))(jax.random.split(streams_of[1], GROUPS)).reshape((GROUPS, SEQS)).astype(jnp.int32)
    out_grad = normal_values(streams_of[2], (GROUPS, GROUP_TOK, D), 1.0, 6.0, ((0, 8), (1, 4)))
    w_receptance = normal_values(streams_of[3], (D, D), D ** -0.5, 0.125, ((0, 32),))
    w_key = normal_values(streams_of[4], (D, D), D ** -0.5, 0.125, ((0, 32),))
    w_value = normal_values(streams_of[5], (D, D), D ** -0.5, 0.125, ((0, 32),))
    w_gate = normal_values(streams_of[6], (D, D), D ** -0.5, 0.125, ((0, 32),))
    w_output = normal_values(streams_of[7], (D, D), (D // 4) ** -0.5, 0.25, ((0, 32),))
    ffn_key = normal_values(streams_of[8], (D, FF), D ** -0.5, 0.125, ((0, 32),))
    ffn_receptance = normal_values(streams_of[9], (D, D), D ** -0.5, 0.125, ((0, 32),))
    ffn_value = normal_values(streams_of[10], (FF, D), FF ** -0.5, 0.0625, ((0, 32),))
    vectors = draw_vectors(jax.random.fold_in(streams_of[12], 71), 0)
    return {"tokens": tokens, "seq_lengths": seq_lengths, "out_grad": out_grad, "w_receptance": w_receptance, "w_key": w_key, "w_value": w_value, "w_gate": w_gate, "w_output": w_output, "ffn_key": ffn_key, "ffn_receptance": ffn_receptance, "ffn_value": ffn_value, "vectors": vectors}


EPSILON = 1e-05
GROUP_EPSILON = 1.0
HIGH = lax.Precision.HIGHEST

@jax.custom_vjp
def low(v):
    return lax.optimization_barrier(v.astype(jnp.bfloat16)).astype(jnp.float32)

@jax.custom_vjp
def low_back(v):
    return v

def low_keep(v):
    return (low(v), None)

def low_pass(kept, grad):
    return (grad,)

def back_keep(v):
    return (v, None)

def back_low(kept, grad):
    return (low(grad),)
low.defvjp(low_keep, low_pass)
low_back.defvjp(back_keep, back_low)

def hdot(left, right):
    return jnp.dot(left, right, precision=HIGH, preferred_element_type=jnp.float32)

def layer_norm(values, norm_gain, norm_bias):
    mean_value = lax.optimization_barrier(jnp.mean(values, axis=-1, keepdims=True))
    centred = values - mean_value
    spread = lax.optimization_barrier(jnp.mean(centred * centred, axis=-1, keepdims=True))
    return centred * lax.rsqrt(spread + EPSILON) * norm_gain + norm_bias

def segment_of(lengths, positions):
    starts = (jnp.cumsum(lengths) - lengths).astype(jnp.int32)
    later_flags = (positions[:, None] >= starts[None, 1:]).astype(jnp.int32)
    first_flags = jnp.any(positions[:, None] == starts[None, :], axis=1)
    return (lax.optimization_barrier(jnp.sum(later_flags, axis=1)).astype(jnp.int32), first_flags)

def mix_inputs(normed, received, mixes, keep_rows):
    previous = jnp.concatenate([received, normed[:-1]], axis=0) * keep_rows[:, None]
    return tuple((normed * factor + previous * (1.0 - factor) for factor in mixes))

def stretch_carry(logged_fading, starting_reward, attention_recurrence_memory, stretch_source_entries):
    acceptor_entries, lookup_entries, payload_entries, piece_number, seg_before = stretch_source_entries
    span_len = acceptor_entries.shape[0]
    offsets = jnp.arange(span_len).astype(jnp.float32)
    growth = jnp.exp(offsets[:, None, None] * logged_fading)
    shrink = jnp.exp(-(offsets[:, None, None] + 1.0) * logged_fading)
    recept_grown = acceptor_entries * growth
    scores = jnp.einsum('thi,shi->hts', recept_grown, lookup_entries * shrink, precision=HIGH)
    allowed = (piece_number[:, None] == piece_number[None, :]) & (offsets[:, None] > offsets[None, :])
    scores = jnp.where(allowed[None], scores, 0.0)
    diagonal_share = lax.optimization_barrier(jnp.sum(acceptor_entries * starting_reward * lookup_entries, axis=-1))
    reaches = (piece_number == seg_before).astype(jnp.float32)
    result_entries = jnp.einsum('hts,shj->thj', scores, payload_entries, precision=HIGH) + diagonal_share[:, :, None] * payload_entries
    result_entries = result_entries + reaches[:, None, None] * jnp.einsum('thi,hij->thj', recept_grown, attention_recurrence_memory, precision=HIGH)
    tail_decay = jnp.exp((span_len - 1.0 - offsets)[:, None, None] * logged_fading)
    last_same = (piece_number == piece_number[span_len - 1]).astype(jnp.float32)
    fresh_part = jnp.einsum('shi,shj->hij', lookup_entries * tail_decay * last_same[:, None, None], payload_entries, precision=HIGH)
    attention_recurrence_memory = reaches[span_len - 1] * jnp.exp(span_len * logged_fading)[:, :, None] * attention_recurrence_memory + fresh_part
    return (attention_recurrence_memory, result_entries)

def attention_recurrence_results(acceptor_entries, lookup_entries, payload_entries, fading_coefficient, starting_reward, arriving_memory, piece_number, prior_stretch):
    resident_entries, head_count, head_size = acceptor_entries.shape
    blocks = resident_entries // SPAN
    logged_fading = -jnp.exp(fading_coefficient)
    stretch_source_entries = (acceptor_entries.reshape(blocks, SPAN, head_count, head_size), lookup_entries.reshape(blocks, SPAN, head_count, head_size), payload_entries.reshape(blocks, SPAN, head_count, head_size), piece_number.reshape(blocks, SPAN), prior_stretch)
    closing_memory, result_entries = lax.scan(jax.checkpoint(partial(stretch_carry, logged_fading, starting_reward)), arriving_memory, stretch_source_entries)
    return result_entries.reshape(resident_entries, head_count * head_size)

def norm_gate(attention_recurrence_entries, gate_pre, norm_gain, norm_bias):
    resident_entries = attention_recurrence_entries.shape[0]
    grouped = attention_recurrence_entries.reshape(resident_entries, -1, ATTENDER_WIDTH)
    mean_value = lax.optimization_barrier(jnp.mean(grouped, axis=-1, keepdims=True))
    centred = grouped - mean_value
    spread = lax.optimization_barrier(jnp.mean(centred * centred, axis=-1, keepdims=True))
    normed = (centred * lax.rsqrt(spread + GROUP_EPSILON)).reshape(resident_entries, -1)
    return (normed * norm_gain + norm_bias) * jax.nn.silu(gate_pre)

def layer_forward(inputs_f, w_receptance, w_key, w_value, w_gate, w_output, ffn_key, ffn_receptance, ffn_value, plural_real_arrays, piece_number, keep_rows, prior_stretch):
    resident_entries = inputs_f.shape[0]
    zero_row = jnp.zeros((1, inputs_f.shape[1]), jnp.float32)
    normed = layer_norm(inputs_f, plural_real_arrays[0], plural_real_arrays[1])
    mix_r, mix_k, mix_v, mix_g = mix_inputs(normed, zero_row, (plural_real_arrays[2], plural_real_arrays[3], plural_real_arrays[4], plural_real_arrays[5]), keep_rows)
    acceptor_mapping = low(low_back(hdot(low(mix_r), w_receptance)))
    lookup_mapping = low(low_back(hdot(low(mix_k), w_key)))
    payload_mapping = low(low_back(hdot(low(mix_v), w_value)))
    gate_pre = low_back(hdot(low(mix_g), w_gate))
    fading_coefficient = plural_real_arrays[6].reshape(-1, ATTENDER_WIDTH)
    starting_reward = plural_real_arrays[7].reshape(-1, ATTENDER_WIDTH)
    starting_memory = jnp.zeros((HEADS, ATTENDER_WIDTH, ATTENDER_WIDTH), jnp.float32)
    attention_recurrence_entries = attention_recurrence_results(acceptor_mapping.reshape(resident_entries, -1, ATTENDER_WIDTH), lookup_mapping.reshape(resident_entries, -1, ATTENDER_WIDTH), payload_mapping.reshape(resident_entries, -1, ATTENDER_WIDTH), fading_coefficient, starting_reward, starting_memory, piece_number, prior_stretch)
    mixed = low(norm_gate(attention_recurrence_entries, gate_pre, plural_real_arrays[8], plural_real_arrays[9]))
    after = inputs_f + low_back(hdot(mixed, w_output))
    normed_two = layer_norm(after, plural_real_arrays[10], plural_real_arrays[11])
    mix_k2, mix_r2 = mix_inputs(normed_two, zero_row, (plural_real_arrays[12], plural_real_arrays[13]), keep_rows)
    key_pre = low_back(hdot(low(mix_k2), ffn_key))
    hidden = low(jnp.square(jax.nn.softplus(key_pre)))
    recept_pre = low_back(hdot(low(mix_r2), ffn_receptance))
    value_pre = low_back(hdot(hidden, ffn_value))
    return after + jax.nn.sigmoid(recept_pre) * value_pre

def reference(tokens, seq_lengths, out_grad, w_receptance, w_key, w_value, w_gate, w_output, ffn_key, ffn_receptance, ffn_value, vectors):
    params = tuple((item.astype(jnp.float32) for item in (w_receptance, w_key, w_value, w_gate, w_output, ffn_key, ffn_receptance, ffn_value, vectors)))
    resident_entries = tokens.shape[1]

    def per_group(totals, group_inputs):
        group_tokens, lengths, group_cot = group_inputs
        positions = jnp.arange(resident_entries, dtype=jnp.int32)
        piece_number, first_flags = segment_of(lengths, positions)
        keep_rows = 1.0 - first_flags.astype(jnp.float32)
        span_starts = (jnp.arange(resident_entries // SPAN, dtype=jnp.int32) * SPAN - 1).astype(jnp.int32)
        prior_stretch = segment_of(lengths, span_starts)[0]

        def forward(inputs_f, *weights):
            return layer_forward(inputs_f, *weights, piece_number, keep_rows, prior_stretch)
        result_entries, pull = jax.vjp(forward, group_tokens.astype(jnp.float32), *params)
        grads = pull(group_cot.astype(jnp.float32))
        totals = tuple((total + grad for total, grad in zip(totals, grads[1:])))
        return (totals, (result_entries.astype(jnp.bfloat16), grads[0]))
    start_totals = tuple((jnp.zeros(item.shape, jnp.float32) for item in params))
    totals, (out, tokens_grad) = lax.scan(per_group, start_totals, (tokens, seq_lengths, out_grad))
    return (out, tokens_grad, totals[0], totals[1], totals[2], totals[3], totals[4], totals[5], totals[6], totals[7], totals[8])
```

```python
from functools import partial

import jax
import jax.numpy as jnp
from jax import lax
from jax.sharding import PartitionSpec as P

ATTENDER_WIDTH = 64
SPAN = 64


EPSILON = 1e-05
GROUP_EPSILON = 1.0
HIGH = lax.Precision.HIGHEST


def passed_along(value, axis, by):
    devices = lax.axis_size(axis)
    pairs = [(i, i + by) for i in range(devices) if 0 <= i + by < devices]
    return lax.ppermute(value, axis, pairs)


def entering(value, axis, combine, identity):
    devices, place = (lax.axis_size(axis), lax.axis_index(axis))
    everything = jax.tree.map(
        lambda part, kind: lax.all_gather(part.astype(kind), axis),
        value,
        (jnp.bfloat16, jnp.bfloat16),
    )
    start = jax.tree.map(
        lambda part, zero: jnp.broadcast_to(jnp.asarray(zero, part.dtype), part.shape),
        value,
        identity,
    )

    def step(k, before):
        reached = k < place
        new = combine(
            before, jax.tree.map(lambda part, own: part[k].astype(own.dtype), everything, value)
        )
        return jax.tree.map(lambda a, b: jnp.where(reached, a, b), new, before)

    return lax.fori_loop(0, devices, step, start)


def carried_in(value, axis, join, neutral):
    count = lax.axis_size(axis)
    place = lax.axis_index(axis)
    ahead = count - 1 - place
    gathered = jax.tree.map(
        lambda a, kind: lax.all_gather(a.astype(kind), axis),
        value,
        jax.tree.map(lambda a: jnp.bfloat16 if a.dtype == jnp.float32 else a.dtype, value),
    )
    state = jax.tree.map(lambda a, e: jnp.zeros_like(a) + jnp.asarray(e, a.dtype), value, neutral)

    def one(step, state):
        source = count - 1 - step
        return join(
            state,
            jax.tree.map(
                lambda a, own: lax.dynamic_index_in_dim(a, source, 0, False).astype(own.dtype),
                gathered,
                value,
            ),
        )

    return lax.fori_loop(0, ahead, one, state)


def layer_norm(values, norm_gain, norm_bias):
    mean_value = jnp.mean(values, axis=-1, keepdims=True)
    centred = values - mean_value
    spread = jnp.mean(centred * centred, axis=-1, keepdims=True)
    return centred * lax.rsqrt(spread + EPSILON) * norm_gain + norm_bias


def segment_of(lengths, positions):
    rank = jnp.arange(lengths.shape[0])
    starts = jnp.sum(jnp.where(rank[:, None] > rank[None, :], lengths[None, :], 0), axis=1)
    later_flags = (positions[:, None] >= starts[None, 1:]).astype(jnp.int32)
    first_flags = jnp.any(positions[:, None] == starts[None, :], axis=1)
    return (jnp.sum(later_flags, axis=1), first_flags)


def mix_inputs(normed, received, mixes, keep_rows=None):
    previous = jnp.concatenate([received, normed[:-1]], axis=0) * keep_rows[:, None]
    return tuple((normed * factor + previous * (1.0 - factor) for factor in mixes))


def stretch_carry(
    logged_fading, starting_reward, attention_recurrence_memory, stretch_source_entries
):
    acceptor_entries, lookup_entries, payload_entries, piece_number, seg_before = (
        stretch_source_entries
    )
    span_len = acceptor_entries.shape[0]
    offsets = jnp.arange(span_len).astype(jnp.float32)
    growth = jnp.exp(offsets[:, None, None] * logged_fading)
    shrink = jnp.exp(-(offsets[:, None, None] + 1.0) * logged_fading)
    recept_grown = acceptor_entries * growth
    scores = jnp.einsum("thi,shi->hts", recept_grown, lookup_entries * shrink, precision=HIGH)
    allowed = (piece_number[:, None] == piece_number[None, :]) & (
        offsets[:, None] > offsets[None, :]
    )
    scores = jnp.where(allowed[None], scores, 0.0)
    diagonal_share = jnp.sum(acceptor_entries * starting_reward * lookup_entries, axis=-1)
    reaches = (piece_number == seg_before).astype(jnp.float32)
    result_entries = (
        jnp.einsum("hts,shj->thj", scores, payload_entries, precision=HIGH)
        + diagonal_share[:, :, None] * payload_entries
    )
    result_entries = result_entries + reaches[:, None, None] * jnp.einsum(
        "thi,hij->thj", recept_grown, attention_recurrence_memory, precision=HIGH
    )
    tail_decay = jnp.exp((span_len - 1.0 - offsets)[:, None, None] * logged_fading)
    last_same = (piece_number == piece_number[span_len - 1]).astype(jnp.float32)
    fresh_part = jnp.einsum(
        "shi,shj->hij",
        lookup_entries * tail_decay * last_same[:, None, None],
        payload_entries,
        precision=HIGH,
    )
    attention_recurrence_memory = (
        reaches[span_len - 1]
        * jnp.exp(span_len * logged_fading)[:, :, None]
        * attention_recurrence_memory
        + fresh_part
    )
    return (attention_recurrence_memory, result_entries)


def attention_recurrence_results(
    acceptor_entries,
    lookup_entries,
    payload_entries,
    fading_coefficient,
    starting_reward,
    arriving_memory,
    piece_number=None,
    prior_stretch=None,
):
    resident_entries, head_count, head_size = acceptor_entries.shape
    blocks = resident_entries // SPAN
    logged_fading = -jnp.exp(fading_coefficient)
    stretch_source_entries = (
        acceptor_entries.reshape(blocks, SPAN, head_count, head_size),
        lookup_entries.reshape(blocks, SPAN, head_count, head_size),
        payload_entries.reshape(blocks, SPAN, head_count, head_size),
        piece_number.reshape(blocks, SPAN),
        prior_stretch,
    )
    closing_memory, result_entries = lax.scan(
        partial(stretch_carry, logged_fading, starting_reward),
        arriving_memory,
        stretch_source_entries,
    )
    return result_entries.reshape(resident_entries, head_count * head_size)


def wkv_summary(
    lookup_entries, payload_entries, fading_coefficient, piece_number=None, seg_lead=None
):
    resident_entries = lookup_entries.shape[0]
    logged_fading = -jnp.exp(fading_coefficient)
    offsets = jnp.arange(resident_entries).astype(jnp.float32)
    tail_decay = jnp.exp((resident_entries - 1.0 - offsets)[:, None, None] * logged_fading)
    last_same = (piece_number == piece_number[resident_entries - 1]).astype(jnp.float32)
    total_map = jnp.einsum(
        "shi,shj->hij",
        lookup_entries * tail_decay * last_same[:, None, None],
        payload_entries,
        precision=HIGH,
    )
    carried = (piece_number[resident_entries - 1] == seg_lead).astype(jnp.float32)
    return (total_map, carried * jnp.exp(resident_entries * logged_fading))


def compose(earlier, later):
    return (later[0] * earlier[0], later[0][:, :, None] * earlier[1] + later[1])


def norm_gate(attention_recurrence_entries, gate_pre, norm_gain, norm_bias):
    resident_entries = attention_recurrence_entries.shape[0]
    grouped = attention_recurrence_entries.reshape(resident_entries, -1, ATTENDER_WIDTH)
    mean_value = jnp.mean(grouped, axis=-1, keepdims=True)
    centred = grouped - mean_value
    spread = jnp.mean(centred * centred, axis=-1, keepdims=True)
    normed = (centred * lax.rsqrt(spread + GROUP_EPSILON)).reshape(resident_entries, -1)
    return (normed * norm_gain + norm_bias) * jax.nn.silu(gate_pre)


def project(rows_b, weight):
    return jnp.dot(rows_b, weight, preferred_element_type=jnp.float32)


def weight_grad(left_rows, right_rows):
    return lax.dot_general(
        left_rows, right_rows, (((0,), (0,)), ((), ())), preferred_element_type=jnp.float32
    )


def input_grad(grad_rows, weight):
    return lax.dot_general(
        grad_rows, weight, (((1,), (1,)), ((), ())), preferred_element_type=jnp.float32
    )


def shards(
    tokens,
    seq_lengths,
    out_grad,
    w_receptance,
    w_key,
    w_value,
    w_gate,
    w_output,
    ffn_key,
    ffn_receptance,
    ffn_value,
    vectors,
):
    inputs_f = tokens[0].astype(jnp.float32)
    resident_entries = inputs_f.shape[0]
    width = inputs_f.shape[1]
    lengths = seq_lengths[0]
    start_pos = lax.axis_index("seq") * resident_entries
    positions = start_pos + jnp.arange(resident_entries, dtype=jnp.int32)
    piece_number, first_flags = segment_of(lengths, positions)
    keep_rows = 1.0 - first_flags.astype(jnp.float32)
    span_starts = start_pos + jnp.arange(resident_entries // SPAN, dtype=jnp.int32) * SPAN - 1
    prior_stretch = segment_of(lengths, span_starts)[0]
    seg_lead = segment_of(lengths, jnp.reshape(start_pos - 1, (1,)))[0][0]
    gathered = (
        lax.all_gather(w_receptance, ("seq", "dp"), axis=0, tiled=True),
        lax.all_gather(w_key, ("seq", "dp"), axis=0, tiled=True),
        lax.all_gather(w_value, ("seq", "dp"), axis=0, tiled=True),
        lax.all_gather(w_gate, ("seq", "dp"), axis=0, tiled=True),
        lax.all_gather(w_output, ("seq", "dp"), axis=0, tiled=True),
        lax.all_gather(vectors, ("seq", "dp"), axis=1, tiled=True),
    )
    full_r, full_k, full_v, full_g, full_o, full_vec = gathered
    single_real_array = full_vec.astype(jnp.float32)
    normed, ln_one_pull = jax.vjp(layer_norm, inputs_f, single_real_array[0], single_real_array[1])
    received = passed_along(normed[resident_entries - 1 :], "seq", 1)
    mixes_one = (
        single_real_array[2],
        single_real_array[3],
        single_real_array[4],
        single_real_array[5],
    )
    (mix_r, mix_k, mix_v, mix_g), mix_one_pull = jax.vjp(
        partial(mix_inputs, keep_rows=keep_rows), normed, received, mixes_one
    )
    mix_r_b = mix_r.astype(jnp.bfloat16)
    mix_k_b = mix_k.astype(jnp.bfloat16)
    mix_v_b = mix_v.astype(jnp.bfloat16)
    mix_g_b = mix_g.astype(jnp.bfloat16)
    acceptor_mapping = (
        project(mix_r_b, full_r)
        .astype(jnp.bfloat16)
        .astype(jnp.float32)
        .reshape(resident_entries, -1, ATTENDER_WIDTH)
    )
    lookup_mapping = (
        project(mix_k_b, full_k)
        .astype(jnp.bfloat16)
        .astype(jnp.float32)
        .reshape(resident_entries, -1, ATTENDER_WIDTH)
    )
    payload_mapping = (
        project(mix_v_b, full_v)
        .astype(jnp.bfloat16)
        .astype(jnp.float32)
        .reshape(resident_entries, -1, ATTENDER_WIDTH)
    )
    gate_pre = project(mix_g_b, full_g)
    fading_coefficient = single_real_array[6].reshape(-1, ATTENDER_WIDTH)
    starting_reward = single_real_array[7].reshape(-1, ATTENDER_WIDTH)
    (total_map, carry_decay), summary_pull = jax.vjp(
        partial(wkv_summary, piece_number=piece_number, seg_lead=seg_lead),
        lookup_mapping,
        payload_mapping,
        fading_coefficient,
    )
    head_count = fading_coefficient.shape[0]
    identity = (
        jnp.ones((head_count, ATTENDER_WIDTH), jnp.float32),
        jnp.zeros((head_count, ATTENDER_WIDTH, ATTENDER_WIDTH), jnp.float32),
    )
    arriving_memory = entering((carry_decay, total_map), "seq", compose, identity)[1]
    attention_recurrence_entries, weighted_key_value_pullback = jax.vjp(
        partial(
            attention_recurrence_results, piece_number=piece_number, prior_stretch=prior_stretch
        ),
        acceptor_mapping,
        lookup_mapping,
        payload_mapping,
        fading_coefficient,
        starting_reward,
        arriving_memory,
    )
    gated, gate_pull = jax.vjp(
        norm_gate,
        attention_recurrence_entries,
        gate_pre,
        single_real_array[8],
        single_real_array[9],
    )
    mixed_b = gated.astype(jnp.bfloat16)
    after = inputs_f + project(mixed_b, full_o)
    full_ck, full_cr, full_cv = (
        lax.all_gather(ffn_key, ("seq", "dp"), axis=0, tiled=True),
        lax.all_gather(ffn_receptance, ("seq", "dp"), axis=0, tiled=True),
        lax.all_gather(ffn_value, ("seq", "dp"), axis=0, tiled=True),
    )
    normed_two, ln_two_pull = jax.vjp(
        layer_norm, after, single_real_array[10], single_real_array[11]
    )
    received_two = passed_along(normed_two[resident_entries - 1 :], "seq", 1)
    (mix_k2, mix_r2), mix_two_pull = jax.vjp(
        partial(mix_inputs, keep_rows=keep_rows),
        normed_two,
        received_two,
        (single_real_array[12], single_real_array[13]),
    )
    mix_k2_b = mix_k2.astype(jnp.bfloat16)
    mix_r2_b = mix_r2.astype(jnp.bfloat16)
    key_pre = project(mix_k2_b, full_ck)
    smooth_part = jax.nn.softplus(key_pre)
    hidden_b = (smooth_part * smooth_part).astype(jnp.bfloat16)
    recept_pre = project(mix_r2_b, full_cr)
    value_pre = project(hidden_b, full_cv)
    sigmoid_part = jax.nn.sigmoid(recept_pre)
    out_rows = (after + sigmoid_part * value_pre).astype(jnp.bfloat16)
    full_ck, full_cr, full_cv = (
        lax.all_gather(ffn_key, ("seq", "dp"), axis=0, tiled=True),
        lax.all_gather(ffn_receptance, ("seq", "dp"), axis=0, tiled=True),
        lax.all_gather(ffn_value, ("seq", "dp"), axis=0, tiled=True),
    )
    cotangent = out_grad[0].astype(jnp.float32)
    d_value_b = (cotangent * sigmoid_part).astype(jnp.bfloat16)
    d_recept_two_b = (cotangent * value_pre * sigmoid_part * (1.0 - sigmoid_part)).astype(
        jnp.bfloat16
    )
    d_hidden = input_grad(d_value_b, full_cv)
    d_key_two_b = (d_hidden * 2.0 * smooth_part * jax.nn.sigmoid(key_pre)).astype(jnp.bfloat16)
    grad_cv = weight_grad(hidden_b, d_value_b)
    grad_ck = weight_grad(mix_k2_b, d_key_two_b)
    grad_cr = weight_grad(mix_r2_b, d_recept_two_b)
    d_mix_k2 = input_grad(d_key_two_b, full_ck)
    d_mix_r2 = input_grad(d_recept_two_b, full_cr)
    d_normed_two, d_received_two, d_mixes_two = mix_two_pull((d_mix_k2, d_mix_r2))
    d_last_two = passed_along(d_received_two, "seq", -1)
    d_normed_two = d_normed_two.at[resident_entries - 1].add(d_last_two[0])
    d_after_ln, d_gain_two, d_bias_two = ln_two_pull(d_normed_two)
    d_after = cotangent + d_after_ln
    full_r, full_k, full_v, full_g, full_o = (
        lax.all_gather(w_receptance, ("seq", "dp"), axis=0, tiled=True),
        lax.all_gather(w_key, ("seq", "dp"), axis=0, tiled=True),
        lax.all_gather(w_value, ("seq", "dp"), axis=0, tiled=True),
        lax.all_gather(w_gate, ("seq", "dp"), axis=0, tiled=True),
        lax.all_gather(w_output, ("seq", "dp"), axis=0, tiled=True),
    )
    d_attn_b = d_after.astype(jnp.bfloat16)
    grad_wo = weight_grad(mixed_b, d_attn_b)
    d_mixed = input_grad(d_attn_b, full_o)
    weighted_key_value_gradient, d_gate_pre, d_gn_gain, d_gn_bias = gate_pull(d_mixed)
    d_gate_b = d_gate_pre.astype(jnp.bfloat16)
    (
        receptance_gradient,
        first_keyed_gradient,
        first_valued_gradient,
        first_decay_gradient,
        reward_derivative,
        local_state_gradient,
    ) = weighted_key_value_pullback(weighted_key_value_gradient)
    grads_out = carried_in((carry_decay, local_state_gradient), "seq", compose, identity)[1]
    d_carry = jnp.sum(grads_out * arriving_memory, axis=-1)
    d_keyed_two, d_valued_two, d_decay_two = summary_pull((grads_out, d_carry))
    d_recept_b = receptance_gradient.reshape(resident_entries, width).astype(jnp.bfloat16)
    d_keyed_b = (
        (first_keyed_gradient + d_keyed_two).reshape(resident_entries, width).astype(jnp.bfloat16)
    )
    d_valued_b = (
        (first_valued_gradient + d_valued_two).reshape(resident_entries, width).astype(jnp.bfloat16)
    )
    grad_wr = weight_grad(mix_r_b, d_recept_b)
    grad_wk = weight_grad(mix_k_b, d_keyed_b)
    grad_wv = weight_grad(mix_v_b, d_valued_b)
    grad_wg = weight_grad(mix_g_b, d_gate_b)
    d_mix_r = input_grad(d_recept_b, full_r)
    d_mix_k = input_grad(d_keyed_b, full_k)
    d_mix_v = input_grad(d_valued_b, full_v)
    d_mix_g = input_grad(d_gate_b, full_g)
    d_normed, d_received, d_mixes_one = mix_one_pull((d_mix_r, d_mix_k, d_mix_v, d_mix_g))
    d_last = passed_along(d_received, "seq", -1)
    d_normed = d_normed.at[resident_entries - 1].add(d_last[0])
    d_inputs_ln, d_gain_one, d_bias_one = ln_one_pull(d_normed)
    tokens_grad = d_after + d_inputs_ln
    vector_rows = jnp.stack(
        [
            d_gain_one,
            d_bias_one,
            d_mixes_one[0],
            d_mixes_one[1],
            d_mixes_one[2],
            d_mixes_one[3],
            (first_decay_gradient + d_decay_two).reshape(-1),
            reward_derivative.reshape(-1),
            d_gn_gain,
            d_gn_bias,
            d_gain_two,
            d_bias_two,
            d_mixes_two[0],
            d_mixes_two[1],
        ],
        axis=0,
    )
    all_sums = (
        lax.psum_scatter(grad_wr, ("seq", "dp"), scatter_dimension=0, tiled=True),
        lax.psum_scatter(grad_wk, ("seq", "dp"), scatter_dimension=0, tiled=True),
        lax.psum_scatter(grad_wv, ("seq", "dp"), scatter_dimension=0, tiled=True),
        lax.psum_scatter(grad_wg, ("seq", "dp"), scatter_dimension=0, tiled=True),
        lax.psum_scatter(grad_wo, ("seq", "dp"), scatter_dimension=0, tiled=True),
        lax.psum_scatter(grad_ck, ("seq", "dp"), scatter_dimension=0, tiled=True),
        lax.psum_scatter(grad_cr, ("seq", "dp"), scatter_dimension=0, tiled=True),
        lax.psum_scatter(grad_cv, ("seq", "dp"), scatter_dimension=0, tiled=True),
        lax.psum_scatter(vector_rows, ("seq", "dp"), scatter_dimension=1, tiled=True),
    )
    sum_r, sum_k, sum_v, sum_g, sum_o, sum_ck, sum_cr, sum_cv, sum_vec = all_sums
    return (
        out_rows[None],
        tokens_grad[None],
        sum_r,
        sum_k,
        sum_v,
        sum_g,
        sum_o,
        sum_ck,
        sum_cr,
        sum_cv,
        sum_vec,
    )


def solution(mesh):
    return jax.shard_map(
        shards,
        mesh=mesh,
        in_specs=(
            P("dp", "seq", None),
            P("dp", None),
            P("dp", "seq", None),
            P(("seq", "dp"), None),
            P(("seq", "dp"), None),
            P(("seq", "dp"), None),
            P(("seq", "dp"), None),
            P(("seq", "dp"), None),
            P(("seq", "dp"), None),
            P(("seq", "dp"), None),
            P(("seq", "dp"), None),
            P(None, ("seq", "dp")),
        ),
        out_specs=(
            P("dp", "seq", None),
            P("dp", "seq", None),
            P(("seq", "dp"), None),
            P(("seq", "dp"), None),
            P(("seq", "dp"), None),
            P(("seq", "dp"), None),
            P(("seq", "dp"), None),
            P(("seq", "dp"), None),
            P(("seq", "dp"), None),
            P(("seq", "dp"), None),
            P(None, ("seq", "dp")),
        ),
        check_vma=False,
    )
```

```python
from functools import partial

import jax
import jax.numpy as jnp
from jax import lax
from jax.experimental import pallas as pl
from jax.experimental.pallas import tpu as pltpu
from jax.sharding import PartitionSpec as P

HEAD = 64
PAIR = 128
CHUNK = 128
EPSILON = 1e-05
GROUP_EPSILON = 1.0
BF = jnp.bfloat16
F32 = jnp.float32
NT = (((1,), (1,)), ((), ()))
TN = (((0,), (0,)), ((), ()))
NN = (((1,), (0,)), ((), ()))


def swap(value, axis, distance):
    size = lax.axis_size(axis)
    return lax.ppermute(value, axis, [(i, i ^ distance) for i in range(size)])


def gather_seq(part):
    size, here = lax.axis_size("seq"), lax.axis_index("seq")
    whole = jnp.zeros((size,) + part.shape, part.dtype)

    def put(whole, piece, distance, start=0):
        at = (here ^ distance, start) + (0,) * (part.ndim - 1)
        return lax.dynamic_update_slice(whole, piece[None], at)

    whole = put(whole, part, 0)
    if size == 4:
        half = part.shape[0] // 2
        one, two = swap(part, "seq", 1), swap(part, "seq", 2)
        low, high = swap(one[:half], "seq", 2), swap(two[half:], "seq", 1)
        whole = put(put(whole, one, 1), two, 2)
        return put(put(whole, low, 3), high, 3, half)
    for distance in range(1, size):
        whole = put(whole, swap(part, "seq", distance), distance)
    return whole


def scatter_seq(parts):
    size, here = lax.axis_size("seq"), lax.axis_index("seq")

    def take(distance):
        return lax.dynamic_index_in_dim(parts, here ^ distance, 0, False)

    own = take(0).astype(F32)
    if size == 4:
        far = take(3)
        half = far.shape[0] // 2
        low, high = swap(far[:half], "seq", 1), swap(far[half:], "seq", 2)
        one, two = take(1), take(2)
        two = jnp.concatenate([(two[:half].astype(F32) + low.astype(F32)).astype(BF), two[half:]], axis=0)
        one = jnp.concatenate([one[:half], (one[half:].astype(F32) + high.astype(F32)).astype(BF)], axis=0)
        return own + swap(one, "seq", 1).astype(F32) + swap(two, "seq", 2).astype(F32)
    for distance in range(1, size):
        own = own + swap(take(distance), "seq", distance).astype(F32)
    return own


def trade_seq(parts):
    size, here = lax.axis_size("seq"), lax.axis_index("seq")
    result = jnp.zeros_like(parts)
    for distance in range(size):
        piece = lax.dynamic_index_in_dim(parts, here ^ distance, 0, True)
        if distance:
            piece = swap(piece, "seq", distance)
        result = lax.dynamic_update_slice_in_dim(result, piece, here ^ distance, 0)
    return result


def bits_of(size):
    return [1 << b for b in range(size.bit_length() - 1)]


def gather_small(part):
    for axis in ("dp", "seq"):
        for bit in bits_of(lax.axis_size(axis)):
            other = swap(part, axis, bit)
            second = (lax.axis_index(axis) & bit) != 0
            part = jnp.concatenate(
                [jnp.where(second, other, part), jnp.where(second, part, other)], axis=0
            )
    return part


def scatter_small(parts):
    for axis in ("seq", "dp"):
        for bit in reversed(bits_of(lax.axis_size(axis))):
            half = parts.shape[0] // 2
            second = (lax.axis_index(axis) & bit) != 0
            low, high = parts[:half], parts[half:]
            parts = jnp.where(second, high, low) + swap(jnp.where(second, low, high), axis, bit)
    return parts[0]


def by_columns(weight):
    rows, columns = weight.shape
    size = lax.axis_size("seq")
    return trade_seq(weight.reshape(rows, size, columns // size).transpose(1, 0, 2))


def all_rows(parts):
    gathered = lax.all_gather(parts, "dp", axis=0)
    return gathered.transpose(1, 0, 2, 3).reshape(-1, parts.shape[-1])


def owners_rows(grad):
    seq, dp = lax.axis_size("seq"), lax.axis_size("dp")
    rows, columns = grad.shape[0] // (seq * dp), grad.shape[1]
    parts = grad.astype(BF).reshape(seq, dp, rows, columns).transpose(1, 0, 2, 3).reshape(-1, columns)
    summed = lax.psum_scatter(parts, "dp", scatter_dimension=0, tiled=True).reshape(seq, rows, columns)
    return trade_seq(summed).transpose(1, 0, 2).reshape(rows, seq * columns).astype(F32)


def head_masks():
    lane = lax.broadcasted_iota(jnp.int32, (1, PAIR), 1)
    first = (lane < HEAD).astype(F32)
    return first, 1.0 - first


def same_head():
    row = lax.broadcasted_iota(jnp.int32, (PAIR, PAIR), 0) < HEAD
    column = lax.broadcasted_iota(jnp.int32, (PAIR, PAIR), 1) < HEAD
    return row == column


def dot(left, right, dims):
    return lax.dot_general(left, right, dims, preferred_element_type=F32)


def head_sum(values, ones):
    return dot(values.astype(BF), ones, NN)


def head_sum_fine(values, ones):
    coarse = values.astype(BF)
    rest = (values - coarse.astype(F32)).astype(BF)
    return dot(coarse, ones, NN) + dot(rest, ones, NN)


def stacked(values, first, second):
    return jnp.concatenate([(values * first).astype(BF), (values * second).astype(BF)], axis=0)


def masks_of(rows_ref, columns_ref):
    segment = rows_ref[:, 0:1]
    reaches = rows_ref[:, 1:2]
    last_same = rows_ref[:, 2:3]
    reach_last = rows_ref[CHUNK - 1 : CHUNK, 1:2]
    before = lax.broadcasted_iota(jnp.int32, (CHUNK, CHUNK), 1) < lax.broadcasted_iota(
        jnp.int32, (CHUNK, CHUNK), 0
    )
    allowed = jnp.where((segment == columns_ref[0:1, :]) & before, 1.0, 0.0)
    return reaches, last_same, reach_last, jnp.concatenate([allowed, allowed], axis=0)


def wkv_forward_body(
    r_ref, k_ref, v_ref, g_ref, rows_ref, columns_ref, grow_ref, shrink_ref, tail_ref, par_ref,
    mixed_ref, wkv_ref, states_ref, state,
):
    @pl.when(pl.program_id(0) == 0)
    def _():
        state[...] = jnp.zeros_like(state)

    first, second = head_masks()
    block = same_head()
    ones = jnp.where(block, 1.0, 0.0).astype(BF)
    reaches, last_same, reach_last, allowed = masks_of(rows_ref, columns_ref)
    for pair in range(r_ref.shape[1] // PAIR):
        at = slice(pair * PAIR, (pair + 1) * PAIR)
        r, k, v = r_ref[:, at].astype(F32), k_ref[:, at].astype(F32), v_ref[:, at].astype(F32)
        bonus, gain, bias, decay = (par_ref[i : i + 1, at] for i in range(4))
        held = state[at, :]
        held_b = held.astype(BF)
        states_ref[0, at, :] = held_b
        grown = r * grow_ref[:, at]
        shrunk = (k * shrink_ref[:, at]).astype(BF)
        scores = (dot(stacked(grown, first, second), shrunk, NT) * allowed).astype(BF)
        both = jnp.concatenate([scores[:CHUNK], scores[CHUNK:]], axis=1)
        wkv = dot(both, stacked(v, first, second), NN)
        wkv = wkv + dot((grown * reaches).astype(BF), held_b, NT)
        wkv = wkv + head_sum(r * bonus * k, ones) * v
        fresh = dot(v_ref[:, at], (k * tail_ref[:, at] * last_same).astype(BF), TN)
        state[at, :] = held * (decay * reach_last) + jnp.where(block, fresh, 0.0)
        wkv_ref[:, at] = wkv
        centred = wkv - head_sum_fine(wkv, ones) * (1.0 / HEAD)
        spread = head_sum(centred * centred, ones) * (1.0 / HEAD)
        normed = centred * lax.rsqrt(spread + GROUP_EPSILON) * gain + bias
        gate = g_ref[:, at]
        mixed_ref[:, at] = (normed * (gate / (1.0 + jnp.exp(-gate)))).astype(BF)


def wkv_backward_body(
    r_ref, k_ref, v_ref, g_ref, wkv_ref, d_mixed_ref, states_ref,
    rows_ref, columns_ref, grow_ref, shrink_ref, tail_ref, par_ref,
    d_r_ref, d_k_ref, d_v_ref, d_g_ref, sums_ref, d_state,
):
    @pl.when(pl.program_id(0) == 0)
    def _():
        d_state[...] = jnp.zeros_like(d_state)
        sums_ref[...] = jnp.zeros_like(sums_ref)

    first, second = head_masks()
    block = same_head()
    ones = jnp.where(block, 1.0, 0.0).astype(BF)
    reaches, last_same, reach_last, allowed = masks_of(rows_ref, columns_ref)
    offset = lax.broadcasted_iota(jnp.int32, (CHUNK, PAIR), 0).astype(F32)
    for pair in range(r_ref.shape[1] // PAIR):
        at = slice(pair * PAIR, (pair + 1) * PAIR)
        bonus, gain, bias, decay = (par_ref[i : i + 1, at] for i in range(4))
        wkv, gate, d_mixed = wkv_ref[:, at], g_ref[:, at], d_mixed_ref[:, at]
        centred = wkv - head_sum_fine(wkv, ones) * (1.0 / HEAD)
        spread = head_sum(centred * centred, ones) * (1.0 / HEAD)
        inverse = lax.rsqrt(spread + GROUP_EPSILON)
        normed = centred * inverse
        opened = 1.0 / (1.0 + jnp.exp(-gate))
        d_scaled = d_mixed * gate * opened
        d_g = d_mixed * (normed * gain + bias) * opened * (1.0 + gate * (1.0 - opened))
        d_g_ref[:, at] = d_g.astype(BF)
        d_normed = d_scaled * gain
        mean_one = head_sum(d_normed, ones) * (1.0 / HEAD)
        mean_two = head_sum(d_normed * normed, ones) * (1.0 / HEAD)
        d_wkv = inverse * (d_normed - mean_one - normed * mean_two)
        r, k, v = r_ref[:, at].astype(F32), k_ref[:, at].astype(F32), v_ref[:, at].astype(F32)
        v_b, d_wkv_b = v_ref[:, at], d_wkv.astype(BF)
        grow, shrink, tail = grow_ref[:, at], shrink_ref[:, at], tail_ref[:, at] * last_same
        held = states_ref[0, at, :]
        later = d_state[at, :]
        later_b = later.astype(BF)
        grown = r * grow
        shrunk = k * shrink
        shrunk_b = shrunk.astype(BF)
        tailed_b = (k * tail).astype(BF)
        grown_two = stacked(grown, first, second)
        d_wkv_two = stacked(d_wkv, first, second)
        scores = (dot(grown_two, shrunk_b, NT) * allowed).astype(BF)
        d_scores = (dot(d_wkv_two, v_b, NT) * allowed).astype(BF)
        d_both = jnp.concatenate([d_scores[:CHUNK], d_scores[CHUNK:]], axis=1)
        d_grown = dot(d_both, stacked(shrunk, first, second), NN)
        d_grown = d_grown + dot((d_wkv * reaches).astype(BF), held, NN)
        d_shrunk = dot(d_scores, grown_two, TN)
        d_tailed = dot(v_b, later_b, NN)
        share = head_sum(r * bonus * k, ones)
        d_share = head_sum(d_wkv * v, ones)
        d_v = dot(scores, d_wkv_two, TN) + dot(tailed_b, later_b, NT) + share * d_wkv
        d_r_ref[:, at] = (d_grown * grow + d_share * bonus * k).astype(BF)
        d_k_ref[:, at] = (d_shrunk * shrink + d_tailed * tail + d_share * bonus * r).astype(BF)
        d_v_ref[:, at] = d_v.astype(BF)
        carried = decay * reach_last
        d_fresh = dot(d_wkv_b, (grown * reaches).astype(BF), TN)
        d_state[at, :] = later * carried + jnp.where(block, d_fresh, 0.0)
        grown_b = grown.astype(BF).astype(F32)
        d_log = (
            offset * grown_b * d_grown
            - (offset + 1.0) * shrunk_b.astype(F32) * d_shrunk
            + (CHUNK - 1.0 - offset) * tailed_b.astype(F32) * d_tailed
        )
        kept = CHUNK * carried * jnp.sum(held.astype(F32) * later, axis=0, keepdims=True)
        sums_ref[0:1, at] += jnp.sum(d_log, axis=0, keepdims=True) + kept
        sums_ref[1:2, at] += jnp.sum(d_share * r * k, axis=0, keepdims=True)
        sums_ref[2:3, at] += jnp.sum(d_scaled * normed, axis=0, keepdims=True)
        sums_ref[3:4, at] += jnp.sum(d_scaled, axis=0, keepdims=True)


def wkv_specs(width, chunks, backward):
    def chunk(i):
        return chunks - 1 - i if backward else i

    tokens = pl.BlockSpec((CHUNK, width), lambda i: (chunk(i), 0))
    states = pl.BlockSpec((1, width, PAIR), lambda i: (chunk(i), 0, 0))
    rows = pl.BlockSpec((CHUNK, PAIR), lambda i: (chunk(i), 0))
    columns = pl.BlockSpec((8, CHUNK), lambda i: (0, chunk(i)))
    table = pl.BlockSpec((CHUNK, width), lambda i: (0, 0))
    params = pl.BlockSpec((8, width), lambda i: (0, 0))
    return tokens, states, [rows, columns, table, table, table, params], params


def wkv_forward(r, k, v, gate, tables):
    length, width = r.shape
    chunks = length // CHUNK
    tokens, states, fixed, _ = wkv_specs(width, chunks, False)
    return pl.pallas_call(
        wkv_forward_body,
        grid=(chunks,),
        in_specs=[tokens] * 4 + fixed,
        out_specs=[tokens, tokens, states],
        out_shape=[
            jax.ShapeDtypeStruct((length, width), BF),
            jax.ShapeDtypeStruct((length, width), F32),
            jax.ShapeDtypeStruct((chunks, width, PAIR), BF),
        ],
        scratch_shapes=[pltpu.VMEM((width, PAIR), F32)],
        compiler_params=pltpu.CompilerParams(vmem_limit_bytes=40 * 2**20),
        name="wkv_forward",
    )(r, k, v, gate, *tables)


def wkv_backward(r, k, v, gate, wkv, d_mixed, states_kept, tables):
    length, width = r.shape
    chunks = length // CHUNK
    tokens, states, fixed, params = wkv_specs(width, chunks, True)
    return pl.pallas_call(
        wkv_backward_body,
        grid=(chunks,),
        in_specs=[tokens] * 6 + [states] + fixed,
        out_specs=[tokens] * 4 + [params],
        out_shape=[jax.ShapeDtypeStruct((length, width), BF)] * 4
        + [jax.ShapeDtypeStruct((8, width), F32)],
        scratch_shapes=[pltpu.VMEM((width, PAIR), F32)],
        compiler_params=pltpu.CompilerParams(vmem_limit_bytes=40 * 2**20),
        name="wkv_backward",
    )(r, k, v, gate, wkv, d_mixed, states_kept, *tables)


def wkv_tables(piece, log_decay, bonus, gain, bias):
    length, width = piece.shape[0], log_decay.shape[0]
    chunks = length // CHUNK
    by_chunk = piece.reshape(chunks, CHUNK)
    before = jnp.concatenate([jnp.full((1,), -1, piece.dtype), by_chunk[:-1, -1]])
    reaches = (by_chunk == before[:, None]).reshape(-1)
    last_same = (by_chunk == by_chunk[:, -1:]).reshape(-1)
    marks = jnp.stack([piece.astype(F32), reaches.astype(F32), last_same.astype(F32)], axis=1)
    rows = jnp.pad(marks, ((0, 0), (0, PAIR - 3)))
    columns = jnp.broadcast_to(piece.astype(F32)[None], (8, length))
    offset = jnp.arange(CHUNK).astype(F32)[:, None]
    grow = jnp.exp(offset * log_decay)
    shrink = jnp.exp(-(offset + 1.0) * log_decay)
    tail = jnp.exp((CHUNK - 1.0 - offset) * log_decay)
    zero = jnp.zeros_like(bonus)
    params = jnp.stack([bonus, gain, bias, jnp.exp(CHUNK * log_decay)] + [zero] * 4)
    return rows, columns, grow, shrink, tail, params


def layer_norm(values, norm_gain, norm_bias):
    mean_value = jnp.mean(values, axis=-1, keepdims=True)
    centred = values - mean_value
    spread = jnp.mean(centred * centred, axis=-1, keepdims=True)
    return centred * lax.rsqrt(spread + EPSILON) * norm_gain + norm_bias


def segment_of(lengths, positions):
    rank = jnp.arange(lengths.shape[0])
    starts = jnp.sum(jnp.where(rank[:, None] > rank[None, :], lengths[None, :], 0), axis=1)
    later_flags = (positions[:, None] >= starts[None, 1:]).astype(jnp.int32)
    first_flags = jnp.any(positions[:, None] == starts[None, :], axis=1)
    return (jnp.sum(later_flags, axis=1), first_flags)


def before(values, keep):
    return jnp.concatenate([jnp.zeros_like(values[:1]), values[:-1]], axis=0) * keep


def to_before(values, keep):
    kept = values * keep
    return jnp.concatenate([kept[1:], jnp.zeros_like(kept[:1])], axis=0)


def mix(values, previous, factor):
    return (values * factor + previous * (1.0 - factor)).astype(BF)


def project(rows_b, weight):
    return dot(rows_b, weight, NN)


def weight_grad(left_rows, right_rows):
    return dot(left_rows, right_rows, TN)


def input_grad(grad_rows, weight):
    return dot(grad_rows, weight, NT)


def shards(
    tokens, seq_lengths, out_grad, w_receptance, w_key, w_value, w_gate, w_output,
    ffn_key, ffn_receptance, ffn_value, vectors,
):
    seq = lax.axis_size("seq")
    here = lax.axis_index("seq")
    inputs_b, grad_b = tokens[0], out_grad[0]
    own_rows, width = inputs_b.shape
    length = own_rows * seq
    part = width // seq

    def own_columns(values):
        return lax.dynamic_slice_in_dim(values, here * part, part, 1)

    def whole(values):
        return gather_seq(values).reshape(length, width)

    positions = jnp.arange(length, dtype=jnp.int32)
    piece, first_flags = segment_of(seq_lengths[0], positions)
    keep = 1.0 - first_flags.astype(F32)[:, None]

    vec = gather_small(vectors[None]).transpose(1, 0, 2).reshape(vectors.shape[0], width).astype(F32)
    vec_own = own_columns(vec)
    tokens_all = whole(inputs_b)
    projections = jnp.stack([by_columns(w) for w in (w_receptance, w_key, w_value, w_gate)], axis=1)
    gathered = lax.all_gather(projections, "dp", axis=0)
    full_r, full_k, full_v, full_g = (
        gathered[:, :, i].transpose(1, 0, 2, 3).reshape(width, part) for i in range(4)
    )
    full_o = lax.all_gather(w_output, "dp", axis=0, tiled=True)
    grad_all = whole(grad_b)
    ffn_columns = jnp.concatenate([by_columns(ffn_key), by_columns(ffn_receptance)], axis=2)
    full_c = all_rows(ffn_columns)
    hidden_width = ffn_key.shape[1] // seq
    full_ck, full_cr = full_c[:, :hidden_width], full_c[:, hidden_width:]
    full_cv = lax.all_gather(ffn_value, "dp", axis=0, tiled=True)

    normed = layer_norm(tokens_all.astype(F32), vec[0], vec[1])
    previous = before(normed, keep)
    mix_r, mix_k, mix_v, mix_g = (mix(normed, previous, vec[i]) for i in (2, 3, 4, 5))
    recept = project(mix_r, full_r).astype(BF)
    keyed = project(mix_k, full_k).astype(BF)
    valued = project(mix_v, full_v).astype(BF)
    gate_pre = project(mix_g, full_g)
    log_decay = -jnp.exp(vec_own[6])
    tables = wkv_tables(piece, log_decay, vec_own[7], vec_own[8], vec_own[9])
    mixed, wkv, states = wkv_forward(recept, keyed, valued, gate_pre, tables)
    attn = project(mixed, full_o).astype(BF).reshape(seq, own_rows, width)
    inputs_f = inputs_b.astype(F32)
    after = inputs_f + scatter_seq(attn)

    normed_two, norm_two_pull = jax.vjp(layer_norm, after, vec[10], vec[11])
    normed_two = whole(normed_two.astype(BF)).astype(F32)
    previous_two = before(normed_two, keep)
    mix_k2, mix_r2 = mix(normed_two, previous_two, vec[12]), mix(normed_two, previous_two, vec[13])
    opened = jax.nn.sigmoid(project(mix_r2, full_cr))
    opened_all = gather_seq(opened.astype(BF))
    key_pre = project(mix_k2, full_ck)
    smooth = jax.nn.softplus(key_pre)
    hidden = (smooth * smooth).astype(BF)
    value_parts = project(hidden, full_cv).astype(BF).reshape(length, seq, part).transpose(1, 0, 2)
    value_pre = scatter_seq(value_parts)
    channel = trade_seq((opened * value_pre).astype(BF).reshape(seq, own_rows, part))
    out_rows = (after + channel.transpose(1, 0, 2).reshape(own_rows, width).astype(F32)).astype(BF)

    d_value = (
        (grad_all.reshape(length, seq, part).astype(F32) * opened_all.transpose(1, 0, 2).astype(F32))
        .astype(BF)
        .reshape(length, width)
    )
    d_recept_two = (
        own_columns(grad_all).astype(F32) * value_pre * opened * (1.0 - opened)
    ).astype(BF)
    d_hidden = input_grad(d_value, full_cv)
    d_key_two = (d_hidden * 2.0 * smooth * jax.nn.sigmoid(key_pre)).astype(BF)
    d_mix_k2 = input_grad(d_key_two, full_ck)
    d_mix_r2 = input_grad(d_recept_two, full_cr)
    step_two = normed_two - previous_two
    d_normed_two = (
        d_mix_k2 * vec[12]
        + d_mix_r2 * vec[13]
        + to_before(d_mix_k2 * (1.0 - vec[12]) + d_mix_r2 * (1.0 - vec[13]), keep)
    )
    d_mixes_two = [jnp.sum(d * step_two, axis=0) for d in (d_mix_k2, d_mix_r2)]
    d_normed_two = scatter_seq(d_normed_two.astype(BF).reshape(seq, own_rows, width))
    grad_cv = weight_grad(hidden, d_value)
    grad_ck = weight_grad(mix_k2, d_key_two)
    grad_cr = weight_grad(mix_r2, d_recept_two)
    d_after_norm, d_gain_two, d_bias_two = norm_two_pull(d_normed_two)
    d_after = grad_b.astype(F32) + d_after_norm

    d_attn = whole(d_after.astype(BF))
    d_mixed = input_grad(d_attn, full_o)
    grad_wo = weight_grad(mixed, d_attn)
    d_recept, d_keyed, d_valued, d_gate, sums = wkv_backward(
        recept, keyed, valued, gate_pre, wkv, d_mixed, states, tables
    )
    d_mix = [
        input_grad(d, w)
        for d, w in ((d_recept, full_r), (d_keyed, full_k), (d_valued, full_v), (d_gate, full_g))
    ]
    step = normed - previous
    d_normed = sum(d * vec[2 + i] for i, d in enumerate(d_mix)) + to_before(
        sum(d * (1.0 - vec[2 + i]) for i, d in enumerate(d_mix)), keep
    )
    d_mixes = [jnp.sum(d * step, axis=0) for d in d_mix]
    d_normed = scatter_seq(d_normed.astype(BF).reshape(seq, own_rows, width))
    grads_in = (
        weight_grad(mix_r, d_recept),
        weight_grad(mix_k, d_keyed),
        weight_grad(mix_v, d_valued),
        weight_grad(mix_g, d_gate),
    )
    _, norm_pull = jax.vjp(layer_norm, inputs_f, vec[0], vec[1])
    d_inputs, d_gain_one, d_bias_one = norm_pull(d_normed)
    tokens_grad = d_after + d_inputs

    own_sums = jnp.stack([sums[0] * log_decay, sums[1], sums[2], sums[3]])
    placed = lax.dynamic_update_slice(jnp.zeros((4, width), F32), own_sums, (0, here * part))
    vector_rows = jnp.concatenate(
        [
            jnp.stack([d_gain_one, d_bias_one] + d_mixes),
            placed,
            jnp.stack([d_gain_two, d_bias_two] + d_mixes_two),
        ]
    )
    rows = vector_rows.shape[0]
    sum_vec = scatter_small(vector_rows.reshape(rows, -1, vectors.shape[1]).transpose(1, 0, 2))

    def natural(grad):
        return lax.psum_scatter(grad.astype(BF), "dp", scatter_dimension=0, tiled=True).astype(F32)

    sum_cv = natural(grad_cv)
    sum_c = owners_rows(jnp.concatenate([grad_ck, grad_cr], axis=1))
    own = sum_c.reshape(sum_c.shape[0], seq, hidden_width + part)
    sum_ck = own[:, :, :hidden_width].reshape(ffn_key.shape)
    sum_cr = own[:, :, hidden_width:].reshape(ffn_receptance.shape)
    sum_o = natural(grad_wo)
    sum_in = owners_rows(jnp.concatenate(grads_in, axis=1)).reshape(-1, seq, 4, part)
    sum_r, sum_k, sum_v, sum_g = (sum_in[:, :, i].reshape(w_key.shape) for i in range(4))
    return (
        out_rows[None], tokens_grad[None], sum_r, sum_k, sum_v, sum_g, sum_o,
        sum_ck, sum_cr, sum_cv, sum_vec,
    )


def solution(mesh):
    tokens = P("dp", "seq", None)
    rows = P(("seq", "dp"), None)
    columns = P(None, ("seq", "dp"))
    return jax.shard_map(
        shards,
        mesh=mesh,
        in_specs=(tokens, P("dp", None), tokens) + (rows,) * 8 + (columns,),
        out_specs=(tokens, tokens) + (rows,) * 8 + (columns,),
        check_vma=False,
    )
```

```python
from functools import partial

import jax
import jax.numpy as jnp
from jax import lax
from jax.experimental import pallas as pl
from jax.experimental.pallas import tpu as pltpu
from jax.sharding import PartitionSpec as P

HEAD = 64
PAIR = 128
CHUNK = 128
EPSILON = 1e-05
GROUP_EPSILON = 1.0
BF = jnp.bfloat16
F32 = jnp.float32
NT = (((1,), (1,)), ((), ()))
TN = (((0,), (0,)), ((), ()))
NN = (((1,), (0,)), ((), ()))


def swap(value, axis, distance):
    size = lax.axis_size(axis)
    return lax.ppermute(value, axis, [(i, i ^ distance) for i in range(size)])


def gather_seq(part):
    size = lax.axis_size("seq")
    if size == 4:
        half = part.shape[0] // 2
        one, two = swap(part, "seq", 1), swap(part, "seq", 2)
        low, high = swap(one[:half], "seq", 2), swap(two[half:], "seq", 1)
        return [part, one, two, jnp.concatenate([low, high], axis=0)]
    return [part] + [swap(part, "seq", distance) for distance in range(1, size)]


def scatter_seq(parts):
    size = lax.axis_size("seq")
    if size == 4:
        own, one, two, far = parts
        half = far.shape[0] // 2
        low, high = swap(far[:half], "seq", 1), swap(far[half:], "seq", 2)
        two = jnp.concatenate([(two[:half].astype(F32) + low.astype(F32)).astype(BF), two[half:]], axis=0)
        one = jnp.concatenate([one[:half], (one[half:].astype(F32) + high.astype(F32)).astype(BF)], axis=0)
        return [own, swap(one, "seq", 1), swap(two, "seq", 2)]
    return [parts[0]] + [swap(parts[distance], "seq", distance) for distance in range(1, size)]


def trade_seq(parts):
    return [parts[0]] + [swap(part, "seq", j + 1) for j, part in enumerate(parts[1:])]


def blocks_of(values, size):
    rows = values.shape[0] // size
    return [values[j * rows : (j + 1) * rows] for j in range(size)]


def bits_of(size):
    return [1 << b for b in range(size.bit_length() - 1)]


def gather_small(part, axis):
    for bit in bits_of(lax.axis_size(axis)):
        other = swap(part, axis, bit)
        second = (lax.axis_index(axis) & bit) != 0
        part = jnp.concatenate([jnp.where(second, other, part), jnp.where(second, part, other)], axis=0)
    return part


def scatter_small(parts):
    for axis in ("seq", "dp"):
        for bit in reversed(bits_of(lax.axis_size(axis))):
            half = parts.shape[0] // 2
            second = (lax.axis_index(axis) & bit) != 0
            low, high = parts[:half], parts[half:]
            parts = jnp.where(second, high, low) + swap(jnp.where(second, low, high), axis, bit)
    return parts[0]


def block(shape, index):
    return pl.BlockSpec(shape, lambda *i: index(*i[:-1], i[-1][0]))


def fixed(shape):
    return pl.BlockSpec(shape, lambda *i: (0,) * len(shape))


def relative(tile, per, here):
    return (lax.div(tile, per) ^ here) * per + lax.rem(tile, per)


def kernel(body, name, grid, here, ins, outs, scratch=(), vmem=48):
    return pl.pallas_call(
        body,
        out_shape=[jax.ShapeDtypeStruct(shape, kind) for shape, kind, _ in outs],
        grid_spec=pltpu.PrefetchScalarGridSpec(
            num_scalar_prefetch=1,
            grid=grid,
            in_specs=[spec for _, spec in ins],
            out_specs=[spec for _, _, spec in outs],
            scratch_shapes=list(scratch),
        ),
        compiler_params=pltpu.CompilerParams(vmem_limit_bytes=vmem * 2**20),
        name=name,
    )(here, *[array for array, _ in ins])


def row_index(rows):
    return lax.broadcasted_iota(jnp.int32, (rows, 1), 0)


def placed(place, width):
    return pl.ds(pl.multiple_of(place * width, width), width)


def cut_body(count, parts, here, *refs):
    ins, outs = refs[:count], refs[count:]
    at = 0
    for ref in ins:
        width = ref.shape[1] // parts
        for j in range(parts):
            outs[j][:, at : at + width] = ref[:, placed(here[0] ^ j, width)]
        at += width


def cut_columns(weights, here, parts):
    rows, width = weights[0].shape[0], sum(w.shape[1] for w in weights) // parts
    return kernel(
        partial(cut_body, len(weights), parts), "cut_columns", (1,), here,
        [(w, fixed(w.shape)) for w in weights],
        [((rows, width), BF, fixed((rows, width)))] * parts,
    )


def stack_body(parts, here, *refs):
    for j in range(parts):
        refs[-1][here[0] ^ j] = refs[j][...]


def stack_rows(pieces, here):
    parts, (rows, width) = len(pieces), pieces[0].shape
    (stacked,) = kernel(
        partial(stack_body, parts), "stack_rows", (1,), here,
        [(p, fixed(p.shape)) for p in pieces],
        [((parts, rows, width), BF, fixed((parts, rows, width)))],
    )
    return stacked


def join_body(parts, count, here, *refs):
    ins, outs = refs[:parts], refs[parts:]
    at = 0
    for ref in outs:
        width = ref.shape[1] // parts
        for j in range(parts):
            ref[:, placed(here[0] ^ j, width)] = ins[j][:, at : at + width].astype(F32)
        at += width


def join_columns(pieces, widths, here):
    parts, rows = len(pieces), pieces[0].shape[0]
    return kernel(
        partial(join_body, parts, len(widths)), "join_columns", (1,), here,
        [(p, fixed(p.shape)) for p in pieces],
        [((rows, width), F32, fixed((rows, width))) for width in widths],
    )


def spread_body(parts, product, here, base_ref, *refs):
    out = refs[-1]
    width = refs[0].shape[1]
    for j in range(parts):
        at = placed(here[0] ^ j, width)
        piece, base = refs[j][...].astype(F32), base_ref[:, at].astype(F32)
        out[:, at] = (base * piece if product else base + piece).astype(BF)


def spread_columns(base, pieces, here, product, turn, tile):
    rows, width = base.shape
    (result,) = kernel(
        partial(spread_body, len(pieces), product), "spread_columns", (rows // tile,), here,
        [(base, block((tile, width), lambda i, h: (i, 0)))]
        + [(p, block((tile, p.shape[1]), lambda i, h, j=j: (i ^ j if turn else i, 0))) for j, p in enumerate(pieces)],
        [((rows, width), BF, block((tile, width), lambda i, h: (i, 0)))],
    )
    return result


def shuffled(values, groups, back=False):
    seq, dp = groups
    if back:
        seq, dp = dp, seq
    lane = lax.broadcasted_iota(jnp.int32, (1, PAIR), 1) < HEAD
    source = [s * dp + d for d in range(dp) for s in range(seq)]
    columns = []
    for one, two in zip(source[::2], source[1::2]):
        low = values[:, one // 2 * PAIR : (one // 2 + 1) * PAIR]
        high = values[:, two // 2 * PAIR : (two // 2 + 1) * PAIR]
        low = pltpu.roll(low, HEAD, 1) if one % 2 else low
        high = high if two % 2 else pltpu.roll(high, HEAD, 1)
        columns.append(jnp.where(lane, low, high))
    return jnp.concatenate(columns, axis=1)


def outside(values, groups, channels, back=False):
    seq, dp = groups[::-1] if back else groups
    return values.reshape(-1, seq, dp, channels).swapaxes(1, 2).reshape(values.shape)


def centre(values):
    centred = values - jnp.mean(values, axis=-1, keepdims=True)
    spread = jnp.mean(centred * centred, axis=-1, keepdims=True)
    return centred, lax.rsqrt(spread + EPSILON)


def mix_body(count, norm, groups, here, x_ref, marks_ref, vec_ref, *refs):
    outs, last = refs[:-1], refs[-1]

    @pl.when(pl.program_id(0) == 0)
    def _():
        last[...] = jnp.zeros_like(last)

    values = x_ref[...].astype(F32)
    if norm:
        centred, inverse = centre(values)
        values = centred * inverse
    if groups:
        values = shuffled(values, groups)
    if norm:
        values = values * vec_ref[0:1, :] + vec_ref[1:2, :]
    rows = values.shape[0]
    previous = jnp.where(row_index(rows) == 0, last[0:1, :], pltpu.roll(values, 1, 0)) * marks_ref[:, 3:4]
    last[0:1, :] = values[rows - 1 :, :]
    step = values - previous
    outs[count][...] = step.astype(BF)
    for i in range(count):
        outs[i][...] = (previous + step * vec_ref[2 + i : 3 + i, :]).astype(BF)


def mixes(values, marks, vec, count, norm, groups, here, per):
    rows, width = values.shape
    tile = CHUNK
    own = block((tile, width), lambda i, h: (relative(i, per, h), 0))
    return kernel(
        partial(mix_body, count, norm, groups), "mixes", (rows // tile,), here,
        [
            (values, own),
            (marks, block((tile, PAIR), lambda i, h: (i, 0))),
            (vec, fixed(vec.shape)),
        ],
        [((rows, width), BF, own)] * (count + 1),
        [pltpu.VMEM((8, width), F32)],
    )


def mixes_back_body(count, here, *refs):
    grads, weights = refs[:count], refs[count : 2 * count]
    step_ref, marks_ref, vec_ref, out_ref, sums_ref, later = refs[2 * count :]

    @pl.when(pl.program_id(1) == 0)
    def _():
        later[...] = jnp.zeros_like(later)
        sums_ref[...] = jnp.zeros_like(sums_ref)

    step = step_ref[...].astype(F32)
    for i in range(count):
        grad = dot(grads[i][...], weights[i][...], NT)
        sums_ref[i : i + 1, :] += jnp.sum(grad * step, axis=0, keepdims=True)
        part = grad * vec_ref[i : i + 1, :]
        total, straight = (total + grad, straight + part) if i else (grad, part)
    kept = (total - straight) * marks_ref[:, 3:4]
    rows = kept.shape[0]
    up = jnp.where(row_index(rows) == rows - 1, later[0:1, :], pltpu.roll(kept, rows - 1, 0))
    later[0:1, :] = kept[0:1, :]
    out_ref[...] = (straight + up).astype(BF)


def mixes_back(grads, weights, step, marks, vec, here, seq):
    rows, width = step.shape
    tile, columns, count = rows // seq, min(512, width), len(grads)
    last = rows // tile - 1

    def natural(i):
        return last - i

    ins = [(g, block((tile, g.shape[1]), lambda c, i, h: (relative(natural(i), 1, h), 0))) for g in grads]
    for g, (w, at) in zip(grads, weights):
        ins.append((w, pl.BlockSpec((columns, g.shape[1]), lambda c, i, h, at=at: (c, at))))
    ins += [
        (step, block((tile, columns), lambda c, i, h: (relative(natural(i), 1, h), c))),
        (marks, block((tile, PAIR), lambda c, i, h: (natural(i), 0))),
        (vec, block((8, columns), lambda c, i, h: (0, c))),
    ]
    return kernel(
        partial(mixes_back_body, count), "mixes_back", (width // columns, last + 1), here, ins,
        [
            ((rows, width), BF, block((tile, columns), lambda c, i, h: (relative(natural(i), 1, h), c))),
            ((8, width), F32, block((8, columns), lambda c, i, h: (0, c))),
        ],
        [pltpu.VMEM((8, columns), F32)],
    )


def after_body(count, here, x_ref, vec_ref, *refs):
    after_ref, normed_ref = refs[count:]
    after = x_ref[...].astype(F32)
    for ref in refs[:count]:
        after = after + ref[...].astype(F32)
    after_ref[...] = after
    centred, inverse = centre(after)
    normed_ref[...] = (centred * inverse * vec_ref[0:1, :] + vec_ref[1:2, :]).astype(BF)


def after_norm(inputs, terms, vec, here):
    rows, width = inputs.shape
    own = block((CHUNK, width), lambda i, h: (i, 0))
    return kernel(
        partial(after_body, len(terms)), "after_norm", (rows // CHUNK,), here,
        [(inputs, own), (vec, fixed(vec.shape))] + [(t, own) for t in terms],
        [((rows, width), F32, own), ((rows, width), BF, own)],
    )


def norm_back_body(count, groups, here, x_ref, base_ref, vec_ref, *refs):
    wide_ref, narrow_ref, sums_ref = refs[count:]

    @pl.when(pl.program_id(0) == 0)
    def _():
        sums_ref[...] = jnp.zeros_like(sums_ref)

    grad = refs[0][...].astype(F32)
    for ref in refs[1:count]:
        grad = grad + ref[...].astype(F32)
    if groups:
        grad = shuffled(grad, groups, back=True)
    centred, inverse = centre(x_ref[...].astype(F32))
    normed = centred * inverse
    sums_ref[0:1, :] += jnp.sum(grad * normed, axis=0, keepdims=True)
    sums_ref[1:2, :] += jnp.sum(grad, axis=0, keepdims=True)
    grad = grad * vec_ref[0:1, :]
    grad = grad - jnp.mean(grad, axis=-1, keepdims=True) - normed * jnp.mean(grad * normed, axis=-1, keepdims=True)
    result = base_ref[...].astype(F32) + inverse * grad
    wide_ref[...] = result
    narrow_ref[...] = result.astype(BF)


def norm_back(terms, inputs, base, vec, groups, here):
    rows, width = inputs.shape
    own = block((CHUNK, width), lambda i, h: (i, 0))
    return kernel(
        partial(norm_back_body, len(terms), groups), "norm_back", (rows // CHUNK,), here,
        [(inputs, own), (base, own), (vec, fixed(vec.shape))] + [(t, own) for t in terms],
        [((rows, width), F32, own), ((rows, width), BF, own), ((8, width), F32, fixed((8, width)))],
    )


def gate_body(mix_ref, weight_ref, wkv_ref, par_ref, gate_ref, mixed_ref):
    gate = dot(mix_ref[...], weight_ref[...], NN)
    gate_ref[...] = gate
    ones = jnp.where(same_head(), 1.0, 0.0).astype(BF)
    for pair in range(gate.shape[1] // PAIR):
        at = slice(pair * PAIR, (pair + 1) * PAIR)
        wkv = wkv_ref[:, at]
        centred = wkv - head_sum_fine(wkv, ones) * (1.0 / HEAD)
        spread = head_sum(centred * centred, ones) * (1.0 / HEAD)
        normed = centred * lax.rsqrt(spread + GROUP_EPSILON) * par_ref[1:2, at] + par_ref[2:3, at]
        mixed_ref[:, at] = (normed * (gate[:, at] / (1.0 + jnp.exp(-gate[:, at])))).astype(BF)


def gated(mix_g, weights, wkv, params, here, seq):
    rows, width = mix_g.shape
    tile, part = rows // seq, wkv.shape[1]
    own = block((tile, part), lambda i, h: (i, 0))
    return kernel(
        lambda here, *refs: gate_body(*refs), "gate", (seq,), here,
        [
            (mix_g, block((tile, width), lambda i, h: (i, 0))),
            (weights, block((width, part), lambda i, h: (0, 0))),
            (wkv, own),
            (params, fixed(params.shape)),
        ],
        [((rows, part), F32, own), ((rows, part), BF, own)],
    )


def columns_body(here, left_ref, right_ref, out_ref):
    out_ref[...] = dot(left_ref[...], right_ref[...], NN).astype(BF)


def columns_product(left, right, part, relative_to, here, seq):
    rows, depth = left.shape
    tile = rows // seq
    (result,) = kernel(
        columns_body, "value_columns", (seq,), here,
        [
            (left, block((tile, depth), lambda i, h: (i, 0))),
            (right, block((depth, part), lambda i, h: (0, h ^ relative_to))),
        ],
        [((rows, part), BF, block((tile, part), lambda i, h: (i ^ relative_to, 0)))],
    )
    return result


def channel_body(count, here, pre_ref, grad_ref, *refs):
    channel_ref, d_recept_ref = refs[count:]
    value = refs[0][...].astype(F32)
    for ref in refs[1:count]:
        value = value + ref[...].astype(F32)
    opened = 1.0 / (1.0 + jnp.exp(-pre_ref[...]))
    channel = opened * value
    channel_ref[...] = channel.astype(BF)
    d_recept_ref[...] = (grad_ref[...].astype(F32) * channel * (1.0 - opened)).astype(BF)


def channel_out(terms, pre, grad_all, here, seq):
    rows, part = pre.shape
    tile = rows // seq
    own = block((tile, part), lambda i, h: (i, 0))
    return kernel(
        partial(channel_body, len(terms)), "channel", (seq,), here,
        [(pre, own), (grad_all, block((tile, part), lambda i, h: (i, h)))] + [(t, own) for t in terms],
        [((rows, part), BF, own)] * 2,
    )


def head_masks():
    lane = lax.broadcasted_iota(jnp.int32, (1, PAIR), 1)
    first = (lane < HEAD).astype(F32)
    return first, 1.0 - first


def same_head():
    row = lax.broadcasted_iota(jnp.int32, (PAIR, PAIR), 0) < HEAD
    column = lax.broadcasted_iota(jnp.int32, (PAIR, PAIR), 1) < HEAD
    return row == column


def dot(left, right, dims):
    return lax.dot_general(left, right, dims, preferred_element_type=F32)


def head_sum(values, ones):
    return dot(values.astype(BF), ones, NN)


def head_sum_fine(values, ones):
    coarse = values.astype(BF)
    rest = (values - coarse.astype(F32)).astype(BF)
    return dot(coarse, ones, NN) + dot(rest, ones, NN)


def stacked(values, first, second):
    return jnp.concatenate([(values * first).astype(BF), (values * second).astype(BF)], axis=0)


def masks_of(rows_ref, columns_ref):
    segment = rows_ref[:, 0:1]
    reaches = rows_ref[:, 1:2]
    last_same = rows_ref[:, 2:3]
    reach_last = rows_ref[CHUNK - 1 : CHUNK, 1:2]
    before = lax.broadcasted_iota(jnp.int32, (CHUNK, CHUNK), 1) < lax.broadcasted_iota(
        jnp.int32, (CHUNK, CHUNK), 0
    )
    allowed = jnp.where((segment == columns_ref[0:1, :]) & before, 1.0, 0.0)
    return reaches, last_same, reach_last, jnp.concatenate([allowed, allowed], axis=0)


def wkv_forward_body(
    here, r_ref, k_ref, v_ref, rows_ref, columns_ref, grow_ref, shrink_ref, tail_ref, par_ref,
    wkv_ref, states_ref, state,
):
    @pl.when(pl.program_id(0) == 0)
    def _():
        state[...] = jnp.zeros_like(state)

    first, second = head_masks()
    block = same_head()
    ones = jnp.where(block, 1.0, 0.0).astype(BF)
    reaches, last_same, reach_last, allowed = masks_of(rows_ref, columns_ref)
    for pair in range(r_ref.shape[1] // PAIR):
        at = slice(pair * PAIR, (pair + 1) * PAIR)
        r, k, v = r_ref[:, at].astype(F32), k_ref[:, at].astype(F32), v_ref[:, at].astype(F32)
        bonus, decay = par_ref[0:1, at], par_ref[3:4, at]
        held = state[at, :]
        held_b = held.astype(BF)
        states_ref[0, at, :] = held_b
        grown = r * grow_ref[:, at]
        shrunk = (k * shrink_ref[:, at]).astype(BF)
        scores = (dot(stacked(grown, first, second), shrunk, NT) * allowed).astype(BF)
        both = jnp.concatenate([scores[:CHUNK], scores[CHUNK:]], axis=1)
        wkv = dot(both, stacked(v, first, second), NN)
        wkv = wkv + dot((grown * reaches).astype(BF), held_b, NT)
        wkv = wkv + head_sum(r * bonus * k, ones) * v
        fresh = dot(v_ref[:, at], (k * tail_ref[:, at] * last_same).astype(BF), TN)
        state[at, :] = held * (decay * reach_last) + jnp.where(block, fresh, 0.0)
        wkv_ref[:, at] = wkv


def wkv_backward_body(
    here, r_ref, k_ref, v_ref, g_ref, wkv_ref, d_mixed_ref, states_ref,
    rows_ref, columns_ref, grow_ref, shrink_ref, tail_ref, par_ref,
    d_r_ref, d_k_ref, d_v_ref, d_g_ref, sums_ref, d_state,
):
    @pl.when(pl.program_id(0) == 0)
    def _():
        d_state[...] = jnp.zeros_like(d_state)
        sums_ref[...] = jnp.zeros_like(sums_ref)

    first, second = head_masks()
    block = same_head()
    ones = jnp.where(block, 1.0, 0.0).astype(BF)
    reaches, last_same, reach_last, allowed = masks_of(rows_ref, columns_ref)
    offset = lax.broadcasted_iota(jnp.int32, (CHUNK, PAIR), 0).astype(F32)
    for pair in range(r_ref.shape[1] // PAIR):
        at = slice(pair * PAIR, (pair + 1) * PAIR)
        bonus, gain, bias, decay = (par_ref[i : i + 1, at] for i in range(4))
        wkv, gate, d_mixed = wkv_ref[:, at], g_ref[:, at], d_mixed_ref[:, at]
        centred = wkv - head_sum_fine(wkv, ones) * (1.0 / HEAD)
        spread = head_sum(centred * centred, ones) * (1.0 / HEAD)
        inverse = lax.rsqrt(spread + GROUP_EPSILON)
        normed = centred * inverse
        opened = 1.0 / (1.0 + jnp.exp(-gate))
        d_scaled = d_mixed * gate * opened
        d_g = d_mixed * (normed * gain + bias) * opened * (1.0 + gate * (1.0 - opened))
        d_g_ref[:, at] = d_g.astype(BF)
        d_normed = d_scaled * gain
        mean_one = head_sum(d_normed, ones) * (1.0 / HEAD)
        mean_two = head_sum(d_normed * normed, ones) * (1.0 / HEAD)
        d_wkv = inverse * (d_normed - mean_one - normed * mean_two)
        r, k, v = r_ref[:, at].astype(F32), k_ref[:, at].astype(F32), v_ref[:, at].astype(F32)
        v_b, d_wkv_b = v_ref[:, at], d_wkv.astype(BF)
        grow, shrink, tail = grow_ref[:, at], shrink_ref[:, at], tail_ref[:, at] * last_same
        held = states_ref[0, at, :]
        later = d_state[at, :]
        later_b = later.astype(BF)
        grown = r * grow
        shrunk = k * shrink
        shrunk_b = shrunk.astype(BF)
        tailed_b = (k * tail).astype(BF)
        grown_two = stacked(grown, first, second)
        d_wkv_two = stacked(d_wkv, first, second)
        scores = (dot(grown_two, shrunk_b, NT) * allowed).astype(BF)
        d_scores = (dot(d_wkv_two, v_b, NT) * allowed).astype(BF)
        d_both = jnp.concatenate([d_scores[:CHUNK], d_scores[CHUNK:]], axis=1)
        d_grown = dot(d_both, stacked(shrunk, first, second), NN)
        d_grown = d_grown + dot((d_wkv * reaches).astype(BF), held, NN)
        d_shrunk = dot(d_scores, grown_two, TN)
        d_tailed = dot(v_b, later_b, NN)
        share = head_sum(r * bonus * k, ones)
        d_share = head_sum(d_wkv * v, ones)
        d_v = dot(scores, d_wkv_two, TN) + dot(tailed_b, later_b, NT) + share * d_wkv
        d_r_ref[:, at] = (d_grown * grow + d_share * bonus * k).astype(BF)
        d_k_ref[:, at] = (d_shrunk * shrink + d_tailed * tail + d_share * bonus * r).astype(BF)
        d_v_ref[:, at] = d_v.astype(BF)
        carried = decay * reach_last
        d_fresh = dot(d_wkv_b, (grown * reaches).astype(BF), TN)
        d_state[at, :] = later * carried + jnp.where(block, d_fresh, 0.0)
        grown_b = grown.astype(BF).astype(F32)
        d_log = (
            offset * grown_b * d_grown
            - (offset + 1.0) * shrunk_b.astype(F32) * d_shrunk
            + (CHUNK - 1.0 - offset) * tailed_b.astype(F32) * d_tailed
        )
        kept = CHUNK * carried * jnp.sum(held.astype(F32) * later, axis=0, keepdims=True)
        sums_ref[0:1, at] += jnp.sum(d_log, axis=0, keepdims=True) + kept
        sums_ref[1:2, at] += jnp.sum(d_share * r * k, axis=0, keepdims=True)
        sums_ref[2:3, at] += jnp.sum(d_scaled * normed, axis=0, keepdims=True)
        sums_ref[3:4, at] += jnp.sum(d_scaled, axis=0, keepdims=True)


def wkv_blocks(width, chunks, per, backward):
    def chunk(i):
        return chunks - 1 - i if backward else i

    tokens = block((CHUNK, width), lambda i, h: (relative(chunk(i), per, h), 0))
    states = block((1, width, PAIR), lambda i, h: (chunk(i), 0, 0))
    tables = [
        block((CHUNK, PAIR), lambda i, h: (chunk(i), 0)),
        block((8, CHUNK), lambda i, h: (0, chunk(i))),
    ]
    return tokens, states, tables + [fixed((CHUNK, width))] * 3 + [fixed((8, width))]


def wkv_forward(r, k, v, tables, here, per):
    length, width = r.shape
    chunks = length // CHUNK
    tokens, states, blocks = wkv_blocks(width, chunks, per, False)
    return kernel(
        wkv_forward_body, "wkv_forward", (chunks,), here,
        [(a, tokens) for a in (r, k, v)] + list(zip(tables, blocks)),
        [((length, width), F32, tokens), ((chunks, width, PAIR), BF, states)],
        [pltpu.VMEM((width, PAIR), F32)],
    )


def wkv_backward(r, k, v, gate, wkv, d_mixed, states_kept, tables, here, per):
    length, width = r.shape
    chunks = length // CHUNK
    tokens, states, blocks = wkv_blocks(width, chunks, per, True)
    return kernel(
        wkv_backward_body, "wkv_backward", (chunks,), here,
        [(a, tokens) for a in (r, k, v, gate, wkv, d_mixed)] + [(states_kept, states)] + list(zip(tables, blocks)),
        [((length, width), BF, tokens)] * 4 + [((8, width), F32, fixed((8, width)))],
        [pltpu.VMEM((width, PAIR), F32)],
    )


def wkv_tables(piece, keep, log_decay, bonus, gain, bias):
    length = piece.shape[0]
    by_chunk = piece.reshape(length // CHUNK, CHUNK)
    before = jnp.concatenate([jnp.full((1,), -1, piece.dtype), by_chunk[:-1, -1]])
    reaches = (by_chunk == before[:, None]).reshape(-1)
    last_same = (by_chunk == by_chunk[:, -1:]).reshape(-1)
    marks = jnp.stack([piece.astype(F32), reaches.astype(F32), last_same.astype(F32), keep], axis=1)
    rows = jnp.pad(marks, ((0, 0), (0, PAIR - 4)))
    columns = jnp.broadcast_to(piece.astype(F32)[None], (8, length))
    offset = jnp.arange(CHUNK).astype(F32)[:, None]
    grow = jnp.exp(offset * log_decay)
    shrink = jnp.exp(-(offset + 1.0) * log_decay)
    tail = jnp.exp((CHUNK - 1.0 - offset) * log_decay)
    zero = jnp.zeros_like(bonus)
    params = jnp.stack([bonus, gain, bias, jnp.exp(CHUNK * log_decay)] + [zero] * 4)
    return rows, columns, grow, shrink, tail, params


def segment_of(lengths, positions):
    rank = jnp.arange(lengths.shape[0])
    starts = jnp.sum(jnp.where(rank[:, None] > rank[None, :], lengths[None, :], 0), axis=1)
    later_flags = (positions[:, None] >= starts[None, 1:]).astype(jnp.int32)
    first_flags = jnp.any(positions[:, None] == starts[None, :], axis=1)
    return (jnp.sum(later_flags, axis=1), first_flags)


def rows_of(vec, *rows):
    return jnp.pad(jnp.stack([vec[i] for i in rows]), ((0, 8 - len(rows)), (0, 0)))


def shards(
    tokens, seq_lengths, out_grad, w_receptance, w_key, w_value, w_gate, w_output,
    ffn_key, ffn_receptance, ffn_value, vectors,
):
    seq, dp = lax.axis_size("seq"), lax.axis_size("dp")
    place = lax.axis_index("seq")
    here = jnp.reshape(place, (1,)).astype(jnp.int32)
    inputs_b, grad_b = tokens[0], out_grad[0]
    own_rows, width = inputs_b.shape
    length, part, unit = own_rows * seq, width // seq, vectors.shape[1]
    per = own_rows // CHUNK
    hidden_width = ffn_key.shape[1] // seq
    groups = (seq, dp)
    within = groups if unit == HEAD else None

    def whole(values):
        return jnp.concatenate(gather_seq(values), axis=0)

    def all_rows(weights):
        pieces = trade_seq(cut_columns(weights, here, seq))
        stacked = stack_rows(pieces, here)
        return lax.all_gather(stacked.reshape(-1, stacked.shape[-1]), "dp", axis=0, tiled=True)

    def owners_rows(grads, widths):
        grad = jnp.concatenate([g.astype(BF) for g in grads], axis=1)
        summed = lax.psum_scatter(grad, "dp", scatter_dimension=0, tiled=True)
        rows = summed.shape[0] // seq
        parts = [lax.dynamic_slice_in_dim(summed, (place ^ j) * rows, rows, 0) for j in range(seq)]
        return join_columns(trade_seq(parts), widths, here)

    def natural(grad):
        return lax.psum_scatter(grad.astype(BF), "dp", scatter_dimension=0, tiled=True).astype(F32)

    full_in = all_rows([w_receptance, w_key, w_value])
    vec_own = gather_small(vectors[None], "dp")
    vec_parts = gather_small(vec_own[None], "seq").astype(F32)
    vec_own = vec_own.transpose(1, 0, 2).reshape(-1, part).astype(F32)
    vec = vec_parts.transpose(2, 0, 1, 3).reshape(-1, width)
    turned = vec_parts.transpose(2, 1, 0, 3).reshape(-1, width)
    tokens_all = whole(inputs_b)
    full_gc = all_rows([w_gate, ffn_receptance])
    full_o = lax.all_gather(w_output, "dp", axis=0, tiled=True)
    grad_all = whole(grad_b)
    full_ck = all_rows([ffn_key])
    full_cv = lax.all_gather(ffn_value, "dp", axis=0, tiled=True)

    positions = jnp.arange(length, dtype=jnp.int32)
    piece, first_flags = segment_of(seq_lengths[0], positions)
    log_decay = -jnp.exp(vec_own[6])
    tables = wkv_tables(
        piece, 1.0 - first_flags.astype(F32), log_decay, vec_own[7], vec_own[8], vec_own[9]
    )
    marks = tables[0]

    if within is None:
        tokens_all = outside(tokens_all, groups, unit)
    mix_r, mix_k, mix_v, mix_g, step = mixes(
        tokens_all, marks, rows_of(turned, 0, 1, 2, 3, 4, 5), 4, True, within, here, per
    )
    recept, keyed, valued = (
        dot(m, full_in[:, i * part : (i + 1) * part], NN).astype(BF)
        for i, m in enumerate((mix_r, mix_k, mix_v))
    )
    wkv, states = wkv_forward(recept, keyed, valued, tables, here, per)
    gate_pre, mixed = gated(mix_g, full_gc, wkv, tables[5], here, seq)
    attn = [dot(rows, full_o, NN).astype(BF) for rows in blocks_of(mixed, seq)]
    after, normed_two = after_norm(inputs_b, scatter_seq(attn), rows_of(vec, 10, 11), here)

    normed_two = whole(normed_two)
    if within is None:
        normed_two = outside(normed_two, groups, unit)
    mix_k2, mix_r2, step_two = mixes(
        normed_two, marks, rows_of(turned, 10, 11, 12, 13), 2, False, within, here, per
    )
    recept_pre = dot(mix_r2, full_gc[:, part:], NN)
    opened = gather_seq(jax.nn.sigmoid(recept_pre).astype(BF))
    key_pre = dot(mix_k2, full_ck, NN)
    smooth = jax.nn.softplus(key_pre)
    hidden = (smooth * smooth).astype(BF)
    value_parts = [columns_product(hidden, full_cv, part, j, here, seq) for j in reversed(range(seq))]
    value_terms = scatter_seq(value_parts[::-1])
    d_value = spread_columns(grad_all, opened, here, True, True, own_rows)
    channel, d_recept_two = channel_out(value_terms, recept_pre, grad_all, here, seq)
    channel = trade_seq(blocks_of(channel, seq))
    out_rows = spread_columns(after, channel, here, False, False, CHUNK)

    d_hidden = dot(d_value, full_cv, NT)
    d_key_two = (d_hidden * 2.0 * smooth * jax.nn.sigmoid(key_pre)).astype(BF)
    d_normed_two, sums_two = mixes_back(
        [d_key_two, d_recept_two], [(full_ck, 0), (full_gc, 1)], step_two, marks,
        rows_of(turned, 12, 13), here, seq,
    )
    terms_two = scatter_seq(blocks_of(d_normed_two, seq))
    grad_cv = dot(hidden, d_value, TN)
    grad_ck = dot(mix_k2, d_key_two, TN)
    grad_cr = dot(mix_r2, d_recept_two, TN)
    if within is None:
        terms_two = [outside(t, groups, unit, back=True) for t in terms_two]
    d_after, d_attn, norm_sums_two = norm_back(terms_two, after, grad_b, rows_of(vec, 10), within, here)

    d_attn = whole(d_attn)
    d_mixed = dot(d_attn, full_o, NT)
    grad_wo = dot(mixed, d_attn, TN)
    d_recept, d_keyed, d_valued, d_gate, sums = wkv_backward(
        recept, keyed, valued, gate_pre, wkv, d_mixed, states, tables, here, per
    )
    d_normed, sums_one = mixes_back(
        [d_recept, d_keyed, d_valued, d_gate], [(full_in, 0), (full_in, 1), (full_in, 2), (full_gc, 0)],
        step, marks, rows_of(turned, 2, 3, 4, 5), here, seq,
    )
    terms = scatter_seq(blocks_of(d_normed, seq))
    grads_in = [
        dot(mix_r, d_recept, TN), dot(mix_k, d_keyed, TN), dot(mix_v, d_valued, TN), dot(mix_g, d_gate, TN)
    ]
    if within is None:
        terms = [outside(t, groups, unit, back=True) for t in terms]
    tokens_grad, _, norm_sums = norm_back(terms, inputs_b, d_after, rows_of(vec, 0), within, here)

    sum_cv = natural(grad_cv)
    sum_ck, sum_cr = owners_rows([grad_ck, grad_cr], [ffn_key.shape[1], width])
    sum_o = natural(grad_wo)
    sum_r, sum_k, sum_v, sum_g = owners_rows(grads_in, [width] * 4)

    def by_device(rows, turn):
        if turn:
            return rows.reshape(-1, dp, seq, unit).transpose(2, 1, 0, 3)
        return rows.reshape(-1, seq, dp, unit).transpose(1, 2, 0, 3)

    own_sums = jnp.stack([sums[0] * log_decay, sums[1], sums[2], sums[3]])
    own_sums = lax.dynamic_update_slice(jnp.zeros((4, width), F32), own_sums, (0, place * part))
    vector_rows = jnp.concatenate(
        [
            by_device(norm_sums[:2], False), by_device(sums_one[:4], True), by_device(own_sums, False),
            by_device(norm_sums_two[:2], False), by_device(sums_two[:2], True),
        ],
        axis=2,
    )
    sum_vec = scatter_small(vector_rows.reshape((-1,) + vector_rows.shape[2:]))
    return (
        out_rows[None], tokens_grad[None], sum_r, sum_k, sum_v, sum_g, sum_o,
        sum_ck, sum_cr, sum_cv, sum_vec,
    )


def solution(mesh):
    tokens = P("dp", "seq", None)
    rows = P(("seq", "dp"), None)
    columns = P(None, ("seq", "dp"))
    return jax.shard_map(
        shards,
        mesh=mesh,
        in_specs=(tokens, P("dp", None), tokens) + (rows,) * 8 + (columns,),
        out_specs=(tokens, tokens) + (rows,) * 8 + (columns,),
        check_vma=False,
    )
```

```python
import math
from functools import partial

import jax
import jax.numpy as jnp
from jax import lax
from jax.experimental import pallas as pl
from jax.experimental.pallas import tpu as pltpu
from jax.sharding import PartitionSpec as P

HEAD = 64
PAIR = 128
CHUNK = 128
EPSILON = 1e-05
GROUP_EPSILON = 1.0
BF = jnp.bfloat16
F32 = jnp.float32
NT = (((1,), (1,)), ((), ()))
TN = (((0,), (0,)), ((), ()))
NN = (((1,), (0,)), ((), ()))


def swap(value, axis, distance):
    size = lax.axis_size(axis)
    return lax.ppermute(value, axis, [(i, i ^ distance) for i in range(size)])


def after(value, *others):
    return lax.optimization_barrier((value, others))[0]


def gather_seq(part, first=()):
    size = lax.axis_size("seq")
    if size == 4:
        half = part.shape[0] // 2
        one, two = swap(part, "seq", 1), swap(part, "seq", 2)
        one, two = after((one, two), first)
        low, high = swap(one[:half], "seq", 2), swap(two[half:], "seq", 1)
        return [part, one, two, low, high]
    return [part] + [swap(part, "seq", distance) for distance in range(1, size)]


def by_block(pieces):
    if lax.axis_size("seq") == 4:
        return pieces[:3] + [jnp.concatenate(pieces[3:], axis=0)]
    return pieces


def scatter_start(parts):
    if lax.axis_size("seq") != 4:
        return ()
    half = parts[3].shape[0] // 2
    return swap(parts[3][:half], "seq", 1), swap(parts[3][half:], "seq", 2)


def scatter_seq(parts, first=(), second=(), started=None):
    started = scatter_start(parts) if started is None else started
    size = lax.axis_size("seq")
    if size == 4:
        own, one, two, far = parts
        half = far.shape[0] // 2
        low, high = after(started, first)
        two = jnp.concatenate([(two[:half].astype(F32) + low.astype(F32)).astype(BF), two[half:]], axis=0)
        one = jnp.concatenate([one[:half], (one[half:].astype(F32) + high.astype(F32)).astype(BF)], axis=0)
        return after([own, swap(one, "seq", 1), swap(two, "seq", 2)], second)
    return after([parts[0]] + [swap(parts[distance], "seq", distance) for distance in range(1, size)], first, second)


def trade_seq(parts):
    return [parts[0]] + [swap(part, "seq", j + 1) for j, part in enumerate(parts[1:])]


def blocks_of(values, size):
    rows = values.shape[0] // size
    return [values[j * rows : (j + 1) * rows] for j in range(size)]


def bits_of(size):
    return [1 << b for b in range(size.bit_length() - 1)]


def gather_small(part, axis):
    for bit in bits_of(lax.axis_size(axis)):
        other = swap(part, axis, bit)
        second = (lax.axis_index(axis) & bit) != 0
        part = jnp.concatenate([jnp.where(second, other, part), jnp.where(second, part, other)], axis=0)
    return part


def scatter_small(parts):
    for axis in ("seq", "dp"):
        for bit in reversed(bits_of(lax.axis_size(axis))):
            half = parts.shape[0] // 2
            second = (lax.axis_index(axis) & bit) != 0
            low, high = parts[:half], parts[half:]
            parts = jnp.where(second, high, low) + swap(jnp.where(second, low, high), axis, bit)
    return parts[0]


def block(shape, index):
    return pl.BlockSpec(shape, lambda *i: index(*i[:-1], i[-1][0]))


def fixed(shape):
    return pl.BlockSpec(shape, lambda *i: (0,) * len(shape))


def relative(tile, per, here):
    return (lax.div(tile, per) ^ here) * per + lax.rem(tile, per)


def kernel(body, name, grid, here, ins, outs, scratch=(), vmem=48, flops=0):
    moved = sum(a.size * a.dtype.itemsize for a, _ in ins)
    moved += sum(math.prod(shape) * jnp.dtype(kind).itemsize for shape, kind, _ in outs)
    return pl.pallas_call(
        body,
        out_shape=[jax.ShapeDtypeStruct(shape, kind) for shape, kind, _ in outs],
        grid_spec=pltpu.PrefetchScalarGridSpec(
            num_scalar_prefetch=1,
            grid=grid,
            in_specs=[spec for _, spec in ins],
            out_specs=[spec for _, _, spec in outs],
            scratch_shapes=list(scratch),
        ),
        cost_estimate=pl.CostEstimate(flops=flops, bytes_accessed=moved, transcendentals=0),
        compiler_params=pltpu.CompilerParams(vmem_limit_bytes=vmem * 2**20),
        name=name,
    )(here, *[array for array, _ in ins])


def pieced(pieces, tile, columns, column, place):
    ins, start = [], 0
    for piece in pieces:
        count = piece.shape[0] // tile

        def index(i, h, start=start, count=count):
            return jnp.clip(place(i, h) - start, 0, count - 1), column(h)

        ins.append((piece, block((tile, columns), index)))
        start += count
    return ins


def picked(refs, counts, tile, held):
    start = 0
    for ref, count in zip(refs, counts):

        @pl.when((tile >= start) & (tile < start + count))
        def _(ref=ref):
            held[...] = ref[...]

        start += count
    return held[...].astype(F32)


def counts_of(pieces, tile):
    return [piece.shape[0] // tile for piece in pieces]


def row_index(rows):
    return lax.broadcasted_iota(jnp.int32, (rows, 1), 0)


def placed(place, width):
    return pl.ds(pl.multiple_of(place * width, width), width)


def cut_body(count, parts, here, *refs):
    ins, outs = refs[:count], refs[count:]
    at = 0
    for ref in ins:
        width = ref.shape[1] // parts
        for j in range(parts):
            outs[j][:, at : at + width] = ref[:, placed(here[0] ^ j, width)]
        at += width


def cut_columns(weights, here, parts):
    rows, width = weights[0].shape[0], sum(w.shape[1] for w in weights) // parts
    return kernel(
        partial(cut_body, len(weights), parts), "cut_columns", (1,), here,
        [(w, fixed(w.shape)) for w in weights],
        [((rows, width), BF, fixed((rows, width)))] * parts,
    )


def stack_body(parts, here, *refs):
    for j in range(parts):
        refs[-1][here[0] ^ j] = refs[j][...]


def stack_rows(pieces, here):
    parts, (rows, width) = len(pieces), pieces[0].shape
    (stacked,) = kernel(
        partial(stack_body, parts), "stack_rows", (1,), here,
        [(p, fixed(p.shape)) for p in pieces],
        [((parts, rows, width), BF, fixed((parts, rows, width)))],
    )
    return stacked


def join_body(parts, count, here, *refs):
    ins, outs = refs[:parts], refs[parts:]
    at = 0
    for ref in outs:
        width = ref.shape[1] // parts
        for j in range(parts):
            ref[:, placed(here[0] ^ j, width)] = ins[j][:, at : at + width].astype(F32)
        at += width


def join_columns(pieces, widths, here):
    parts, rows = len(pieces), pieces[0].shape[0]
    return kernel(
        partial(join_body, parts, len(widths)), "join_columns", (1,), here,
        [(p, fixed(p.shape)) for p in pieces],
        [((rows, width), F32, fixed((rows, width))) for width in widths],
    )


def spread_body(counts, parts, product, here, *refs):
    bases, pieces, out, held = refs[: len(counts)], refs[len(counts) : -2], refs[-2], refs[-1]
    picked(bases, counts, pl.program_id(0), held)
    width = pieces[0].shape[1]
    for j in range(parts):
        at = placed(here[0] ^ j, width)
        piece, base = pieces[j][...].astype(F32), held[:, at].astype(F32)
        out[:, at] = (base * piece if product else base + piece).astype(BF)


def spread_columns(bases, columns, here, product, turn, tile, per):
    rows, width = sum(base.shape[0] for base in bases), bases[0].shape[1]

    def turned(i, j):
        return (lax.div(i, per) ^ j) * per + lax.rem(i, per) if turn else i

    (result,) = kernel(
        partial(spread_body, counts_of(bases, tile), len(columns), product), "spread_columns", (rows // tile,), here,
        pieced(bases, tile, width, lambda h: 0, lambda i, h: i)
        + [(c, block((tile, c.shape[1]), lambda i, h, j=j: (turned(i, j), 0))) for j, c in enumerate(columns)],
        [((rows, width), BF, block((tile, width), lambda i, h: (i, 0)))],
        [pltpu.VMEM((tile, width), bases[0].dtype)],
    )
    return result


def shuffled(values, groups, back=False):
    seq, dp = groups
    if back:
        seq, dp = dp, seq
    lane = lax.broadcasted_iota(jnp.int32, (1, PAIR), 1) < HEAD
    source = [s * dp + d for d in range(dp) for s in range(seq)]
    columns = []
    for one, two in zip(source[::2], source[1::2]):
        low = values[:, one // 2 * PAIR : (one // 2 + 1) * PAIR]
        high = values[:, two // 2 * PAIR : (two // 2 + 1) * PAIR]
        low = pltpu.roll(low, HEAD, 1) if one % 2 else low
        high = high if two % 2 else pltpu.roll(high, HEAD, 1)
        columns.append(jnp.where(lane, low, high))
    return jnp.concatenate(columns, axis=1)


def outside(values, groups, channels, back=False):
    seq, dp = groups[::-1] if back else groups
    return values.reshape(-1, seq, dp, channels).swapaxes(1, 2).reshape(values.shape)


def centre(values):
    centred = values - jnp.mean(values, axis=-1, keepdims=True)
    spread = jnp.mean(centred * centred, axis=-1, keepdims=True)
    return centred, lax.rsqrt(spread + EPSILON)


def mix_body(count, norm, groups, counts, per, here, *refs):
    pieces, (marks_ref, vec_ref) = refs[: len(counts)], refs[len(counts) : len(counts) + 2]
    outs, last, held = refs[len(counts) + 2 : -2], refs[-2], refs[-1]

    @pl.when(pl.program_id(0) == 0)
    def _():
        last[...] = jnp.zeros_like(last)

    values = picked(pieces, counts, relative(pl.program_id(0), per, here[0]), held)
    if norm:
        centred, inverse = centre(values)
        values = centred * inverse
    if groups:
        values = shuffled(values, groups)
    if norm:
        values = values * vec_ref[0:1, :] + vec_ref[1:2, :]
    rows = values.shape[0]
    previous = jnp.where(row_index(rows) == 0, last[0:1, :], pltpu.roll(values, 1, 0)) * marks_ref[:, 3:4]
    last[0:1, :] = values[rows - 1 :, :]
    step = values - previous
    outs[count][...] = step.astype(BF)
    for i in range(count):
        outs[i][...] = (previous + step * vec_ref[2 + i : 3 + i, :]).astype(BF)


def mixes(pieces, marks, vec, count, norm, groups, here, tile, per):
    rows, width = marks.shape[0], pieces[0].shape[1]
    own = block((tile, width), lambda i, h: (relative(i, per, h), 0))
    return kernel(
        partial(mix_body, count, norm, groups, counts_of(pieces, tile), per), "mixes", (rows // tile,), here,
        pieced(pieces, tile, width, lambda h: 0, lambda i, h: relative(i, per, h))
        + [(marks, block((tile, PAIR), lambda i, h: (i, 0))), (vec, fixed(vec.shape))],
        [((rows, width), BF, own)] * (count + 1),
        [pltpu.VMEM((8, width), F32), pltpu.VMEM((tile, width), BF)],
    )


def mixes_back_body(which, here, *refs):
    count = len(which)
    grads, weights = refs[:count], refs[count : 2 * count]
    step_ref, marks_ref, vec_ref, out_ref, sums_ref, later = refs[2 * count :]

    @pl.when(pl.program_id(1) == 0)
    def _():
        later[...] = jnp.zeros_like(later)
        sums_ref[...] = jnp.zeros_like(sums_ref)

    step = step_ref[...].astype(F32)
    total = straight = None
    for i in range(which[-1] + 1):
        grad = sum(dot(grads[k][...], weights[k][...], NT) for k in range(count) if which[k] == i)
        sums_ref[i : i + 1, :] += jnp.sum(grad * step, axis=0, keepdims=True)
        part = grad * vec_ref[i : i + 1, :]
        total, straight = (total + grad, straight + part) if i else (grad, part)
    kept = (total - straight) * marks_ref[:, 3:4]
    rows = kept.shape[0]
    up = jnp.where(row_index(rows) == rows - 1, later[0:1, :], pltpu.roll(kept, rows - 1, 0))
    later[0:1, :] = kept[0:1, :]
    out_ref[...] = (straight + up).astype(BF)


def mixes_back(terms, step, marks, vec, here, seq):
    rows, width = step.shape
    tile, columns = rows // seq, min(512, width)
    last = rows // tile - 1

    def own(i, h):
        return relative(last - i, 1, h)

    ins = [(g, block((tile, n), lambda c, i, h, at=at: (own(i, h), at))) for _, g, at, _, _, n in terms]
    ins += [(w, block((columns, n), lambda c, i, h, at=at: (c, at))) for _, _, _, w, at, n in terms]
    ins += [
        (step, block((tile, columns), lambda c, i, h: (own(i, h), c))),
        (marks, block((tile, PAIR), lambda c, i, h: (last - i, 0))),
        (vec, block((8, columns), lambda c, i, h: (0, c))),
    ]
    return kernel(
        partial(mixes_back_body, [t[0] for t in terms]), "mixes_back", (width // columns, last + 1), here, ins,
        [
            ((rows, width), BF, block((tile, columns), lambda c, i, h: (own(i, h), c))),
            ((8, width), F32, block((8, columns), lambda c, i, h: (0, c))),
        ],
        [pltpu.VMEM((8, columns), F32)],
        flops=2 * rows * width * sum(t[-1] for t in terms),
    )


def after_body(parts, count, here, x_ref, vec_ref, *refs):
    mixed, weights, (after_ref, normed_ref) = refs[:parts], refs[parts : parts + count], refs[parts + count :]
    after = x_ref[...].astype(F32)
    start, width = 0, mixed[0].shape[1]
    for ref in weights:
        stop = start + ref.shape[0]
        left = mixed[start // width][:, start % width : (stop - 1) % width + 1]
        after = after + dot(left, ref[...], NN)
        start = stop
    after_ref[...] = after
    centred, inverse = centre(after)
    normed_ref[...] = (centred * inverse * vec_ref[0:1, :] + vec_ref[1:2, :]).astype(BF)


def after_norm(inputs, mixed, weights, vec, here):
    rows, width = inputs.shape
    own = block((CHUNK, width), lambda i, h: (i, 0))
    return kernel(
        partial(after_body, len(mixed), len(weights)), "after_norm", (rows // CHUNK,), here,
        [(inputs, own), (vec, fixed(vec.shape))]
        + [(m, block((CHUNK, m.shape[1]), lambda i, h: (i, 0))) for m in mixed]
        + [(w, fixed(w.shape)) for w in weights],
        [((rows, width), F32, own), ((rows, width), BF, own)],
        flops=2 * rows * width * width,
    )


def norm_back_body(count, groups, here, x_ref, base_ref, vec_ref, *refs):
    wide_ref, narrow_ref, sums_ref = refs[count:]

    @pl.when(pl.program_id(0) == 0)
    def _():
        sums_ref[...] = jnp.zeros_like(sums_ref)

    grad = refs[0][...].astype(F32)
    for ref in refs[1:count]:
        grad = grad + ref[...].astype(F32)
    if groups:
        grad = shuffled(grad, groups, back=True)
    centred, inverse = centre(x_ref[...].astype(F32))
    normed = centred * inverse
    sums_ref[0:1, :] += jnp.sum(grad * normed, axis=0, keepdims=True)
    sums_ref[1:2, :] += jnp.sum(grad, axis=0, keepdims=True)
    grad = grad * vec_ref[0:1, :]
    grad = grad - jnp.mean(grad, axis=-1, keepdims=True) - normed * jnp.mean(grad * normed, axis=-1, keepdims=True)
    result = base_ref[...].astype(F32) + inverse * grad
    wide_ref[...] = result
    narrow_ref[...] = result.astype(BF)


def norm_back(terms, inputs, base, vec, groups, here):
    rows, width = inputs.shape
    own = block((CHUNK, width), lambda i, h: (i, 0))
    return kernel(
        partial(norm_back_body, len(terms), groups), "norm_back", (rows // CHUNK,), here,
        [(inputs, own), (base, own), (vec, fixed(vec.shape))] + [(t, own) for t in terms],
        [((rows, width), F32, own), ((rows, width), BF, own), ((8, width), F32, fixed((8, width)))],
    )


def gate_body(mix_ref, weight_ref, wkv_ref, par_ref, gate_ref, mixed_ref):
    gate = dot(mix_ref[...], weight_ref[...], NN)
    gate_ref[...] = gate
    ones = jnp.where(same_head(), 1.0, 0.0).astype(BF)
    for pair in range(gate.shape[1] // PAIR):
        at = slice(pair * PAIR, (pair + 1) * PAIR)
        wkv = wkv_ref[:, at]
        centred = wkv - head_sum_fine(wkv, ones) * (1.0 / HEAD)
        spread = head_sum(centred * centred, ones) * (1.0 / HEAD)
        normed = centred * lax.rsqrt(spread + GROUP_EPSILON) * par_ref[1:2, at] + par_ref[2:3, at]
        mixed_ref[:, at] = (normed * (gate[:, at] / (1.0 + jnp.exp(-gate[:, at])))).astype(BF)


def gated(mix_g, weights, wkv, params, here, seq):
    rows, width = mix_g.shape
    tile, part = rows // seq, wkv.shape[1]
    own = block((tile, part), lambda i, h: (i, 0))
    return kernel(
        lambda here, *refs: gate_body(*refs), "gate", (seq,), here,
        [
            (mix_g, block((tile, width), lambda i, h: (i, 0))),
            (weights, block((width, part), lambda i, h: (0, 0))),
            (wkv, own),
            (params, fixed(params.shape)),
        ],
        [((rows, part), F32, own), ((rows, part), BF, own)],
        flops=2 * rows * width * part,
    )


def columns_body(here, left_ref, right_ref, out_ref):
    out_ref[...] = dot(left_ref[...], right_ref[...], NN).astype(BF)


def columns_product(left, right, part, relative_to, here, seq):
    rows, depth = left.shape
    tile = rows // seq
    (result,) = kernel(
        columns_body, "value_columns", (seq,), here,
        [
            (left, block((tile, depth), lambda i, h: (i, 0))),
            (right, block((depth, part), lambda i, h: (0, h ^ relative_to))),
        ],
        [((rows, part), BF, block((tile, part), lambda i, h: (i ^ relative_to, 0)))],
        flops=2 * rows * depth * part,
    )
    return result


def channel_body(counts, here, pre_ref, *refs):
    grads, terms, (channel_ref, d_recept_ref, held) = refs[: len(counts)], refs[len(counts) : -3], refs[-3:]
    value = sum(ref[...].astype(F32) for ref in terms)
    opened = 1.0 / (1.0 + jnp.exp(-pre_ref[...]))
    channel = opened * value
    channel_ref[...] = channel.astype(BF)
    grad = picked(grads, counts, pl.program_id(0), held)
    d_recept_ref[...] = (grad * channel * (1.0 - opened)).astype(BF)


def channel_out(terms, pre, grads, here, tile):
    rows, part = pre.shape
    own = block((tile, part), lambda i, h: (i, 0))
    return kernel(
        partial(channel_body, counts_of(grads, tile)), "channel", (rows // tile,), here,
        [(pre, own)] + pieced(grads, tile, part, lambda h: h, lambda i, h: i) + [(t, own) for t in terms],
        [((rows, part), BF, own)] * 2,
        [pltpu.VMEM((tile, part), BF)],
    )


def head_masks():
    lane = lax.broadcasted_iota(jnp.int32, (1, PAIR), 1)
    first = (lane < HEAD).astype(F32)
    return first, 1.0 - first


def same_head():
    row = lax.broadcasted_iota(jnp.int32, (PAIR, PAIR), 0) < HEAD
    column = lax.broadcasted_iota(jnp.int32, (PAIR, PAIR), 1) < HEAD
    return row == column


def dot(left, right, dims):
    return lax.dot_general(left, right, dims, preferred_element_type=F32)


def head_sum(values, ones):
    return dot(values.astype(BF), ones, NN)


def head_sum_fine(values, ones):
    coarse = values.astype(BF)
    rest = (values - coarse.astype(F32)).astype(BF)
    return dot(coarse, ones, NN) + dot(rest, ones, NN)


def stacked(values, first, second):
    return jnp.concatenate([(values * first).astype(BF), (values * second).astype(BF)], axis=0)


def masks_of(rows_ref, columns_ref):
    segment = rows_ref[:, 0:1]
    reaches = rows_ref[:, 1:2]
    last_same = rows_ref[:, 2:3]
    reach_last = rows_ref[CHUNK - 1 : CHUNK, 1:2]
    before = lax.broadcasted_iota(jnp.int32, (CHUNK, CHUNK), 1) < lax.broadcasted_iota(
        jnp.int32, (CHUNK, CHUNK), 0
    )
    allowed = jnp.where((segment == columns_ref[0:1, :]) & before, 1.0, 0.0)
    return reaches, last_same, reach_last, jnp.concatenate([allowed, allowed], axis=0)


def wkv_forward_body(
    here, r_ref, k_ref, v_ref, rows_ref, columns_ref, grow_ref, shrink_ref, tail_ref, par_ref,
    wkv_ref, states_ref, state,
):
    @pl.when(pl.program_id(0) == 0)
    def _():
        state[...] = jnp.zeros_like(state)

    first, second = head_masks()
    block = same_head()
    ones = jnp.where(block, 1.0, 0.0).astype(BF)
    reaches, last_same, reach_last, allowed = masks_of(rows_ref, columns_ref)
    for pair in range(r_ref.shape[1] // PAIR):
        at = slice(pair * PAIR, (pair + 1) * PAIR)
        r, k, v = r_ref[:, at].astype(F32), k_ref[:, at].astype(F32), v_ref[:, at].astype(F32)
        bonus, decay = par_ref[0:1, at], par_ref[3:4, at]
        held = state[at, :]
        held_b = held.astype(BF)
        states_ref[0, at, :] = held_b
        grown = r * grow_ref[:, at]
        shrunk = (k * shrink_ref[:, at]).astype(BF)
        scores = (dot(stacked(grown, first, second), shrunk, NT) * allowed).astype(BF)
        both = jnp.concatenate([scores[:CHUNK], scores[CHUNK:]], axis=1)
        wkv = dot(both, stacked(v, first, second), NN)
        wkv = wkv + dot((grown * reaches).astype(BF), held_b, NT)
        wkv = wkv + head_sum(r * bonus * k, ones) * v
        fresh = dot(v_ref[:, at], (k * tail_ref[:, at] * last_same).astype(BF), TN)
        state[at, :] = held * (decay * reach_last) + jnp.where(block, fresh, 0.0)
        wkv_ref[:, at] = wkv


def wkv_backward_body(
    here, r_ref, k_ref, v_ref, g_ref, wkv_ref, d_mixed_ref, states_ref,
    rows_ref, columns_ref, grow_ref, shrink_ref, tail_ref, par_ref,
    d_r_ref, d_k_ref, d_v_ref, d_g_ref, sums_ref, d_state,
):
    @pl.when(pl.program_id(0) == 0)
    def _():
        d_state[...] = jnp.zeros_like(d_state)
        sums_ref[...] = jnp.zeros_like(sums_ref)

    first, second = head_masks()
    block = same_head()
    ones = jnp.where(block, 1.0, 0.0).astype(BF)
    reaches, last_same, reach_last, allowed = masks_of(rows_ref, columns_ref)
    offset = lax.broadcasted_iota(jnp.int32, (CHUNK, PAIR), 0).astype(F32)
    for pair in range(r_ref.shape[1] // PAIR):
        at = slice(pair * PAIR, (pair + 1) * PAIR)
        bonus, gain, bias, decay = (par_ref[i : i + 1, at] for i in range(4))
        wkv, gate, d_mixed = wkv_ref[:, at], g_ref[:, at], d_mixed_ref[:, at].astype(F32)
        centred = wkv - head_sum_fine(wkv, ones) * (1.0 / HEAD)
        spread = head_sum(centred * centred, ones) * (1.0 / HEAD)
        inverse = lax.rsqrt(spread + GROUP_EPSILON)
        normed = centred * inverse
        opened = 1.0 / (1.0 + jnp.exp(-gate))
        d_scaled = d_mixed * gate * opened
        d_g = d_mixed * (normed * gain + bias) * opened * (1.0 + gate * (1.0 - opened))
        d_g_ref[:, at] = d_g.astype(BF)
        d_normed = d_scaled * gain
        mean_one = head_sum(d_normed, ones) * (1.0 / HEAD)
        mean_two = head_sum(d_normed * normed, ones) * (1.0 / HEAD)
        d_wkv = inverse * (d_normed - mean_one - normed * mean_two)
        r, k, v = r_ref[:, at].astype(F32), k_ref[:, at].astype(F32), v_ref[:, at].astype(F32)
        v_b, d_wkv_b = v_ref[:, at], d_wkv.astype(BF)
        grow, shrink, tail = grow_ref[:, at], shrink_ref[:, at], tail_ref[:, at] * last_same
        held = states_ref[0, at, :]
        later = d_state[at, :]
        later_b = later.astype(BF)
        grown = r * grow
        shrunk = k * shrink
        shrunk_b = shrunk.astype(BF)
        tailed_b = (k * tail).astype(BF)
        grown_two = stacked(grown, first, second)
        d_wkv_two = stacked(d_wkv, first, second)
        scores = (dot(grown_two, shrunk_b, NT) * allowed).astype(BF)
        d_scores = (dot(d_wkv_two, v_b, NT) * allowed).astype(BF)
        d_both = jnp.concatenate([d_scores[:CHUNK], d_scores[CHUNK:]], axis=1)
        d_grown = dot(d_both, stacked(shrunk, first, second), NN)
        d_grown = d_grown + dot((d_wkv * reaches).astype(BF), held, NN)
        d_shrunk = dot(d_scores, grown_two, TN)
        d_tailed = dot(v_b, later_b, NN)
        share = head_sum(r * bonus * k, ones)
        d_share = head_sum(d_wkv * v, ones)
        d_v = dot(scores, d_wkv_two, TN) + dot(tailed_b, later_b, NT) + share * d_wkv
        d_r_ref[:, at] = (d_grown * grow + d_share * bonus * k).astype(BF)
        d_k_ref[:, at] = (d_shrunk * shrink + d_tailed * tail + d_share * bonus * r).astype(BF)
        d_v_ref[:, at] = d_v.astype(BF)
        carried = decay * reach_last
        d_fresh = dot(d_wkv_b, (grown * reaches).astype(BF), TN)
        d_state[at, :] = later * carried + jnp.where(block, d_fresh, 0.0)
        grown_b = grown.astype(BF).astype(F32)
        d_log = (
            offset * grown_b * d_grown
            - (offset + 1.0) * shrunk_b.astype(F32) * d_shrunk
            + (CHUNK - 1.0 - offset) * tailed_b.astype(F32) * d_tailed
        )
        kept = CHUNK * carried * jnp.sum(held.astype(F32) * later, axis=0, keepdims=True)
        sums_ref[0:1, at] += jnp.sum(d_log, axis=0, keepdims=True) + kept
        sums_ref[1:2, at] += jnp.sum(d_share * r * k, axis=0, keepdims=True)
        sums_ref[2:3, at] += jnp.sum(d_scaled * normed, axis=0, keepdims=True)
        sums_ref[3:4, at] += jnp.sum(d_scaled, axis=0, keepdims=True)


def wkv_blocks(width, chunks, per, backward):
    def chunk(i):
        return chunks - 1 - i if backward else i

    tokens = block((CHUNK, width), lambda i, h: (relative(chunk(i), per, h), 0))
    states = block((1, width, PAIR), lambda i, h: (chunk(i), 0, 0))
    tables = [
        block((CHUNK, PAIR), lambda i, h: (chunk(i), 0)),
        block((8, CHUNK), lambda i, h: (0, chunk(i))),
    ]
    return tokens, states, tables + [fixed((CHUNK, width))] * 3 + [fixed((8, width))]


def wkv_forward(r, k, v, tables, here, per):
    length, width = r.shape
    chunks = length // CHUNK
    tokens, states, blocks = wkv_blocks(width, chunks, per, False)
    return kernel(
        wkv_forward_body, "wkv_forward", (chunks,), here,
        [(a, tokens) for a in (r, k, v)] + list(zip(tables, blocks)),
        [((length, width), F32, tokens), ((chunks, width, PAIR), BF, states)],
        [pltpu.VMEM((width, PAIR), F32)],
        flops=length * width * 8000,
    )


def wkv_backward(r, k, v, gate, wkv, d_mixed, states_kept, tables, here, per):
    length, width = r.shape
    chunks = length // CHUNK
    tokens, states, blocks = wkv_blocks(width, chunks, per, True)
    return kernel(
        wkv_backward_body, "wkv_backward", (chunks,), here,
        [(a, tokens) for a in (r, k, v, gate, wkv, d_mixed)] + [(states_kept, states)] + list(zip(tables, blocks)),
        [((length, width), BF, tokens)] * 4 + [((8, width), F32, fixed((8, width)))],
        [pltpu.VMEM((width, PAIR), F32)],
        flops=length * width * 32000,
    )


def wkv_tables(piece, keep, log_decay, bonus, gain, bias):
    length = piece.shape[0]
    by_chunk = piece.reshape(length // CHUNK, CHUNK)
    before = jnp.concatenate([jnp.full((1,), -1, piece.dtype), by_chunk[:-1, -1]])
    reaches = (by_chunk == before[:, None]).reshape(-1)
    last_same = (by_chunk == by_chunk[:, -1:]).reshape(-1)
    marks = jnp.stack([piece.astype(F32), reaches.astype(F32), last_same.astype(F32), keep], axis=1)
    rows = jnp.pad(marks, ((0, 0), (0, PAIR - 4)))
    columns = jnp.broadcast_to(piece.astype(F32)[None], (8, length))
    offset = jnp.arange(CHUNK).astype(F32)[:, None]
    grow = jnp.exp(offset * log_decay)
    shrink = jnp.exp(-(offset + 1.0) * log_decay)
    tail = jnp.exp((CHUNK - 1.0 - offset) * log_decay)
    zero = jnp.zeros_like(bonus)
    params = jnp.stack([bonus, gain, bias, jnp.exp(CHUNK * log_decay)] + [zero] * 4)
    return rows, columns, grow, shrink, tail, params


def segment_of(lengths, positions):
    rank = jnp.arange(lengths.shape[0])
    starts = jnp.sum(jnp.where(rank[:, None] > rank[None, :], lengths[None, :], 0), axis=1)
    later_flags = (positions[:, None] >= starts[None, 1:]).astype(jnp.int32)
    first_flags = jnp.any(positions[:, None] == starts[None, :], axis=1)
    return (jnp.sum(later_flags, axis=1), first_flags)


def rows_of(vec, *rows):
    return jnp.pad(jnp.stack([vec[i] for i in rows]), ((0, 8 - len(rows)), (0, 0)))


def shards(
    tokens, seq_lengths, out_grad, w_receptance, w_key, w_value, w_gate, w_output,
    ffn_key, ffn_receptance, ffn_value, vectors,
):
    seq, dp = lax.axis_size("seq"), lax.axis_size("dp")
    place = lax.axis_index("seq")
    here = jnp.reshape(place, (1,)).astype(jnp.int32)
    inputs_b, grad_b = tokens[0], out_grad[0]
    own_rows, width = inputs_b.shape
    length, part, unit = own_rows * seq, width // seq, vectors.shape[1]
    per, tile = own_rows // CHUNK, own_rows // 2
    hidden_width = ffn_key.shape[1] // seq
    groups = (seq, dp)
    within = groups if unit == HEAD else None

    def stacked_columns(weights, beside=()):
        stacked = stack_rows(after(trade_seq(cut_columns(weights, here, seq)), beside), here)
        return stacked.reshape(-1, stacked.shape[-1])

    def gather_dp(rows):
        return lax.all_gather(rows, "dp", axis=0, tiled=True)

    def scatter_dp(grad):
        return lax.psum_scatter(grad, "dp", scatter_dimension=0, tiled=True)

    def owners_rows(summed, widths, beside=()):
        rows = summed.shape[0] // seq
        parts = [lax.dynamic_slice_in_dim(summed, (place ^ j) * rows, rows, 0) for j in range(seq)]
        return join_columns(after(trade_seq(parts), beside), widths, here)

    def turn_pieces(pieces):
        if within is not None:
            return pieces
        return [outside(p, groups, unit) for p in pieces]

    columns_in = stacked_columns([w_receptance, w_key, w_value])
    full_in = gather_dp(columns_in)
    vec_own = gather_small(vectors[None], "dp")
    vec_parts = gather_small(vec_own[None], "seq")
    tokens_all = gather_seq(after(inputs_b, columns_in), vec_parts)
    vectors_there, vec_parts = vec_parts, vec_parts.astype(F32)
    vec_own = vec_own.transpose(1, 0, 2).reshape(-1, part).astype(F32)
    vec = vec_parts.transpose(2, 0, 1, 3).reshape(-1, width)
    turned = vec_parts.transpose(2, 1, 0, 3).reshape(-1, width)
    arrived = tokens_all[1:3] + [vectors_there]
    own_o = gather_dp(after(w_output, arrived))
    full_g = gather_dp(stacked_columns([after(w_gate, arrived)]))

    positions = jnp.arange(length, dtype=jnp.int32)
    piece, first_flags = segment_of(seq_lengths[0], positions)
    log_decay = -jnp.exp(vec_own[6])
    tables = wkv_tables(
        piece, 1.0 - first_flags.astype(F32), log_decay, vec_own[7], vec_own[8], vec_own[9]
    )
    marks = tables[0]

    mix_r, mix_k, mix_v, mix_g, step = mixes(
        turn_pieces(tokens_all), marks, rows_of(turned, 0, 1, 2, 3, 4, 5), 4, True, within, here, tile, own_rows // tile
    )
    full_c = gather_dp(stacked_columns(after([ffn_key, ffn_receptance], tokens_all), mix_r))
    full_ck, full_cr = full_c[:, :hidden_width], full_c[:, hidden_width:]
    full_cv = gather_dp(after(ffn_value, mix_r))
    recept, keyed, valued = (
        dot(m, full_in[:, i * part : (i + 1) * part], NN).astype(BF)
        for i, m in enumerate((mix_r, mix_k, mix_v))
    )
    projected = (recept, keyed, valued)
    grad_all = gather_seq(after(grad_b, arrived), projected)
    recept = after(recept, grad_all[1:3], projected)
    own_o = after(own_o, grad_all[1:3], projected)
    wkv, states = wkv_forward(recept, keyed, valued, tables, here, per)
    gate_pre, mixed = gated(mix_g, full_g, after(wkv, grad_all), tables[5], here, seq)
    full_o = gather_seq(own_o, mixed)
    mixed = trade_seq(blocks_of(mixed, seq))
    after_mix, normed_two = after_norm(inputs_b, mixed, full_o, rows_of(vec, 10, 11), here)

    mix_k2, mix_r2, step_two = mixes(
        turn_pieces(gather_seq(normed_two)), marks, rows_of(turned, 10, 11, 12, 13), 2, False, within, here, tile,
        own_rows // tile,
    )
    recept_pre = dot(mix_r2, full_cr, NN)
    opened = gather_seq(jax.nn.sigmoid(recept_pre).astype(BF))
    key_pre = dot(mix_k2, full_ck, NN)
    smooth = jax.nn.softplus(key_pre)
    hidden = (smooth * smooth).astype(BF)
    slope = (2.0 * smooth * jax.nn.sigmoid(key_pre)).astype(BF)
    hidden, slope = lax.optimization_barrier((hidden, slope))
    later = after(hidden, opened[1:3])
    value_parts = [columns_product(later if j < 2 else hidden, full_cv, part, j, here, seq) for j in reversed(range(seq))]
    value_started = scatter_start(value_parts[::-1])
    d_value = spread_columns(grad_all, by_block(after(opened, value_parts)), here, True, True, tile, own_rows // tile)

    grad_cv = dot(hidden, after(d_value, value_started), TN).astype(BF)
    summed_cv = scatter_dp(grad_cv)
    d_hidden = dot(after(d_value, grad_cv), full_cv, NT)
    d_key_two = (d_hidden * slope.astype(F32)).astype(BF)
    value_terms = scatter_seq(value_parts[::-1], started=value_started)
    channel, d_recept_two = channel_out(value_terms, recept_pre, grad_all, here, tile)
    half, first = part // 2, hidden_width // (part // 2)
    d_normed_two, sums_two = mixes_back(
        [(0, d_key_two, 0, full_c, 0, hidden_width)]
        + [(1, d_recept_two, i, full_c, first + i, half) for i in range(2)],
        step_two, marks, rows_of(turned, 12, 13), here, seq,
    )
    grad_ck = dot(after(mix_k2, d_normed_two), d_key_two, TN).astype(BF)
    d_normed_two = blocks_of(d_normed_two, seq)
    started = scatter_start(d_normed_two)
    grad_cr = dot(after(mix_r2, grad_ck, started), d_recept_two, TN).astype(BF)
    terms_two = scatter_seq(d_normed_two, grad_ck, (grad_cr, summed_cv), started)
    summed_ck = scatter_dp(grad_ck)
    summed_cr = scatter_dp(grad_cr)
    if within is None:
        terms_two = [outside(t, groups, unit, back=True) for t in terms_two]
    d_after, d_attn, norm_sums_two = norm_back(terms_two, after_mix, grad_b, rows_of(vec, 10), within, here)

    o_parts = by_block(full_o)
    d_mixed = trade_seq([dot(d_attn, w, NT).astype(BF) for w in o_parts])
    grads_o = [dot(m, d_attn, TN).astype(BF) for m in mixed]
    d_mixed = after(jnp.concatenate(d_mixed, axis=0), grads_o)
    d_recept, d_keyed, d_valued, d_gate, sums = wkv_backward(
        recept, keyed, valued, gate_pre, wkv, d_mixed, states, tables, here, per
    )
    grad_wo = sum(t.astype(F32) for t in scatter_seq(grads_o)).astype(BF)
    grads_in = [
        dot(m, d, TN).astype(BF)
        for m, d in ((mix_r, d_recept), (mix_k, d_keyed), (mix_v, d_valued), (mix_g, d_gate))
    ]
    summed_o = scatter_dp(grad_wo)
    summed_in = scatter_dp(after(jnp.concatenate(grads_in, axis=1), grad_wo))
    d_recept = after(d_recept, grads_in)
    d_normed, sums_one = mixes_back(
        [(i, d, 0, full_in, i, part) for i, d in enumerate((d_recept, d_keyed, d_valued))]
        + [(3, d_gate, 0, full_g, 0, part)],
        step, marks, rows_of(turned, 2, 3, 4, 5), here, seq,
    )
    channel = after(trade_seq(blocks_of(channel, seq)), d_normed)
    out_rows = spread_columns([after_mix], channel, here, False, False, CHUNK, per)
    (sum_ck,) = owners_rows(summed_ck, [ffn_key.shape[1]], d_normed)
    (sum_cr,) = owners_rows(summed_cr, [width], d_normed)
    sum_cv = after(summed_cv, d_normed).astype(F32)
    terms = scatter_seq(blocks_of(d_normed, seq), (out_rows, sum_cv), (sum_ck, sum_cr))
    if within is None:
        terms = [outside(t, groups, unit, back=True) for t in terms]
    tokens_grad, _, norm_sums = norm_back(terms, inputs_b, d_after, rows_of(vec, 0), within, here)

    sum_o = summed_o.astype(F32)
    sum_r, sum_k, sum_v, sum_g = owners_rows(summed_in, [width] * 4)

    def by_device(rows, turn):
        if turn:
            return rows.reshape(-1, dp, seq, unit).transpose(2, 1, 0, 3)
        return rows.reshape(-1, seq, dp, unit).transpose(1, 2, 0, 3)

    own_sums = jnp.stack([sums[0] * log_decay, sums[1], sums[2], sums[3]])
    own_sums = lax.dynamic_update_slice(jnp.zeros((4, width), F32), own_sums, (0, place * part))
    vector_rows = jnp.concatenate(
        [
            by_device(norm_sums[:2], False), by_device(sums_one[:4], True), by_device(own_sums, False),
            by_device(norm_sums_two[:2], False), by_device(sums_two[:2], True),
        ],
        axis=2,
    )
    sum_vec = scatter_small(vector_rows.reshape((-1,) + vector_rows.shape[2:]))
    return (
        out_rows[None], tokens_grad[None], sum_r, sum_k, sum_v, sum_g, sum_o,
        sum_ck, sum_cr, sum_cv, sum_vec,
    )


def solution(mesh):
    tokens = P("dp", "seq", None)
    rows = P(("seq", "dp"), None)
    columns = P(None, ("seq", "dp"))
    return jax.shard_map(
        shards,
        mesh=mesh,
        in_specs=(tokens, P("dp", None), tokens) + (rows,) * 8 + (columns,),
        out_specs=(tokens, tokens) + (rows,) * 8 + (columns,),
        check_vma=False,
    )
```

```python
import math
from functools import partial

import jax
import jax.numpy as jnp
from jax import lax
from jax.experimental import pallas as pl
from jax.experimental.pallas import tpu as pltpu
from jax.sharding import PartitionSpec as P

HEAD = 64
PAIR = 128
CHUNK = 128
EPSILON = 1e-05
GROUP_EPSILON = 1.0
BF = jnp.bfloat16
F32 = jnp.float32
NT = (((1,), (1,)), ((), ()))
TN = (((0,), (0,)), ((), ()))
NN = (((1,), (0,)), ((), ()))


def swap(value, axis, distance):
    size = lax.axis_size(axis)
    return lax.ppermute(value, axis, [(i, i ^ distance) for i in range(size)])


def after(value, *others):
    return lax.optimization_barrier((value, others))[0]


def gather_seq(part, first=()):
    size = lax.axis_size("seq")
    if size == 4:
        half = part.shape[0] // 2
        one, two = swap(part, "seq", 1), swap(part, "seq", 2)
        one, two = after((one, two), first)
        low, high = swap(one[:half], "seq", 2), swap(two[half:], "seq", 1)
        return [part, one, two, low, high]
    return [part] + [swap(part, "seq", distance) for distance in range(1, size)]


def by_block(pieces):
    if lax.axis_size("seq") == 4:
        return pieces[:3] + [jnp.concatenate(pieces[3:], axis=0)]
    return pieces


def scatter_start(parts):
    if lax.axis_size("seq") != 4:
        return ()
    half = parts[3].shape[0] // 2
    return swap(parts[3][:half], "seq", 1), swap(parts[3][half:], "seq", 2)


def scatter_seq(parts, first=(), second=(), started=None):
    started = scatter_start(parts) if started is None else started
    size = lax.axis_size("seq")
    if size == 4:
        own, one, two, far = parts
        half = far.shape[0] // 2
        low, high = after(started, first)
        two = jnp.concatenate([(two[:half].astype(F32) + low.astype(F32)).astype(BF), two[half:]], axis=0)
        one = jnp.concatenate([one[:half], (one[half:].astype(F32) + high.astype(F32)).astype(BF)], axis=0)
        return after([own, swap(one, "seq", 1), swap(two, "seq", 2)], second)
    return after([parts[0]] + [swap(parts[distance], "seq", distance) for distance in range(1, size)], first, second)


def trade_seq(parts):
    return [parts[0]] + [swap(part, "seq", j + 1) for j, part in enumerate(parts[1:])]


def blocks_of(values, size):
    rows = values.shape[0] // size
    return [values[j * rows : (j + 1) * rows] for j in range(size)]


def bits_of(size):
    return [1 << b for b in range(size.bit_length() - 1)]


def gather_small(part, axis):
    for bit in bits_of(lax.axis_size(axis)):
        other = swap(part, axis, bit)
        second = (lax.axis_index(axis) & bit) != 0
        part = jnp.concatenate([jnp.where(second, other, part), jnp.where(second, part, other)], axis=0)
    return part


def scatter_small(parts):
    for axis in ("seq", "dp"):
        for bit in reversed(bits_of(lax.axis_size(axis))):
            half = parts.shape[0] // 2
            second = (lax.axis_index(axis) & bit) != 0
            low, high = parts[:half], parts[half:]
            parts = jnp.where(second, high, low) + swap(jnp.where(second, low, high), axis, bit)
    return parts[0]


def block(shape, index):
    return pl.BlockSpec(shape, lambda *i: index(*i[:-1], i[-1][0]))


def fixed(shape):
    return pl.BlockSpec(shape, lambda *i: (0,) * len(shape))


def relative(tile, per, here):
    return (lax.div(tile, per) ^ here) * per + lax.rem(tile, per)


def kernel(body, name, grid, here, ins, outs, scratch=(), vmem=48, flops=0):
    moved = sum(a.size * a.dtype.itemsize for a, _ in ins)
    moved += sum(math.prod(shape) * jnp.dtype(kind).itemsize for shape, kind, _ in outs)
    return pl.pallas_call(
        body,
        out_shape=[jax.ShapeDtypeStruct(shape, kind) for shape, kind, _ in outs],
        grid_spec=pltpu.PrefetchScalarGridSpec(
            num_scalar_prefetch=1,
            grid=grid,
            in_specs=[spec for _, spec in ins],
            out_specs=[spec for _, _, spec in outs],
            scratch_shapes=list(scratch),
        ),
        cost_estimate=pl.CostEstimate(flops=flops, bytes_accessed=moved, transcendentals=0),
        compiler_params=pltpu.CompilerParams(vmem_limit_bytes=vmem * 2**20),
        name=name,
    )(here, *[array for array, _ in ins])


def pieced(pieces, tile, columns, column, place):
    ins, start = [], 0
    for piece in pieces:
        count = piece.shape[0] // tile

        def index(i, h, start=start, count=count):
            return jnp.clip(place(i, h) - start, 0, count - 1), column(h)

        ins.append((piece, block((tile, columns), index)))
        start += count
    return ins


def picked(refs, counts, tile, held):
    start = 0
    for ref, count in zip(refs, counts):

        @pl.when((tile >= start) & (tile < start + count))
        def _(ref=ref):
            held[...] = ref[...]

        start += count
    return held[...].astype(F32)


def counts_of(pieces, tile):
    return [piece.shape[0] // tile for piece in pieces]


def row_index(rows):
    return lax.broadcasted_iota(jnp.int32, (rows, 1), 0)


def placed(place, width):
    return pl.ds(pl.multiple_of(place * width, width), width)


def cut_body(count, parts, here, *refs):
    ins, outs = refs[:count], refs[count:]
    at = 0
    for ref in ins:
        width = ref.shape[1] // parts
        for j in range(parts):
            outs[j][:, at : at + width] = ref[:, placed(here[0] ^ j, width)]
        at += width


def cut_columns(weights, here, parts):
    rows, width = weights[0].shape[0], sum(w.shape[1] for w in weights) // parts
    return kernel(
        partial(cut_body, len(weights), parts), "cut_columns", (1,), here,
        [(w, fixed(w.shape)) for w in weights],
        [((rows, width), BF, fixed((rows, width)))] * parts,
    )


def stack_body(parts, here, *refs):
    for j in range(parts):
        refs[-1][here[0] ^ j] = refs[j][...]


def stack_rows(pieces, here):
    parts, (rows, width) = len(pieces), pieces[0].shape
    (stacked,) = kernel(
        partial(stack_body, parts), "stack_rows", (1,), here,
        [(p, fixed(p.shape)) for p in pieces],
        [((parts, rows, width), BF, fixed((parts, rows, width)))],
    )
    return stacked


def join_body(parts, count, here, *refs):
    ins, outs = refs[:parts], refs[parts:]
    at = 0
    for ref in outs:
        width = ref.shape[1] // parts
        for j in range(parts):
            ref[:, placed(here[0] ^ j, width)] = ins[j][:, at : at + width].astype(F32)
        at += width


def join_columns(pieces, widths, here):
    parts, rows = len(pieces), pieces[0].shape[0]
    return kernel(
        partial(join_body, parts, len(widths)), "join_columns", (1,), here,
        [(p, fixed(p.shape)) for p in pieces],
        [((rows, width), F32, fixed((rows, width))) for width in widths],
    )


def spread_body(counts, parts, product, here, *refs):
    bases, pieces, out, held = refs[: len(counts)], refs[len(counts) : -2], refs[-2], refs[-1]
    picked(bases, counts, pl.program_id(0), held)
    width = pieces[0].shape[1]
    for j in range(parts):
        at = placed(here[0] ^ j, width)
        piece, base = pieces[j][...].astype(F32), held[:, at].astype(F32)
        out[:, at] = (base * piece if product else base + piece).astype(BF)


def spread_columns(bases, columns, here, product, turn, tile, per):
    rows, width = sum(base.shape[0] for base in bases), bases[0].shape[1]

    def turned(i, j):
        return (lax.div(i, per) ^ j) * per + lax.rem(i, per) if turn else i

    (result,) = kernel(
        partial(spread_body, counts_of(bases, tile), len(columns), product), "spread_columns", (rows // tile,), here,
        pieced(bases, tile, width, lambda h: 0, lambda i, h: i)
        + [(c, block((tile, c.shape[1]), lambda i, h, j=j: (turned(i, j), 0))) for j, c in enumerate(columns)],
        [((rows, width), BF, block((tile, width), lambda i, h: (i, 0)))],
        [pltpu.VMEM((tile, width), bases[0].dtype)],
    )
    return result


def shuffled(values, groups, back=False):
    seq, dp = groups
    if back:
        seq, dp = dp, seq
    lane = lax.broadcasted_iota(jnp.int32, (1, PAIR), 1) < HEAD
    source = [s * dp + d for d in range(dp) for s in range(seq)]
    columns = []
    for one, two in zip(source[::2], source[1::2]):
        low = values[:, one // 2 * PAIR : (one // 2 + 1) * PAIR]
        high = values[:, two // 2 * PAIR : (two // 2 + 1) * PAIR]
        low = pltpu.roll(low, HEAD, 1) if one % 2 else low
        high = high if two % 2 else pltpu.roll(high, HEAD, 1)
        columns.append(jnp.where(lane, low, high))
    return jnp.concatenate(columns, axis=1)


def outside(values, groups, channels, back=False):
    seq, dp = groups[::-1] if back else groups
    return values.reshape(-1, seq, dp, channels).swapaxes(1, 2).reshape(values.shape)


def centre(values):
    centred = values - jnp.mean(values, axis=-1, keepdims=True)
    spread = jnp.mean(centred * centred, axis=-1, keepdims=True)
    return centred, lax.rsqrt(spread + EPSILON)


def mix_body(count, norm, groups, counts, per, here, *refs):
    pieces, (marks_ref, vec_ref) = refs[: len(counts)], refs[len(counts) : len(counts) + 2]
    outs, last, held = refs[len(counts) + 2 : -2], refs[-2], refs[-1]

    @pl.when(pl.program_id(0) == 0)
    def _():
        last[...] = jnp.zeros_like(last)

    values = picked(pieces, counts, relative(pl.program_id(0), per, here[0]), held)
    if norm:
        centred, inverse = centre(values)
        values = centred * inverse
    if groups:
        values = shuffled(values, groups)
    if norm:
        values = values * vec_ref[0:1, :] + vec_ref[1:2, :]
    rows = values.shape[0]
    previous = jnp.where(row_index(rows) == 0, last[0:1, :], pltpu.roll(values, 1, 0)) * marks_ref[:, 3:4]
    last[0:1, :] = values[rows - 1 :, :]
    step = values - previous
    outs[count][...] = step.astype(BF)
    for i in range(count):
        outs[i][...] = (previous + step * vec_ref[2 + i : 3 + i, :]).astype(BF)


def mixes(pieces, marks, vec, count, norm, groups, here, tile, per):
    rows, width = marks.shape[0], pieces[0].shape[1]
    own = block((tile, width), lambda i, h: (relative(i, per, h), 0))
    return kernel(
        partial(mix_body, count, norm, groups, counts_of(pieces, tile), per), "mixes", (rows // tile,), here,
        pieced(pieces, tile, width, lambda h: 0, lambda i, h: relative(i, per, h))
        + [(marks, block((tile, PAIR), lambda i, h: (i, 0))), (vec, fixed(vec.shape))],
        [((rows, width), BF, own)] * (count + 1),
        [pltpu.VMEM((8, width), F32), pltpu.VMEM((tile, width), BF)],
    )


def mixes_back_body(which, here, *refs):
    count = len(which)
    grads, weights = refs[:count], refs[count : 2 * count]
    step_ref, marks_ref, vec_ref, out_ref, sums_ref, later = refs[2 * count :]

    @pl.when(pl.program_id(1) == 0)
    def _():
        later[...] = jnp.zeros_like(later)
        sums_ref[...] = jnp.zeros_like(sums_ref)

    step = step_ref[...].astype(F32)
    total = straight = None
    for i in range(which[-1] + 1):
        grad = sum(dot(grads[k][...], weights[k][...], NT) for k in range(count) if which[k] == i)
        sums_ref[i : i + 1, :] += jnp.sum(grad * step, axis=0, keepdims=True)
        part = grad * vec_ref[i : i + 1, :]
        total, straight = (total + grad, straight + part) if i else (grad, part)
    kept = (total - straight) * marks_ref[:, 3:4]
    rows = kept.shape[0]
    up = jnp.where(row_index(rows) == rows - 1, later[0:1, :], pltpu.roll(kept, rows - 1, 0))
    later[0:1, :] = kept[0:1, :]
    out_ref[...] = (straight + up).astype(BF)


def mixes_back(terms, step, marks, vec, here, seq):
    rows, width = step.shape
    tile, columns = rows // seq, min(512, width)
    last = rows // tile - 1

    def own(i, h):
        return relative(last - i, 1, h)

    ins = [(g, block((tile, n), lambda c, i, h, at=at: (own(i, h), at))) for _, g, at, _, _, n in terms]
    ins += [(w, block((columns, n), lambda c, i, h, at=at: (c, at))) for _, _, _, w, at, n in terms]
    ins += [
        (step, block((tile, columns), lambda c, i, h: (own(i, h), c))),
        (marks, block((tile, PAIR), lambda c, i, h: (last - i, 0))),
        (vec, block((8, columns), lambda c, i, h: (0, c))),
    ]
    return kernel(
        partial(mixes_back_body, [t[0] for t in terms]), "mixes_back", (width // columns, last + 1), here, ins,
        [
            ((rows, width), BF, block((tile, columns), lambda c, i, h: (own(i, h), c))),
            ((8, width), F32, block((8, columns), lambda c, i, h: (0, c))),
        ],
        [pltpu.VMEM((8, columns), F32)],
        flops=2 * rows * width * sum(t[-1] for t in terms),
    )


def after_body(count, here, x_ref, vec_ref, *refs):
    after_ref, normed_ref = refs[count:]
    after = x_ref[...].astype(F32)
    for ref in refs[:count]:
        after = after + ref[...].astype(F32)
    after_ref[...] = after
    centred, inverse = centre(after)
    normed_ref[...] = (centred * inverse * vec_ref[0:1, :] + vec_ref[1:2, :]).astype(BF)


def after_norm(inputs, terms, vec, here):
    rows, width = inputs.shape
    own = block((CHUNK, width), lambda i, h: (i, 0))
    return kernel(
        partial(after_body, len(terms)), "after_norm", (rows // CHUNK,), here,
        [(inputs, own), (vec, fixed(vec.shape))] + [(t, own) for t in terms],
        [((rows, width), F32, own), ((rows, width), BF, own)],
    )


def norm_back_body(count, groups, here, x_ref, base_ref, vec_ref, *refs):
    wide_ref, narrow_ref, sums_ref = refs[count:]

    @pl.when(pl.program_id(0) == 0)
    def _():
        sums_ref[...] = jnp.zeros_like(sums_ref)

    grad = refs[0][...].astype(F32)
    for ref in refs[1:count]:
        grad = grad + ref[...].astype(F32)
    if groups:
        grad = shuffled(grad, groups, back=True)
    centred, inverse = centre(x_ref[...].astype(F32))
    normed = centred * inverse
    sums_ref[0:1, :] += jnp.sum(grad * normed, axis=0, keepdims=True)
    sums_ref[1:2, :] += jnp.sum(grad, axis=0, keepdims=True)
    grad = grad * vec_ref[0:1, :]
    grad = grad - jnp.mean(grad, axis=-1, keepdims=True) - normed * jnp.mean(grad * normed, axis=-1, keepdims=True)
    result = base_ref[...].astype(F32) + inverse * grad
    wide_ref[...] = result
    narrow_ref[...] = result.astype(BF)


def norm_back(terms, inputs, base, vec, groups, here):
    rows, width = inputs.shape
    own = block((CHUNK, width), lambda i, h: (i, 0))
    return kernel(
        partial(norm_back_body, len(terms), groups), "norm_back", (rows // CHUNK,), here,
        [(inputs, own), (base, own), (vec, fixed(vec.shape))] + [(t, own) for t in terms],
        [((rows, width), F32, own), ((rows, width), BF, own), ((8, width), F32, fixed((8, width)))],
    )


def gate_body(mix_ref, weight_ref, wkv_ref, par_ref, gate_ref, mixed_ref):
    gate = dot(mix_ref[...], weight_ref[...], NN)
    gate_ref[...] = gate
    ones = jnp.where(same_head(), 1.0, 0.0).astype(BF)
    for pair in range(gate.shape[1] // PAIR):
        at = slice(pair * PAIR, (pair + 1) * PAIR)
        wkv = wkv_ref[:, at]
        centred = wkv - head_sum_fine(wkv, ones) * (1.0 / HEAD)
        spread = head_sum(centred * centred, ones) * (1.0 / HEAD)
        normed = centred * lax.rsqrt(spread + GROUP_EPSILON) * par_ref[1:2, at] + par_ref[2:3, at]
        mixed_ref[:, at] = (normed * (gate[:, at] / (1.0 + jnp.exp(-gate[:, at])))).astype(BF)


def gated(mix_g, weights, wkv, params, here, seq):
    rows, width = mix_g.shape
    tile, part = rows // seq, wkv.shape[1]
    own = block((tile, part), lambda i, h: (i, 0))
    return kernel(
        lambda here, *refs: gate_body(*refs), "gate", (seq,), here,
        [
            (mix_g, block((tile, width), lambda i, h: (i, 0))),
            (weights, block((width, part), lambda i, h: (0, 0))),
            (wkv, own),
            (params, fixed(params.shape)),
        ],
        [((rows, part), F32, own), ((rows, part), BF, own)],
        flops=2 * rows * width * part,
    )


def columns_body(here, left_ref, right_ref, out_ref):
    out_ref[...] = dot(left_ref[...], right_ref[...], NN).astype(BF)


def columns_product(left, right, part, relative_to, here, seq):
    rows, depth = left.shape
    tile = rows // seq
    (result,) = kernel(
        columns_body, "value_columns", (seq,), here,
        [
            (left, block((tile, depth), lambda i, h: (i, 0))),
            (right, block((depth, part), lambda i, h: (0, h ^ relative_to))),
        ],
        [((rows, part), BF, block((tile, part), lambda i, h: (i ^ relative_to, 0)))],
        flops=2 * rows * depth * part,
    )
    return result


def channel_body(counts, here, pre_ref, *refs):
    grads, terms, (channel_ref, d_recept_ref, held) = refs[: len(counts)], refs[len(counts) : -3], refs[-3:]
    value = sum(ref[...].astype(F32) for ref in terms)
    opened = 1.0 / (1.0 + jnp.exp(-pre_ref[...]))
    channel = opened * value
    channel_ref[...] = channel.astype(BF)
    grad = picked(grads, counts, pl.program_id(0), held)
    d_recept_ref[...] = (grad * channel * (1.0 - opened)).astype(BF)


def channel_out(terms, pre, grads, here, tile):
    rows, part = pre.shape
    own = block((tile, part), lambda i, h: (i, 0))
    return kernel(
        partial(channel_body, counts_of(grads, tile)), "channel", (rows // tile,), here,
        [(pre, own)] + pieced(grads, tile, part, lambda h: h, lambda i, h: i) + [(t, own) for t in terms],
        [((rows, part), BF, own)] * 2,
        [pltpu.VMEM((tile, part), BF)],
    )


def head_masks():
    lane = lax.broadcasted_iota(jnp.int32, (1, PAIR), 1)
    first = (lane < HEAD).astype(F32)
    return first, 1.0 - first


def same_head():
    row = lax.broadcasted_iota(jnp.int32, (PAIR, PAIR), 0) < HEAD
    column = lax.broadcasted_iota(jnp.int32, (PAIR, PAIR), 1) < HEAD
    return row == column


def dot(left, right, dims):
    return lax.dot_general(left, right, dims, preferred_element_type=F32)


def head_sum(values, ones):
    return dot(values.astype(BF), ones, NN)


def head_sum_fine(values, ones):
    coarse = values.astype(BF)
    rest = (values - coarse.astype(F32)).astype(BF)
    return dot(coarse, ones, NN) + dot(rest, ones, NN)


def stacked(values, first, second):
    return jnp.concatenate([(values * first).astype(BF), (values * second).astype(BF)], axis=0)


def masks_of(rows_ref, columns_ref):
    segment = rows_ref[:, 0:1]
    reaches = rows_ref[:, 1:2]
    last_same = rows_ref[:, 2:3]
    reach_last = rows_ref[CHUNK - 1 : CHUNK, 1:2]
    before = lax.broadcasted_iota(jnp.int32, (CHUNK, CHUNK), 1) < lax.broadcasted_iota(
        jnp.int32, (CHUNK, CHUNK), 0
    )
    allowed = jnp.where((segment == columns_ref[0:1, :]) & before, 1.0, 0.0)
    return reaches, last_same, reach_last, jnp.concatenate([allowed, allowed], axis=0)


def wkv_forward_body(
    here, r_ref, k_ref, v_ref, rows_ref, columns_ref, grow_ref, shrink_ref, tail_ref, par_ref,
    wkv_ref, states_ref, state,
):
    @pl.when(pl.program_id(0) == 0)
    def _():
        state[...] = jnp.zeros_like(state)

    first, second = head_masks()
    block = same_head()
    ones = jnp.where(block, 1.0, 0.0).astype(BF)
    reaches, last_same, reach_last, allowed = masks_of(rows_ref, columns_ref)
    for pair in range(r_ref.shape[1] // PAIR):
        at = slice(pair * PAIR, (pair + 1) * PAIR)
        r, k, v = r_ref[:, at].astype(F32), k_ref[:, at].astype(F32), v_ref[:, at].astype(F32)
        bonus, decay = par_ref[0:1, at], par_ref[3:4, at]
        held = state[at, :]
        held_b = held.astype(BF)
        states_ref[0, at, :] = held_b
        grown = r * grow_ref[:, at]
        shrunk = (k * shrink_ref[:, at]).astype(BF)
        scores = (dot(stacked(grown, first, second), shrunk, NT) * allowed).astype(BF)
        both = jnp.concatenate([scores[:CHUNK], scores[CHUNK:]], axis=1)
        wkv = dot(both, stacked(v, first, second), NN)
        wkv = wkv + dot((grown * reaches).astype(BF), held_b, NT)
        wkv = wkv + head_sum(r * bonus * k, ones) * v
        fresh = dot(v_ref[:, at], (k * tail_ref[:, at] * last_same).astype(BF), TN)
        state[at, :] = held * (decay * reach_last) + jnp.where(block, fresh, 0.0)
        wkv_ref[:, at] = wkv


def wkv_backward_body(
    here, r_ref, k_ref, v_ref, g_ref, wkv_ref, d_mixed_ref, states_ref,
    rows_ref, columns_ref, grow_ref, shrink_ref, tail_ref, par_ref,
    d_r_ref, d_k_ref, d_v_ref, d_g_ref, sums_ref, d_state,
):
    @pl.when(pl.program_id(0) == 0)
    def _():
        d_state[...] = jnp.zeros_like(d_state)
        sums_ref[...] = jnp.zeros_like(sums_ref)

    first, second = head_masks()
    block = same_head()
    ones = jnp.where(block, 1.0, 0.0).astype(BF)
    reaches, last_same, reach_last, allowed = masks_of(rows_ref, columns_ref)
    offset = lax.broadcasted_iota(jnp.int32, (CHUNK, PAIR), 0).astype(F32)
    for pair in range(r_ref.shape[1] // PAIR):
        at = slice(pair * PAIR, (pair + 1) * PAIR)
        bonus, gain, bias, decay = (par_ref[i : i + 1, at] for i in range(4))
        wkv, gate, d_mixed = wkv_ref[:, at], g_ref[:, at], d_mixed_ref[:, at].astype(F32)
        centred = wkv - head_sum_fine(wkv, ones) * (1.0 / HEAD)
        spread = head_sum(centred * centred, ones) * (1.0 / HEAD)
        inverse = lax.rsqrt(spread + GROUP_EPSILON)
        normed = centred * inverse
        opened = 1.0 / (1.0 + jnp.exp(-gate))
        d_scaled = d_mixed * gate * opened
        d_g = d_mixed * (normed * gain + bias) * opened * (1.0 + gate * (1.0 - opened))
        d_g_ref[:, at] = d_g.astype(BF)
        d_normed = d_scaled * gain
        mean_one = head_sum(d_normed, ones) * (1.0 / HEAD)
        mean_two = head_sum(d_normed * normed, ones) * (1.0 / HEAD)
        d_wkv = inverse * (d_normed - mean_one - normed * mean_two)
        r, k, v = r_ref[:, at].astype(F32), k_ref[:, at].astype(F32), v_ref[:, at].astype(F32)
        v_b, d_wkv_b = v_ref[:, at], d_wkv.astype(BF)
        grow, shrink, tail = grow_ref[:, at], shrink_ref[:, at], tail_ref[:, at] * last_same
        held = states_ref[0, at, :]
        later = d_state[at, :]
        later_b = later.astype(BF)
        grown = r * grow
        shrunk = k * shrink
        shrunk_b = shrunk.astype(BF)
        tailed_b = (k * tail).astype(BF)
        grown_two = stacked(grown, first, second)
        d_wkv_two = stacked(d_wkv, first, second)
        scores = (dot(grown_two, shrunk_b, NT) * allowed).astype(BF)
        d_scores = (dot(d_wkv_two, v_b, NT) * allowed).astype(BF)
        d_both = jnp.concatenate([d_scores[:CHUNK], d_scores[CHUNK:]], axis=1)
        d_grown = dot(d_both, stacked(shrunk, first, second), NN)
        d_grown = d_grown + dot((d_wkv * reaches).astype(BF), held, NN)
        d_shrunk = dot(d_scores, grown_two, TN)
        d_tailed = dot(v_b, later_b, NN)
        share = head_sum(r * bonus * k, ones)
        d_share = head_sum(d_wkv * v, ones)
        d_v = dot(scores, d_wkv_two, TN) + dot(tailed_b, later_b, NT) + share * d_wkv
        d_r_ref[:, at] = (d_grown * grow + d_share * bonus * k).astype(BF)
        d_k_ref[:, at] = (d_shrunk * shrink + d_tailed * tail + d_share * bonus * r).astype(BF)
        d_v_ref[:, at] = d_v.astype(BF)
        carried = decay * reach_last
        d_fresh = dot(d_wkv_b, (grown * reaches).astype(BF), TN)
        d_state[at, :] = later * carried + jnp.where(block, d_fresh, 0.0)
        grown_b = grown.astype(BF).astype(F32)
        d_log = (
            offset * grown_b * d_grown
            - (offset + 1.0) * shrunk_b.astype(F32) * d_shrunk
            + (CHUNK - 1.0 - offset) * tailed_b.astype(F32) * d_tailed
        )
        kept = CHUNK * carried * jnp.sum(held.astype(F32) * later, axis=0, keepdims=True)
        sums_ref[0:1, at] += jnp.sum(d_log, axis=0, keepdims=True) + kept
        sums_ref[1:2, at] += jnp.sum(d_share * r * k, axis=0, keepdims=True)
        sums_ref[2:3, at] += jnp.sum(d_scaled * normed, axis=0, keepdims=True)
        sums_ref[3:4, at] += jnp.sum(d_scaled, axis=0, keepdims=True)


def wkv_blocks(width, chunks, per, backward):
    def chunk(i):
        return chunks - 1 - i if backward else i

    tokens = block((CHUNK, width), lambda i, h: (relative(chunk(i), per, h), 0))
    states = block((1, width, PAIR), lambda i, h: (chunk(i), 0, 0))
    tables = [
        block((CHUNK, PAIR), lambda i, h: (chunk(i), 0)),
        block((8, CHUNK), lambda i, h: (0, chunk(i))),
    ]
    return tokens, states, tables + [fixed((CHUNK, width))] * 3 + [fixed((8, width))]


def wkv_forward(r, k, v, tables, here, per):
    length, width = r.shape
    chunks = length // CHUNK
    tokens, states, blocks = wkv_blocks(width, chunks, per, False)
    return kernel(
        wkv_forward_body, "wkv_forward", (chunks,), here,
        [(a, tokens) for a in (r, k, v)] + list(zip(tables, blocks)),
        [((length, width), F32, tokens), ((chunks, width, PAIR), BF, states)],
        [pltpu.VMEM((width, PAIR), F32)],
        flops=length * width * 8000,
    )


def wkv_backward(r, k, v, gate, wkv, d_mixed, states_kept, tables, here, per):
    length, width = r.shape
    chunks = length // CHUNK
    tokens, states, blocks = wkv_blocks(width, chunks, per, True)
    return kernel(
        wkv_backward_body, "wkv_backward", (chunks,), here,
        [(a, tokens) for a in (r, k, v, gate, wkv, d_mixed)] + [(states_kept, states)] + list(zip(tables, blocks)),
        [((length, width), BF, tokens)] * 4 + [((8, width), F32, fixed((8, width)))],
        [pltpu.VMEM((width, PAIR), F32)],
        flops=length * width * 32000,
    )


def wkv_tables(piece, keep, log_decay, bonus, gain, bias):
    length = piece.shape[0]
    by_chunk = piece.reshape(length // CHUNK, CHUNK)
    before = jnp.concatenate([jnp.full((1,), -1, piece.dtype), by_chunk[:-1, -1]])
    reaches = (by_chunk == before[:, None]).reshape(-1)
    last_same = (by_chunk == by_chunk[:, -1:]).reshape(-1)
    marks = jnp.stack([piece.astype(F32), reaches.astype(F32), last_same.astype(F32), keep], axis=1)
    rows = jnp.pad(marks, ((0, 0), (0, PAIR - 4)))
    columns = jnp.broadcast_to(piece.astype(F32)[None], (8, length))
    offset = jnp.arange(CHUNK).astype(F32)[:, None]
    grow = jnp.exp(offset * log_decay)
    shrink = jnp.exp(-(offset + 1.0) * log_decay)
    tail = jnp.exp((CHUNK - 1.0 - offset) * log_decay)
    zero = jnp.zeros_like(bonus)
    params = jnp.stack([bonus, gain, bias, jnp.exp(CHUNK * log_decay)] + [zero] * 4)
    return rows, columns, grow, shrink, tail, params


def segment_of(lengths, positions):
    rank = jnp.arange(lengths.shape[0])
    starts = jnp.sum(jnp.where(rank[:, None] > rank[None, :], lengths[None, :], 0), axis=1)
    later_flags = (positions[:, None] >= starts[None, 1:]).astype(jnp.int32)
    first_flags = jnp.any(positions[:, None] == starts[None, :], axis=1)
    return (jnp.sum(later_flags, axis=1), first_flags)


def rows_of(vec, *rows):
    return jnp.pad(jnp.stack([vec[i] for i in rows]), ((0, 8 - len(rows)), (0, 0)))


def shards(
    tokens, seq_lengths, out_grad, w_receptance, w_key, w_value, w_gate, w_output,
    ffn_key, ffn_receptance, ffn_value, vectors,
):
    seq, dp = lax.axis_size("seq"), lax.axis_size("dp")
    place = lax.axis_index("seq")
    here = jnp.reshape(place, (1,)).astype(jnp.int32)
    inputs_b, grad_b = tokens[0], out_grad[0]
    own_rows, width = inputs_b.shape
    length, part, unit = own_rows * seq, width // seq, vectors.shape[1]
    per, tile = own_rows // CHUNK, own_rows // 2
    hidden_width = ffn_key.shape[1] // seq
    groups = (seq, dp)
    within = groups if unit == HEAD else None

    def stacked_columns(weights, beside=()):
        stacked = stack_rows(after(trade_seq(cut_columns(weights, here, seq)), beside), here)
        return stacked.reshape(-1, stacked.shape[-1])

    def gather_dp(rows):
        return lax.all_gather(rows, "dp", axis=0, tiled=True)

    def scatter_dp(grad):
        return lax.psum_scatter(grad, "dp", scatter_dimension=0, tiled=True)

    def owners_rows(summed, widths, beside=()):
        rows = summed.shape[0] // seq
        parts = [lax.dynamic_slice_in_dim(summed, (place ^ j) * rows, rows, 0) for j in range(seq)]
        return join_columns(after(trade_seq(parts), beside), widths, here)

    def turn_pieces(pieces):
        if within is not None:
            return pieces
        return [outside(p, groups, unit) for p in pieces]

    vec_seq = gather_small(vectors[None], "seq")
    columns_in = stacked_columns([w_receptance, w_key, w_value])
    full_in = gather_dp(columns_in)
    vec_parts = gather_small(vec_seq[None], "dp")
    tokens_all = gather_seq(after(inputs_b, vec_seq), vec_parts)
    arrived = tokens_all[1:3] + [vec_parts]
    vec_parts = vec_parts.astype(F32)
    vec = vec_parts.transpose(2, 1, 0, 3).reshape(-1, width)
    turned = vec_parts.transpose(2, 0, 1, 3).reshape(-1, width)
    vec_own = lax.dynamic_slice_in_dim(vec, place * part, part, 1)
    full_g = gather_dp(stacked_columns([after(w_gate, arrived)], tokens_all))
    own_o = gather_dp(after(w_output, tokens_all))
    grad_b_later = after(grad_b, tokens_all)

    positions = jnp.arange(length, dtype=jnp.int32)
    piece, first_flags = segment_of(seq_lengths[0], positions)
    log_decay = -jnp.exp(vec_own[6])
    tables = wkv_tables(
        piece, 1.0 - first_flags.astype(F32), log_decay, vec_own[7], vec_own[8], vec_own[9]
    )
    marks = tables[0]

    mix_r, mix_k, mix_v, mix_g, step = mixes(
        turn_pieces(tokens_all), marks, rows_of(turned, 0, 1, 2, 3, 4, 5), 4, True, within, here, tile, own_rows // tile
    )
    full_c = gather_dp(stacked_columns(after([ffn_key, ffn_receptance], arrived), mix_r))
    full_ck, full_cr = full_c[:, :hidden_width], full_c[:, hidden_width:]
    full_cv = gather_dp(after(ffn_value, mix_r))
    recept, keyed, valued = (
        dot(m, full_in[:, i * part : (i + 1) * part], NN).astype(BF)
        for i, m in enumerate((mix_r, mix_k, mix_v))
    )
    projected = (recept, keyed, valued)
    grad_all = gather_seq(grad_b_later, projected)
    wkv, states = wkv_forward(recept, keyed, valued, tables, here, per)
    gate_pre, mixed = gated(mix_g, full_g, wkv, tables[5], here, seq)
    attn = [dot(rows, own_o, NN).astype(BF) for rows in blocks_of(after(mixed, grad_all[3:]), seq)]
    after_mix, normed_two = after_norm(inputs_b, scatter_seq(attn), rows_of(vec, 10, 11), here)

    mix_k2, mix_r2, step_two = mixes(
        turn_pieces(gather_seq(normed_two)), marks, rows_of(turned, 10, 11, 12, 13), 2, False, within, here, tile,
        own_rows // tile,
    )
    recept_pre = dot(mix_r2, full_cr, NN)
    opened = gather_seq(jax.nn.sigmoid(recept_pre).astype(BF))
    key_pre = dot(mix_k2, full_ck, NN)
    smooth = jax.nn.softplus(key_pre)
    hidden = (smooth * smooth).astype(BF)
    slope = (2.0 * smooth * jax.nn.sigmoid(key_pre)).astype(BF)
    hidden, slope = lax.optimization_barrier((hidden, slope))
    later = after(hidden, opened[1:3])
    value_parts = [columns_product(later if j < 2 else hidden, full_cv, part, j, here, seq) for j in reversed(range(seq))]
    value_started = scatter_start(value_parts[::-1])
    d_value = spread_columns(grad_all, by_block(after(opened, value_parts)), here, True, True, tile, own_rows // tile)

    grad_cv = dot(hidden, after(d_value, value_started), TN).astype(BF)
    summed_cv = scatter_dp(grad_cv)
    d_hidden = dot(after(d_value, grad_cv), full_cv, NT)
    d_key_two = (d_hidden * slope.astype(F32)).astype(BF)
    value_terms = scatter_seq(value_parts[::-1], started=value_started)
    channel, d_recept_two = channel_out(value_terms, recept_pre, grad_all, here, tile)
    half, first = part // 2, hidden_width // (part // 2)
    d_normed_two, sums_two = mixes_back(
        [(0, d_key_two, 0, full_c, 0, hidden_width)]
        + [(1, d_recept_two, i, full_c, first + i, half) for i in range(2)],
        step_two, marks, rows_of(turned, 12, 13), here, seq,
    )
    grad_ck = dot(after(mix_k2, d_normed_two), d_key_two, TN).astype(BF)
    d_normed_two = blocks_of(d_normed_two, seq)
    started = scatter_start(d_normed_two)
    grad_cr = dot(after(mix_r2, grad_ck, started), d_recept_two, TN).astype(BF)
    terms_two = scatter_seq(d_normed_two, grad_ck, (grad_cr, summed_cv), started)
    summed_ck = scatter_dp(grad_ck)
    summed_cr = scatter_dp(grad_cr)
    if within is None:
        terms_two = [outside(t, groups, unit, back=True) for t in terms_two]
    d_after, d_attn, norm_sums_two = norm_back(terms_two, after_mix, grad_b, rows_of(vec, 10), within, here)

    d_attn = jnp.concatenate(gather_seq(d_attn), axis=0)
    d_mixed = dot(d_attn, own_o, NT).astype(BF)
    grad_wo = dot(mixed, d_attn, TN).astype(BF)
    d_mixed = after(d_mixed, grad_wo)
    summed_o = scatter_dp(grad_wo)
    d_recept, d_keyed, d_valued, d_gate, sums = wkv_backward(
        recept, keyed, valued, gate_pre, wkv, d_mixed, states, tables, here, per
    )
    channel = after(trade_seq(blocks_of(after(channel, d_mixed), seq)), d_recept)
    out_rows = spread_columns([after_mix], channel, here, False, False, CHUNK, per)
    (sum_ck,) = owners_rows(after(summed_ck, d_mixed), [ffn_key.shape[1]], d_recept)
    grads_in = [
        dot(after(m, out_rows, sum_ck), d, TN).astype(BF)
        for m, d in ((mix_r, d_recept), (mix_k, d_keyed), (mix_v, d_valued), (mix_g, d_gate))
    ]
    summed_in = scatter_dp(jnp.concatenate(grads_in, axis=1))
    d_recept = after(d_recept, grads_in, summed_o)
    d_normed, sums_one = mixes_back(
        [(i, d, 0, full_in, i, part) for i, d in enumerate((d_recept, d_keyed, d_valued))]
        + [(3, d_gate, 0, full_g, 0, part)],
        step, marks, rows_of(turned, 2, 3, 4, 5), here, seq,
    )
    sum_cv = after(summed_cv, d_normed).astype(F32)
    terms = scatter_seq(blocks_of(d_normed, seq), sum_cv)
    if within is None:
        terms = [outside(t, groups, unit, back=True) for t in terms]
    tokens_grad, _, norm_sums = norm_back(terms, inputs_b, d_after, rows_of(vec, 0), within, here)

    (sum_cr,) = owners_rows(summed_cr, [width])
    sum_o = summed_o.astype(F32)
    sum_r, sum_k, sum_v, sum_g = owners_rows(summed_in, [width] * 4)

    def by_device(rows, turn):
        if turn:
            return rows.reshape(-1, dp, seq, unit).transpose(2, 1, 0, 3)
        return rows.reshape(-1, seq, dp, unit).transpose(1, 2, 0, 3)

    own_sums = jnp.stack([sums[0] * log_decay, sums[1], sums[2], sums[3]])
    own_sums = lax.dynamic_update_slice(jnp.zeros((4, width), F32), own_sums, (0, place * part))
    vector_rows = jnp.concatenate(
        [
            by_device(norm_sums[:2], False), by_device(sums_one[:4], True), by_device(own_sums, False),
            by_device(norm_sums_two[:2], False), by_device(sums_two[:2], True),
        ],
        axis=2,
    )
    sum_vec = scatter_small(vector_rows.reshape((-1,) + vector_rows.shape[2:]))
    return (
        out_rows[None], tokens_grad[None], sum_r, sum_k, sum_v, sum_g, sum_o,
        sum_ck, sum_cr, sum_cv, sum_vec,
    )


def solution(mesh):
    tokens = P("dp", "seq", None)
    rows = P(("seq", "dp"), None)
    columns = P(None, ("seq", "dp"))
    return jax.shard_map(
        shards,
        mesh=mesh,
        in_specs=(tokens, P("dp", None), tokens) + (rows,) * 8 + (columns,),
        out_specs=(tokens, tokens) + (rows,) * 8 + (columns,),
        check_vma=False,
    )
```

```python
import math
from functools import partial

import jax
import jax.numpy as jnp
from jax import lax
from jax.experimental import pallas as pl
from jax.experimental.pallas import tpu as pltpu
from jax.sharding import PartitionSpec as P

HEAD = 64
PAIR = 128
CHUNK = 128
EPSILON = 1e-05
GROUP_EPSILON = 1.0
BF = jnp.bfloat16
F32 = jnp.float32
NT = (((1,), (1,)), ((), ()))
TN = (((0,), (0,)), ((), ()))
NN = (((1,), (0,)), ((), ()))


def swap(value, axis, distance):
    size = lax.axis_size(axis)
    return lax.ppermute(value, axis, [(i, i ^ distance) for i in range(size)])


def after(value, *others):
    return lax.optimization_barrier((value, others))[0]


def gather_seq(part, first=()):
    size = lax.axis_size("seq")
    if size == 4:
        half = part.shape[0] // 2
        one, two = swap(part, "seq", 1), swap(part, "seq", 2)
        one, two = after((one, two), first)
        low, high = swap(one[:half], "seq", 2), swap(two[half:], "seq", 1)
        return [part, one, two, low, high]
    return [part] + [swap(part, "seq", distance) for distance in range(1, size)]


def by_block(pieces):
    if lax.axis_size("seq") == 4:
        return pieces[:3] + [jnp.concatenate(pieces[3:], axis=0)]
    return pieces


def scatter_start(parts):
    if lax.axis_size("seq") != 4:
        return ()
    half = parts[3].shape[0] // 2
    return swap(parts[3][:half], "seq", 1), swap(parts[3][half:], "seq", 2)


def scatter_relay(parts, started):
    if lax.axis_size("seq") != 4:
        return parts[1:]
    (_, one, two, _), (low, high) = parts, started
    half = low.shape[0]
    two = jnp.concatenate([(two[:half].astype(F32) + low.astype(F32)).astype(BF), two[half:]], axis=0)
    one = jnp.concatenate([one[:half], (one[half:].astype(F32) + high.astype(F32)).astype(BF)], axis=0)
    return [one, two]


def scatter_end(own, relayed):
    return [own] + [swap(part, "seq", j + 1) for j, part in enumerate(relayed)]


def scatter_seq(parts):
    return scatter_end(parts[0], scatter_relay(parts, scatter_start(parts)))


def trade_seq(parts):
    return [parts[0]] + [swap(part, "seq", j + 1) for j, part in enumerate(parts[1:])]


def blocks_of(values, size):
    rows = values.shape[0] // size
    return [values[j * rows : (j + 1) * rows] for j in range(size)]


def bits_of(size):
    return [1 << b for b in range(size.bit_length() - 1)]


def gather_small(part, axis):
    for bit in bits_of(lax.axis_size(axis)):
        other = swap(part, axis, bit)
        second = (lax.axis_index(axis) & bit) != 0
        part = jnp.concatenate([jnp.where(second, other, part), jnp.where(second, part, other)], axis=0)
    return part


def scatter_small(parts):
    for axis in ("seq", "dp"):
        for bit in reversed(bits_of(lax.axis_size(axis))):
            half = parts.shape[0] // 2
            second = (lax.axis_index(axis) & bit) != 0
            low, high = parts[:half], parts[half:]
            parts = jnp.where(second, high, low) + swap(jnp.where(second, low, high), axis, bit)
    return parts[0]


def block(shape, index):
    return pl.BlockSpec(shape, lambda *i: index(*i[:-1], i[-1][0]))


def fixed(shape):
    return pl.BlockSpec(shape, lambda *i: (0,) * len(shape))


def relative(tile, per, here):
    return (lax.div(tile, per) ^ here) * per + lax.rem(tile, per)


def kernel(body, name, grid, here, ins, outs, scratch=(), vmem=48, flops=0):
    moved = sum(a.size * a.dtype.itemsize for a, _ in ins)
    moved += sum(math.prod(shape) * jnp.dtype(kind).itemsize for shape, kind, _ in outs)
    return pl.pallas_call(
        body,
        out_shape=[jax.ShapeDtypeStruct(shape, kind) for shape, kind, _ in outs],
        grid_spec=pltpu.PrefetchScalarGridSpec(
            num_scalar_prefetch=1,
            grid=grid,
            in_specs=[spec for _, spec in ins],
            out_specs=[spec for _, _, spec in outs],
            scratch_shapes=list(scratch),
        ),
        compiler_params=pltpu.CompilerParams(vmem_limit_bytes=vmem * 2**20),
        name=name,
    )(here, *[array for array, _ in ins])


def pieced(pieces, tile, columns, column, place):
    ins, start = [], 0
    for piece in pieces:
        count = piece.shape[0] // tile

        def index(i, h, start=start, count=count):
            return jnp.clip(place(i, h) - start, 0, count - 1), column(h)

        ins.append((piece, block((tile, columns), index)))
        start += count
    return ins


def picked(refs, counts, tile, held):
    start = 0
    for ref, count in zip(refs, counts):

        @pl.when((tile >= start) & (tile < start + count))
        def _(ref=ref):
            held[...] = ref[...]

        start += count
    return held[...].astype(F32)


def counts_of(pieces, tile):
    return [piece.shape[0] // tile for piece in pieces]


def row_index(rows):
    return lax.broadcasted_iota(jnp.int32, (rows, 1), 0)


def placed(place, width):
    return pl.ds(pl.multiple_of(place * width, width), width)


def cut_body(count, parts, here, *refs):
    ins, outs = refs[:count], refs[count:]
    at = 0
    for ref in ins:
        width = ref.shape[1] // parts
        for j in range(parts):
            outs[j][:, at : at + width] = ref[:, placed(here[0] ^ j, width)]
        at += width


def cut_columns(weights, here, parts):
    rows, width = weights[0].shape[0], sum(w.shape[1] for w in weights) // parts
    return kernel(
        partial(cut_body, len(weights), parts), "cut_columns", (1,), here,
        [(w, fixed(w.shape)) for w in weights],
        [((rows, width), BF, fixed((rows, width)))] * parts,
    )


def stack_body(parts, here, *refs):
    start = 0
    for out in refs[parts:]:
        for j in range(parts):
            out[here[0] ^ j] = refs[j][:, start : start + out.shape[2]]
        start += out.shape[2]


def stack_rows(pieces, widths, here):
    parts, rows = len(pieces), pieces[0].shape[0]
    return kernel(
        partial(stack_body, parts), "stack_rows", (1,), here,
        [(p, fixed(p.shape)) for p in pieces],
        [((parts, rows, width), BF, fixed((parts, rows, width))) for width in widths],
    )


def hold_body(here, in_ref, *refs):
    refs[-1][...] = in_ref[...]


def held_back(values, here, *others):
    rows, width = values.shape
    own = block((rows // 2, width), lambda i, h: (i, 0))
    (copy,) = kernel(
        hold_body, "hold", (2,), here,
        [(values, own)] + [(o, pl.BlockSpec(memory_space=pl.ANY)) for o in others],
        [((rows, width), values.dtype, own)],
    )
    return copy


def join_body(parts, count, here, *refs):
    ins, outs = refs[:parts], refs[parts:]
    at = 0
    for ref in outs:
        width = ref.shape[1] // parts
        for j in range(parts):
            ref[:, placed(here[0] ^ j, width)] = ins[j][:, at : at + width].astype(F32)
        at += width


def join_columns(pieces, widths, here):
    parts, rows = len(pieces), pieces[0].shape[0]
    return kernel(
        partial(join_body, parts, len(widths)), "join_columns", (1,), here,
        [(p, fixed(p.shape)) for p in pieces],
        [((rows, width), F32, fixed((rows, width))) for width in widths],
    )


def spread_body(counts, parts, product, here, *refs):
    bases, pieces, out, held = refs[: len(counts)], refs[len(counts) : -2], refs[-2], refs[-1]
    picked(bases, counts, pl.program_id(0), held)
    width = pieces[0].shape[1]
    for j in range(parts):
        at = placed(here[0] ^ j, width)
        piece, base = pieces[j][...].astype(F32), held[:, at].astype(F32)
        out[:, at] = (base * piece if product else base + piece).astype(BF)


def spread_columns(bases, columns, here, product, turn, tile, per):
    rows, width = sum(base.shape[0] for base in bases), bases[0].shape[1]

    def turned(i, j):
        return (lax.div(i, per) ^ j) * per + lax.rem(i, per) if turn else i

    (result,) = kernel(
        partial(spread_body, counts_of(bases, tile), len(columns), product), "spread_columns", (rows // tile,), here,
        pieced(bases, tile, width, lambda h: 0, lambda i, h: i)
        + [(c, block((tile, c.shape[1]), lambda i, h, j=j: (turned(i, j), 0))) for j, c in enumerate(columns)],
        [((rows, width), BF, block((tile, width), lambda i, h: (i, 0)))],
        [pltpu.VMEM((tile, width), bases[0].dtype)],
    )
    return result


def shuffled(values, groups, back=False):
    seq, dp = groups
    if back:
        seq, dp = dp, seq
    lane = lax.broadcasted_iota(jnp.int32, (1, PAIR), 1) < HEAD
    source = [s * dp + d for d in range(dp) for s in range(seq)]
    columns = []
    for one, two in zip(source[::2], source[1::2]):
        low = values[:, one // 2 * PAIR : (one // 2 + 1) * PAIR]
        high = values[:, two // 2 * PAIR : (two // 2 + 1) * PAIR]
        low = pltpu.roll(low, HEAD, 1) if one % 2 else low
        high = high if two % 2 else pltpu.roll(high, HEAD, 1)
        columns.append(jnp.where(lane, low, high))
    return jnp.concatenate(columns, axis=1)


def outside(values, groups, channels, back=False):
    seq, dp = groups[::-1] if back else groups
    return values.reshape(-1, seq, dp, channels).swapaxes(1, 2).reshape(values.shape)


def centre(values):
    centred = values - jnp.mean(values, axis=-1, keepdims=True)
    spread = jnp.mean(centred * centred, axis=-1, keepdims=True)
    return centred, lax.rsqrt(spread + EPSILON)


def mix_body(count, norm, groups, counts, per, here, *refs):
    pieces, (marks_ref, vec_ref) = refs[: len(counts)], refs[len(counts) : len(counts) + 2]
    outs, last, held = refs[len(counts) + 2 : -2], refs[-2], refs[-1]

    @pl.when(pl.program_id(0) == 0)
    def _():
        last[...] = jnp.zeros_like(last)

    values = picked(pieces, counts, relative(pl.program_id(0), per, here[0]), held)
    if norm:
        centred, inverse = centre(values)
        values = centred * inverse
    if groups:
        values = shuffled(values, groups)
    if norm:
        values = values * vec_ref[0:1, :] + vec_ref[1:2, :]
    rows = values.shape[0]
    previous = jnp.where(row_index(rows) == 0, last[0:1, :], pltpu.roll(values, 1, 0)) * marks_ref[:, 3:4]
    last[0:1, :] = values[rows - 1 :, :]
    step = values - previous
    outs[count][...] = step.astype(BF)
    for i in range(count):
        outs[i][...] = (previous + step * vec_ref[2 + i : 3 + i, :]).astype(BF)


def mixes(pieces, marks, vec, count, norm, groups, here, tile, per):
    rows, width = marks.shape[0], pieces[0].shape[1]
    own = block((tile, width), lambda i, h: (relative(i, per, h), 0))
    return kernel(
        partial(mix_body, count, norm, groups, counts_of(pieces, tile), per), "mixes", (rows // tile,), here,
        pieced(pieces, tile, width, lambda h: 0, lambda i, h: relative(i, per, h))
        + [(marks, block((tile, PAIR), lambda i, h: (i, 0))), (vec, fixed(vec.shape))],
        [((rows, width), BF, own)] * (count + 1),
        [pltpu.VMEM((8, width), F32), pltpu.VMEM((tile, width), BF)],
    )


def mixes_back_body(which, first, seq, here, *refs):
    count = len(which)
    grads, nexts, weights = refs[:count], refs[count : 2 * count], refs[2 * count : 3 * count]
    step_ref, marks_ref, next_marks_ref, vec_ref, out_ref, sums_ref = refs[3 * count :]

    @pl.when(pl.program_id(1) == 0)
    def _():
        sums_ref[...] = jnp.zeros_like(sums_ref)

    step = step_ref[...].astype(F32)
    rows = step.shape[0]
    total = straight = None
    for i in range(which[-1] + 1):
        grad = sum(
            dot(jnp.concatenate([grads[k][...], nexts[k][...]], axis=0), weights[k][...], NT)
            for k in range(count)
            if which[k] == i
        )
        sums_ref[i : i + 1, :] += jnp.sum(grad[:rows] * step, axis=0, keepdims=True)
        part = grad * vec_ref[i : i + 1, :]
        total, straight = (total + grad, straight + part) if i else (grad, part)
    inside = ((first + pl.program_id(1)) ^ here[0]) < seq - 1
    keep = jnp.concatenate([marks_ref[:, 3:4], jnp.where(inside, next_marks_ref[:, 3:4], 0.0)], axis=0)
    kept = (total - straight) * keep
    up = pltpu.roll(kept, kept.shape[0] - 1, 0)
    out_ref[...] = (straight[:rows] + up[:rows]).astype(BF)


EXTRA = 16


def mixes_back(terms, step, marks, vec, here, seq, first, count):
    rows, width = step.shape
    tile, columns = rows // seq, min(512, width)
    extras = tile // EXTRA

    def following(i, h):
        return jnp.minimum(((first + i) ^ h) + 1, seq - 1)

    ins = [(g, block((tile, n), lambda c, i, h, at=at: (first + i, at))) for _, g, at, _, _, n in terms]
    ins += [
        (g, block((EXTRA, n), lambda c, i, h, at=at: ((following(i, h) ^ h) * extras, at)))
        for _, g, at, _, _, n in terms
    ]
    ins += [(w, block((columns, n), lambda c, i, h, at=at: (c, at))) for _, _, _, w, at, n in terms]
    ins += [
        (step, block((tile, columns), lambda c, i, h: (first + i, c))),
        (marks, block((tile, PAIR), lambda c, i, h: ((first + i) ^ h, 0))),
        (marks, block((EXTRA, PAIR), lambda c, i, h: (following(i, h) * extras, 0))),
        (vec, block((8, columns), lambda c, i, h: (0, c))),
    ]
    return kernel(
        partial(mixes_back_body, [t[0] for t in terms], first, seq), "mixes_back", (width // columns, count), here, ins,
        [
            ((count * tile, width), BF, block((tile, columns), lambda c, i, h: (i, c))),
            ((8, width), F32, block((8, columns), lambda c, i, h: (0, c))),
        ],
        flops=2 * count * tile * width * sum(t[-1] for t in terms),
    )


def mixes_back_scatter(terms, step, marks, vec, here, seq, beside, ready=()):
    if seq != 4:
        grad, sums = mixes_back(terms, step, marks, vec, here, seq, 0, seq)
        return after(scatter_seq(blocks_of(grad, seq)), beside(grad)), sums

    def call(first, count, *before):
        ordered = after([t[1] for t in terms], *before)
        return mixes_back(
            [(t[0], g) + t[2:] for t, g in zip(terms, ordered)], step, marks, vec, here, seq, first, count
        )

    far, sums_far = call(3, 1, ready)
    near, sums_near = call(1, 2, far)
    parts = [None] + blocks_of(near, 2) + [far]
    started = after(scatter_start(parts), near)
    relayed = scatter_relay(parts, started)
    own, sums_own = call(0, 1, near, relayed)
    return after(scatter_end(own, relayed), beside(relayed)), sums_far + sums_near + sums_own


def after_body(count, here, x_ref, vec_ref, *refs):
    after_ref, normed_ref = refs[count:]
    after = x_ref[...].astype(F32)
    for ref in refs[:count]:
        after = after + ref[...].astype(F32)
    after_ref[...] = after
    centred, inverse = centre(after)
    normed_ref[...] = (centred * inverse * vec_ref[0:1, :] + vec_ref[1:2, :]).astype(BF)


def after_norm(inputs, terms, vec, here):
    rows, width = inputs.shape
    own = block((CHUNK, width), lambda i, h: (i, 0))
    return kernel(
        partial(after_body, len(terms)), "after_norm", (rows // CHUNK,), here,
        [(inputs, own), (vec, fixed(vec.shape))] + [(t, own) for t in terms],
        [((rows, width), F32, own), ((rows, width), BF, own)],
    )


def norm_back_body(count, groups, here, x_ref, base_ref, vec_ref, *refs):
    wide_ref, narrow_ref, sums_ref = refs[count:]

    @pl.when(pl.program_id(0) == 0)
    def _():
        sums_ref[...] = jnp.zeros_like(sums_ref)

    grad = refs[0][...].astype(F32)
    for ref in refs[1:count]:
        grad = grad + ref[...].astype(F32)
    if groups:
        grad = shuffled(grad, groups, back=True)
    centred, inverse = centre(x_ref[...].astype(F32))
    normed = centred * inverse
    sums_ref[0:1, :] += jnp.sum(grad * normed, axis=0, keepdims=True)
    sums_ref[1:2, :] += jnp.sum(grad, axis=0, keepdims=True)
    grad = grad * vec_ref[0:1, :]
    grad = grad - jnp.mean(grad, axis=-1, keepdims=True) - normed * jnp.mean(grad * normed, axis=-1, keepdims=True)
    result = base_ref[...].astype(F32) + inverse * grad
    wide_ref[...] = result
    narrow_ref[...] = result.astype(BF)


def norm_back(terms, inputs, base, vec, groups, here):
    rows, width = inputs.shape
    own = block((CHUNK, width), lambda i, h: (i, 0))
    return kernel(
        partial(norm_back_body, len(terms), groups), "norm_back", (rows // CHUNK,), here,
        [(inputs, own), (base, own), (vec, fixed(vec.shape))] + [(t, own) for t in terms],
        [((rows, width), F32, own), ((rows, width), BF, own), ((8, width), F32, fixed((8, width)))],
    )


def gate_body(mix_ref, weight_ref, wkv_ref, par_ref, gate_ref, mixed_ref):
    gate = dot(mix_ref[...], weight_ref[...], NN)
    gate_ref[...] = gate
    ones = jnp.where(same_head(), 1.0, 0.0).astype(BF)
    for pair in range(gate.shape[1] // PAIR):
        at = slice(pair * PAIR, (pair + 1) * PAIR)
        wkv = wkv_ref[:, at]
        centred = wkv - head_sum_fine(wkv, ones) * (1.0 / HEAD)
        spread = head_sum(centred * centred, ones) * (1.0 / HEAD)
        normed = centred * lax.rsqrt(spread + GROUP_EPSILON) * par_ref[1:2, at] + par_ref[2:3, at]
        mixed_ref[:, at] = (normed * (gate[:, at] / (1.0 + jnp.exp(-gate[:, at])))).astype(BF)


def gated(mix_g, weights, wkv, params, here, seq):
    rows, width = mix_g.shape
    tile, part = rows // seq, wkv.shape[1]
    own = block((tile, part), lambda i, h: (i, 0))
    return kernel(
        lambda here, *refs: gate_body(*refs), "gate", (seq,), here,
        [
            (mix_g, block((tile, width), lambda i, h: (i, 0))),
            (weights, block((width, part), lambda i, h: (0, 0))),
            (wkv, own),
            (params, fixed(params.shape)),
        ],
        [((rows, part), F32, own), ((rows, part), BF, own)],
        flops=2 * rows * width * part,
    )


def columns_body(here, left_ref, right_ref, out_ref):
    out_ref[...] = dot(left_ref[...], right_ref[...], NN).astype(BF)


def columns_product(left, right, part, relative_to, here, seq):
    rows, depth = left.shape
    tile = rows // seq
    (result,) = kernel(
        columns_body, "value_columns", (seq,), here,
        [
            (left, block((tile, depth), lambda i, h: (i, 0))),
            (right, block((depth, part), lambda i, h: (0, h ^ relative_to))),
        ],
        [((rows, part), BF, block((tile, part), lambda i, h: (i ^ relative_to, 0)))],
        flops=2 * rows * depth * part,
    )
    return result


def channel_body(counts, here, pre_ref, *refs):
    grads, terms, (channel_ref, d_recept_ref, held) = refs[: len(counts)], refs[len(counts) : -3], refs[-3:]
    value = sum(ref[...].astype(F32) for ref in terms)
    opened = 1.0 / (1.0 + jnp.exp(-pre_ref[...]))
    channel = opened * value
    channel_ref[...] = channel.astype(BF)
    grad = picked(grads, counts, pl.program_id(0), held)
    d_recept_ref[...] = (grad * channel * (1.0 - opened)).astype(BF)


def channel_out(terms, pre, grads, here, tile):
    rows, part = pre.shape
    own = block((tile, part), lambda i, h: (i, 0))
    return kernel(
        partial(channel_body, counts_of(grads, tile)), "channel", (rows // tile,), here,
        [(pre, own)] + pieced(grads, tile, part, lambda h: h, lambda i, h: i) + [(t, own) for t in terms],
        [((rows, part), BF, own)] * 2,
        [pltpu.VMEM((tile, part), BF)],
    )


def head_masks():
    lane = lax.broadcasted_iota(jnp.int32, (1, PAIR), 1)
    first = (lane < HEAD).astype(F32)
    return first, 1.0 - first


def same_head():
    row = lax.broadcasted_iota(jnp.int32, (PAIR, PAIR), 0) < HEAD
    column = lax.broadcasted_iota(jnp.int32, (PAIR, PAIR), 1) < HEAD
    return row == column


def dot(left, right, dims):
    return lax.dot_general(left, right, dims, preferred_element_type=F32)


def head_sum(values, ones):
    return dot(values.astype(BF), ones, NN)


def head_sum_fine(values, ones):
    coarse = values.astype(BF)
    rest = (values - coarse.astype(F32)).astype(BF)
    return dot(coarse, ones, NN) + dot(rest, ones, NN)


def stacked(values, first, second):
    return jnp.concatenate([(values * first).astype(BF), (values * second).astype(BF)], axis=0)


def masks_of(rows_ref, columns_ref):
    segment = rows_ref[:, 0:1]
    reaches = rows_ref[:, 1:2]
    last_same = rows_ref[:, 2:3]
    reach_last = rows_ref[CHUNK - 1 : CHUNK, 1:2]
    before = lax.broadcasted_iota(jnp.int32, (CHUNK, CHUNK), 1) < lax.broadcasted_iota(
        jnp.int32, (CHUNK, CHUNK), 0
    )
    allowed = jnp.where((segment == columns_ref[0:1, :]) & before, 1.0, 0.0)
    return reaches, last_same, reach_last, jnp.concatenate([allowed, allowed], axis=0)


def wkv_forward_body(
    here, r_ref, k_ref, v_ref, rows_ref, columns_ref, grow_ref, shrink_ref, tail_ref, par_ref,
    wkv_ref, states_ref, state,
):
    @pl.when(pl.program_id(0) == 0)
    def _():
        state[...] = jnp.zeros_like(state)

    first, second = head_masks()
    block = same_head()
    ones = jnp.where(block, 1.0, 0.0).astype(BF)
    reaches, last_same, reach_last, allowed = masks_of(rows_ref, columns_ref)
    for pair in range(r_ref.shape[1] // PAIR):
        at = slice(pair * PAIR, (pair + 1) * PAIR)
        r, k, v = r_ref[:, at].astype(F32), k_ref[:, at].astype(F32), v_ref[:, at].astype(F32)
        bonus, decay = par_ref[0:1, at], par_ref[3:4, at]
        held = state[at, :]
        held_b = held.astype(BF)
        states_ref[0, at, :] = held_b
        grown = r * grow_ref[:, at]
        shrunk = (k * shrink_ref[:, at]).astype(BF)
        scores = (dot(stacked(grown, first, second), shrunk, NT) * allowed).astype(BF)
        both = jnp.concatenate([scores[:CHUNK], scores[CHUNK:]], axis=1)
        wkv = dot(both, stacked(v, first, second), NN)
        wkv = wkv + dot((grown * reaches).astype(BF), held_b, NT)
        wkv = wkv + head_sum(r * bonus * k, ones) * v
        fresh = dot(v_ref[:, at], (k * tail_ref[:, at] * last_same).astype(BF), TN)
        state[at, :] = held * (decay * reach_last) + jnp.where(block, fresh, 0.0)
        wkv_ref[:, at] = wkv


def wkv_backward_body(
    here, r_ref, k_ref, v_ref, g_ref, wkv_ref, d_mixed_ref, states_ref,
    rows_ref, columns_ref, grow_ref, shrink_ref, tail_ref, par_ref,
    d_r_ref, d_k_ref, d_v_ref, d_g_ref, sums_ref, d_state,
):
    @pl.when(pl.program_id(0) == 0)
    def _():
        d_state[...] = jnp.zeros_like(d_state)
        sums_ref[...] = jnp.zeros_like(sums_ref)

    first, second = head_masks()
    block = same_head()
    ones = jnp.where(block, 1.0, 0.0).astype(BF)
    reaches, last_same, reach_last, allowed = masks_of(rows_ref, columns_ref)
    offset = lax.broadcasted_iota(jnp.int32, (CHUNK, PAIR), 0).astype(F32)
    for pair in range(r_ref.shape[1] // PAIR):
        at = slice(pair * PAIR, (pair + 1) * PAIR)
        bonus, gain, bias, decay = (par_ref[i : i + 1, at] for i in range(4))
        wkv, gate, d_mixed = wkv_ref[:, at], g_ref[:, at], d_mixed_ref[:, at].astype(F32)
        centred = wkv - head_sum_fine(wkv, ones) * (1.0 / HEAD)
        spread = head_sum(centred * centred, ones) * (1.0 / HEAD)
        inverse = lax.rsqrt(spread + GROUP_EPSILON)
        normed = centred * inverse
        opened = 1.0 / (1.0 + jnp.exp(-gate))
        d_scaled = d_mixed * gate * opened
        d_g = d_mixed * (normed * gain + bias) * opened * (1.0 + gate * (1.0 - opened))
        d_g_ref[:, at] = d_g.astype(BF)
        d_normed = d_scaled * gain
        mean_one = head_sum(d_normed, ones) * (1.0 / HEAD)
        mean_two = head_sum(d_normed * normed, ones) * (1.0 / HEAD)
        d_wkv = inverse * (d_normed - mean_one - normed * mean_two)
        r, k, v = r_ref[:, at].astype(F32), k_ref[:, at].astype(F32), v_ref[:, at].astype(F32)
        v_b, d_wkv_b = v_ref[:, at], d_wkv.astype(BF)
        grow, shrink, tail = grow_ref[:, at], shrink_ref[:, at], tail_ref[:, at] * last_same
        held = states_ref[0, at, :]
        later = d_state[at, :]
        later_b = later.astype(BF)
        grown = r * grow
        shrunk = k * shrink
        shrunk_b = shrunk.astype(BF)
        tailed_b = (k * tail).astype(BF)
        grown_two = stacked(grown, first, second)
        d_wkv_two = stacked(d_wkv, first, second)
        scores = (dot(grown_two, shrunk_b, NT) * allowed).astype(BF)
        d_scores = (dot(d_wkv_two, v_b, NT) * allowed).astype(BF)
        d_both = jnp.concatenate([d_scores[:CHUNK], d_scores[CHUNK:]], axis=1)
        d_grown = dot(d_both, stacked(shrunk, first, second), NN)
        d_grown = d_grown + dot((d_wkv * reaches).astype(BF), held, NN)
        d_shrunk = dot(d_scores, grown_two, TN)
        d_tailed = dot(v_b, later_b, NN)
        share = head_sum(r * bonus * k, ones)
        d_share = head_sum(d_wkv * v, ones)
        d_v = dot(scores, d_wkv_two, TN) + dot(tailed_b, later_b, NT) + share * d_wkv
        d_r_ref[:, at] = (d_grown * grow + d_share * bonus * k).astype(BF)
        d_k_ref[:, at] = (d_shrunk * shrink + d_tailed * tail + d_share * bonus * r).astype(BF)
        d_v_ref[:, at] = d_v.astype(BF)
        carried = decay * reach_last
        d_fresh = dot(d_wkv_b, (grown * reaches).astype(BF), TN)
        d_state[at, :] = later * carried + jnp.where(block, d_fresh, 0.0)
        grown_b = grown.astype(BF).astype(F32)
        d_log = (
            offset * grown_b * d_grown
            - (offset + 1.0) * shrunk_b.astype(F32) * d_shrunk
            + (CHUNK - 1.0 - offset) * tailed_b.astype(F32) * d_tailed
        )
        kept = CHUNK * carried * jnp.sum(held.astype(F32) * later, axis=0, keepdims=True)
        sums_ref[0:1, at] += jnp.sum(d_log, axis=0, keepdims=True) + kept
        sums_ref[1:2, at] += jnp.sum(d_share * r * k, axis=0, keepdims=True)
        sums_ref[2:3, at] += jnp.sum(d_scaled * normed, axis=0, keepdims=True)
        sums_ref[3:4, at] += jnp.sum(d_scaled, axis=0, keepdims=True)


def wkv_blocks(width, chunks, per, backward):
    def chunk(i):
        return chunks - 1 - i if backward else i

    tokens = block((CHUNK, width), lambda i, h: (relative(chunk(i), per, h), 0))
    states = block((1, width, PAIR), lambda i, h: (chunk(i), 0, 0))
    tables = [
        block((CHUNK, PAIR), lambda i, h: (chunk(i), 0)),
        block((8, CHUNK), lambda i, h: (0, chunk(i))),
    ]
    return tokens, states, tables + [fixed((CHUNK, width))] * 3 + [fixed((8, width))]


def wkv_forward(r, k, v, tables, here, per):
    length, width = r.shape
    chunks = length // CHUNK
    tokens, states, blocks = wkv_blocks(width, chunks, per, False)
    return kernel(
        wkv_forward_body, "wkv_forward", (chunks,), here,
        [(a, tokens) for a in (r, k, v)] + list(zip(tables, blocks)),
        [((length, width), F32, tokens), ((chunks, width, PAIR), BF, states)],
        [pltpu.VMEM((width, PAIR), F32)],
        flops=length * width * 8000,
    )


def wkv_backward(r, k, v, gate, wkv, d_mixed, states_kept, tables, here, per):
    length, width = r.shape
    chunks = length // CHUNK
    tokens, states, blocks = wkv_blocks(width, chunks, per, True)
    return kernel(
        wkv_backward_body, "wkv_backward", (chunks,), here,
        [(a, tokens) for a in (r, k, v, gate, wkv, d_mixed)] + [(states_kept, states)] + list(zip(tables, blocks)),
        [((length, width), BF, tokens)] * 4 + [((8, width), F32, fixed((8, width)))],
        [pltpu.VMEM((width, PAIR), F32)],
        flops=length * width * 32000,
    )


def wkv_tables(piece, keep, log_decay, bonus, gain, bias):
    length = piece.shape[0]
    by_chunk = piece.reshape(length // CHUNK, CHUNK)
    before = jnp.concatenate([jnp.full((1,), -1, piece.dtype), by_chunk[:-1, -1]])
    reaches = (by_chunk == before[:, None]).reshape(-1)
    last_same = (by_chunk == by_chunk[:, -1:]).reshape(-1)
    marks = jnp.stack([piece.astype(F32), reaches.astype(F32), last_same.astype(F32), keep], axis=1)
    rows = jnp.pad(marks, ((0, 0), (0, PAIR - 4)))
    columns = jnp.broadcast_to(piece.astype(F32)[None], (8, length))
    offset = jnp.arange(CHUNK).astype(F32)[:, None]
    grow = jnp.exp(offset * log_decay)
    shrink = jnp.exp(-(offset + 1.0) * log_decay)
    tail = jnp.exp((CHUNK - 1.0 - offset) * log_decay)
    zero = jnp.zeros_like(bonus)
    params = jnp.stack([bonus, gain, bias, jnp.exp(CHUNK * log_decay)] + [zero] * 4)
    return rows, columns, grow, shrink, tail, params


def segment_of(lengths, positions):
    rank = jnp.arange(lengths.shape[0])
    starts = jnp.sum(jnp.where(rank[:, None] > rank[None, :], lengths[None, :], 0), axis=1)
    later_flags = (positions[:, None] >= starts[None, 1:]).astype(jnp.int32)
    first_flags = jnp.any(positions[:, None] == starts[None, :], axis=1)
    return (jnp.sum(later_flags, axis=1), first_flags)


def rows_of(vec, *rows):
    return jnp.pad(jnp.stack([vec[i] for i in rows]), ((0, 8 - len(rows)), (0, 0)))


def shards(
    tokens, seq_lengths, out_grad, w_receptance, w_key, w_value, w_gate, w_output,
    ffn_key, ffn_receptance, ffn_value, vectors,
):
    seq, dp = lax.axis_size("seq"), lax.axis_size("dp")
    place = lax.axis_index("seq")
    here = jnp.reshape(place, (1,)).astype(jnp.int32)
    inputs_b, grad_b = tokens[0], out_grad[0]
    own_rows, width = inputs_b.shape
    length, part, unit = own_rows * seq, width // seq, vectors.shape[1]
    per, tile = own_rows // CHUNK, own_rows // 2
    hidden_width = ffn_key.shape[1] // seq
    groups = (seq, dp)
    within = groups if unit == HEAD else None

    def stacked_columns(weights, widths, beside=()):
        stacked = stack_rows(after(trade_seq(cut_columns(weights, here, seq)), beside), widths, here)
        return [w.reshape(-1, w.shape[-1]) for w in stacked]

    def gather_dp(rows):
        return lax.all_gather(rows, "dp", axis=0, tiled=True)

    def scatter_dp(grad):
        return lax.psum_scatter(grad, "dp", scatter_dimension=0, tiled=True)

    def owners_rows(summed, widths, beside=()):
        rows = summed.shape[0] // seq
        parts = [lax.dynamic_slice_in_dim(summed, (place ^ j) * rows, rows, 0) for j in range(seq)]
        return join_columns(after(trade_seq(parts), beside), widths, here)

    def turn_pieces(pieces):
        if within is not None:
            return pieces
        return [outside(p, groups, unit) for p in pieces]

    positions = jnp.arange(length, dtype=jnp.int32)
    piece, first_flags = segment_of(seq_lengths[0], positions)

    columns_in, columns_g = stacked_columns([w_receptance, w_key, w_value, w_gate], [3 * part, part])
    full_in = gather_dp(columns_in)
    vec_seq = gather_small(vectors[None], "seq")
    tokens_held = held_back(inputs_b, here, vec_seq)
    vec_parts = gather_small(vec_seq[None], "dp").astype(F32)
    vec = vec_parts.transpose(2, 1, 0, 3).reshape(-1, width)
    turned = vec_parts.transpose(2, 0, 1, 3).reshape(-1, width)
    vec_own = lax.dynamic_slice_in_dim(vec, place * part, part, 1)
    log_decay = -jnp.exp(vec_own[6])
    tables = wkv_tables(
        piece, 1.0 - first_flags.astype(F32), log_decay, vec_own[7], vec_own[8], vec_own[9]
    )
    marks = tables[0]
    rows_one = rows_of(turned, 0, 1, 2, 3, 4, 5)
    tokens_all = gather_seq(tokens_held, (rows_one, tables))
    full_g = gather_dp(after(columns_g, tokens_all[1:3], rows_one))
    own_o = gather_dp(after(w_output, tokens_all))

    mix_r, mix_k, mix_v, mix_g, step = mixes(
        turn_pieces(tokens_all), marks, rows_one, 4, True, within, here, tile, own_rows // tile
    )
    recept, keyed, valued = (
        dot(m, full_in[:, i * part : (i + 1) * part], NN).astype(BF)
        for i, m in enumerate((mix_r, mix_k, mix_v))
    )
    projected = (recept, keyed, valued)
    (columns_c,) = stacked_columns(after([ffn_key, ffn_receptance], mix_r), [hidden_width + part], projected)
    full_c = gather_dp(columns_c)
    full_ck, full_cr = full_c[:, :hidden_width], full_c[:, hidden_width:]
    full_cv = gather_dp(after(ffn_value, columns_c))
    grad_all = gather_seq(after(grad_b, mix_r), projected)
    wkv, states = wkv_forward(recept, keyed, valued, tables, here, per)
    gate_pre, mixed = gated(mix_g, full_g, wkv, tables[5], here, seq)
    attn = [dot(rows, own_o, NN).astype(BF) for rows in blocks_of(after(mixed, grad_all[3:]), seq)]
    after_mix, normed_two = after_norm(inputs_b, scatter_seq(attn), rows_of(vec, 10, 11), here)

    mix_k2, mix_r2, step_two = mixes(
        turn_pieces(gather_seq(normed_two)), marks, rows_of(turned, 10, 11, 12, 13), 2, False, within, here, tile,
        own_rows // tile,
    )
    recept_pre = dot(mix_r2, full_cr, NN)
    opened = gather_seq(jax.nn.sigmoid(recept_pre).astype(BF))
    key_pre = dot(mix_k2, full_ck, NN)
    smooth = jax.nn.softplus(key_pre)
    hidden = (smooth * smooth).astype(BF)
    slope = (2.0 * smooth * jax.nn.sigmoid(key_pre)).astype(BF)
    hidden, slope = lax.optimization_barrier((hidden, slope))
    later = after(hidden, opened[1:3])
    value_parts = [columns_product(later if j < 2 else hidden, full_cv, part, j, here, seq) for j in reversed(range(seq))]
    value_parts = value_parts[::-1]
    value_relayed = scatter_relay(value_parts, scatter_start(value_parts))
    d_value = spread_columns(
        grad_all, by_block(after(opened, value_parts, value_relayed)), here, True, True, tile, own_rows // tile
    )

    grad_cv = dot(hidden, d_value, TN).astype(BF)
    summed_cv = scatter_dp(grad_cv)
    value_terms = scatter_end(value_parts[0], value_relayed)
    d_hidden = dot(after(d_value, grad_cv), full_cv, NT)
    d_key_two = (d_hidden * slope.astype(F32)).astype(BF)
    channel, d_recept_two = channel_out(value_terms, recept_pre, grad_all, here, tile)
    half, first = part // 2, hidden_width // (part // 2)
    grad_ck, grad_cr = [], []

    def beside_two(relayed):
        grad_ck.append(dot(after(mix_k2, relayed), d_key_two, TN).astype(BF))
        grad_cr.append(dot(after(mix_r2, relayed, grad_ck), d_recept_two, TN).astype(BF))
        return grad_ck, grad_cr

    terms_two, sums_two = mixes_back_scatter(
        [(0, d_key_two, 0, full_c, 0, hidden_width)]
        + [(1, d_recept_two, i, full_c, first + i, half) for i in range(2)],
        step_two, marks, rows_of(turned, 12, 13), here, seq, beside_two,
    )
    summed_ck, summed_cr = scatter_dp(grad_ck[0]), scatter_dp(grad_cr[0])
    if within is None:
        terms_two = [outside(t, groups, unit, back=True) for t in terms_two]
    d_after, d_attn, norm_sums_two = norm_back(terms_two, after_mix, grad_b, rows_of(vec, 10), within, here)

    d_attn = jnp.concatenate(after(gather_seq(d_attn), summed_cv), axis=0)
    d_mixed = dot(d_attn, own_o, NT).astype(BF)
    grad_wo = dot(mixed, d_attn, TN).astype(BF)
    d_mixed = after(d_mixed, grad_wo)
    summed_o = scatter_dp(grad_wo)
    d_recept, d_keyed, d_valued, d_gate, sums = wkv_backward(
        recept, keyed, valued, gate_pre, wkv, d_mixed, states, tables, here, per
    )
    channel = trade_seq(blocks_of(after(channel, d_mixed), seq))
    channel = after(channel, d_recept)
    grads_vg = [dot(mix_v, d_valued, TN).astype(BF), dot(mix_g, d_gate, TN).astype(BF)]
    summed_vg = scatter_dp(jnp.concatenate(grads_vg, axis=1))
    grads_rk, out_rows, sums_early = [], [], []

    def beside(relayed):
        grads_rk.extend(
            dot(after(m, relayed), d, TN).astype(BF) for m, d in ((mix_r, d_recept), (mix_k, d_keyed))
        )
        out_rows.append(spread_columns([after_mix], after(channel, relayed), here, False, False, CHUNK, per))
        sums_early.append(after(summed_cv, relayed).astype(F32))
        sums_early.extend(owners_rows(summed_ck, [ffn_key.shape[1]], relayed))
        return grads_rk, out_rows, sums_early

    d_recept, d_keyed = after((d_recept, d_keyed), grads_vg, summed_o, channel)
    terms, sums_one = mixes_back_scatter(
        [(i, d, 0, full_in, i, part) for i, d in enumerate((d_recept, d_keyed, d_valued))]
        + [(3, d_gate, 0, full_g, 0, part)],
        step, marks, rows_of(turned, 2, 3, 4, 5), here, seq, beside, summed_ck,
    )
    summed_rk = scatter_dp(jnp.concatenate(grads_rk, axis=1))
    (out_rows,), (sum_cv, sum_ck) = out_rows, sums_early
    if within is None:
        terms = [outside(t, groups, unit, back=True) for t in terms]
    tokens_grad, _, norm_sums = norm_back(terms, inputs_b, d_after, rows_of(vec, 0), within, here)

    (sum_cr,) = owners_rows(summed_cr, [width])
    sum_o = summed_o.astype(F32)
    sum_v, sum_g = owners_rows(summed_vg, [width] * 2)
    sum_r, sum_k = owners_rows(summed_rk, [width] * 2)

    def by_device(rows, turn):
        if turn:
            return rows.reshape(-1, dp, seq, unit).transpose(2, 1, 0, 3)
        return rows.reshape(-1, seq, dp, unit).transpose(1, 2, 0, 3)

    own_sums = jnp.stack([sums[0] * log_decay, sums[1], sums[2], sums[3]])
    own_sums = lax.dynamic_update_slice(jnp.zeros((4, width), F32), own_sums, (0, place * part))
    vector_rows = jnp.concatenate(
        [
            by_device(norm_sums[:2], False), by_device(sums_one[:4], True), by_device(own_sums, False),
            by_device(norm_sums_two[:2], False), by_device(sums_two[:2], True),
        ],
        axis=2,
    )
    sum_vec = scatter_small(vector_rows.reshape((-1,) + vector_rows.shape[2:]))
    return (
        out_rows[None], tokens_grad[None], sum_r, sum_k, sum_v, sum_g, sum_o,
        sum_ck, sum_cr, sum_cv, sum_vec,
    )


def solution(mesh):
    tokens = P("dp", "seq", None)
    rows = P(("seq", "dp"), None)
    columns = P(None, ("seq", "dp"))
    return jax.shard_map(
        shards,
        mesh=mesh,
        in_specs=(tokens, P("dp", None), tokens) + (rows,) * 8 + (columns,),
        out_specs=(tokens, tokens) + (rows,) * 8 + (columns,),
        check_vma=False,
    )
```

```python
from functools import partial

import jax
import jax.numpy as jnp
from jax import lax
from jax.experimental import pallas as pl
from jax.experimental.pallas import tpu as pltpu
from jax.sharding import PartitionSpec as P

HEAD = 64
PAIR = 128
CHUNK = 128
EPSILON = 1e-05
GROUP_EPSILON = 1.0
BF = jnp.bfloat16
F32 = jnp.float32
NT = (((1,), (1,)), ((), ()))
TN = (((0,), (0,)), ((), ()))
NN = (((1,), (0,)), ((), ()))


def swap(value, axis, distance):
    size = lax.axis_size(axis)
    return lax.ppermute(value, axis, [(i, i ^ distance) for i in range(size)])


def after(value, *others):
    return lax.optimization_barrier((value, others))[0]


def gather_seq(part, first=()):
    size = lax.axis_size("seq")
    if size == 4:
        half = part.shape[0] // 2
        one, two = swap(part, "seq", 1), swap(part, "seq", 2)
        one, two = after((one, two), first)
        low, high = swap(one[:half], "seq", 2), swap(two[half:], "seq", 1)
        return [part, one, two, low, high]
    return [part] + [swap(part, "seq", distance) for distance in range(1, size)]


def by_block(pieces):
    if lax.axis_size("seq") == 4:
        return pieces[:3] + [jnp.concatenate(pieces[3:], axis=0)]
    return pieces


def scatter_start(parts):
    if lax.axis_size("seq") != 4:
        return ()
    half = parts[3].shape[0] // 2
    return swap(parts[3][:half], "seq", 1), swap(parts[3][half:], "seq", 2)


def scatter_relay(parts, started):
    if lax.axis_size("seq") != 4:
        return parts[1:]
    (_, one, two, _), (low, high) = parts, started
    half = low.shape[0]
    two = jnp.concatenate([(two[:half].astype(F32) + low.astype(F32)).astype(BF), two[half:]], axis=0)
    one = jnp.concatenate([one[:half], (one[half:].astype(F32) + high.astype(F32)).astype(BF)], axis=0)
    return [one, two]


def scatter_end(own, relayed):
    return [own] + [swap(part, "seq", j + 1) for j, part in enumerate(relayed)]


def scatter_seq(parts):
    return scatter_end(parts[0], scatter_relay(parts, scatter_start(parts)))


def trade_seq(parts):
    return [parts[0]] + [swap(part, "seq", j + 1) for j, part in enumerate(parts[1:])]


def blocks_of(values, size):
    rows = values.shape[0] // size
    return [values[j * rows : (j + 1) * rows] for j in range(size)]


def bits_of(size):
    return [1 << b for b in range(size.bit_length() - 1)]


def gather_small(part, axis):
    for bit in bits_of(lax.axis_size(axis)):
        other = swap(part, axis, bit)
        second = (lax.axis_index(axis) & bit) != 0
        part = jnp.concatenate([jnp.where(second, other, part), jnp.where(second, part, other)], axis=0)
    return part


def scatter_small(parts):
    for axis in ("dp", "seq"):
        for bit in reversed(bits_of(lax.axis_size(axis))):
            half = parts.shape[0] // 2
            second = (lax.axis_index(axis) & bit) != 0
            low, high = parts[:half], parts[half:]
            parts = jnp.where(second, high, low) + swap(jnp.where(second, low, high), axis, bit)
    return parts[0]


def block(shape, index):
    return pl.BlockSpec(shape, lambda *i: index(*i[:-1], i[-1][0]))


def fixed(shape):
    return pl.BlockSpec(shape, lambda *i: (0,) * len(shape))


def relative(tile, per, here):
    return (lax.div(tile, per) ^ here) * per + lax.rem(tile, per)


def kernel(body, name, grid, here, ins, outs, scratch=(), vmem=48):
    return pl.pallas_call(
        body,
        out_shape=[jax.ShapeDtypeStruct(shape, kind) for shape, kind, _ in outs],
        grid_spec=pltpu.PrefetchScalarGridSpec(
            num_scalar_prefetch=1,
            grid=grid,
            in_specs=[spec for _, spec in ins],
            out_specs=[spec for _, _, spec in outs],
            scratch_shapes=list(scratch),
        ),
        compiler_params=pltpu.CompilerParams(vmem_limit_bytes=vmem * 2**20),
        name=name,
    )(here, *[array for array, _ in ins])


def pieced(pieces, tile, columns, column, place):
    ins, start = [], 0
    for piece in pieces:
        count = piece.shape[0] // tile

        def index(i, h, start=start, count=count):
            return jnp.clip(place(i, h) - start, 0, count - 1), column(h)

        ins.append((piece, block((tile, columns), index)))
        start += count
    return ins


def picked(refs, counts, tile, held):
    start = 0
    for ref, count in zip(refs, counts):

        @pl.when((tile >= start) & (tile < start + count))
        def _(ref=ref):
            held[...] = ref[...]

        start += count
    return held[...].astype(F32)


def counts_of(pieces, tile):
    return [piece.shape[0] // tile for piece in pieces]


def row_index(rows):
    return lax.broadcasted_iota(jnp.int32, (rows, 1), 0)


def placed(place, width):
    return pl.ds(pl.multiple_of(place * width, width), width)


def cut_body(count, parts, here, *refs):
    ins, outs = refs[:count], refs[count:]
    at = 0
    for ref in ins:
        width = ref.shape[1] // parts
        for j in range(parts):
            outs[j][:, at : at + width] = ref[:, placed(here[0] ^ j, width)]
        at += width


def cut_columns(weights, here, parts):
    rows, width = weights[0].shape[0], sum(w.shape[1] for w in weights) // parts
    return kernel(
        partial(cut_body, len(weights), parts), "cut_columns", (1,), here,
        [(w, fixed(w.shape)) for w in weights],
        [((rows, width), BF, fixed((rows, width)))] * parts,
    )


def stack_body(parts, here, *refs):
    start = 0
    for out in refs[parts:]:
        for j in range(parts):
            out[here[0] ^ j] = refs[j][:, start : start + out.shape[2]]
        start += out.shape[2]


def stack_rows(pieces, widths, here):
    parts, rows = len(pieces), pieces[0].shape[0]
    return kernel(
        partial(stack_body, parts), "stack_rows", (1,), here,
        [(p, fixed(p.shape)) for p in pieces],
        [((parts, rows, width), BF, fixed((parts, rows, width))) for width in widths],
    )


def hold_body(here, in_ref, *refs):
    refs[-1][...] = in_ref[...]


def held_back(values, here, *others):
    rows, width = values.shape
    own = block((rows // 2, width), lambda i, h: (i, 0))
    (copy,) = kernel(
        hold_body, "hold", (2,), here,
        [(values, own)] + [(o, pl.BlockSpec(memory_space=pl.ANY)) for o in others],
        [((rows, width), values.dtype, own)],
    )
    return copy


def join_body(parts, count, here, *refs):
    ins, outs = refs[:parts], refs[parts:]
    at = 0
    for ref in outs:
        width = ref.shape[1] // parts
        for j in range(parts):
            ref[:, placed(here[0] ^ j, width)] = ins[j][:, at : at + width].astype(F32)
        at += width


def join_columns(pieces, widths, here):
    parts, rows = len(pieces), pieces[0].shape[0]
    return kernel(
        partial(join_body, parts, len(widths)), "join_columns", (1,), here,
        [(p, fixed(p.shape)) for p in pieces],
        [((rows, width), F32, fixed((rows, width))) for width in widths],
    )


def spread_body(counts, parts, product, here, *refs):
    bases, pieces, out, held = refs[: len(counts)], refs[len(counts) : -2], refs[-2], refs[-1]
    picked(bases, counts, pl.program_id(0), held)
    width = pieces[0].shape[1]
    for j in range(parts):
        at = placed(here[0] ^ j, width)
        piece, base = pieces[j][...].astype(F32), held[:, at].astype(F32)
        out[:, at] = (base * piece if product else base + piece).astype(BF)


def spread_columns(bases, columns, here, product, turn, tile, per):
    rows, width = sum(base.shape[0] for base in bases), bases[0].shape[1]

    def turned(i, j):
        return (lax.div(i, per) ^ j) * per + lax.rem(i, per) if turn else i

    (result,) = kernel(
        partial(spread_body, counts_of(bases, tile), len(columns), product), "spread_columns", (rows // tile,), here,
        pieced(bases, tile, width, lambda h: 0, lambda i, h: i)
        + [(c, block((tile, c.shape[1]), lambda i, h, j=j: (turned(i, j), 0))) for j, c in enumerate(columns)],
        [((rows, width), BF, block((tile, width), lambda i, h: (i, 0)))],
        [pltpu.VMEM((tile, width), bases[0].dtype)],
    )
    return result


def shuffled(values, groups, back=False):
    seq, dp = groups
    if back:
        seq, dp = dp, seq
    lane = lax.broadcasted_iota(jnp.int32, (1, PAIR), 1) < HEAD
    source = [s * dp + d for d in range(dp) for s in range(seq)]
    columns = []
    for one, two in zip(source[::2], source[1::2]):
        low = values[:, one // 2 * PAIR : (one // 2 + 1) * PAIR]
        high = values[:, two // 2 * PAIR : (two // 2 + 1) * PAIR]
        low = pltpu.roll(low, HEAD, 1) if one % 2 else low
        high = high if two % 2 else pltpu.roll(high, HEAD, 1)
        columns.append(jnp.where(lane, low, high))
    return jnp.concatenate(columns, axis=1)


def outside(values, groups, channels, back=False):
    seq, dp = groups[::-1] if back else groups
    return values.reshape(-1, seq, dp, channels).swapaxes(1, 2).reshape(values.shape)


def centre(values):
    centred = values - jnp.mean(values, axis=-1, keepdims=True)
    spread = jnp.mean(centred * centred, axis=-1, keepdims=True)
    return centred, lax.rsqrt(spread + EPSILON)


def mix_body(count, norm, groups, counts, per, here, *refs):
    pieces, (marks_ref, vec_ref) = refs[: len(counts)], refs[len(counts) : len(counts) + 2]
    outs, last, held = refs[len(counts) + 2 : -2], refs[-2], refs[-1]

    @pl.when(pl.program_id(0) == 0)
    def _():
        last[...] = jnp.zeros_like(last)

    values = picked(pieces, counts, relative(pl.program_id(0), per, here[0]), held)
    if norm:
        centred, inverse = centre(values)
        values = centred * inverse
    if groups:
        values = shuffled(values, groups)
    if norm:
        values = values * vec_ref[0:1, :] + vec_ref[1:2, :]
    rows = values.shape[0]
    previous = jnp.where(row_index(rows) == 0, last[0:1, :], pltpu.roll(values, 1, 0)) * marks_ref[:, 3:4]
    last[0:1, :] = values[rows - 1 :, :]
    step = values - previous
    outs[count][...] = step.astype(BF)
    for i in range(count):
        outs[i][...] = (previous + step * vec_ref[2 + i : 3 + i, :]).astype(BF)


def mixes(pieces, marks, vec, count, norm, groups, here, tile, per):
    rows, width = marks.shape[0], pieces[0].shape[1]
    own = block((tile, width), lambda i, h: (relative(i, per, h), 0))
    return kernel(
        partial(mix_body, count, norm, groups, counts_of(pieces, tile), per), "mixes", (rows // tile,), here,
        pieced(pieces, tile, width, lambda h: 0, lambda i, h: relative(i, per, h))
        + [(marks, block((tile, PAIR), lambda i, h: (i, 0))), (vec, fixed(vec.shape))],
        [((rows, width), BF, own)] * (count + 1),
        [pltpu.VMEM((8, width), F32), pltpu.VMEM((tile, width), BF)],
    )


def mixes_back_body(which, first, seq, here, *refs):
    count = len(which)
    grads, nexts, weights = refs[:count], refs[count : 2 * count], refs[2 * count : 3 * count]
    step_ref, marks_ref, next_marks_ref, vec_ref, out_ref, sums_ref = refs[3 * count :]

    @pl.when(pl.program_id(1) == 0)
    def _():
        sums_ref[...] = jnp.zeros_like(sums_ref)

    step = step_ref[...].astype(F32)
    rows = step.shape[0]
    total = straight = None
    for i in range(which[-1] + 1):
        grad = sum(
            dot(jnp.concatenate([grads[k][...], nexts[k][...]], axis=0), weights[k][...], NT)
            for k in range(count)
            if which[k] == i
        )
        sums_ref[i : i + 1, :] += jnp.sum(grad[:rows] * step, axis=0, keepdims=True)
        part = grad * vec_ref[i : i + 1, :]
        total, straight = (total + grad, straight + part) if i else (grad, part)
    inside = ((first + pl.program_id(1)) ^ here[0]) < seq - 1
    keep = jnp.concatenate([marks_ref[:, 3:4], jnp.where(inside, next_marks_ref[:, 3:4], 0.0)], axis=0)
    kept = (total - straight) * keep
    up = pltpu.roll(kept, kept.shape[0] - 1, 0)
    out_ref[...] = (straight[:rows] + up[:rows]).astype(BF)


EXTRA = 16


def mixes_back(terms, step, marks, vec, here, seq, first, count):
    rows, width = step.shape
    tile, columns = rows // seq, min(512, width)
    extras = tile // EXTRA

    def following(i, h):
        return jnp.minimum(((first + i) ^ h) + 1, seq - 1)

    ins = [(g, block((tile, n), lambda c, i, h, at=at: (first + i, at))) for _, g, at, _, _, n in terms]
    ins += [
        (g, block((EXTRA, n), lambda c, i, h, at=at: ((following(i, h) ^ h) * extras, at)))
        for _, g, at, _, _, n in terms
    ]
    ins += [(w, block((columns, n), lambda c, i, h, at=at: (c, at))) for _, _, _, w, at, n in terms]
    ins += [
        (step, block((tile, columns), lambda c, i, h: (first + i, c))),
        (marks, block((tile, PAIR), lambda c, i, h: ((first + i) ^ h, 0))),
        (marks, block((EXTRA, PAIR), lambda c, i, h: (following(i, h) * extras, 0))),
        (vec, block((8, columns), lambda c, i, h: (0, c))),
    ]
    return kernel(
        partial(mixes_back_body, [t[0] for t in terms], first, seq), "mixes_back", (width // columns, count), here, ins,
        [
            ((count * tile, width), BF, block((tile, columns), lambda c, i, h: (i, c))),
            ((8, width), F32, block((8, columns), lambda c, i, h: (0, c))),
        ],
    )


def mixes_back_scatter(terms, step, marks, vec, here, seq, beside):
    if seq != 4:
        grad, sums = mixes_back(terms, step, marks, vec, here, seq, 0, seq)
        return after(scatter_seq(blocks_of(grad, seq)), beside(grad)), sums

    def call(first, count, *before):
        ordered = after([t[1] for t in terms], *before)
        return mixes_back(
            [(t[0], g) + t[2:] for t, g in zip(terms, ordered)], step, marks, vec, here, seq, first, count
        )

    far, sums_far = call(3, 1)
    near, sums_near = call(1, 2, far)
    parts = [None] + blocks_of(near, 2) + [far]
    started = after(scatter_start(parts), near)
    relayed = scatter_relay(parts, started)
    own, sums_own = call(0, 1, near, relayed)
    return after(scatter_end(own, relayed), beside(relayed)), sums_far + sums_near + sums_own


def after_body(count, here, x_ref, vec_ref, *refs):
    after_ref, normed_ref = refs[count:]
    after = x_ref[...].astype(F32)
    for ref in refs[:count]:
        after = after + ref[...].astype(F32)
    after_ref[...] = after
    centred, inverse = centre(after)
    normed_ref[...] = (centred * inverse * vec_ref[0:1, :] + vec_ref[1:2, :]).astype(BF)


def after_norm(inputs, terms, vec, here):
    rows, width = inputs.shape
    own = block((CHUNK, width), lambda i, h: (i, 0))
    return kernel(
        partial(after_body, len(terms)), "after_norm", (rows // CHUNK,), here,
        [(inputs, own), (vec, fixed(vec.shape))] + [(t, own) for t in terms],
        [((rows, width), F32, own), ((rows, width), BF, own)],
    )


def norm_back_body(count, groups, here, x_ref, base_ref, vec_ref, *refs):
    wide_ref, narrow_ref, sums_ref = refs[count:]

    @pl.when(pl.program_id(0) == 0)
    def _():
        sums_ref[...] = jnp.zeros_like(sums_ref)

    grad = refs[0][...].astype(F32)
    for ref in refs[1:count]:
        grad = grad + ref[...].astype(F32)
    if groups:
        grad = shuffled(grad, groups, back=True)
    centred, inverse = centre(x_ref[...].astype(F32))
    normed = centred * inverse
    sums_ref[0:1, :] += jnp.sum(grad * normed, axis=0, keepdims=True)
    sums_ref[1:2, :] += jnp.sum(grad, axis=0, keepdims=True)
    grad = grad * vec_ref[0:1, :]
    grad = grad - jnp.mean(grad, axis=-1, keepdims=True) - normed * jnp.mean(grad * normed, axis=-1, keepdims=True)
    result = base_ref[...].astype(F32) + inverse * grad
    wide_ref[...] = result
    narrow_ref[...] = result.astype(BF)


def norm_back(terms, inputs, base, vec, groups, here):
    rows, width = inputs.shape
    own = block((CHUNK, width), lambda i, h: (i, 0))
    return kernel(
        partial(norm_back_body, len(terms), groups), "norm_back", (rows // CHUNK,), here,
        [(inputs, own), (base, own), (vec, fixed(vec.shape))] + [(t, own) for t in terms],
        [((rows, width), F32, own), ((rows, width), BF, own), ((8, width), F32, fixed((8, width)))],
    )


def gate_body(mix_ref, weight_ref, wkv_ref, par_ref, gate_ref, mixed_ref):
    gate = dot(mix_ref[...], weight_ref[...], NN)
    gate_ref[...] = gate
    ones = jnp.where(same_head(), 1.0, 0.0).astype(BF)
    for pair in range(gate.shape[1] // PAIR):
        at = slice(pair * PAIR, (pair + 1) * PAIR)
        wkv = wkv_ref[:, at]
        centred = wkv - head_sum_fine(wkv, ones) * (1.0 / HEAD)
        spread = head_sum(centred * centred, ones) * (1.0 / HEAD)
        normed = centred * lax.rsqrt(spread + GROUP_EPSILON) * par_ref[1:2, at] + par_ref[2:3, at]
        mixed_ref[:, at] = (normed * (gate[:, at] / (1.0 + jnp.exp(-gate[:, at])))).astype(BF)


def gated(mix_g, weights, wkv, params, here, seq):
    rows, width = mix_g.shape
    tile, part = rows // seq, wkv.shape[1]
    own = block((tile, part), lambda i, h: (i, 0))
    return kernel(
        lambda here, *refs: gate_body(*refs), "gate", (seq,), here,
        [
            (mix_g, block((tile, width), lambda i, h: (i, 0))),
            (weights, block((width, part), lambda i, h: (0, 0))),
            (wkv, own),
            (params, fixed(params.shape)),
        ],
        [((rows, part), F32, own), ((rows, part), BF, own)],
    )


def columns_body(here, left_ref, right_ref, out_ref):
    out_ref[...] = dot(left_ref[...], right_ref[...], NN).astype(BF)


def columns_product(left, right, part, relative_to, here, seq):
    rows, depth = left.shape
    tile = rows // seq
    (result,) = kernel(
        columns_body, "value_columns", (seq,), here,
        [
            (left, block((tile, depth), lambda i, h: (i, 0))),
            (right, block((depth, part), lambda i, h: (0, h ^ relative_to))),
        ],
        [((rows, part), BF, block((tile, part), lambda i, h: (i ^ relative_to, 0)))],
    )
    return result


def channel_body(counts, here, pre_ref, *refs):
    grads, terms, (channel_ref, d_recept_ref, held) = refs[: len(counts)], refs[len(counts) : -3], refs[-3:]
    value = sum(ref[...].astype(F32) for ref in terms)
    opened = 1.0 / (1.0 + jnp.exp(-pre_ref[...]))
    channel = opened * value
    channel_ref[...] = channel.astype(BF)
    grad = picked(grads, counts, pl.program_id(0), held)
    d_recept_ref[...] = (grad * channel * (1.0 - opened)).astype(BF)


def channel_out(terms, pre, grads, here, tile):
    rows, part = pre.shape
    own = block((tile, part), lambda i, h: (i, 0))
    return kernel(
        partial(channel_body, counts_of(grads, tile)), "channel", (rows // tile,), here,
        [(pre, own)] + pieced(grads, tile, part, lambda h: h, lambda i, h: i) + [(t, own) for t in terms],
        [((rows, part), BF, own)] * 2,
        [pltpu.VMEM((tile, part), BF)],
    )


def head_masks():
    lane = lax.broadcasted_iota(jnp.int32, (1, PAIR), 1)
    first = (lane < HEAD).astype(F32)
    return first, 1.0 - first


def same_head():
    row = lax.broadcasted_iota(jnp.int32, (PAIR, PAIR), 0) < HEAD
    column = lax.broadcasted_iota(jnp.int32, (PAIR, PAIR), 1) < HEAD
    return row == column


def dot(left, right, dims):
    return lax.dot_general(left, right, dims, preferred_element_type=F32)


def head_sum(values, ones):
    return dot(values.astype(BF), ones, NN)


def head_sum_fine(values, ones):
    coarse = values.astype(BF)
    rest = (values - coarse.astype(F32)).astype(BF)
    return dot(coarse, ones, NN) + dot(rest, ones, NN)


def stacked(values, first, second):
    return jnp.concatenate([(values * first).astype(BF), (values * second).astype(BF)], axis=0)


def masks_of(rows_ref, columns_ref):
    segment = rows_ref[:, 0:1]
    reaches = rows_ref[:, 1:2]
    last_same = rows_ref[:, 2:3]
    reach_last = rows_ref[CHUNK - 1 : CHUNK, 1:2]
    before = lax.broadcasted_iota(jnp.int32, (CHUNK, CHUNK), 1) < lax.broadcasted_iota(
        jnp.int32, (CHUNK, CHUNK), 0
    )
    allowed = jnp.where((segment == columns_ref[0:1, :]) & before, 1.0, 0.0)
    return reaches, last_same, reach_last, jnp.concatenate([allowed, allowed], axis=0)


def wkv_forward_body(
    here, r_ref, k_ref, v_ref, rows_ref, columns_ref, grow_ref, shrink_ref, tail_ref, par_ref,
    wkv_ref, states_ref, state,
):
    @pl.when(pl.program_id(0) == 0)
    def _():
        state[...] = jnp.zeros_like(state)

    first, second = head_masks()
    block = same_head()
    ones = jnp.where(block, 1.0, 0.0).astype(BF)
    reaches, last_same, reach_last, allowed = masks_of(rows_ref, columns_ref)
    for pair in range(r_ref.shape[1] // PAIR):
        at = slice(pair * PAIR, (pair + 1) * PAIR)
        r, k, v = r_ref[:, at].astype(F32), k_ref[:, at].astype(F32), v_ref[:, at].astype(F32)
        bonus, decay = par_ref[0:1, at], par_ref[3:4, at]
        held = state[at, :]
        held_b = held.astype(BF)
        states_ref[0, at, :] = held_b
        grown = r * grow_ref[:, at]
        shrunk = (k * shrink_ref[:, at]).astype(BF)
        scores = (dot(stacked(grown, first, second), shrunk, NT) * allowed).astype(BF)
        both = jnp.concatenate([scores[:CHUNK], scores[CHUNK:]], axis=1)
        wkv = dot(both, stacked(v, first, second), NN)
        wkv = wkv + dot((grown * reaches).astype(BF), held_b, NT)
        wkv = wkv + head_sum(r * bonus * k, ones) * v
        fresh = dot(v_ref[:, at], (k * tail_ref[:, at] * last_same).astype(BF), TN)
        state[at, :] = held * (decay * reach_last) + jnp.where(block, fresh, 0.0)
        wkv_ref[:, at] = wkv


def wkv_backward_body(
    here, r_ref, k_ref, v_ref, g_ref, wkv_ref, d_mixed_ref, states_ref,
    rows_ref, columns_ref, grow_ref, shrink_ref, tail_ref, par_ref,
    d_r_ref, d_k_ref, d_v_ref, d_g_ref, sums_ref, d_state,
):
    @pl.when(pl.program_id(0) == 0)
    def _():
        d_state[...] = jnp.zeros_like(d_state)
        sums_ref[...] = jnp.zeros_like(sums_ref)

    first, second = head_masks()
    block = same_head()
    ones = jnp.where(block, 1.0, 0.0).astype(BF)
    reaches, last_same, reach_last, allowed = masks_of(rows_ref, columns_ref)
    offset = lax.broadcasted_iota(jnp.int32, (CHUNK, PAIR), 0).astype(F32)
    for pair in range(r_ref.shape[1] // PAIR):
        at = slice(pair * PAIR, (pair + 1) * PAIR)
        bonus, gain, bias, decay = (par_ref[i : i + 1, at] for i in range(4))
        wkv, gate, d_mixed = wkv_ref[:, at], g_ref[:, at], d_mixed_ref[:, at].astype(F32)
        centred = wkv - head_sum_fine(wkv, ones) * (1.0 / HEAD)
        spread = head_sum(centred * centred, ones) * (1.0 / HEAD)
        inverse = lax.rsqrt(spread + GROUP_EPSILON)
        normed = centred * inverse
        opened = 1.0 / (1.0 + jnp.exp(-gate))
        d_scaled = d_mixed * gate * opened
        d_g = d_mixed * (normed * gain + bias) * opened * (1.0 + gate * (1.0 - opened))
        d_g_ref[:, at] = d_g.astype(BF)
        d_normed = d_scaled * gain
        mean_one = head_sum(d_normed, ones) * (1.0 / HEAD)
        mean_two = head_sum(d_normed * normed, ones) * (1.0 / HEAD)
        d_wkv = inverse * (d_normed - mean_one - normed * mean_two)
        r, k, v = r_ref[:, at].astype(F32), k_ref[:, at].astype(F32), v_ref[:, at].astype(F32)
        v_b, d_wkv_b = v_ref[:, at], d_wkv.astype(BF)
        grow, shrink, tail = grow_ref[:, at], shrink_ref[:, at], tail_ref[:, at] * last_same
        held = states_ref[0, at, :]
        later = d_state[at, :]
        later_b = later.astype(BF)
        grown = r * grow
        shrunk = k * shrink
        shrunk_b = shrunk.astype(BF)
        tailed_b = (k * tail).astype(BF)
        grown_two = stacked(grown, first, second)
        d_wkv_two = stacked(d_wkv, first, second)
        scores = (dot(grown_two, shrunk_b, NT) * allowed).astype(BF)
        d_scores = (dot(d_wkv_two, v_b, NT) * allowed).astype(BF)
        d_both = jnp.concatenate([d_scores[:CHUNK], d_scores[CHUNK:]], axis=1)
        d_grown = dot(d_both, stacked(shrunk, first, second), NN)
        d_grown = d_grown + dot((d_wkv * reaches).astype(BF), held, NN)
        d_shrunk = dot(d_scores, grown_two, TN)
        d_tailed = dot(v_b, later_b, NN)
        share = head_sum(r * bonus * k, ones)
        d_share = head_sum(d_wkv * v, ones)
        d_v = dot(scores, d_wkv_two, TN) + dot(tailed_b, later_b, NT) + share * d_wkv
        d_r_ref[:, at] = (d_grown * grow + d_share * bonus * k).astype(BF)
        d_k_ref[:, at] = (d_shrunk * shrink + d_tailed * tail + d_share * bonus * r).astype(BF)
        d_v_ref[:, at] = d_v.astype(BF)
        carried = decay * reach_last
        d_fresh = dot(d_wkv_b, (grown * reaches).astype(BF), TN)
        d_state[at, :] = later * carried + jnp.where(block, d_fresh, 0.0)
        grown_b = grown.astype(BF).astype(F32)
        d_log = (
            offset * grown_b * d_grown
            - (offset + 1.0) * shrunk_b.astype(F32) * d_shrunk
            + (CHUNK - 1.0 - offset) * tailed_b.astype(F32) * d_tailed
        )
        kept = CHUNK * carried * jnp.sum(held.astype(F32) * later, axis=0, keepdims=True)
        sums_ref[0:1, at] += jnp.sum(d_log, axis=0, keepdims=True) + kept
        sums_ref[1:2, at] += jnp.sum(d_share * r * k, axis=0, keepdims=True)
        sums_ref[2:3, at] += jnp.sum(d_scaled * normed, axis=0, keepdims=True)
        sums_ref[3:4, at] += jnp.sum(d_scaled, axis=0, keepdims=True)


def wkv_blocks(width, chunks, per, backward):
    def chunk(i):
        return chunks - 1 - i if backward else i

    tokens = block((CHUNK, width), lambda i, h: (relative(chunk(i), per, h), 0))
    states = block((1, width, PAIR), lambda i, h: (chunk(i), 0, 0))
    tables = [
        block((CHUNK, PAIR), lambda i, h: (chunk(i), 0)),
        block((8, CHUNK), lambda i, h: (0, chunk(i))),
    ]
    return tokens, states, tables + [fixed((CHUNK, width))] * 3 + [fixed((8, width))]


def wkv_forward(r, k, v, tables, here, per):
    length, width = r.shape
    chunks = length // CHUNK
    tokens, states, blocks = wkv_blocks(width, chunks, per, False)
    return kernel(
        wkv_forward_body, "wkv_forward", (chunks,), here,
        [(a, tokens) for a in (r, k, v)] + list(zip(tables, blocks)),
        [((length, width), F32, tokens), ((chunks, width, PAIR), BF, states)],
        [pltpu.VMEM((width, PAIR), F32)],
    )


def wkv_backward(r, k, v, gate, wkv, d_mixed, states_kept, tables, here, per):
    length, width = r.shape
    chunks = length // CHUNK
    tokens, states, blocks = wkv_blocks(width, chunks, per, True)
    return kernel(
        wkv_backward_body, "wkv_backward", (chunks,), here,
        [(a, tokens) for a in (r, k, v, gate, wkv, d_mixed)] + [(states_kept, states)] + list(zip(tables, blocks)),
        [((length, width), BF, tokens)] * 4 + [((8, width), F32, fixed((8, width)))],
        [pltpu.VMEM((width, PAIR), F32)],
    )


def wkv_tables(piece, keep, log_decay, bonus, gain, bias):
    length = piece.shape[0]
    by_chunk = piece.reshape(length // CHUNK, CHUNK)
    before = jnp.concatenate([jnp.full((1,), -1, piece.dtype), by_chunk[:-1, -1]])
    reaches = (by_chunk == before[:, None]).reshape(-1)
    last_same = (by_chunk == by_chunk[:, -1:]).reshape(-1)
    marks = jnp.stack([piece.astype(F32), reaches.astype(F32), last_same.astype(F32), keep], axis=1)
    rows = jnp.pad(marks, ((0, 0), (0, PAIR - 4)))
    columns = jnp.broadcast_to(piece.astype(F32)[None], (8, length))
    offset = jnp.arange(CHUNK).astype(F32)[:, None]
    grow = jnp.exp(offset * log_decay)
    shrink = jnp.exp(-(offset + 1.0) * log_decay)
    tail = jnp.exp((CHUNK - 1.0 - offset) * log_decay)
    zero = jnp.zeros_like(bonus)
    params = jnp.stack([bonus, gain, bias, jnp.exp(CHUNK * log_decay)] + [zero] * 4)
    return rows, columns, grow, shrink, tail, params


def segment_of(lengths, positions):
    rank = jnp.arange(lengths.shape[0])
    starts = jnp.sum(jnp.where(rank[:, None] > rank[None, :], lengths[None, :], 0), axis=1)
    later_flags = (positions[:, None] >= starts[None, 1:]).astype(jnp.int32)
    first_flags = jnp.any(positions[:, None] == starts[None, :], axis=1)
    return (jnp.sum(later_flags, axis=1), first_flags)


def rows_of(vec, *rows):
    return jnp.pad(jnp.stack([vec[i] for i in rows]), ((0, 8 - len(rows)), (0, 0)))


def shards(
    tokens, seq_lengths, out_grad, w_receptance, w_key, w_value, w_gate, w_output,
    ffn_key, ffn_receptance, ffn_value, vectors,
):
    seq, dp = lax.axis_size("seq"), lax.axis_size("dp")
    place = lax.axis_index("seq")
    here = jnp.reshape(place, (1,)).astype(jnp.int32)
    inputs_b, grad_b = tokens[0], out_grad[0]
    own_rows, width = inputs_b.shape
    length, part, unit = own_rows * seq, width // seq, vectors.shape[1]
    per, tile = own_rows // CHUNK, own_rows // 2
    hidden_width = ffn_key.shape[1] // seq
    groups = (seq, dp)
    within = groups if unit == HEAD else None

    def stacked_columns(weights, widths, beside=()):
        stacked = stack_rows(after(trade_seq(cut_columns(weights, here, seq)), beside), widths, here)
        return [w.reshape(-1, w.shape[-1]) for w in stacked]

    def gather_dp(rows):
        return lax.all_gather(rows, "dp", axis=0, tiled=True)

    def scatter_dp(grad):
        return lax.psum_scatter(grad, "dp", scatter_dimension=0, tiled=True)

    def owners_rows(summed, widths):
        rows = summed.shape[0] // seq
        parts = [lax.dynamic_slice_in_dim(summed, (place ^ j) * rows, rows, 0) for j in range(seq)]
        return join_columns(trade_seq(parts), widths, here)

    def turn_pieces(pieces):
        if within is not None:
            return pieces
        return [outside(p, groups, unit) for p in pieces]

    positions = jnp.arange(length, dtype=jnp.int32)
    piece, first_flags = segment_of(seq_lengths[0], positions)

    vec_seq = gather_small(vectors[None], "seq")
    tokens_held = held_back(inputs_b, here, vec_seq)
    columns_in, columns_g = stacked_columns([w_receptance, w_key, w_value, w_gate], [3 * part, part], tokens_held)
    full_in = gather_dp(columns_in)
    vec_parts = gather_small(vec_seq[None], "dp").astype(F32)
    vec = vec_parts.transpose(2, 1, 0, 3).reshape(-1, width)
    turned = vec_parts.transpose(2, 0, 1, 3).reshape(-1, width)
    vec_own = lax.dynamic_slice_in_dim(vec, place * part, part, 1)
    log_decay = -jnp.exp(vec_own[6])
    tables = wkv_tables(
        piece, 1.0 - first_flags.astype(F32), log_decay, vec_own[7], vec_own[8], vec_own[9]
    )
    marks = tables[0]
    rows_one = rows_of(turned, 0, 1, 2, 3, 4, 5)
    tokens_all = gather_seq(tokens_held, (rows_one, tables))
    full_g = gather_dp(after(columns_g, tokens_all[1:3], rows_one))
    own_o = gather_dp(after(w_output, tokens_all))

    mix_r, mix_k, mix_v, mix_g, step = mixes(
        turn_pieces(tokens_all), marks, rows_one, 4, True, within, here, tile, own_rows // tile
    )
    recept, keyed, valued = (
        dot(m, full_in[:, i * part : (i + 1) * part], NN).astype(BF)
        for i, m in enumerate((mix_r, mix_k, mix_v))
    )
    projected = (recept, keyed, valued)
    (columns_c,) = stacked_columns(after([ffn_key, ffn_receptance], mix_r), [hidden_width + part], projected)
    full_c = gather_dp(columns_c)
    full_ck, full_cr = full_c[:, :hidden_width], full_c[:, hidden_width:]
    full_cv = gather_dp(after(ffn_value, columns_c))
    wkv, states = wkv_forward(recept, keyed, valued, tables, here, per)
    grad_all = gather_seq(after(grad_b, mix_r), wkv)
    gate_pre, mixed = gated(mix_g, full_g, wkv, tables[5], here, seq)
    attn = [dot(rows, own_o, NN).astype(BF) for rows in blocks_of(after(mixed, grad_all[3:]), seq)]
    after_mix, normed_two = after_norm(inputs_b, scatter_seq(attn), rows_of(vec, 10, 11), here)

    mix_k2, mix_r2, step_two = mixes(
        turn_pieces(gather_seq(normed_two)), marks, rows_of(turned, 10, 11, 12, 13), 2, False, within, here, tile,
        own_rows // tile,
    )
    recept_pre = dot(mix_r2, full_cr, NN)
    opened = gather_seq(jax.nn.sigmoid(recept_pre).astype(BF))
    key_pre = dot(mix_k2, full_ck, NN)
    smooth = jax.nn.softplus(key_pre)
    hidden = (smooth * smooth).astype(BF)
    slope = (2.0 * smooth * jax.nn.sigmoid(key_pre)).astype(BF)
    hidden, slope = lax.optimization_barrier((hidden, slope))
    later = after(hidden, opened[1:3])
    value_parts = [columns_product(later if j < 2 else hidden, full_cv, part, j, here, seq) for j in reversed(range(seq))]
    value_parts = value_parts[::-1]
    value_relayed = scatter_relay(value_parts, scatter_start(value_parts))
    d_value = spread_columns(
        grad_all, by_block(after(opened, value_parts, value_relayed)), here, True, True, tile, own_rows // tile
    )

    grad_cv = dot(hidden, d_value, TN).astype(BF)
    summed_cv = scatter_dp(grad_cv)
    value_terms = scatter_end(value_parts[0], value_relayed)
    d_hidden = dot(after(d_value, grad_cv), full_cv, NT)
    d_key_two = (d_hidden * slope.astype(F32)).astype(BF)
    channel, d_recept_two = channel_out(value_terms, recept_pre, grad_all, here, tile)
    half, first = part // 2, hidden_width // (part // 2)
    grad_ck, grad_cr = [], []

    def beside_two(relayed):
        grad_ck.append(dot(after(mix_k2, relayed), d_key_two, TN).astype(BF))
        grad_cr.append(dot(after(mix_r2, relayed, grad_ck), d_recept_two, TN).astype(BF))
        return grad_ck, grad_cr

    terms_two, sums_two = mixes_back_scatter(
        [(0, d_key_two, 0, full_c, 0, hidden_width)]
        + [(1, d_recept_two, i, full_c, first + i, half) for i in range(2)],
        step_two, marks, rows_of(turned, 12, 13), here, seq, beside_two,
    )
    summed_ck, summed_cr = scatter_dp(grad_ck[0]), scatter_dp(grad_cr[0])
    if within is None:
        terms_two = [outside(t, groups, unit, back=True) for t in terms_two]
    d_after, d_attn, norm_sums_two = norm_back(terms_two, after_mix, grad_b, rows_of(vec, 10), within, here)

    d_attn = jnp.concatenate(after(gather_seq(d_attn), summed_cv), axis=0)
    d_mixed = dot(d_attn, own_o, NT).astype(BF)
    grad_wo = dot(mixed, d_attn, TN).astype(BF)
    d_mixed = after(d_mixed, grad_wo, summed_ck)
    summed_o = scatter_dp(grad_wo)
    d_recept, d_keyed, d_valued, d_gate, sums = wkv_backward(
        recept, keyed, valued, gate_pre, wkv, d_mixed, states, tables, here, per
    )
    grads_vg = [dot(mix_v, d_valued, TN).astype(BF), dot(mix_g, d_gate, TN).astype(BF)]
    summed_vg = scatter_dp(jnp.concatenate(grads_vg, axis=1))
    grads_rk, sum_cv = [], []

    def beside(relayed):
        grads_rk.extend(
            dot(after(m, relayed), d, TN).astype(BF) for m, d in ((mix_r, d_recept), (mix_k, d_keyed))
        )
        sum_cv.append(after(summed_cv, relayed).astype(F32))
        return grads_rk, sum_cv

    d_recept, d_keyed = after((d_recept, d_keyed), grads_vg, summed_o)
    terms, sums_one = mixes_back_scatter(
        [(i, d, 0, full_in, i, part) for i, d in enumerate((d_recept, d_keyed, d_valued))]
        + [(3, d_gate, 0, full_g, 0, part)],
        step, marks, rows_of(turned, 2, 3, 4, 5), here, seq, beside,
    )
    summed_rk = scatter_dp(jnp.concatenate(grads_rk, axis=1))
    channel = trade_seq(blocks_of(after(channel, terms), seq))
    out_rows = spread_columns([after_mix], channel, here, False, False, CHUNK, per)
    (sum_ck,) = owners_rows(after(summed_ck, terms), [ffn_key.shape[1]])
    if within is None:
        terms = [outside(t, groups, unit, back=True) for t in terms]
    tokens_grad, _, norm_sums = norm_back(terms, inputs_b, d_after, rows_of(vec, 0), within, here)

    (sum_cr,) = owners_rows(after(summed_cr, terms), [width])
    (sum_cv,) = sum_cv
    sum_o = summed_o.astype(F32)
    sum_v, sum_g = owners_rows(summed_vg, [width] * 2)
    sum_r, sum_k = owners_rows(summed_rk, [width] * 2)

    def by_device(rows, turn):
        if turn:
            return rows.reshape(-1, dp, seq, unit).transpose(1, 2, 0, 3)
        return rows.reshape(-1, seq, dp, unit).transpose(2, 1, 0, 3)

    own_sums = jnp.stack([sums[0] * log_decay, sums[1], sums[2], sums[3]])
    own_sums = lax.dynamic_update_slice(jnp.zeros((4, width), F32), own_sums, (0, place * part))
    vector_rows = jnp.concatenate(
        [
            by_device(norm_sums[:2], False), by_device(sums_one[:4], True), by_device(own_sums, False),
            by_device(norm_sums_two[:2], False), by_device(sums_two[:2], True),
        ],
        axis=2,
    )
    sum_vec = scatter_small(vector_rows.reshape((-1,) + vector_rows.shape[2:]))
    return (
        out_rows[None], tokens_grad[None], sum_r, sum_k, sum_v, sum_g, sum_o,
        sum_ck, sum_cr, sum_cv, sum_vec,
    )


def solution(mesh):
    tokens = P("dp", "seq", None)
    rows = P(("seq", "dp"), None)
    columns = P(None, ("seq", "dp"))
    return jax.shard_map(
        shards,
        mesh=mesh,
        in_specs=(tokens, P("dp", None), tokens) + (rows,) * 8 + (columns,),
        out_specs=(tokens, tokens) + (rows,) * 8 + (columns,),
        check_vma=False,
    )
```

```python
from functools import partial

import jax
import jax.numpy as jnp
from jax import lax
from jax.experimental import pallas as pl
from jax.experimental.pallas import tpu as pltpu
from jax.sharding import PartitionSpec as P

HEAD = 64
PAIR = 128
CHUNK = 128
EPSILON = 1e-05
GROUP_EPSILON = 1.0
BF = jnp.bfloat16
F32 = jnp.float32
NT = (((1,), (1,)), ((), ()))
TN = (((0,), (0,)), ((), ()))
NN = (((1,), (0,)), ((), ()))


def swap(value, axis, distance):
    size = lax.axis_size(axis)
    return lax.ppermute(value, axis, [(i, i ^ distance) for i in range(size)])


def after(value, *others):
    return lax.optimization_barrier((value, others))[0]


def gather_seq(part, first=()):
    size = lax.axis_size("seq")
    if size == 4:
        half = part.shape[0] // 2
        one, two = swap(part, "seq", 1), swap(part, "seq", 2)
        one, two = after((one, two), first)
        low, high = swap(one[:half], "seq", 2), swap(two[half:], "seq", 1)
        return [part, one, two, low, high]
    return [part] + [swap(part, "seq", distance) for distance in range(1, size)]


def by_block(pieces):
    if lax.axis_size("seq") == 4:
        return pieces[:3] + [jnp.concatenate(pieces[3:], axis=0)]
    return pieces


def scatter_start(parts):
    if lax.axis_size("seq") != 4:
        return ()
    low, high = parts[3:] if len(parts) == 5 else blocks_of(parts[3], 2)
    return swap(low, "seq", 1), swap(high, "seq", 2)


def relay_body(here, one_ref, two_ref, low_ref, high_ref, one_out, two_out):
    one, two = one_ref[...], two_ref[...]
    first = pl.program_id(0) == 0
    low, high = low_ref[...].astype(F32), high_ref[...].astype(F32)
    one_out[...] = jnp.where(first, one, (one.astype(F32) + high).astype(BF))
    two_out[...] = jnp.where(first, (two.astype(F32) + low).astype(BF), two)


def scatter_relay(parts, started, here):
    if lax.axis_size("seq") != 4:
        return parts[1:]
    (_, one, two, *_), (low, high) = parts, started
    (rows, width), half = one.shape, block(low.shape, lambda i, h: (i, 0))
    return kernel(
        relay_body, "relay", (2,), here,
        [(one, half), (two, half), (low, fixed(low.shape)), (high, fixed(low.shape))],
        [((rows, width), BF, half)] * 2,
    )


def scatter_end(own, relayed):
    return [own] + [swap(part, "seq", j + 1) for j, part in enumerate(relayed)]


def scatter_seq(parts, here):
    return scatter_end(parts[0], scatter_relay(parts, scatter_start(parts), here))


def trade_seq(parts):
    return [parts[0]] + [swap(part, "seq", j + 1) for j, part in enumerate(parts[1:])]


def blocks_of(values, size):
    rows = values.shape[0] // size
    return [values[j * rows : (j + 1) * rows] for j in range(size)]


def bits_of(size):
    return [1 << b for b in range(size.bit_length() - 1)]


def gather_small(part, axis):
    for bit in bits_of(lax.axis_size(axis)):
        other = swap(part, axis, bit)
        second = (lax.axis_index(axis) & bit) != 0
        part = jnp.concatenate([jnp.where(second, other, part), jnp.where(second, part, other)], axis=0)
    return part


def scatter_small(parts):
    for axis in ("dp", "seq"):
        for bit in reversed(bits_of(lax.axis_size(axis))):
            half = parts.shape[0] // 2
            second = (lax.axis_index(axis) & bit) != 0
            low, high = parts[:half], parts[half:]
            parts = jnp.where(second, high, low) + swap(jnp.where(second, low, high), axis, bit)
    return parts[0]


def block(shape, index):
    return pl.BlockSpec(shape, lambda *i: index(*i[:-1], i[-1][0]))


def fixed(shape):
    return pl.BlockSpec(shape, lambda *i: (0,) * len(shape))


def relative(tile, per, here):
    return (lax.div(tile, per) ^ here) * per + lax.rem(tile, per)


def kernel(body, name, grid, here, ins, outs, scratch=(), vmem=48):
    return pl.pallas_call(
        body,
        out_shape=[jax.ShapeDtypeStruct(shape, kind) for shape, kind, _ in outs],
        grid_spec=pltpu.PrefetchScalarGridSpec(
            num_scalar_prefetch=1,
            grid=grid,
            in_specs=[spec for _, spec in ins],
            out_specs=[spec for _, _, spec in outs],
            scratch_shapes=list(scratch),
        ),
        compiler_params=pltpu.CompilerParams(vmem_limit_bytes=vmem * 2**20),
        name=name,
    )(here, *[array for array, _ in ins])


def pieced(pieces, tile, columns, column, place):
    ins, start = [], 0
    for piece in pieces:
        count = piece.shape[0] // tile

        def index(i, h, start=start, count=count):
            return jnp.clip(place(i, h) - start, 0, count - 1), column(h)

        ins.append((piece, block((tile, columns), index)))
        start += count
    return ins


def picked(refs, counts, tile, held):
    start = 0
    for ref, count in zip(refs, counts):

        @pl.when((tile >= start) & (tile < start + count))
        def _(ref=ref):
            held[...] = ref[...]

        start += count
    return held[...].astype(F32)


def counts_of(pieces, tile):
    return [piece.shape[0] // tile for piece in pieces]


def row_index(rows):
    return lax.broadcasted_iota(jnp.int32, (rows, 1), 0)


def placed(place, width):
    return pl.ds(pl.multiple_of(place * width, width), width)


def cut_body(count, parts, here, *refs):
    ins, beside, outs = refs[:count], refs[count], refs[count + 1 :]
    rows = ins[0].shape[0]
    for j in range(parts):
        outs[j][rows:, :] = jnp.zeros_like(outs[j][rows:, :])
        outs[j][rows:, : beside.shape[1]] = beside[...]
    at = 0
    for ref in ins:
        width = ref.shape[1] // parts
        for j in range(parts):
            outs[j][:rows, at : at + width] = ref[:, placed(here[0] ^ j, width)]
        at += width


def cut_columns(weights, beside, here, parts):
    rows, width = weights[0].shape[0] + beside.shape[0], sum(w.shape[1] for w in weights) // parts
    return kernel(
        partial(cut_body, len(weights), parts), "cut_columns", (1,), here,
        [(w, fixed(w.shape)) for w in [*weights, beside]],
        [((rows, width), BF, fixed((rows, width)))] * parts,
    )


def stack_body(parts, here, *refs):
    start = 0
    outs, beside = refs[parts:-1], refs[-1]
    for out in outs:
        for j in range(parts):
            out[here[0] ^ j] = refs[j][: out.shape[1], start : start + out.shape[2]]
        start += out.shape[2]
    for j in range(parts):
        beside[here[0] ^ j] = refs[j][out.shape[1] :, : beside.shape[2]]


def stack_rows(pieces, widths, beside, here):
    parts, rows = len(pieces), pieces[0].shape[0] - beside.shape[0]
    shapes = [(parts, rows, width) for width in widths] + [(parts,) + beside.shape]
    return kernel(
        partial(stack_body, parts), "stack_rows", (1,), here,
        [(p, fixed(p.shape)) for p in pieces],
        [(shape, BF, fixed(shape)) for shape in shapes],
    )


def hold_body(here, in_ref, *refs):
    refs[-1][...] = in_ref[...]


def held_back(values, here, *others):
    rows, width = values.shape
    own = block((rows // 2, width), lambda i, h: (i, 0))
    (copy,) = kernel(
        hold_body, "hold", (2,), here,
        [(values, own)] + [(o, pl.BlockSpec(memory_space=pl.ANY)) for o in others],
        [((rows, width), values.dtype, own)],
    )
    return copy


def join_body(parts, count, here, *refs):
    ins, outs = refs[:parts], refs[parts:]
    at = 0
    for ref in outs:
        width = ref.shape[1] // parts
        for j in range(parts):
            ref[:, placed(here[0] ^ j, width)] = ins[j][:, at : at + width].astype(F32)
        at += width


def join_columns(pieces, widths, here):
    parts, rows = len(pieces), pieces[0].shape[0]
    return kernel(
        partial(join_body, parts, len(widths)), "join_columns", (1,), here,
        [(p, fixed(p.shape)) for p in pieces],
        [((rows, width), F32, fixed((rows, width))) for width in widths],
    )


def spread_body(counts, parts, product, here, *refs):
    bases, pieces, out, held = refs[: len(counts)], refs[len(counts) : -2], refs[-2], refs[-1]
    picked(bases, counts, pl.program_id(0), held)
    width = pieces[0].shape[1]
    for j in range(parts):
        at = placed(here[0] ^ j, width)
        piece, base = pieces[j][...].astype(F32), held[:, at].astype(F32)
        out[:, at] = (base * piece if product else base + piece).astype(BF)


def spread_columns(bases, columns, here, product, turn, tile, per):
    rows, width = sum(base.shape[0] for base in bases), bases[0].shape[1]

    def turned(i, j):
        return (lax.div(i, per) ^ j) * per + lax.rem(i, per) if turn else i

    (result,) = kernel(
        partial(spread_body, counts_of(bases, tile), len(columns), product), "spread_columns", (rows // tile,), here,
        pieced(bases, tile, width, lambda h: 0, lambda i, h: i)
        + [(c, block((tile, c.shape[1]), lambda i, h, j=j: (turned(i, j), 0))) for j, c in enumerate(columns)],
        [((rows, width), BF, block((tile, width), lambda i, h: (i, 0)))],
        [pltpu.VMEM((tile, width), bases[0].dtype)],
    )
    return result


def shuffled(values, groups, back=False):
    seq, dp = groups
    if back:
        seq, dp = dp, seq
    lane = lax.broadcasted_iota(jnp.int32, (1, PAIR), 1) < HEAD
    source = [s * dp + d for d in range(dp) for s in range(seq)]
    columns = []
    for one, two in zip(source[::2], source[1::2]):
        low = values[:, one // 2 * PAIR : (one // 2 + 1) * PAIR]
        high = values[:, two // 2 * PAIR : (two // 2 + 1) * PAIR]
        low = pltpu.roll(low, HEAD, 1) if one % 2 else low
        high = high if two % 2 else pltpu.roll(high, HEAD, 1)
        columns.append(jnp.where(lane, low, high))
    return jnp.concatenate(columns, axis=1)


def outside(values, groups, channels, back=False):
    seq, dp = groups[::-1] if back else groups
    return values.reshape(-1, seq, dp, channels).swapaxes(1, 2).reshape(values.shape)


def centre(values):
    centred = values - jnp.mean(values, axis=-1, keepdims=True)
    spread = jnp.mean(centred * centred, axis=-1, keepdims=True)
    return centred, lax.rsqrt(spread + EPSILON)


def mix_body(count, norm, groups, counts, per, here, *refs):
    pieces, (marks_ref, vec_ref) = refs[: len(counts)], refs[len(counts) : len(counts) + 2]
    outs, last, held = refs[len(counts) + 2 : -2], refs[-2], refs[-1]

    @pl.when(pl.program_id(0) == 0)
    def _():
        last[...] = jnp.zeros_like(last)

    values = picked(pieces, counts, relative(pl.program_id(0), per, here[0]), held)
    if norm:
        centred, inverse = centre(values)
        values = centred * inverse
    if groups:
        values = shuffled(values, groups)
    if norm:
        values = values * vec_ref[0:1, :] + vec_ref[1:2, :]
    rows = values.shape[0]
    previous = jnp.where(row_index(rows) == 0, last[0:1, :], pltpu.roll(values, 1, 0)) * marks_ref[:, 3:4]
    last[0:1, :] = values[rows - 1 :, :]
    step = values - previous
    outs[count][...] = step.astype(BF)
    for i in range(count):
        outs[i][...] = (previous + step * vec_ref[2 + i : 3 + i, :]).astype(BF)


def mixes(pieces, marks, vec, count, norm, groups, here, tile, per):
    rows, width = marks.shape[0], pieces[0].shape[1]
    own = block((tile, width), lambda i, h: (relative(i, per, h), 0))
    return kernel(
        partial(mix_body, count, norm, groups, counts_of(pieces, tile), per), "mixes", (rows // tile,), here,
        pieced(pieces, tile, width, lambda h: 0, lambda i, h: relative(i, per, h))
        + [(marks, block((tile, PAIR), lambda i, h: (i, 0))), (vec, fixed(vec.shape))],
        [((rows, width), BF, own)] * (count + 1),
        [pltpu.VMEM((8, width), F32), pltpu.VMEM((tile, width), BF)],
    )


def mixes_back_body(which, first, seq, outs, here, *refs):
    count = len(which)
    grads, nexts, weights = refs[:count], refs[count : 2 * count], refs[2 * count : 3 * count]
    step_ref, marks_ref, next_marks_ref, vec_ref, *out_refs, sums_ref = refs[3 * count :]

    @pl.when(pl.program_id(1) == 0)
    def _():
        sums_ref[...] = jnp.zeros_like(sums_ref)

    step = step_ref[...].astype(F32)
    rows = step.shape[0]
    total = straight = None
    for i in range(which[-1] + 1):
        grad = sum(
            dot(jnp.concatenate([grads[k][...], nexts[k][...]], axis=0), weights[k][...], NT)
            for k in range(count)
            if which[k] == i
        )
        sums_ref[i : i + 1, :] += jnp.sum(grad[:rows] * step, axis=0, keepdims=True)
        part = grad * vec_ref[i : i + 1, :]
        total, straight = (total + grad, straight + part) if i else (grad, part)
    inside = ((first + pl.program_id(1)) ^ here[0]) < seq - 1
    keep = jnp.concatenate([marks_ref[:, 3:4], jnp.where(inside, next_marks_ref[:, 3:4], 0.0)], axis=0)
    kept = (total - straight) * keep
    up = pltpu.roll(kept, kept.shape[0] - 1, 0)
    result = (straight[:rows] + up[:rows]).astype(BF)
    if len(out_refs) == 1:
        out_refs[0][...] = result
        return
    if outs == 1:
        out_refs[0][...] = result[: rows // 2]
        out_refs[1][...] = result[rows // 2 :]
        return
    for k, out_ref in enumerate(out_refs):

        @pl.when(pl.program_id(1) == k)
        def _(out_ref=out_ref):
            out_ref[...] = result


EXTRA = 16


def mixes_back(terms, step, marks, vec, here, seq, first, count, halves=False):
    rows, width = step.shape
    tile, columns = rows // seq, min(512, width)
    extras = tile // EXTRA

    def following(i, h):
        return jnp.minimum(((first + i) ^ h) + 1, seq - 1)

    ins = [(g, block((tile, n), lambda c, i, h, at=at: (first + i, at))) for _, g, at, _, _, n in terms]
    ins += [
        (g, block((EXTRA, n), lambda c, i, h, at=at: ((following(i, h) ^ h) * extras, at)))
        for _, g, at, _, _, n in terms
    ]
    ins += [(w, block((columns, n), lambda c, i, h, at=at: (c, at))) for _, _, _, w, at, n in terms]
    ins += [
        (step, block((tile, columns), lambda c, i, h: (first + i, c))),
        (marks, block((tile, PAIR), lambda c, i, h: ((first + i) ^ h, 0))),
        (marks, block((EXTRA, PAIR), lambda c, i, h: (following(i, h) * extras, 0))),
        (vec, block((8, columns), lambda c, i, h: (0, c))),
    ]
    size = tile // 2 if halves else tile
    *parts, sums = kernel(
        partial(mixes_back_body, [t[0] for t in terms], first, seq, count), "mixes_back", (width // columns, count), here, ins,
        [((size, width), BF, block((size, columns), lambda c, i, h: (0, c)))] * (2 if halves else count)
        + [((8, width), F32, block((8, columns), lambda c, i, h: (0, c)))],
    )
    return parts, sums


def mixes_back_scatter(terms, step, marks, vec, here, seq, beside):
    if seq != 4:
        parts, sums = mixes_back(terms, step, marks, vec, here, seq, 0, seq)
        return after(scatter_seq(parts, here), beside(parts)), sums

    def call(first, count, *before):
        ordered = after([t[1] for t in terms], *before)
        return mixes_back(
            [(t[0], g) + t[2:] for t, g in zip(terms, ordered)], step, marks, vec, here, seq, first, count, first == 3
        )

    far, sums_far = call(3, 1)
    near, sums_near = call(1, 2, far)
    parts = [None, *near, *far]
    started = after(scatter_start(parts), near)
    relayed = scatter_relay(parts, started, here)
    (own,), sums_own = call(0, 1, near, relayed)
    return after(scatter_end(own, relayed), beside(relayed)), sums_far + sums_near + sums_own


def after_body(count, here, x_ref, vec_ref, *refs):
    after_ref, normed_ref = refs[count:]
    after = x_ref[...].astype(F32)
    for ref in refs[:count]:
        after = after + ref[...].astype(F32)
    after_ref[...] = after
    centred, inverse = centre(after)
    normed_ref[...] = (centred * inverse * vec_ref[0:1, :] + vec_ref[1:2, :]).astype(BF)


def after_norm(inputs, terms, vec, here):
    rows, width = inputs.shape
    own = block((CHUNK, width), lambda i, h: (i, 0))
    return kernel(
        partial(after_body, len(terms)), "after_norm", (rows // CHUNK,), here,
        [(inputs, own), (vec, fixed(vec.shape))] + [(t, own) for t in terms],
        [((rows, width), F32, own), ((rows, width), BF, own)],
    )


def norm_back_body(count, groups, here, x_ref, base_ref, vec_ref, *refs):
    wide_ref, narrow_ref, sums_ref = refs[count:]

    @pl.when(pl.program_id(0) == 0)
    def _():
        sums_ref[...] = jnp.zeros_like(sums_ref)

    grad = refs[0][...].astype(F32)
    for ref in refs[1:count]:
        grad = grad + ref[...].astype(F32)
    if groups:
        grad = shuffled(grad, groups, back=True)
    centred, inverse = centre(x_ref[...].astype(F32))
    normed = centred * inverse
    sums_ref[0:1, :] += jnp.sum(grad * normed, axis=0, keepdims=True)
    sums_ref[1:2, :] += jnp.sum(grad, axis=0, keepdims=True)
    grad = grad * vec_ref[0:1, :]
    grad = grad - jnp.mean(grad, axis=-1, keepdims=True) - normed * jnp.mean(grad * normed, axis=-1, keepdims=True)
    result = base_ref[...].astype(F32) + inverse * grad
    wide_ref[...] = result
    narrow_ref[...] = result.astype(BF)


def norm_back(terms, inputs, base, vec, groups, here):
    rows, width = inputs.shape
    own = block((CHUNK, width), lambda i, h: (i, 0))
    return kernel(
        partial(norm_back_body, len(terms), groups), "norm_back", (rows // CHUNK,), here,
        [(inputs, own), (base, own), (vec, fixed(vec.shape))] + [(t, own) for t in terms],
        [((rows, width), F32, own), ((rows, width), BF, own), ((8, width), F32, fixed((8, width)))],
    )


def gate_body(mix_ref, weight_ref, wkv_ref, par_ref, gate_ref, mixed_ref):
    gate = dot(mix_ref[...], weight_ref[...], NN)
    gate_ref[...] = gate
    ones = jnp.where(same_head(), 1.0, 0.0).astype(BF)
    for pair in range(gate.shape[1] // PAIR):
        at = slice(pair * PAIR, (pair + 1) * PAIR)
        wkv = wkv_ref[:, at]
        centred = wkv - head_sum_fine(wkv, ones) * (1.0 / HEAD)
        spread = head_sum(centred * centred, ones) * (1.0 / HEAD)
        normed = centred * lax.rsqrt(spread + GROUP_EPSILON) * par_ref[1:2, at] + par_ref[2:3, at]
        mixed_ref[:, at] = (normed * (gate[:, at] / (1.0 + jnp.exp(-gate[:, at])))).astype(BF)


def gated(mix_g, weights, wkv, params, here, seq):
    rows, width = mix_g.shape
    tile, part = rows // seq, wkv.shape[1]
    own = block((tile, part), lambda i, h: (i, 0))
    return kernel(
        lambda here, *refs: gate_body(*refs), "gate", (seq,), here,
        [
            (mix_g, block((tile, width), lambda i, h: (i, 0))),
            (weights, block((width, part), lambda i, h: (0, 0))),
            (wkv, own),
            (params, fixed(params.shape)),
        ],
        [((rows, part), F32, own), ((rows, part), BF, own)],
    )


def columns_body(here, left_ref, right_ref, out_ref):
    out_ref[...] = dot(left_ref[...], right_ref[...], NN).astype(BF)


def columns_product(left, right, part, relative_to, here, seq):
    rows, depth = left.shape
    tile = rows // seq
    (result,) = kernel(
        columns_body, "value_columns", (seq,), here,
        [
            (left, block((tile, depth), lambda i, h: (i, 0))),
            (right, block((depth, part), lambda i, h: (0, h ^ relative_to))),
        ],
        [((rows, part), BF, block((tile, part), lambda i, h: (i ^ relative_to, 0)))],
    )
    return result


def channel_body(counts, here, pre_ref, *refs):
    grads, terms, (channel_ref, d_recept_ref, held) = refs[: len(counts)], refs[len(counts) : -3], refs[-3:]
    value = sum(ref[...].astype(F32) for ref in terms)
    opened = 1.0 / (1.0 + jnp.exp(-pre_ref[...]))
    channel = opened * value
    channel_ref[...] = channel.astype(BF)
    grad = picked(grads, counts, pl.program_id(0), held)
    d_recept_ref[...] = (grad * channel * (1.0 - opened)).astype(BF)


def channel_out(terms, pre, grads, here, tile):
    rows, part = pre.shape
    own = block((tile, part), lambda i, h: (i, 0))
    return kernel(
        partial(channel_body, counts_of(grads, tile)), "channel", (rows // tile,), here,
        [(pre, own)] + pieced(grads, tile, part, lambda h: h, lambda i, h: i) + [(t, own) for t in terms],
        [((rows, part), BF, own)] * 2,
        [pltpu.VMEM((tile, part), BF)],
    )


def head_masks():
    lane = lax.broadcasted_iota(jnp.int32, (1, PAIR), 1)
    first = (lane < HEAD).astype(F32)
    return first, 1.0 - first


def same_head():
    row = lax.broadcasted_iota(jnp.int32, (PAIR, PAIR), 0) < HEAD
    column = lax.broadcasted_iota(jnp.int32, (PAIR, PAIR), 1) < HEAD
    return row == column


def dot(left, right, dims):
    return lax.dot_general(left, right, dims, preferred_element_type=F32)


def head_sum(values, ones):
    return dot(values.astype(BF), ones, NN)


def head_sum_fine(values, ones):
    coarse = values.astype(BF)
    rest = (values - coarse.astype(F32)).astype(BF)
    return dot(coarse, ones, NN) + dot(rest, ones, NN)


def stacked(values, first, second):
    return jnp.concatenate([(values * first).astype(BF), (values * second).astype(BF)], axis=0)


def masks_of(rows_ref, columns_ref):
    segment = rows_ref[:, 0:1]
    reaches = rows_ref[:, 1:2]
    last_same = rows_ref[:, 2:3]
    reach_last = rows_ref[CHUNK - 1 : CHUNK, 1:2]
    before = lax.broadcasted_iota(jnp.int32, (CHUNK, CHUNK), 1) < lax.broadcasted_iota(
        jnp.int32, (CHUNK, CHUNK), 0
    )
    allowed = jnp.where((segment == columns_ref[0:1, :]) & before, 1.0, 0.0)
    return reaches, last_same, reach_last, jnp.concatenate([allowed, allowed], axis=0)


def wkv_forward_body(
    here, r_ref, k_ref, v_ref, rows_ref, columns_ref, grow_ref, shrink_ref, tail_ref, par_ref,
    wkv_ref, states_ref, state,
):
    @pl.when(pl.program_id(0) == 0)
    def _():
        state[...] = jnp.zeros_like(state)

    first, second = head_masks()
    block = same_head()
    ones = jnp.where(block, 1.0, 0.0).astype(BF)
    reaches, last_same, reach_last, allowed = masks_of(rows_ref, columns_ref)
    for pair in range(r_ref.shape[1] // PAIR):
        at = slice(pair * PAIR, (pair + 1) * PAIR)
        r, k, v = r_ref[:, at].astype(F32), k_ref[:, at].astype(F32), v_ref[:, at].astype(F32)
        bonus, decay = par_ref[0:1, at], par_ref[3:4, at]
        held = state[at, :]
        held_b = held.astype(BF)
        states_ref[0, at, :] = held_b
        grown = r * grow_ref[:, at]
        shrunk = (k * shrink_ref[:, at]).astype(BF)
        scores = (dot(stacked(grown, first, second), shrunk, NT) * allowed).astype(BF)
        both = jnp.concatenate([scores[:CHUNK], scores[CHUNK:]], axis=1)
        wkv = dot(both, stacked(v, first, second), NN)
        wkv = wkv + dot((grown * reaches).astype(BF), held_b, NT)
        wkv = wkv + head_sum(r * bonus * k, ones) * v
        fresh = dot(v_ref[:, at], (k * tail_ref[:, at] * last_same).astype(BF), TN)
        state[at, :] = held * (decay * reach_last) + jnp.where(block, fresh, 0.0)
        wkv_ref[:, at] = wkv


def wkv_backward_body(
    here, r_ref, k_ref, v_ref, g_ref, wkv_ref, d_mixed_ref, states_ref,
    rows_ref, columns_ref, grow_ref, shrink_ref, tail_ref, par_ref,
    d_r_ref, d_k_ref, d_v_ref, d_g_ref, sums_ref, d_state,
):
    @pl.when(pl.program_id(0) == 0)
    def _():
        d_state[...] = jnp.zeros_like(d_state)
        sums_ref[...] = jnp.zeros_like(sums_ref)

    first, second = head_masks()
    block = same_head()
    ones = jnp.where(block, 1.0, 0.0).astype(BF)
    reaches, last_same, reach_last, allowed = masks_of(rows_ref, columns_ref)
    offset = lax.broadcasted_iota(jnp.int32, (CHUNK, PAIR), 0).astype(F32)
    for pair in range(r_ref.shape[1] // PAIR):
        at = slice(pair * PAIR, (pair + 1) * PAIR)
        bonus, gain, bias, decay = (par_ref[i : i + 1, at] for i in range(4))
        wkv, gate, d_mixed = wkv_ref[:, at], g_ref[:, at], d_mixed_ref[:, at].astype(F32)
        centred = wkv - head_sum_fine(wkv, ones) * (1.0 / HEAD)
        spread = head_sum(centred * centred, ones) * (1.0 / HEAD)
        inverse = lax.rsqrt(spread + GROUP_EPSILON)
        normed = centred * inverse
        opened = 1.0 / (1.0 + jnp.exp(-gate))
        d_scaled = d_mixed * gate * opened
        d_g = d_mixed * (normed * gain + bias) * opened * (1.0 + gate * (1.0 - opened))
        d_g_ref[:, at] = d_g.astype(BF)
        d_normed = d_scaled * gain
        mean_one = head_sum(d_normed, ones) * (1.0 / HEAD)
        mean_two = head_sum(d_normed * normed, ones) * (1.0 / HEAD)
        d_wkv = inverse * (d_normed - mean_one - normed * mean_two)
        r, k, v = r_ref[:, at].astype(F32), k_ref[:, at].astype(F32), v_ref[:, at].astype(F32)
        v_b, d_wkv_b = v_ref[:, at], d_wkv.astype(BF)
        grow, shrink, tail = grow_ref[:, at], shrink_ref[:, at], tail_ref[:, at] * last_same
        held = states_ref[0, at, :]
        later = d_state[at, :]
        later_b = later.astype(BF)
        grown = r * grow
        shrunk = k * shrink
        shrunk_b = shrunk.astype(BF)
        tailed_b = (k * tail).astype(BF)
        grown_two = stacked(grown, first, second)
        d_wkv_two = stacked(d_wkv, first, second)
        scores = (dot(grown_two, shrunk_b, NT) * allowed).astype(BF)
        d_scores = (dot(d_wkv_two, v_b, NT) * allowed).astype(BF)
        d_both = jnp.concatenate([d_scores[:CHUNK], d_scores[CHUNK:]], axis=1)
        d_grown = dot(d_both, stacked(shrunk, first, second), NN)
        d_grown = d_grown + dot((d_wkv * reaches).astype(BF), held, NN)
        d_shrunk = dot(d_scores, grown_two, TN)
        d_tailed = dot(v_b, later_b, NN)
        share = head_sum(r * bonus * k, ones)
        d_share = head_sum(d_wkv * v, ones)
        d_v = dot(scores, d_wkv_two, TN) + dot(tailed_b, later_b, NT) + share * d_wkv
        d_r_ref[:, at] = (d_grown * grow + d_share * bonus * k).astype(BF)
        d_k_ref[:, at] = (d_shrunk * shrink + d_tailed * tail + d_share * bonus * r).astype(BF)
        d_v_ref[:, at] = d_v.astype(BF)
        carried = decay * reach_last
        d_fresh = dot(d_wkv_b, (grown * reaches).astype(BF), TN)
        d_state[at, :] = later * carried + jnp.where(block, d_fresh, 0.0)
        grown_b = grown.astype(BF).astype(F32)
        d_log = (
            offset * grown_b * d_grown
            - (offset + 1.0) * shrunk_b.astype(F32) * d_shrunk
            + (CHUNK - 1.0 - offset) * tailed_b.astype(F32) * d_tailed
        )
        kept = CHUNK * carried * jnp.sum(held.astype(F32) * later, axis=0, keepdims=True)
        sums_ref[0:1, at] += jnp.sum(d_log, axis=0, keepdims=True) + kept
        sums_ref[1:2, at] += jnp.sum(d_share * r * k, axis=0, keepdims=True)
        sums_ref[2:3, at] += jnp.sum(d_scaled * normed, axis=0, keepdims=True)
        sums_ref[3:4, at] += jnp.sum(d_scaled, axis=0, keepdims=True)


def wkv_blocks(width, chunks, per, backward):
    def chunk(i):
        return chunks - 1 - i if backward else i

    tokens = block((CHUNK, width), lambda i, h: (relative(chunk(i), per, h), 0))
    states = block((1, width, PAIR), lambda i, h: (chunk(i), 0, 0))
    tables = [
        block((CHUNK, PAIR), lambda i, h: (chunk(i), 0)),
        block((8, CHUNK), lambda i, h: (0, chunk(i))),
    ]
    return tokens, states, tables + [fixed((CHUNK, width))] * 3 + [fixed((8, width))]


def wkv_forward(r, k, v, tables, here, per):
    length, width = r.shape
    chunks = length // CHUNK
    tokens, states, blocks = wkv_blocks(width, chunks, per, False)
    return kernel(
        wkv_forward_body, "wkv_forward", (chunks,), here,
        [(a, tokens) for a in (r, k, v)] + list(zip(tables, blocks)),
        [((length, width), F32, tokens), ((chunks, width, PAIR), BF, states)],
        [pltpu.VMEM((width, PAIR), F32)],
    )


def wkv_backward(r, k, v, gate, wkv, d_mixed, states_kept, tables, here, per):
    length, width = r.shape
    chunks = length // CHUNK
    tokens, states, blocks = wkv_blocks(width, chunks, per, True)
    return kernel(
        wkv_backward_body, "wkv_backward", (chunks,), here,
        [(a, tokens) for a in (r, k, v, gate, wkv, d_mixed)] + [(states_kept, states)] + list(zip(tables, blocks)),
        [((length, width), BF, tokens)] * 4 + [((8, width), F32, fixed((8, width)))],
        [pltpu.VMEM((width, PAIR), F32)],
    )


def wkv_tables(piece, keep, log_decay, bonus, gain, bias):
    length = piece.shape[0]
    by_chunk = piece.reshape(length // CHUNK, CHUNK)
    before = jnp.concatenate([jnp.full((1,), -1, piece.dtype), by_chunk[:-1, -1]])
    reaches = (by_chunk == before[:, None]).reshape(-1)
    last_same = (by_chunk == by_chunk[:, -1:]).reshape(-1)
    marks = jnp.stack([piece.astype(F32), reaches.astype(F32), last_same.astype(F32), keep], axis=1)
    rows = jnp.pad(marks, ((0, 0), (0, PAIR - 4)))
    columns = jnp.broadcast_to(piece.astype(F32)[None], (8, length))
    offset = jnp.arange(CHUNK).astype(F32)[:, None]
    grow = jnp.exp(offset * log_decay)
    shrink = jnp.exp(-(offset + 1.0) * log_decay)
    tail = jnp.exp((CHUNK - 1.0 - offset) * log_decay)
    zero = jnp.zeros_like(bonus)
    params = jnp.stack([bonus, gain, bias, jnp.exp(CHUNK * log_decay)] + [zero] * 4)
    return rows, columns, grow, shrink, tail, params


def segment_of(lengths, positions):
    rank = jnp.arange(lengths.shape[0])
    starts = jnp.sum(jnp.where(rank[:, None] > rank[None, :], lengths[None, :], 0), axis=1)
    later_flags = (positions[:, None] >= starts[None, 1:]).astype(jnp.int32)
    first_flags = jnp.any(positions[:, None] == starts[None, :], axis=1)
    return (jnp.sum(later_flags, axis=1), first_flags)


def rows_of(vec, *rows):
    return jnp.pad(jnp.stack([vec[i] for i in rows]), ((0, 8 - len(rows)), (0, 0)))


def shards(
    tokens, seq_lengths, out_grad, w_receptance, w_key, w_value, w_gate, w_output,
    ffn_key, ffn_receptance, ffn_value, vectors,
):
    seq, dp = lax.axis_size("seq"), lax.axis_size("dp")
    place = lax.axis_index("seq")
    here = jnp.reshape(place, (1,)).astype(jnp.int32)
    inputs_b, grad_b = tokens[0], out_grad[0]
    own_rows, width = inputs_b.shape
    length, part, unit = own_rows * seq, width // seq, vectors.shape[1]
    per, tile = own_rows // CHUNK, own_rows // 2
    hidden_width = ffn_key.shape[1] // seq
    groups = (seq, dp)
    within = groups if unit == HEAD else None

    vectors_b = jnp.pad(vectors, ((0, 16 - vectors.shape[0]), (0, 0)))

    def stacked_columns(weights, widths, beside=()):
        cut = cut_columns(weights, vectors_b, here, seq)
        *stacked, last = stack_rows(after(trade_seq(cut), beside), widths, vectors_b, here)
        return [w.reshape(-1, w.shape[-1]) for w in stacked] + [last], cut

    def gather_dp(rows):
        return lax.all_gather(rows, "dp", axis=0, tiled=True)

    def scatter_dp(grad):
        return lax.psum_scatter(grad, "dp", scatter_dimension=0, tiled=True)

    def owners_parts(summed):
        rows = summed.shape[0] // seq
        return trade_seq([lax.dynamic_slice_in_dim(summed, (place ^ j) * rows, rows, 0) for j in range(seq)])

    def owners_rows(summed, widths):
        return join_columns(owners_parts(summed), widths, here)

    def turn_pieces(pieces):
        if within is not None:
            return pieces
        return [outside(p, groups, unit) for p in pieces]

    positions = jnp.arange(length, dtype=jnp.int32)
    piece, first_flags = segment_of(seq_lengths[0], positions)

    (columns_in, columns_g, vec_seq), cut = stacked_columns(
        [w_receptance, w_key, w_value, w_gate], [3 * part, part]
    )
    tokens_held = held_back(inputs_b, here, *cut)
    full_in = gather_dp(columns_in)
    vec_parts = gather_small(vec_seq[None, :, : vectors.shape[0]], "dp").astype(F32)
    vec = vec_parts.transpose(2, 1, 0, 3).reshape(-1, width)
    turned = vec_parts.transpose(2, 0, 1, 3).reshape(-1, width)
    vec_own = lax.dynamic_slice_in_dim(vec, place * part, part, 1)
    log_decay = -jnp.exp(vec_own[6])
    tables = wkv_tables(
        piece, 1.0 - first_flags.astype(F32), log_decay, vec_own[7], vec_own[8], vec_own[9]
    )
    marks = tables[0]
    rows_one = rows_of(turned, 0, 1, 2, 3, 4, 5)
    tokens_all = gather_seq(tokens_held, (rows_one, tables))
    full_g = gather_dp(after(columns_g, tokens_all[1:3], rows_one))
    own_o = gather_dp(after(w_output, tokens_all))

    mix_r, mix_k, mix_v, mix_g, step = mixes(
        turn_pieces(tokens_all), marks, rows_one, 4, True, within, here, tile, own_rows // tile
    )
    recept, keyed, valued = (
        dot(m, full_in[:, i * part : (i + 1) * part], NN).astype(BF)
        for i, m in enumerate((mix_r, mix_k, mix_v))
    )
    projected = (recept, keyed, valued)
    (columns_c, _), _ = stacked_columns(after([ffn_key, ffn_receptance], mix_r), [hidden_width + part], projected)
    full_c = gather_dp(columns_c)
    full_ck, full_cr = full_c[:, :hidden_width], full_c[:, hidden_width:]
    full_cv = gather_dp(after(ffn_value, columns_c))
    wkv, states = wkv_forward(recept, keyed, valued, tables, here, per)
    grad_all = gather_seq(after(grad_b, mix_r), wkv)
    gate_pre, mixed = gated(mix_g, full_g, wkv, tables[5], here, seq)
    attn = [dot(rows, own_o, NN).astype(BF) for rows in blocks_of(after(mixed, grad_all[3:]), seq)]
    after_mix, normed_two = after_norm(inputs_b, scatter_seq(attn, here), rows_of(vec, 10, 11), here)

    mix_k2, mix_r2, step_two = mixes(
        turn_pieces(gather_seq(normed_two)), marks, rows_of(turned, 10, 11, 12, 13), 2, False, within, here, tile,
        own_rows // tile,
    )
    recept_pre = dot(mix_r2, full_cr, NN)
    opened = gather_seq(jax.nn.sigmoid(recept_pre).astype(BF))
    key_pre = dot(mix_k2, full_ck, NN)
    smooth = jax.nn.softplus(key_pre)
    hidden = (smooth * smooth).astype(BF)
    slope = (2.0 * smooth * jax.nn.sigmoid(key_pre)).astype(BF)
    hidden, slope = lax.optimization_barrier((hidden, slope))
    later = after(hidden, opened[1:3])
    value_parts = [columns_product(later if j < 2 else hidden, full_cv, part, j, here, seq) for j in reversed(range(seq))]
    value_parts = value_parts[::-1]
    value_relayed = scatter_relay(value_parts, scatter_start(value_parts), here)
    d_value = spread_columns(
        grad_all, by_block(after(opened, value_parts, value_relayed)), here, True, True, tile, own_rows // tile
    )

    grad_cv = dot(hidden, d_value, TN).astype(BF)
    summed_cv = scatter_dp(grad_cv)
    value_terms = scatter_end(value_parts[0], value_relayed)
    d_hidden = dot(after(d_value, grad_cv), full_cv, NT)
    d_key_two = (d_hidden * slope.astype(F32)).astype(BF)
    channel, d_recept_two = channel_out(value_terms, recept_pre, grad_all, here, tile)
    half, first = part // 2, hidden_width // (part // 2)
    grad_ck, grad_cr = [], []

    def beside_two(relayed):
        grad_ck.append(dot(after(mix_k2, relayed), d_key_two, TN).astype(BF))
        grad_cr.append(dot(after(mix_r2, relayed, grad_ck), d_recept_two, TN).astype(BF))
        return grad_ck, grad_cr

    terms_two, sums_two = mixes_back_scatter(
        [(0, d_key_two, 0, full_c, 0, hidden_width)]
        + [(1, d_recept_two, i, full_c, first + i, half) for i in range(2)],
        step_two, marks, rows_of(turned, 12, 13), here, seq, beside_two,
    )
    summed_ck, summed_cr = scatter_dp(grad_ck[0]), scatter_dp(grad_cr[0])
    if within is None:
        terms_two = [outside(t, groups, unit, back=True) for t in terms_two]
    d_after, d_attn, norm_sums_two = norm_back(terms_two, after_mix, grad_b, rows_of(vec, 10), within, here)

    d_attn = jnp.concatenate(after(gather_seq(d_attn), summed_cv), axis=0)
    d_mixed = dot(d_attn, own_o, NT).astype(BF)
    grad_wo = dot(mixed, d_attn, TN).astype(BF)
    d_mixed = after(d_mixed, grad_wo, summed_ck)
    summed_o = scatter_dp(grad_wo)
    d_recept, d_keyed, d_valued, d_gate, sums = wkv_backward(
        recept, keyed, valued, gate_pre, wkv, d_mixed, states, tables, here, per
    )
    channel = after(trade_seq(blocks_of(after(channel, d_mixed), seq)), d_recept)
    grads_vg = [
        dot(after(m, channel), d, TN).astype(BF) for m, d in ((mix_v, d_valued), (mix_g, d_gate))
    ]
    summed_vg = scatter_dp(jnp.concatenate(grads_vg, axis=1))
    grads_rk, others = [], []

    def beside(relayed):
        grads_rk.extend(
            dot(after(m, relayed), d, TN).astype(BF) for m, d in ((mix_r, d_recept), (mix_k, d_keyed))
        )
        others.append(spread_columns([after_mix], after(channel, relayed), here, False, False, CHUNK, per))
        others.append(after(summed_cv, relayed).astype(F32))
        return grads_rk, others

    d_recept, d_keyed = after((d_recept, d_keyed), grads_vg, summed_o)
    terms, sums_one = mixes_back_scatter(
        [(i, d, 0, full_in, i, part) for i, d in enumerate((d_recept, d_keyed, d_valued))]
        + [(3, d_gate, 0, full_g, 0, part)],
        step, marks, rows_of(turned, 2, 3, 4, 5), here, seq, beside,
    )
    summed_rk = scatter_dp(jnp.concatenate(grads_rk, axis=1))
    out_rows, sum_cv = others
    if within is None:
        terms = [outside(t, groups, unit, back=True) for t in terms]
    tokens_grad, _, norm_sums = norm_back(terms, inputs_b, d_after, rows_of(vec, 0), within, here)

    summed_c = jnp.concatenate(after([summed_ck, summed_cr], terms), axis=1)
    sum_ck, sum_cr = owners_rows(summed_c, [ffn_key.shape[1], width])
    sum_o = summed_o.astype(F32)
    sum_v, sum_g = owners_rows(summed_vg, [width] * 2)

    def by_device(rows, turn):
        if turn:
            return rows.reshape(-1, dp, seq, unit).transpose(1, 2, 0, 3)
        return rows.reshape(-1, seq, dp, unit).transpose(2, 1, 0, 3)

    own_sums = jnp.stack([sums[0] * log_decay, sums[1], sums[2], sums[3]])
    own_sums = lax.dynamic_update_slice(jnp.zeros((4, width), F32), own_sums, (0, place * part))
    vector_rows = jnp.concatenate(
        [
            by_device(norm_sums[:2], False), by_device(sums_one[:4], True), by_device(own_sums, False),
            by_device(norm_sums_two[:2], False), by_device(sums_two[:2], True),
        ],
        axis=2,
    )
    sum_vec = scatter_small(vector_rows.reshape((-1,) + vector_rows.shape[2:]))
    sum_r, sum_k = owners_rows(after(summed_rk, sum_ck, sum_v, sum_vec), [width] * 2)
    return (
        out_rows[None], tokens_grad[None], sum_r, sum_k, sum_v, sum_g, sum_o,
        sum_ck, sum_cr, sum_cv, sum_vec,
    )


def solution(mesh):
    tokens = P("dp", "seq", None)
    rows = P(("seq", "dp"), None)
    columns = P(None, ("seq", "dp"))
    return jax.shard_map(
        shards,
        mesh=mesh,
        in_specs=(tokens, P("dp", None), tokens) + (rows,) * 8 + (columns,),
        out_specs=(tokens, tokens) + (rows,) * 8 + (columns,),
        check_vma=False,
    )
```

```python
from functools import partial

import jax
import jax.numpy as jnp
from jax import lax
from jax.experimental import pallas as pl
from jax.experimental.pallas import tpu as pltpu
from jax.sharding import PartitionSpec as P

HEAD = 64
PAIR = 128
CHUNK = 128
EPSILON = 1e-05
GROUP_EPSILON = 1.0
BF = jnp.bfloat16
F32 = jnp.float32
NT = (((1,), (1,)), ((), ()))
TN = (((0,), (0,)), ((), ()))
NN = (((1,), (0,)), ((), ()))


def swap(value, axis, distance):
    size = lax.axis_size(axis)
    return lax.ppermute(value, axis, [(i, i ^ distance) for i in range(size)])


def after(value, *others):
    return lax.optimization_barrier((value, others))[0]


def gather_second(part, one, two):
    half = part.shape[0] // 2
    columns = part.shape[1]
    low, high = swap(one[:half, :columns], "seq", 2), swap(two[half : 2 * half, :columns], "seq", 1)
    return [part, one, two, low, high]


def gather_seq(part, first=()):
    size = lax.axis_size("seq")
    if size == 4:
        half = part.shape[0] // 2
        one, two = swap(part, "seq", 1), swap(part, "seq", 2)
        one, two = after((one, two), first)
        low, high = swap(one[:half], "seq", 2), swap(two[half:], "seq", 1)
        return [part, one, two, low, high]
    return [part] + [swap(part, "seq", distance) for distance in range(1, size)]


def by_block(pieces):
    if lax.axis_size("seq") == 4:
        return pieces[:3] + [jnp.concatenate(pieces[3:], axis=0)]
    return pieces


def scatter_start(parts):
    if lax.axis_size("seq") != 4:
        return ()
    low, high = parts[3:] if len(parts) == 5 else blocks_of(parts[3], 2)
    return swap(low, "seq", 1), swap(high, "seq", 2)


def relay_body(here, one_ref, two_ref, low_ref, high_ref, one_out, two_out):
    one, two = one_ref[...], two_ref[...]
    first = pl.program_id(0) == 0
    low, high = low_ref[...].astype(F32), high_ref[...].astype(F32)
    one_out[...] = jnp.where(first, one, (one.astype(F32) + high).astype(BF))
    two_out[...] = jnp.where(first, (two.astype(F32) + low).astype(BF), two)


def scatter_relay(parts, started, here):
    if lax.axis_size("seq") != 4:
        return parts[1:]
    (_, one, two, *_), (low, high) = parts, started
    (rows, width), half = one.shape, block(low.shape, lambda i, h: (i, 0))
    return kernel(
        relay_body, "relay", (2,), here,
        [(one, half), (two, half), (low, fixed(low.shape)), (high, fixed(low.shape))],
        [((rows, width), BF, half)] * 2,
    )


def scatter_end(own, relayed):
    return [own] + [swap(part, "seq", j + 1) for j, part in enumerate(relayed)]


def scatter_seq(parts, here):
    return scatter_end(parts[0], scatter_relay(parts, scatter_start(parts), here))


def trade_seq(parts):
    return [parts[0]] + [swap(part, "seq", j + 1) for j, part in enumerate(parts[1:])]


def blocks_of(values, size):
    rows = values.shape[0] // size
    return [values[j * rows : (j + 1) * rows] for j in range(size)]


def bits_of(size):
    return [1 << b for b in range(size.bit_length() - 1)]


def gather_small(part, axis):
    for bit in bits_of(lax.axis_size(axis)):
        other = swap(part, axis, bit)
        second = (lax.axis_index(axis) & bit) != 0
        part = jnp.concatenate([jnp.where(second, other, part), jnp.where(second, part, other)], axis=0)
    return part


def scatter_small(parts):
    for axis in ("dp", "seq"):
        for bit in reversed(bits_of(lax.axis_size(axis))):
            half = parts.shape[0] // 2
            second = (lax.axis_index(axis) & bit) != 0
            low, high = parts[:half], parts[half:]
            parts = jnp.where(second, high, low) + swap(jnp.where(second, low, high), axis, bit)
    return parts[0]


def block(shape, index):
    return pl.BlockSpec(shape, lambda *i: index(*i[:-1], i[-1][0]))


def fixed(shape):
    return pl.BlockSpec(shape, lambda *i: (0,) * len(shape))


def relative(tile, per, here):
    return (lax.div(tile, per) ^ here) * per + lax.rem(tile, per)


def kernel(body, name, grid, here, ins, outs, scratch=(), vmem=48):
    return pl.pallas_call(
        body,
        out_shape=[jax.ShapeDtypeStruct(shape, kind) for shape, kind, _ in outs],
        grid_spec=pltpu.PrefetchScalarGridSpec(
            num_scalar_prefetch=1,
            grid=grid,
            in_specs=[spec for _, spec in ins],
            out_specs=[spec for _, _, spec in outs],
            scratch_shapes=list(scratch),
        ),
        compiler_params=pltpu.CompilerParams(vmem_limit_bytes=vmem * 2**20),
        name=name,
    )(here, *[array for array, _ in ins])


def pieced(pieces, tile, columns, column, place):
    ins, start = [], 0
    for piece in pieces:
        count = piece.shape[0] // tile

        def index(i, h, start=start, count=count):
            return jnp.clip(place(i, h) - start, 0, count - 1), column(h)

        ins.append((piece, block((tile, columns), index)))
        start += count
    return ins


def picked(refs, counts, tile, held):
    start = 0
    for ref, count in zip(refs, counts):

        @pl.when((tile >= start) & (tile < start + count))
        def _(ref=ref):
            held[...] = ref[...]

        start += count
    return held[...].astype(F32)


def counts_of(pieces, tile):
    return [piece.shape[0] // tile for piece in pieces]


def row_index(rows):
    return lax.broadcasted_iota(jnp.int32, (rows, 1), 0)


def placed(place, width):
    return pl.ds(pl.multiple_of(place * width, width), width)


def cut_body(count, parts, here, *refs):
    ins, beside, outs = refs[:count], refs[count], refs[count + 1 :]
    rows = ins[0].shape[0]
    for j in range(parts):
        outs[j][rows:, :] = jnp.zeros_like(outs[j][rows:, :])
        outs[j][rows:, : beside.shape[1]] = beside[...]
    at = 0
    for ref in ins:
        width = ref.shape[1] // parts
        for j in range(parts):
            outs[j][:rows, at : at + width] = ref[:, placed(here[0] ^ j, width)]
        at += width


def cut_columns(weights, beside, here, parts):
    rows, width = weights[0].shape[0] + beside.shape[0], sum(w.shape[1] for w in weights) // parts
    return kernel(
        partial(cut_body, len(weights), parts), "cut_columns", (1,), here,
        [(w, fixed(w.shape)) for w in [*weights, beside]],
        [((rows, width), BF, fixed((rows, width)))] * parts,
    )


def stack_body(parts, here, *refs):
    start = 0
    outs, beside = refs[parts:-1], refs[-1]
    for out in outs:
        for j in range(parts):
            out[here[0] ^ j] = refs[j][: out.shape[1], start : start + out.shape[2]]
        start += out.shape[2]
    for j in range(parts):
        beside[here[0] ^ j] = refs[j][out.shape[1] :, : beside.shape[2]]


def stack_rows(pieces, widths, beside, here):
    parts, rows = len(pieces), pieces[0].shape[0] - beside.shape[0]
    shapes = [(parts, rows, width) for width in widths] + [(parts,) + beside.shape]
    return kernel(
        partial(stack_body, parts), "stack_rows", (1,), here,
        [(p, fixed(p.shape)) for p in pieces],
        [(shape, BF, fixed(shape)) for shape in shapes],
    )


def ride_body(count, here, *refs):
    ins, rider, outs = refs[:count], refs[count], refs[count + 1 :]
    for j, out in enumerate(outs):
        top, at = 0, 0
        if j in (1, 2):
            top = rider.shape[0]
            out[:top, : rider.shape[1]] = rider[...]
            out[:top, rider.shape[1] :] = jnp.zeros_like(out[:top, rider.shape[1] :])
        for ref in ins:
            width = ref.shape[1] // 4
            out[top:, at : at + width] = ref[:, placed(here[0] ^ j, width)]
            at += width


def cut_with_rider(weights, rider, here):
    rows, width = weights[0].shape[0], sum(w.shape[1] for w in weights) // 4
    return kernel(
        partial(ride_body, len(weights)), "cut_columns", (1,), here,
        [(w, fixed(w.shape)) for w in [*weights, rider]],
        [((n, width), BF, fixed((n, width))) for n in (rows, rows + rider.shape[0], rows + rider.shape[0], rows)],
    )


def unride_body(here, *refs):
    out = refs[-1]
    rows = out.shape[1]
    for j, ref in enumerate(refs[:-1]):
        out[here[0] ^ j] = ref[ref.shape[0] - rows :, :]


def stack_below(pieces, here):
    shape = (4,) + pieces[0].shape
    (stacked,) = kernel(
        unride_body, "stack_rows", (1,), here,
        [(p, fixed(p.shape)) for p in pieces],
        [(shape, BF, fixed(shape))],
    )
    return stacked.reshape(-1, shape[-1])


def hold_body(here, in_ref, *refs):
    refs[-1][...] = in_ref[...]


def held_back(values, here, *others):
    rows, width = values.shape
    own = block((rows // 2, width), lambda i, h: (i, 0))
    (copy,) = kernel(
        hold_body, "hold", (2,), here,
        [(values, own)] + [(o, pl.BlockSpec(memory_space=pl.ANY)) for o in others],
        [((rows, width), values.dtype, own)],
    )
    return copy


def join_body(parts, count, here, *refs):
    ins, outs = refs[:parts], refs[parts:]
    at = 0
    for ref in outs:
        width = ref.shape[1] // parts
        for j in range(parts):
            ref[:, placed(here[0] ^ j, width)] = ins[j][:, at : at + width].astype(F32)
        at += width


def join_columns(pieces, widths, here):
    parts, rows = len(pieces), pieces[0].shape[0]
    return kernel(
        partial(join_body, parts, len(widths)), "join_columns", (1,), here,
        [(p, fixed(p.shape)) for p in pieces],
        [((rows, width), F32, fixed((rows, width))) for width in widths],
    )


def spread_body(counts, parts, product, here, *refs):
    bases, pieces, out, held = refs[: len(counts)], refs[len(counts) : -2], refs[-2], refs[-1]
    picked(bases, counts, pl.program_id(0), held)
    width = pieces[0].shape[1]
    for j in range(parts):
        at = placed(here[0] ^ j, width)
        piece, base = pieces[j][...].astype(F32), held[:, at].astype(F32)
        out[:, at] = (base * piece if product else base + piece).astype(BF)


def spread_columns(bases, columns, here, product, turn, tile, per):
    rows, width = sum(counts_of(bases, tile)) * tile, bases[0].shape[1]

    def turned(i, j):
        return (lax.div(i, per) ^ j) * per + lax.rem(i, per) if turn else i

    (result,) = kernel(
        partial(spread_body, counts_of(bases, tile), len(columns), product), "spread_columns", (rows // tile,), here,
        pieced(bases, tile, width, lambda h: 0, lambda i, h: i)
        + [(c, block((tile, c.shape[1]), lambda i, h, j=j: (turned(i, j), 0))) for j, c in enumerate(columns)],
        [((rows, width), BF, block((tile, width), lambda i, h: (i, 0)))],
        [pltpu.VMEM((tile, width), bases[0].dtype)],
    )
    return result


def shuffled(values, groups, back=False):
    seq, dp = groups
    if back:
        seq, dp = dp, seq
    lane = lax.broadcasted_iota(jnp.int32, (1, PAIR), 1) < HEAD
    source = [s * dp + d for d in range(dp) for s in range(seq)]
    columns = []
    for one, two in zip(source[::2], source[1::2]):
        low = values[:, one // 2 * PAIR : (one // 2 + 1) * PAIR]
        high = values[:, two // 2 * PAIR : (two // 2 + 1) * PAIR]
        low = pltpu.roll(low, HEAD, 1) if one % 2 else low
        high = high if two % 2 else pltpu.roll(high, HEAD, 1)
        columns.append(jnp.where(lane, low, high))
    return jnp.concatenate(columns, axis=1)


def outside(values, groups, channels, back=False):
    seq, dp = groups[::-1] if back else groups
    return values.reshape(-1, seq, dp, channels).swapaxes(1, 2).reshape(values.shape)


def centre(values):
    centred = values - jnp.mean(values, axis=-1, keepdims=True)
    spread = jnp.mean(centred * centred, axis=-1, keepdims=True)
    return centred, lax.rsqrt(spread + EPSILON)


def mix_body(count, norm, groups, counts, per, here, *refs):
    pieces, (marks_ref, vec_ref) = refs[: len(counts)], refs[len(counts) : len(counts) + 2]
    outs, last, held = refs[len(counts) + 2 : -2], refs[-2], refs[-1]

    @pl.when(pl.program_id(0) == 0)
    def _():
        last[...] = jnp.zeros_like(last)

    values = picked(pieces, counts, relative(pl.program_id(0), per, here[0]), held)
    if norm:
        centred, inverse = centre(values)
        values = centred * inverse
    if groups:
        values = shuffled(values, groups)
    if norm:
        values = values * vec_ref[0:1, :] + vec_ref[1:2, :]
    rows = values.shape[0]
    previous = jnp.where(row_index(rows) == 0, last[0:1, :], pltpu.roll(values, 1, 0)) * marks_ref[:, 3:4]
    last[0:1, :] = values[rows - 1 :, :]
    step = values - previous
    outs[count][...] = step.astype(BF)
    for i in range(count):
        outs[i][...] = (previous + step * vec_ref[2 + i : 3 + i, :]).astype(BF)


def mixes(pieces, marks, vec, count, norm, groups, here, tile, per):
    rows, width = marks.shape[0], pieces[0].shape[1]
    own = block((tile, width), lambda i, h: (relative(i, per, h), 0))
    return kernel(
        partial(mix_body, count, norm, groups, counts_of(pieces, tile), per), "mixes", (rows // tile,), here,
        pieced(pieces, tile, width, lambda h: 0, lambda i, h: relative(i, per, h))
        + [(marks, block((tile, PAIR), lambda i, h: (i, 0))), (vec, fixed(vec.shape))],
        [((rows, width), BF, own)] * (count + 1),
        [pltpu.VMEM((8, width), F32), pltpu.VMEM((tile, width), BF)],
    )


def mixes_back_body(which, first, seq, outs, here, *refs):
    count = len(which)
    grads, nexts, weights = refs[:count], refs[count : 2 * count], refs[2 * count : 3 * count]
    step_ref, marks_ref, next_marks_ref, vec_ref, *out_refs, sums_ref = refs[3 * count :]

    @pl.when(pl.program_id(1) == 0)
    def _():
        sums_ref[...] = jnp.zeros_like(sums_ref)

    step = step_ref[...].astype(F32)
    rows = step.shape[0]
    total = straight = None
    for i in range(which[-1] + 1):
        grad = sum(
            dot(jnp.concatenate([grads[k][...], nexts[k][...]], axis=0), weights[k][...], NT)
            for k in range(count)
            if which[k] == i
        )
        sums_ref[i : i + 1, :] += jnp.sum(grad[:rows] * step, axis=0, keepdims=True)
        part = grad * vec_ref[i : i + 1, :]
        total, straight = (total + grad, straight + part) if i else (grad, part)
    inside = ((first + pl.program_id(1)) ^ here[0]) < seq - 1
    keep = jnp.concatenate([marks_ref[:, 3:4], jnp.where(inside, next_marks_ref[:, 3:4], 0.0)], axis=0)
    kept = (total - straight) * keep
    up = pltpu.roll(kept, kept.shape[0] - 1, 0)
    result = (straight[:rows] + up[:rows]).astype(BF)
    if len(out_refs) == 1:
        out_refs[0][...] = result
        return
    if outs == 1:
        out_refs[0][...] = result[: rows // 2]
        out_refs[1][...] = result[rows // 2 :]
        return
    for k, out_ref in enumerate(out_refs):

        @pl.when(pl.program_id(1) == k)
        def _(out_ref=out_ref):
            out_ref[...] = result


EXTRA = 16


def mixes_back(terms, step, marks, vec, here, seq, first, count, halves=False):
    rows, width = step.shape
    tile, columns = rows // seq, min(512, width)
    extras = tile // EXTRA

    def following(i, h):
        return jnp.minimum(((first + i) ^ h) + 1, seq - 1)

    ins = [(g, block((tile, n), lambda c, i, h, at=at: (first + i, at))) for _, g, at, _, _, n in terms]
    ins += [
        (g, block((EXTRA, n), lambda c, i, h, at=at: ((following(i, h) ^ h) * extras, at)))
        for _, g, at, _, _, n in terms
    ]
    ins += [(w, block((columns, n), lambda c, i, h, at=at: (c, at))) for _, _, _, w, at, n in terms]
    ins += [
        (step, block((tile, columns), lambda c, i, h: (first + i, c))),
        (marks, block((tile, PAIR), lambda c, i, h: ((first + i) ^ h, 0))),
        (marks, block((EXTRA, PAIR), lambda c, i, h: (following(i, h) * extras, 0))),
        (vec, block((8, columns), lambda c, i, h: (0, c))),
    ]
    size = tile // 2 if halves else tile
    *parts, sums = kernel(
        partial(mixes_back_body, [t[0] for t in terms], first, seq, count), "mixes_back", (width // columns, count), here, ins,
        [((size, width), BF, block((size, columns), lambda c, i, h: (0, c)))] * (2 if halves else count)
        + [((8, width), F32, block((8, columns), lambda c, i, h: (0, c)))],
    )
    return parts, sums


def mixes_back_scatter(terms, step, marks, vec, here, seq, beside):
    if seq != 4:
        parts, sums = mixes_back(terms, step, marks, vec, here, seq, 0, seq)
        return after(scatter_seq(parts, here), beside(parts)), sums

    def call(first, count, *before):
        ordered = after([t[1] for t in terms], *before)
        return mixes_back(
            [(t[0], g) + t[2:] for t, g in zip(terms, ordered)], step, marks, vec, here, seq, first, count, first == 3
        )

    far, sums_far = call(3, 1)
    near, sums_near = call(1, 2, far)
    parts = [None, *near, *far]
    started = after(scatter_start(parts), near)
    relayed = scatter_relay(parts, started, here)
    (own,), sums_own = call(0, 1, near, relayed)
    return after(scatter_end(own, relayed), beside(relayed)), sums_far + sums_near + sums_own


def after_body(count, here, x_ref, vec_ref, *refs):
    after_ref, normed_ref = refs[count:]
    after = x_ref[...].astype(F32)
    for ref in refs[:count]:
        after = after + ref[...].astype(F32)
    after_ref[...] = after
    centred, inverse = centre(after)
    normed_ref[...] = (centred * inverse * vec_ref[0:1, :] + vec_ref[1:2, :]).astype(BF)


def after_norm(inputs, terms, vec, here):
    rows, width = inputs.shape
    own = block((CHUNK, width), lambda i, h: (i, 0))
    return kernel(
        partial(after_body, len(terms)), "after_norm", (rows // CHUNK,), here,
        [(inputs, own), (vec, fixed(vec.shape))] + [(t, own) for t in terms],
        [((rows, width), F32, own), ((rows, width), BF, own)],
    )


def norm_back_body(count, groups, here, x_ref, base_ref, vec_ref, *refs):
    wide_ref, narrow_ref, sums_ref = refs[count:]

    @pl.when(pl.program_id(0) == 0)
    def _():
        sums_ref[...] = jnp.zeros_like(sums_ref)

    grad = refs[0][...].astype(F32)
    for ref in refs[1:count]:
        grad = grad + ref[...].astype(F32)
    if groups:
        grad = shuffled(grad, groups, back=True)
    centred, inverse = centre(x_ref[...].astype(F32))
    normed = centred * inverse
    sums_ref[0:1, :] += jnp.sum(grad * normed, axis=0, keepdims=True)
    sums_ref[1:2, :] += jnp.sum(grad, axis=0, keepdims=True)
    grad = grad * vec_ref[0:1, :]
    grad = grad - jnp.mean(grad, axis=-1, keepdims=True) - normed * jnp.mean(grad * normed, axis=-1, keepdims=True)
    result = base_ref[...].astype(F32) + inverse * grad
    wide_ref[...] = result
    narrow_ref[...] = result.astype(BF)


def norm_back(terms, inputs, base, vec, groups, here):
    rows, width = inputs.shape
    own = block((CHUNK, width), lambda i, h: (i, 0))
    return kernel(
        partial(norm_back_body, len(terms), groups), "norm_back", (rows // CHUNK,), here,
        [(inputs, own), (base, own), (vec, fixed(vec.shape))] + [(t, own) for t in terms],
        [((rows, width), F32, own), ((rows, width), BF, own), ((8, width), F32, fixed((8, width)))],
    )


def gate_body(mix_ref, weight_ref, wkv_ref, par_ref, gate_ref, mixed_ref):
    gate = dot(mix_ref[...], weight_ref[...], NN)
    gate_ref[...] = gate
    ones = jnp.where(same_head(), 1.0, 0.0).astype(BF)
    for pair in range(gate.shape[1] // PAIR):
        at = slice(pair * PAIR, (pair + 1) * PAIR)
        wkv = wkv_ref[:, at]
        centred = wkv - head_sum_fine(wkv, ones) * (1.0 / HEAD)
        spread = head_sum(centred * centred, ones) * (1.0 / HEAD)
        normed = centred * lax.rsqrt(spread + GROUP_EPSILON) * par_ref[1:2, at] + par_ref[2:3, at]
        mixed_ref[:, at] = (normed * (gate[:, at] / (1.0 + jnp.exp(-gate[:, at])))).astype(BF)


def gated(mix_g, weights, wkv, params, here, seq):
    rows, width = mix_g.shape
    tile, part = rows // seq, wkv.shape[1]
    own = block((tile, part), lambda i, h: (i, 0))
    return kernel(
        lambda here, *refs: gate_body(*refs), "gate", (seq,), here,
        [
            (mix_g, block((tile, width), lambda i, h: (i, 0))),
            (weights, block((width, part), lambda i, h: (0, 0))),
            (wkv, own),
            (params, fixed(params.shape)),
        ],
        [((rows, part), F32, own), ((rows, part), BF, own)],
    )


def columns_body(here, left_ref, right_ref, out_ref):
    out_ref[...] = dot(left_ref[...], right_ref[...], NN).astype(BF)


def columns_product(left, right, part, relative_to, here, seq):
    rows, depth = left.shape
    tile = rows // seq
    (result,) = kernel(
        columns_body, "value_columns", (seq,), here,
        [
            (left, block((tile, depth), lambda i, h: (i, 0))),
            (right, block((depth, part), lambda i, h: (0, h ^ relative_to))),
        ],
        [((rows, part), BF, block((tile, part), lambda i, h: (i ^ relative_to, 0)))],
    )
    return result


def channel_body(counts, here, pre_ref, *refs):
    grads, terms, (channel_ref, d_recept_ref, held) = refs[: len(counts)], refs[len(counts) : -3], refs[-3:]
    value = sum(ref[...].astype(F32) for ref in terms)
    opened = 1.0 / (1.0 + jnp.exp(-pre_ref[...]))
    channel = opened * value
    channel_ref[...] = channel.astype(BF)
    grad = picked(grads, counts, pl.program_id(0), held)
    d_recept_ref[...] = (grad * channel * (1.0 - opened)).astype(BF)


def channel_out(terms, pre, grads, here, tile):
    rows, part = pre.shape
    own = block((tile, part), lambda i, h: (i, 0))
    return kernel(
        partial(channel_body, counts_of(grads, tile)), "channel", (rows // tile,), here,
        [(pre, own)] + pieced(grads, tile, part, lambda h: h, lambda i, h: i) + [(t, own) for t in terms],
        [((rows, part), BF, own)] * 2,
        [pltpu.VMEM((tile, part), BF)],
    )


def head_masks():
    lane = lax.broadcasted_iota(jnp.int32, (1, PAIR), 1)
    first = (lane < HEAD).astype(F32)
    return first, 1.0 - first


def same_head():
    row = lax.broadcasted_iota(jnp.int32, (PAIR, PAIR), 0) < HEAD
    column = lax.broadcasted_iota(jnp.int32, (PAIR, PAIR), 1) < HEAD
    return row == column


def dot(left, right, dims):
    return lax.dot_general(left, right, dims, preferred_element_type=F32)


def head_sum(values, ones):
    return dot(values.astype(BF), ones, NN)


def head_sum_fine(values, ones):
    coarse = values.astype(BF)
    rest = (values - coarse.astype(F32)).astype(BF)
    return dot(coarse, ones, NN) + dot(rest, ones, NN)


def stacked(values, first, second):
    return jnp.concatenate([(values * first).astype(BF), (values * second).astype(BF)], axis=0)


def masks_of(rows_ref, columns_ref):
    segment = rows_ref[:, 0:1]
    reaches = rows_ref[:, 1:2]
    last_same = rows_ref[:, 2:3]
    reach_last = rows_ref[CHUNK - 1 : CHUNK, 1:2]
    before = lax.broadcasted_iota(jnp.int32, (CHUNK, CHUNK), 1) < lax.broadcasted_iota(
        jnp.int32, (CHUNK, CHUNK), 0
    )
    allowed = jnp.where((segment == columns_ref[0:1, :]) & before, 1.0, 0.0)
    return reaches, last_same, reach_last, jnp.concatenate([allowed, allowed], axis=0)


def wkv_forward_body(
    here, r_ref, k_ref, v_ref, rows_ref, columns_ref, grow_ref, shrink_ref, tail_ref, par_ref,
    wkv_ref, states_ref, state,
):
    @pl.when(pl.program_id(0) == 0)
    def _():
        state[...] = jnp.zeros_like(state)

    first, second = head_masks()
    block = same_head()
    ones = jnp.where(block, 1.0, 0.0).astype(BF)
    reaches, last_same, reach_last, allowed = masks_of(rows_ref, columns_ref)
    for pair in range(r_ref.shape[1] // PAIR):
        at = slice(pair * PAIR, (pair + 1) * PAIR)
        r, k, v = r_ref[:, at].astype(F32), k_ref[:, at].astype(F32), v_ref[:, at].astype(F32)
        bonus, decay = par_ref[0:1, at], par_ref[3:4, at]
        held = state[at, :]
        held_b = held.astype(BF)
        states_ref[0, at, :] = held_b
        grown = r * grow_ref[:, at]
        shrunk = (k * shrink_ref[:, at]).astype(BF)
        scores = (dot(stacked(grown, first, second), shrunk, NT) * allowed).astype(BF)
        both = jnp.concatenate([scores[:CHUNK], scores[CHUNK:]], axis=1)
        wkv = dot(both, stacked(v, first, second), NN)
        wkv = wkv + dot((grown * reaches).astype(BF), held_b, NT)
        wkv = wkv + head_sum(r * bonus * k, ones) * v
        fresh = dot(v_ref[:, at], (k * tail_ref[:, at] * last_same).astype(BF), TN)
        state[at, :] = held * (decay * reach_last) + jnp.where(block, fresh, 0.0)
        wkv_ref[:, at] = wkv


def wkv_backward_body(
    here, r_ref, k_ref, v_ref, g_ref, wkv_ref, d_mixed_ref, states_ref,
    rows_ref, columns_ref, grow_ref, shrink_ref, tail_ref, par_ref,
    d_r_ref, d_k_ref, d_v_ref, d_g_ref, sums_ref, d_state,
):
    @pl.when(pl.program_id(0) == 0)
    def _():
        d_state[...] = jnp.zeros_like(d_state)
        sums_ref[...] = jnp.zeros_like(sums_ref)

    first, second = head_masks()
    block = same_head()
    ones = jnp.where(block, 1.0, 0.0).astype(BF)
    reaches, last_same, reach_last, allowed = masks_of(rows_ref, columns_ref)
    offset = lax.broadcasted_iota(jnp.int32, (CHUNK, PAIR), 0).astype(F32)
    for pair in range(r_ref.shape[1] // PAIR):
        at = slice(pair * PAIR, (pair + 1) * PAIR)
        bonus, gain, bias, decay = (par_ref[i : i + 1, at] for i in range(4))
        wkv, gate, d_mixed = wkv_ref[:, at], g_ref[:, at], d_mixed_ref[:, at].astype(F32)
        centred = wkv - head_sum_fine(wkv, ones) * (1.0 / HEAD)
        spread = head_sum(centred * centred, ones) * (1.0 / HEAD)
        inverse = lax.rsqrt(spread + GROUP_EPSILON)
        normed = centred * inverse
        opened = 1.0 / (1.0 + jnp.exp(-gate))
        d_scaled = d_mixed * gate * opened
        d_g = d_mixed * (normed * gain + bias) * opened * (1.0 + gate * (1.0 - opened))
        d_g_ref[:, at] = d_g.astype(BF)
        d_normed = d_scaled * gain
        mean_one = head_sum(d_normed, ones) * (1.0 / HEAD)
        mean_two = head_sum(d_normed * normed, ones) * (1.0 / HEAD)
        d_wkv = inverse * (d_normed - mean_one - normed * mean_two)
        r, k, v = r_ref[:, at].astype(F32), k_ref[:, at].astype(F32), v_ref[:, at].astype(F32)
        v_b, d_wkv_b = v_ref[:, at], d_wkv.astype(BF)
        grow, shrink, tail = grow_ref[:, at], shrink_ref[:, at], tail_ref[:, at] * last_same
        held = states_ref[0, at, :]
        later = d_state[at, :]
        later_b = later.astype(BF)
        grown = r * grow
        shrunk = k * shrink
        shrunk_b = shrunk.astype(BF)
        tailed_b = (k * tail).astype(BF)
        grown_two = stacked(grown, first, second)
        d_wkv_two = stacked(d_wkv, first, second)
        scores = (dot(grown_two, shrunk_b, NT) * allowed).astype(BF)
        d_scores = (dot(d_wkv_two, v_b, NT) * allowed).astype(BF)
        d_both = jnp.concatenate([d_scores[:CHUNK], d_scores[CHUNK:]], axis=1)
        d_grown = dot(d_both, stacked(shrunk, first, second), NN)
        d_grown = d_grown + dot((d_wkv * reaches).astype(BF), held, NN)
        d_shrunk = dot(d_scores, grown_two, TN)
        d_tailed = dot(v_b, later_b, NN)
        share = head_sum(r * bonus * k, ones)
        d_share = head_sum(d_wkv * v, ones)
        d_v = dot(scores, d_wkv_two, TN) + dot(tailed_b, later_b, NT) + share * d_wkv
        d_r_ref[:, at] = (d_grown * grow + d_share * bonus * k).astype(BF)
        d_k_ref[:, at] = (d_shrunk * shrink + d_tailed * tail + d_share * bonus * r).astype(BF)
        d_v_ref[:, at] = d_v.astype(BF)
        carried = decay * reach_last
        d_fresh = dot(d_wkv_b, (grown * reaches).astype(BF), TN)
        d_state[at, :] = later * carried + jnp.where(block, d_fresh, 0.0)
        grown_b = grown.astype(BF).astype(F32)
        d_log = (
            offset * grown_b * d_grown
            - (offset + 1.0) * shrunk_b.astype(F32) * d_shrunk
            + (CHUNK - 1.0 - offset) * tailed_b.astype(F32) * d_tailed
        )
        kept = CHUNK * carried * jnp.sum(held.astype(F32) * later, axis=0, keepdims=True)
        sums_ref[0:1, at] += jnp.sum(d_log, axis=0, keepdims=True) + kept
        sums_ref[1:2, at] += jnp.sum(d_share * r * k, axis=0, keepdims=True)
        sums_ref[2:3, at] += jnp.sum(d_scaled * normed, axis=0, keepdims=True)
        sums_ref[3:4, at] += jnp.sum(d_scaled, axis=0, keepdims=True)


def wkv_blocks(width, chunks, per, backward):
    def chunk(i):
        return chunks - 1 - i if backward else i

    tokens = block((CHUNK, width), lambda i, h: (relative(chunk(i), per, h), 0))
    states = block((1, width, PAIR), lambda i, h: (chunk(i), 0, 0))
    tables = [
        block((CHUNK, PAIR), lambda i, h: (chunk(i), 0)),
        block((8, CHUNK), lambda i, h: (0, chunk(i))),
    ]
    return tokens, states, tables + [fixed((CHUNK, width))] * 3 + [fixed((8, width))]


def wkv_forward(r, k, v, tables, here, per):
    length, width = r.shape
    chunks = length // CHUNK
    tokens, states, blocks = wkv_blocks(width, chunks, per, False)
    return kernel(
        wkv_forward_body, "wkv_forward", (chunks,), here,
        [(a, tokens) for a in (r, k, v)] + list(zip(tables, blocks)),
        [((length, width), F32, tokens), ((chunks, width, PAIR), BF, states)],
        [pltpu.VMEM((width, PAIR), F32)],
    )


def wkv_backward(r, k, v, gate, wkv, d_mixed, states_kept, tables, here, per):
    length, width = r.shape
    chunks = length // CHUNK
    tokens, states, blocks = wkv_blocks(width, chunks, per, True)
    return kernel(
        wkv_backward_body, "wkv_backward", (chunks,), here,
        [(a, tokens) for a in (r, k, v, gate, wkv, d_mixed)] + [(states_kept, states)] + list(zip(tables, blocks)),
        [((length, width), BF, tokens)] * 4 + [((8, width), F32, fixed((8, width)))],
        [pltpu.VMEM((width, PAIR), F32)],
    )


def wkv_tables(piece, keep, log_decay, bonus, gain, bias):
    length = piece.shape[0]
    by_chunk = piece.reshape(length // CHUNK, CHUNK)
    before = jnp.concatenate([jnp.full((1,), -1, piece.dtype), by_chunk[:-1, -1]])
    reaches = (by_chunk == before[:, None]).reshape(-1)
    last_same = (by_chunk == by_chunk[:, -1:]).reshape(-1)
    marks = jnp.stack([piece.astype(F32), reaches.astype(F32), last_same.astype(F32), keep], axis=1)
    rows = jnp.pad(marks, ((0, 0), (0, PAIR - 4)))
    columns = jnp.broadcast_to(piece.astype(F32)[None], (8, length))
    offset = jnp.arange(CHUNK).astype(F32)[:, None]
    grow = jnp.exp(offset * log_decay)
    shrink = jnp.exp(-(offset + 1.0) * log_decay)
    tail = jnp.exp((CHUNK - 1.0 - offset) * log_decay)
    zero = jnp.zeros_like(bonus)
    params = jnp.stack([bonus, gain, bias, jnp.exp(CHUNK * log_decay)] + [zero] * 4)
    return rows, columns, grow, shrink, tail, params


def segment_of(lengths, positions):
    rank = jnp.arange(lengths.shape[0])
    starts = jnp.sum(jnp.where(rank[:, None] > rank[None, :], lengths[None, :], 0), axis=1)
    later_flags = (positions[:, None] >= starts[None, 1:]).astype(jnp.int32)
    first_flags = jnp.any(positions[:, None] == starts[None, :], axis=1)
    return (jnp.sum(later_flags, axis=1), first_flags)


def rows_of(vec, *rows):
    return jnp.pad(jnp.stack([vec[i] for i in rows]), ((0, 8 - len(rows)), (0, 0)))


def shards(
    tokens, seq_lengths, out_grad, w_receptance, w_key, w_value, w_gate, w_output,
    ffn_key, ffn_receptance, ffn_value, vectors,
):
    seq, dp = lax.axis_size("seq"), lax.axis_size("dp")
    place = lax.axis_index("seq")
    here = jnp.reshape(place, (1,)).astype(jnp.int32)
    inputs_b, grad_b = tokens[0], out_grad[0]
    own_rows, width = inputs_b.shape
    length, part, unit = own_rows * seq, width // seq, vectors.shape[1]
    per, tile = own_rows // CHUNK, own_rows // 2
    hidden_width = ffn_key.shape[1] // seq
    groups = (seq, dp)
    within = groups if unit == HEAD else None

    vectors_b = jnp.pad(vectors, ((0, 16 - vectors.shape[0]), (0, 0)))

    def stacked_columns(weights, widths, beside=()):
        cut = cut_columns(weights, vectors_b, here, seq)
        *stacked, last = stack_rows(after(trade_seq(cut), beside), widths, vectors_b, here)
        return [w.reshape(-1, w.shape[-1]) for w in stacked] + [last], cut

    def gather_dp(rows):
        return lax.all_gather(rows, "dp", axis=0, tiled=True)

    def scatter_dp(grad):
        return lax.psum_scatter(grad, "dp", scatter_dimension=0, tiled=True)

    def owners_parts(summed):
        rows = summed.shape[0] // seq
        return trade_seq([lax.dynamic_slice_in_dim(summed, (place ^ j) * rows, rows, 0) for j in range(seq)])

    def owners_rows(summed, widths):
        return join_columns(owners_parts(summed), widths, here)

    def turn_pieces(pieces):
        if within is not None:
            return pieces
        return [outside(p, groups, unit) for p in pieces]

    positions = jnp.arange(length, dtype=jnp.int32)
    piece, first_flags = segment_of(seq_lengths[0], positions)

    (columns_in, columns_g, vec_seq), cut = stacked_columns(
        [w_receptance, w_key, w_value, w_gate], [3 * part, part]
    )
    tokens_held = held_back(inputs_b, here, *cut)
    full_in = gather_dp(columns_in)
    vec_parts = gather_small(vec_seq[None, :, : vectors.shape[0]], "dp").astype(F32)
    vec = vec_parts.transpose(2, 1, 0, 3).reshape(-1, width)
    turned = vec_parts.transpose(2, 0, 1, 3).reshape(-1, width)
    vec_own = lax.dynamic_slice_in_dim(vec, place * part, part, 1)
    log_decay = -jnp.exp(vec_own[6])
    tables = wkv_tables(
        piece, 1.0 - first_flags.astype(F32), log_decay, vec_own[7], vec_own[8], vec_own[9]
    )
    marks = tables[0]
    rows_one = rows_of(turned, 0, 1, 2, 3, 4, 5)
    tokens_all = gather_seq(tokens_held, (rows_one, tables))
    full_g = gather_dp(after(columns_g, tokens_all[1:3], rows_one))
    own_o = gather_dp(after(w_output, tokens_all))

    mix_r, mix_k, mix_v, mix_g, step = mixes(
        turn_pieces(tokens_all), marks, rows_one, 4, True, within, here, tile, own_rows // tile
    )
    recept, keyed, valued = (
        dot(m, full_in[:, i * part : (i + 1) * part], NN).astype(BF)
        for i, m in enumerate((mix_r, mix_k, mix_v))
    )
    projected = (recept, keyed, valued)
    ffn_weights = after([ffn_key, ffn_receptance], mix_r)
    if seq == 4:
        pieces_c = trade_seq(cut_with_rider(ffn_weights, grad_b, here))
    else:
        (columns_c, _), _ = stacked_columns(ffn_weights, [hidden_width + part], projected)
        grad_all = gather_seq(after(grad_b, mix_r), projected)
    wkv, states = wkv_forward(recept, keyed, valued, tables, here, per)
    gate_pre, mixed = gated(mix_g, full_g, wkv, tables[5], here, seq)
    if seq == 4:
        pieces_c = after(pieces_c, mixed)
        columns_c = stack_below(pieces_c, here)
        grad_all = gather_second(grad_b, *pieces_c[1:3])
    full_c = gather_dp(columns_c)
    full_ck, full_cr = full_c[:, :hidden_width], full_c[:, hidden_width:]
    full_cv = gather_dp(after(ffn_value, columns_c))
    attn = [dot(rows, own_o, NN).astype(BF) for rows in blocks_of(mixed, seq)]
    after_mix, normed_two = after_norm(inputs_b, after(scatter_seq(attn, here), grad_all[3:]), rows_of(vec, 10, 11), here)

    mix_k2, mix_r2, step_two = mixes(
        turn_pieces(gather_seq(normed_two)), marks, rows_of(turned, 10, 11, 12, 13), 2, False, within, here, tile,
        own_rows // tile,
    )
    recept_pre = dot(mix_r2, full_cr, NN)
    opened = gather_seq(jax.nn.sigmoid(recept_pre).astype(BF))
    key_pre = dot(mix_k2, full_ck, NN)
    smooth = jax.nn.softplus(key_pre)
    hidden = (smooth * smooth).astype(BF)
    slope = (2.0 * smooth * jax.nn.sigmoid(key_pre)).astype(BF)
    hidden, slope = lax.optimization_barrier((hidden, slope))
    later = after(hidden, opened[1:3])
    value_parts = [columns_product(later if j < 2 else hidden, full_cv, part, j, here, seq) for j in reversed(range(seq))]
    value_parts = value_parts[::-1]
    value_relayed = scatter_relay(value_parts, scatter_start(value_parts), here)
    d_value = spread_columns(
        grad_all, by_block(after(opened, value_parts, value_relayed)), here, True, True, tile, own_rows // tile
    )

    grad_cv = dot(hidden, d_value, TN).astype(BF)
    summed_cv = scatter_dp(grad_cv)
    value_terms = scatter_end(value_parts[0], value_relayed)
    d_hidden = dot(after(d_value, grad_cv), full_cv, NT)
    d_key_two = (d_hidden * slope.astype(F32)).astype(BF)
    channel, d_recept_two = channel_out(value_terms, recept_pre, grad_all, here, tile)
    half, first = part // 2, hidden_width // (part // 2)
    grad_ck, grad_cr = [], []

    def beside_two(relayed):
        grad_ck.append(dot(after(mix_k2, relayed), d_key_two, TN).astype(BF))
        grad_cr.append(dot(after(mix_r2, relayed, grad_ck), d_recept_two, TN).astype(BF))
        return grad_ck, grad_cr

    terms_two, sums_two = mixes_back_scatter(
        [(0, d_key_two, 0, full_c, 0, hidden_width)]
        + [(1, d_recept_two, i, full_c, first + i, half) for i in range(2)],
        step_two, marks, rows_of(turned, 12, 13), here, seq, beside_two,
    )
    summed_ck, summed_cr = scatter_dp(grad_ck[0]), scatter_dp(grad_cr[0])
    if within is None:
        terms_two = [outside(t, groups, unit, back=True) for t in terms_two]
    d_after, d_attn, norm_sums_two = norm_back(terms_two, after_mix, grad_b, rows_of(vec, 10), within, here)

    pieces = gather_seq(d_attn)
    *near, far = by_block(pieces)
    near_mixed = [dot(d, own_o, NT).astype(BF) for d in near]
    *near_rows, far_rows = blocks_of(mixed, seq)
    near_wo = sum(dot(m, d, TN) for m, d in zip(near_rows, near))
    far = after(far, near_mixed, near_wo, summed_cv)
    d_mixed = jnp.concatenate([*near_mixed, dot(far, own_o, NT).astype(BF)], axis=0)
    grad_wo = (near_wo + dot(far_rows, far, TN)).astype(BF)
    summed_o = scatter_dp(grad_wo)
    d_mixed = after(d_mixed, summed_ck, grad_wo)
    d_recept, d_keyed, d_valued, d_gate, sums = wkv_backward(
        recept, keyed, valued, gate_pre, wkv, d_mixed, states, tables, here, per
    )
    channel = after(trade_seq(blocks_of(after(channel, d_mixed), seq)), d_recept)
    grads_vg = [
        dot(after(m, channel), d, TN).astype(BF) for m, d in ((mix_v, d_valued), (mix_g, d_gate))
    ]
    summed_vg = scatter_dp(jnp.concatenate(grads_vg, axis=1))
    grads_rk, others = [], []

    def beside(relayed):
        grads_rk.extend(
            dot(after(m, relayed), d, TN).astype(BF) for m, d in ((mix_r, d_recept), (mix_k, d_keyed))
        )
        others.append(spread_columns([after_mix], after(channel, relayed), here, False, False, CHUNK, per))
        others.append(after(summed_cv, relayed).astype(F32))
        return grads_rk, others

    d_recept, d_keyed = after((d_recept, d_keyed), grads_vg, summed_o)
    terms, sums_one = mixes_back_scatter(
        [(i, d, 0, full_in, i, part) for i, d in enumerate((d_recept, d_keyed, d_valued))]
        + [(3, d_gate, 0, full_g, 0, part)],
        step, marks, rows_of(turned, 2, 3, 4, 5), here, seq, beside,
    )
    summed_rk = scatter_dp(jnp.concatenate(grads_rk, axis=1))
    out_rows, sum_cv = others
    if within is None:
        terms = [outside(t, groups, unit, back=True) for t in terms]
    tokens_grad, _, norm_sums = norm_back(terms, inputs_b, d_after, rows_of(vec, 0), within, here)

    summed_c = jnp.concatenate(after([summed_ck, summed_cr], terms), axis=1)
    sum_ck, sum_cr = owners_rows(summed_c, [ffn_key.shape[1], width])
    sum_o = summed_o.astype(F32)
    sum_v, sum_g = owners_rows(summed_vg, [width] * 2)

    def by_device(rows, turn):
        if turn:
            return rows.reshape(-1, dp, seq, unit).transpose(1, 2, 0, 3)
        return rows.reshape(-1, seq, dp, unit).transpose(2, 1, 0, 3)

    own_sums = jnp.stack([sums[0] * log_decay, sums[1], sums[2], sums[3]])
    own_sums = lax.dynamic_update_slice(jnp.zeros((4, width), F32), own_sums, (0, place * part))
    vector_rows = jnp.concatenate(
        [
            by_device(norm_sums[:2], False), by_device(sums_one[:4], True), by_device(own_sums, False),
            by_device(norm_sums_two[:2], False), by_device(sums_two[:2], True),
        ],
        axis=2,
    )
    sum_vec = scatter_small(vector_rows.reshape((-1,) + vector_rows.shape[2:]))
    sum_r, sum_k = owners_rows(after(summed_rk, sum_ck, sum_v, sum_vec), [width] * 2)
    return (
        out_rows[None], tokens_grad[None], sum_r, sum_k, sum_v, sum_g, sum_o,
        sum_ck, sum_cr, sum_cv, sum_vec,
    )


def solution(mesh):
    tokens = P("dp", "seq", None)
    rows = P(("seq", "dp"), None)
    columns = P(None, ("seq", "dp"))
    return jax.shard_map(
        shards,
        mesh=mesh,
        in_specs=(tokens, P("dp", None), tokens) + (rows,) * 8 + (columns,),
        out_specs=(tokens, tokens) + (rows,) * 8 + (columns,),
        check_vma=False,
    )
```

```python
from functools import partial

import jax
import jax.numpy as jnp
from jax import lax
from jax.experimental import pallas as pl
from jax.experimental.pallas import tpu as pltpu
from jax.sharding import PartitionSpec as P

HEAD = 64
PAIR = 128
CHUNK = 128
EPSILON = 1e-05
GROUP_EPSILON = 1.0
BF = jnp.bfloat16
F32 = jnp.float32
NT = (((1,), (1,)), ((), ()))
TN = (((0,), (0,)), ((), ()))
NN = (((1,), (0,)), ((), ()))


def swap(value, axis, distance):
    size = lax.axis_size(axis)
    return lax.ppermute(value, axis, [(i, i ^ distance) for i in range(size)])


def after(value, *others):
    return lax.optimization_barrier((value, others))[0]


def gather_second(part, one, two):
    half = part.shape[0] // 2
    columns = part.shape[1]
    low, high = swap(one[:half, :columns], "seq", 2), swap(two[half : 2 * half, :columns], "seq", 1)
    return [part, one, two, low, high]


def gather_seq(part, first=()):
    size = lax.axis_size("seq")
    if size == 4:
        half = part.shape[0] // 2
        one, two = swap(part, "seq", 1), swap(part, "seq", 2)
        one, two = after((one, two), first)
        low, high = swap(one[:half], "seq", 2), swap(two[half:], "seq", 1)
        return [part, one, two, low, high]
    return [part] + [swap(part, "seq", distance) for distance in range(1, size)]


def by_block(pieces):
    if lax.axis_size("seq") == 4:
        return pieces[:3] + [jnp.concatenate(pieces[3:], axis=0)]
    return pieces


def scatter_start(parts):
    if lax.axis_size("seq") != 4:
        return ()
    low, high = parts[3:] if len(parts) == 5 else blocks_of(parts[3], 2)
    return swap(low, "seq", 1), swap(high, "seq", 2)


def relay_body(here, one_ref, two_ref, low_ref, high_ref, one_out, two_out):
    one, two = one_ref[...], two_ref[...]
    first = pl.program_id(0) == 0
    low, high = low_ref[...].astype(F32), high_ref[...].astype(F32)
    one_out[...] = jnp.where(first, one, (one.astype(F32) + high).astype(BF))
    two_out[...] = jnp.where(first, (two.astype(F32) + low).astype(BF), two)


def scatter_relay(parts, started, here):
    if lax.axis_size("seq") != 4:
        return parts[1:]
    (_, one, two, *_), (low, high) = parts, started
    (rows, width), half = one.shape, block(low.shape, lambda i, h: (i, 0))
    return kernel(
        relay_body, "relay", (2,), here,
        [(one, half), (two, half), (low, fixed(low.shape)), (high, fixed(low.shape))],
        [((rows, width), BF, half)] * 2,
    )


def scatter_end(own, relayed):
    return [own] + [swap(part, "seq", j + 1) for j, part in enumerate(relayed)]


def scatter_seq(parts, here):
    return scatter_end(parts[0], scatter_relay(parts, scatter_start(parts), here))


def trade_seq(parts):
    return [parts[0]] + [swap(part, "seq", j + 1) for j, part in enumerate(parts[1:])]


def blocks_of(values, size):
    rows = values.shape[0] // size
    return [values[j * rows : (j + 1) * rows] for j in range(size)]


def bits_of(size):
    return [1 << b for b in range(size.bit_length() - 1)]


def gather_small(part, axis):
    for bit in bits_of(lax.axis_size(axis)):
        other = swap(part, axis, bit)
        second = (lax.axis_index(axis) & bit) != 0
        part = jnp.concatenate([jnp.where(second, other, part), jnp.where(second, part, other)], axis=0)
    return part


def scatter_small(parts):
    for axis in ("dp", "seq"):
        for bit in reversed(bits_of(lax.axis_size(axis))):
            half = parts.shape[0] // 2
            second = (lax.axis_index(axis) & bit) != 0
            low, high = parts[:half], parts[half:]
            parts = jnp.where(second, high, low) + swap(jnp.where(second, low, high), axis, bit)
    return parts[0]


def block(shape, index):
    return pl.BlockSpec(shape, lambda *i: index(*i[:-1], i[-1][0]))


def fixed(shape):
    return pl.BlockSpec(shape, lambda *i: (0,) * len(shape))


def relative(tile, per, here):
    return (lax.div(tile, per) ^ here) * per + lax.rem(tile, per)


def kernel(body, name, grid, here, ins, outs, scratch=(), vmem=48):
    return pl.pallas_call(
        body,
        out_shape=[jax.ShapeDtypeStruct(shape, kind) for shape, kind, _ in outs],
        grid_spec=pltpu.PrefetchScalarGridSpec(
            num_scalar_prefetch=1,
            grid=grid,
            in_specs=[spec for _, spec in ins],
            out_specs=[spec for _, _, spec in outs],
            scratch_shapes=list(scratch),
        ),
        compiler_params=pltpu.CompilerParams(vmem_limit_bytes=vmem * 2**20),
        name=name,
    )(here, *[array for array, _ in ins])


def pieced(pieces, tile, columns, column, place):
    ins, start = [], 0
    for piece in pieces:
        count = piece.shape[0] // tile

        def index(i, h, start=start, count=count):
            return jnp.clip(place(i, h) - start, 0, count - 1), column(h)

        ins.append((piece, block((tile, columns), index)))
        start += count
    return ins


def picked(refs, counts, tile, held):
    start = 0
    for ref, count in zip(refs, counts):

        @pl.when((tile >= start) & (tile < start + count))
        def _(ref=ref):
            held[...] = ref[...]

        start += count
    return held[...].astype(F32)


def counts_of(pieces, tile):
    return [piece.shape[0] // tile for piece in pieces]


def row_index(rows):
    return lax.broadcasted_iota(jnp.int32, (rows, 1), 0)


def placed(place, width):
    return pl.ds(pl.multiple_of(place * width, width), width)


def cut_body(count, parts, here, *refs):
    ins, beside, outs = refs[:count], refs[count], refs[count + 1 :]
    rows = ins[0].shape[0]
    for j in range(parts):
        outs[j][rows:, :] = jnp.zeros_like(outs[j][rows:, :])
        outs[j][rows:, : beside.shape[1]] = beside[...]
    at = 0
    for ref in ins:
        width = ref.shape[1] // parts
        for j in range(parts):
            outs[j][:rows, at : at + width] = ref[:, placed(here[0] ^ j, width)]
        at += width


def cut_columns(weights, beside, here, parts):
    rows, width = weights[0].shape[0] + beside.shape[0], sum(w.shape[1] for w in weights) // parts
    return kernel(
        partial(cut_body, len(weights), parts), "cut_columns", (1,), here,
        [(w, fixed(w.shape)) for w in [*weights, beside]],
        [((rows, width), BF, fixed((rows, width)))] * parts,
    )


def stack_body(parts, here, *refs):
    start = 0
    outs, beside = refs[parts:-1], refs[-1]
    for out in outs:
        for j in range(parts):
            out[here[0] ^ j] = refs[j][: out.shape[1], start : start + out.shape[2]]
        start += out.shape[2]
    for j in range(parts):
        beside[here[0] ^ j] = refs[j][out.shape[1] :, : beside.shape[2]]


def stack_rows(pieces, widths, beside, here):
    parts, rows = len(pieces), pieces[0].shape[0] - beside.shape[0]
    shapes = [(parts, rows, width) for width in widths] + [(parts,) + beside.shape]
    return kernel(
        partial(stack_body, parts), "stack_rows", (1,), here,
        [(p, fixed(p.shape)) for p in pieces],
        [(shape, BF, fixed(shape)) for shape in shapes],
    )


def ride_body(count, here, *refs):
    ins, rider, outs = refs[:count], refs[count], refs[count + 1 :]
    for j, out in enumerate(outs):
        top, at = 0, 0
        if j in (1, 2):
            top = rider.shape[0]
            out[:top, : rider.shape[1]] = rider[...]
            out[:top, rider.shape[1] :] = jnp.zeros_like(out[:top, rider.shape[1] :])
        for ref in ins:
            width = ref.shape[1] // 4
            out[top:, at : at + width] = ref[:, placed(here[0] ^ j, width)]
            at += width


def cut_with_rider(weights, rider, here):
    rows, width = weights[0].shape[0], sum(w.shape[1] for w in weights) // 4
    return kernel(
        partial(ride_body, len(weights)), "cut_columns", (1,), here,
        [(w, fixed(w.shape)) for w in [*weights, rider]],
        [((n, width), BF, fixed((n, width))) for n in (rows, rows + rider.shape[0], rows + rider.shape[0], rows)],
    )


def unride_body(here, *refs):
    out = refs[-1]
    rows = out.shape[1]
    for j, ref in enumerate(refs[:-1]):
        out[here[0] ^ j] = ref[ref.shape[0] - rows :, :]


def stack_below(pieces, here):
    shape = (4,) + pieces[0].shape
    (stacked,) = kernel(
        unride_body, "stack_rows", (1,), here,
        [(p, fixed(p.shape)) for p in pieces],
        [(shape, BF, fixed(shape))],
    )
    return stacked.reshape(-1, shape[-1])


def hold_body(here, in_ref, *refs):
    refs[-1][...] = in_ref[...]


def held_back(values, here, *others):
    rows, width = values.shape
    own = block((rows // 2, width), lambda i, h: (i, 0))
    (copy,) = kernel(
        hold_body, "hold", (2,), here,
        [(values, own)] + [(o, pl.BlockSpec(memory_space=pl.ANY)) for o in others],
        [((rows, width), values.dtype, own)],
    )
    return copy


def join_body(parts, count, here, *refs):
    ins, outs = refs[:parts], refs[parts:]
    at = 0
    for ref in outs:
        width = ref.shape[1] // parts
        for j in range(parts):
            ref[:, placed(here[0] ^ j, width)] = ins[j][:, at : at + width].astype(F32)
        at += width


def join_columns(pieces, widths, here):
    parts, rows = len(pieces), pieces[0].shape[0]
    return kernel(
        partial(join_body, parts, len(widths)), "join_columns", (1,), here,
        [(p, fixed(p.shape)) for p in pieces],
        [((rows, width), F32, fixed((rows, width))) for width in widths],
    )


def spread_body(counts, parts, product, here, *refs):
    bases, pieces, out, held = refs[: len(counts)], refs[len(counts) : -2], refs[-2], refs[-1]
    picked(bases, counts, pl.program_id(0), held)
    width = pieces[0].shape[1]
    for j in range(parts):
        at = placed(here[0] ^ j, width)
        piece, base = pieces[j][...].astype(F32), held[:, at].astype(F32)
        out[:, at] = (base * piece if product else base + piece).astype(BF)


def spread_columns(bases, columns, here, product, turn, tile, per):
    rows, width = sum(counts_of(bases, tile)) * tile, bases[0].shape[1]

    def turned(i, j):
        return (lax.div(i, per) ^ j) * per + lax.rem(i, per) if turn else i

    (result,) = kernel(
        partial(spread_body, counts_of(bases, tile), len(columns), product), "spread_columns", (rows // tile,), here,
        pieced(bases, tile, width, lambda h: 0, lambda i, h: i)
        + [(c, block((tile, c.shape[1]), lambda i, h, j=j: (turned(i, j), 0))) for j, c in enumerate(columns)],
        [((rows, width), BF, block((tile, width), lambda i, h: (i, 0)))],
        [pltpu.VMEM((tile, width), bases[0].dtype)],
    )
    return result


def shuffled(values, groups, back=False):
    seq, dp = groups
    if back:
        seq, dp = dp, seq
    lane = lax.broadcasted_iota(jnp.int32, (1, PAIR), 1) < HEAD
    source = [s * dp + d for d in range(dp) for s in range(seq)]
    columns = []
    for one, two in zip(source[::2], source[1::2]):
        low = values[:, one // 2 * PAIR : (one // 2 + 1) * PAIR]
        high = values[:, two // 2 * PAIR : (two // 2 + 1) * PAIR]
        low = pltpu.roll(low, HEAD, 1) if one % 2 else low
        high = high if two % 2 else pltpu.roll(high, HEAD, 1)
        columns.append(jnp.where(lane, low, high))
    return jnp.concatenate(columns, axis=1)


def outside(values, groups, channels, back=False):
    seq, dp = groups[::-1] if back else groups
    return values.reshape(-1, seq, dp, channels).swapaxes(1, 2).reshape(values.shape)


def centre(values):
    centred = values - jnp.mean(values, axis=-1, keepdims=True)
    spread = jnp.mean(centred * centred, axis=-1, keepdims=True)
    return centred, lax.rsqrt(spread + EPSILON)


def mix_body(count, norm, groups, counts, per, here, *refs):
    pieces, (marks_ref, vec_ref) = refs[: len(counts)], refs[len(counts) : len(counts) + 2]
    outs, last, held = refs[len(counts) + 2 : -2], refs[-2], refs[-1]

    @pl.when(pl.program_id(0) == 0)
    def _():
        last[...] = jnp.zeros_like(last)

    values = picked(pieces, counts, relative(pl.program_id(0), per, here[0]), held)
    if norm:
        centred, inverse = centre(values)
        values = centred * inverse
    if groups:
        values = shuffled(values, groups)
    if norm:
        values = values * vec_ref[0:1, :] + vec_ref[1:2, :]
    rows = values.shape[0]
    previous = jnp.where(row_index(rows) == 0, last[0:1, :], pltpu.roll(values, 1, 0)) * marks_ref[:, 3:4]
    last[0:1, :] = values[rows - 1 :, :]
    step = values - previous
    outs[count][...] = step.astype(BF)
    for i in range(count):
        outs[i][...] = (previous + step * vec_ref[2 + i : 3 + i, :]).astype(BF)


def mixes(pieces, marks, vec, count, norm, groups, here, tile, per):
    rows, width = marks.shape[0], pieces[0].shape[1]
    own = block((tile, width), lambda i, h: (relative(i, per, h), 0))
    return kernel(
        partial(mix_body, count, norm, groups, counts_of(pieces, tile), per), "mixes", (rows // tile,), here,
        pieced(pieces, tile, width, lambda h: 0, lambda i, h: relative(i, per, h))
        + [(marks, block((tile, PAIR), lambda i, h: (i, 0))), (vec, fixed(vec.shape))],
        [((rows, width), BF, own)] * (count + 1),
        [pltpu.VMEM((8, width), F32), pltpu.VMEM((tile, width), BF)],
    )


def mixes_back_body(which, first, seq, outs, here, *refs):
    count = len(which)
    grads, nexts, weights = refs[:count], refs[count : 2 * count], refs[2 * count : 3 * count]
    step_ref, marks_ref, next_marks_ref, vec_ref, *out_refs, sums_ref = refs[3 * count :]

    @pl.when(pl.program_id(1) == 0)
    def _():
        sums_ref[...] = jnp.zeros_like(sums_ref)

    step = step_ref[...].astype(F32)
    rows = step.shape[0]
    total = straight = None
    for i in range(which[-1] + 1):
        grad = sum(
            dot(jnp.concatenate([grads[k][...], nexts[k][...]], axis=0), weights[k][...], NT)
            for k in range(count)
            if which[k] == i
        )
        sums_ref[i : i + 1, :] += jnp.sum(grad[:rows] * step, axis=0, keepdims=True)
        part = grad * vec_ref[i : i + 1, :]
        total, straight = (total + grad, straight + part) if i else (grad, part)
    inside = ((first + pl.program_id(1)) ^ here[0]) < seq - 1
    keep = jnp.concatenate([marks_ref[:, 3:4], jnp.where(inside, next_marks_ref[:, 3:4], 0.0)], axis=0)
    kept = (total - straight) * keep
    up = pltpu.roll(kept, kept.shape[0] - 1, 0)
    result = (straight[:rows] + up[:rows]).astype(BF)
    if len(out_refs) == 1:
        out_refs[0][...] = result
        return
    if outs == 1:
        out_refs[0][...] = result[: rows // 2]
        out_refs[1][...] = result[rows // 2 :]
        return
    for k, out_ref in enumerate(out_refs):

        @pl.when(pl.program_id(1) == k)
        def _(out_ref=out_ref):
            out_ref[...] = result


EXTRA = 16


def mixes_back(terms, step, marks, vec, here, seq, first, count, halves=False):
    rows, width = step.shape
    tile, columns = rows // seq, min(512, width)
    extras = tile // EXTRA

    def following(i, h):
        return jnp.minimum(((first + i) ^ h) + 1, seq - 1)

    ins = [(g, block((tile, n), lambda c, i, h, at=at: (first + i, at))) for _, g, at, _, _, n in terms]
    ins += [
        (g, block((EXTRA, n), lambda c, i, h, at=at: ((following(i, h) ^ h) * extras, at)))
        for _, g, at, _, _, n in terms
    ]
    ins += [(w, block((columns, n), lambda c, i, h, at=at: (c, at))) for _, _, _, w, at, n in terms]
    ins += [
        (step, block((tile, columns), lambda c, i, h: (first + i, c))),
        (marks, block((tile, PAIR), lambda c, i, h: ((first + i) ^ h, 0))),
        (marks, block((EXTRA, PAIR), lambda c, i, h: (following(i, h) * extras, 0))),
        (vec, block((8, columns), lambda c, i, h: (0, c))),
    ]
    size = tile // 2 if halves else tile
    *parts, sums = kernel(
        partial(mixes_back_body, [t[0] for t in terms], first, seq, count), "mixes_back", (width // columns, count), here, ins,
        [((size, width), BF, block((size, columns), lambda c, i, h: (0, c)))] * (2 if halves else count)
        + [((8, width), F32, block((8, columns), lambda c, i, h: (0, c)))],
    )
    return parts, sums


def mixes_back_scatter(terms, step, marks, vec, here, seq, beside):
    if seq != 4:
        parts, sums = mixes_back(terms, step, marks, vec, here, seq, 0, seq)
        return after(scatter_seq(parts, here), beside(parts)), sums

    def call(first, count, *before):
        ordered = after([t[1] for t in terms], *before)
        return mixes_back(
            [(t[0], g) + t[2:] for t, g in zip(terms, ordered)], step, marks, vec, here, seq, first, count, first == 3
        )

    far, sums_far = call(3, 1)
    near, sums_near = call(1, 2, far)
    parts = [None, *near, *far]
    started = after(scatter_start(parts), near)
    relayed = scatter_relay(parts, started, here)
    (own,), sums_own = call(0, 1, near, relayed)
    return after(scatter_end(own, relayed), beside(relayed)), sums_far + sums_near + sums_own


def after_body(count, here, x_ref, vec_ref, *refs):
    after_ref, normed_ref = refs[count:]
    after = x_ref[...].astype(F32)
    for ref in refs[:count]:
        after = after + ref[...].astype(F32)
    after_ref[...] = after
    centred, inverse = centre(after)
    normed_ref[...] = (centred * inverse * vec_ref[0:1, :] + vec_ref[1:2, :]).astype(BF)


def after_norm(inputs, terms, vec, here):
    rows, width = inputs.shape
    own = block((CHUNK, width), lambda i, h: (i, 0))
    return kernel(
        partial(after_body, len(terms)), "after_norm", (rows // CHUNK,), here,
        [(inputs, own), (vec, fixed(vec.shape))] + [(t, own) for t in terms],
        [((rows, width), F32, own), ((rows, width), BF, own)],
    )


def norm_back_body(count, groups, here, x_ref, base_ref, vec_ref, *refs):
    wide_ref, narrow_ref, sums_ref = refs[count:]

    @pl.when(pl.program_id(0) == 0)
    def _():
        sums_ref[...] = jnp.zeros_like(sums_ref)

    grad = refs[0][...].astype(F32)
    for ref in refs[1:count]:
        grad = grad + ref[...].astype(F32)
    if groups:
        grad = shuffled(grad, groups, back=True)
    centred, inverse = centre(x_ref[...].astype(F32))
    normed = centred * inverse
    sums_ref[0:1, :] += jnp.sum(grad * normed, axis=0, keepdims=True)
    sums_ref[1:2, :] += jnp.sum(grad, axis=0, keepdims=True)
    grad = grad * vec_ref[0:1, :]
    grad = grad - jnp.mean(grad, axis=-1, keepdims=True) - normed * jnp.mean(grad * normed, axis=-1, keepdims=True)
    result = base_ref[...].astype(F32) + inverse * grad
    wide_ref[...] = result
    narrow_ref[...] = result.astype(BF)


def norm_back(terms, inputs, base, vec, groups, here):
    rows, width = inputs.shape
    own = block((CHUNK, width), lambda i, h: (i, 0))
    return kernel(
        partial(norm_back_body, len(terms), groups), "norm_back", (rows // CHUNK,), here,
        [(inputs, own), (base, own), (vec, fixed(vec.shape))] + [(t, own) for t in terms],
        [((rows, width), F32, own), ((rows, width), BF, own), ((8, width), F32, fixed((8, width)))],
    )


def gate_body(mix_ref, weight_ref, wkv_ref, par_ref, gate_ref, mixed_ref):
    gate = dot(mix_ref[...], weight_ref[...], NN)
    gate_ref[...] = gate
    ones = jnp.where(same_head(), 1.0, 0.0).astype(BF)
    for pair in range(gate.shape[1] // PAIR):
        at = slice(pair * PAIR, (pair + 1) * PAIR)
        wkv = wkv_ref[:, at]
        centred = wkv - head_sum_fine(wkv, ones) * (1.0 / HEAD)
        spread = head_sum(centred * centred, ones) * (1.0 / HEAD)
        normed = centred * lax.rsqrt(spread + GROUP_EPSILON) * par_ref[1:2, at] + par_ref[2:3, at]
        mixed_ref[:, at] = (normed * (gate[:, at] / (1.0 + jnp.exp(-gate[:, at])))).astype(BF)


def gated(mix_g, weights, wkv, params, here, seq):
    rows, width = mix_g.shape
    tile, part = rows // seq, wkv.shape[1]
    own = block((tile, part), lambda i, h: (i, 0))
    return kernel(
        lambda here, *refs: gate_body(*refs), "gate", (seq,), here,
        [
            (mix_g, block((tile, width), lambda i, h: (i, 0))),
            (weights, block((width, part), lambda i, h: (0, 0))),
            (wkv, own),
            (params, fixed(params.shape)),
        ],
        [((rows, part), F32, own), ((rows, part), BF, own)],
    )


def columns_body(here, left_ref, right_ref, out_ref):
    out_ref[...] = dot(left_ref[...], right_ref[...], NN).astype(BF)


def columns_product(left, right, part, relative_to, here, seq):
    rows, depth = left.shape
    tile = rows // seq
    (result,) = kernel(
        columns_body, "value_columns", (seq,), here,
        [
            (left, block((tile, depth), lambda i, h: (i, 0))),
            (right, block((depth, part), lambda i, h: (0, h ^ relative_to))),
        ],
        [((rows, part), BF, block((tile, part), lambda i, h: (i ^ relative_to, 0)))],
    )
    return result


def channel_body(counts, here, pre_ref, *refs):
    grads, terms, (channel_ref, d_recept_ref, held) = refs[: len(counts)], refs[len(counts) : -3], refs[-3:]
    value = sum(ref[...].astype(F32) for ref in terms)
    opened = 1.0 / (1.0 + jnp.exp(-pre_ref[...]))
    channel = opened * value
    channel_ref[...] = channel.astype(BF)
    grad = picked(grads, counts, pl.program_id(0), held)
    d_recept_ref[...] = (grad * channel * (1.0 - opened)).astype(BF)


def channel_out(terms, pre, grads, here, tile):
    rows, part = pre.shape
    own = block((tile, part), lambda i, h: (i, 0))
    return kernel(
        partial(channel_body, counts_of(grads, tile)), "channel", (rows // tile,), here,
        [(pre, own)] + pieced(grads, tile, part, lambda h: h, lambda i, h: i) + [(t, own) for t in terms],
        [((rows, part), BF, own)] * 2,
        [pltpu.VMEM((tile, part), BF)],
    )


def head_masks():
    lane = lax.broadcasted_iota(jnp.int32, (1, PAIR), 1)
    first = (lane < HEAD).astype(F32)
    return first, 1.0 - first


def same_head():
    row = lax.broadcasted_iota(jnp.int32, (PAIR, PAIR), 0) < HEAD
    column = lax.broadcasted_iota(jnp.int32, (PAIR, PAIR), 1) < HEAD
    return row == column


def dot(left, right, dims):
    return lax.dot_general(left, right, dims, preferred_element_type=F32)


def head_sum(values, ones):
    return dot(values.astype(BF), ones, NN)


def head_sum_fine(values, ones):
    coarse = values.astype(BF)
    rest = (values - coarse.astype(F32)).astype(BF)
    return dot(coarse, ones, NN) + dot(rest, ones, NN)


def stacked(values, first, second):
    return jnp.concatenate([(values * first).astype(BF), (values * second).astype(BF)], axis=0)


def masks_of(rows_ref, columns_ref):
    segment = rows_ref[:, 0:1]
    reaches = rows_ref[:, 1:2]
    last_same = rows_ref[:, 2:3]
    reach_last = rows_ref[CHUNK - 1 : CHUNK, 1:2]
    before = lax.broadcasted_iota(jnp.int32, (CHUNK, CHUNK), 1) < lax.broadcasted_iota(
        jnp.int32, (CHUNK, CHUNK), 0
    )
    allowed = jnp.where((segment == columns_ref[0:1, :]) & before, 1.0, 0.0)
    return reaches, last_same, reach_last, jnp.concatenate([allowed, allowed], axis=0)


def wkv_forward_body(
    here, r_ref, k_ref, v_ref, rows_ref, columns_ref, grow_ref, shrink_ref, tail_ref, par_ref,
    wkv_ref, states_ref, state,
):
    @pl.when(pl.program_id(0) == 0)
    def _():
        state[...] = jnp.zeros_like(state)

    first, second = head_masks()
    block = same_head()
    ones = jnp.where(block, 1.0, 0.0).astype(BF)
    reaches, last_same, reach_last, allowed = masks_of(rows_ref, columns_ref)
    for pair in range(r_ref.shape[1] // PAIR):
        at = slice(pair * PAIR, (pair + 1) * PAIR)
        r, k, v = r_ref[:, at].astype(F32), k_ref[:, at].astype(F32), v_ref[:, at].astype(F32)
        bonus, decay = par_ref[0:1, at], par_ref[3:4, at]
        held = state[at, :]
        held_b = held.astype(BF)
        states_ref[0, at, :] = held_b
        grown = r * grow_ref[:, at]
        shrunk = (k * shrink_ref[:, at]).astype(BF)
        scores = (dot(stacked(grown, first, second), shrunk, NT) * allowed).astype(BF)
        both = jnp.concatenate([scores[:CHUNK], scores[CHUNK:]], axis=1)
        wkv = dot(both, stacked(v, first, second), NN)
        wkv = wkv + dot((grown * reaches).astype(BF), held_b, NT)
        wkv = wkv + head_sum(r * bonus * k, ones) * v
        fresh = dot(v_ref[:, at], (k * tail_ref[:, at] * last_same).astype(BF), TN)
        state[at, :] = held * (decay * reach_last) + jnp.where(block, fresh, 0.0)
        wkv_ref[:, at] = wkv


def wkv_backward_body(
    here, r_ref, k_ref, v_ref, g_ref, wkv_ref, d_mixed_ref, states_ref,
    rows_ref, columns_ref, grow_ref, shrink_ref, tail_ref, par_ref,
    d_r_ref, d_k_ref, d_v_ref, d_g_ref, sums_ref, d_state,
):
    @pl.when(pl.program_id(0) == 0)
    def _():
        d_state[...] = jnp.zeros_like(d_state)
        sums_ref[...] = jnp.zeros_like(sums_ref)

    first, second = head_masks()
    block = same_head()
    ones = jnp.where(block, 1.0, 0.0).astype(BF)
    reaches, last_same, reach_last, allowed = masks_of(rows_ref, columns_ref)
    offset = lax.broadcasted_iota(jnp.int32, (CHUNK, PAIR), 0).astype(F32)
    for pair in range(r_ref.shape[1] // PAIR):
        at = slice(pair * PAIR, (pair + 1) * PAIR)
        bonus, gain, bias, decay = (par_ref[i : i + 1, at] for i in range(4))
        wkv, gate, d_mixed = wkv_ref[:, at], g_ref[:, at], d_mixed_ref[:, at].astype(F32)
        centred = wkv - head_sum_fine(wkv, ones) * (1.0 / HEAD)
        spread = head_sum(centred * centred, ones) * (1.0 / HEAD)
        inverse = lax.rsqrt(spread + GROUP_EPSILON)
        normed = centred * inverse
        opened = 1.0 / (1.0 + jnp.exp(-gate))
        d_scaled = d_mixed * gate * opened
        d_g = d_mixed * (normed * gain + bias) * opened * (1.0 + gate * (1.0 - opened))
        d_g_ref[:, at] = d_g.astype(BF)
        d_normed = d_scaled * gain
        mean_one = head_sum(d_normed, ones) * (1.0 / HEAD)
        mean_two = head_sum(d_normed * normed, ones) * (1.0 / HEAD)
        d_wkv = inverse * (d_normed - mean_one - normed * mean_two)
        r, k, v = r_ref[:, at].astype(F32), k_ref[:, at].astype(F32), v_ref[:, at].astype(F32)
        v_b, d_wkv_b = v_ref[:, at], d_wkv.astype(BF)
        grow, shrink, tail = grow_ref[:, at], shrink_ref[:, at], tail_ref[:, at] * last_same
        held = states_ref[0, at, :]
        later = d_state[at, :]
        later_b = later.astype(BF)
        grown = r * grow
        shrunk = k * shrink
        shrunk_b = shrunk.astype(BF)
        tailed_b = (k * tail).astype(BF)
        grown_two = stacked(grown, first, second)
        d_wkv_two = stacked(d_wkv, first, second)
        scores = (dot(grown_two, shrunk_b, NT) * allowed).astype(BF)
        d_scores = (dot(d_wkv_two, v_b, NT) * allowed).astype(BF)
        d_both = jnp.concatenate([d_scores[:CHUNK], d_scores[CHUNK:]], axis=1)
        d_grown = dot(d_both, stacked(shrunk, first, second), NN)
        d_grown = d_grown + dot((d_wkv * reaches).astype(BF), held, NN)
        d_shrunk = dot(d_scores, grown_two, TN)
        d_tailed = dot(v_b, later_b, NN)
        share = head_sum(r * bonus * k, ones)
        d_share = head_sum(d_wkv * v, ones)
        d_v = dot(scores, d_wkv_two, TN) + dot(tailed_b, later_b, NT) + share * d_wkv
        d_r_ref[:, at] = (d_grown * grow + d_share * bonus * k).astype(BF)
        d_k_ref[:, at] = (d_shrunk * shrink + d_tailed * tail + d_share * bonus * r).astype(BF)
        d_v_ref[:, at] = d_v.astype(BF)
        carried = decay * reach_last
        d_fresh = dot(d_wkv_b, (grown * reaches).astype(BF), TN)
        d_state[at, :] = later * carried + jnp.where(block, d_fresh, 0.0)
        grown_b = grown.astype(BF).astype(F32)
        d_log = (
            offset * grown_b * d_grown
            - (offset + 1.0) * shrunk_b.astype(F32) * d_shrunk
            + (CHUNK - 1.0 - offset) * tailed_b.astype(F32) * d_tailed
        )
        kept = CHUNK * carried * jnp.sum(held.astype(F32) * later, axis=0, keepdims=True)
        sums_ref[0:1, at] += jnp.sum(d_log, axis=0, keepdims=True) + kept
        sums_ref[1:2, at] += jnp.sum(d_share * r * k, axis=0, keepdims=True)
        sums_ref[2:3, at] += jnp.sum(d_scaled * normed, axis=0, keepdims=True)
        sums_ref[3:4, at] += jnp.sum(d_scaled, axis=0, keepdims=True)


def wkv_blocks(width, chunks, per, backward):
    def chunk(i):
        return chunks - 1 - i if backward else i

    tokens = block((CHUNK, width), lambda i, h: (relative(chunk(i), per, h), 0))
    states = block((1, width, PAIR), lambda i, h: (chunk(i), 0, 0))
    tables = [
        block((CHUNK, PAIR), lambda i, h: (chunk(i), 0)),
        block((8, CHUNK), lambda i, h: (0, chunk(i))),
    ]
    return tokens, states, tables + [fixed((CHUNK, width))] * 3 + [fixed((8, width))]


def wkv_forward(r, k, v, tables, here, per):
    length, width = r.shape
    chunks = length // CHUNK
    tokens, states, blocks = wkv_blocks(width, chunks, per, False)
    return kernel(
        wkv_forward_body, "wkv_forward", (chunks,), here,
        [(a, tokens) for a in (r, k, v)] + list(zip(tables, blocks)),
        [((length, width), F32, tokens), ((chunks, width, PAIR), BF, states)],
        [pltpu.VMEM((width, PAIR), F32)],
    )


def wkv_backward(r, k, v, gate, wkv, d_mixed, states_kept, tables, here, per):
    length, width = r.shape
    chunks = length // CHUNK
    tokens, states, blocks = wkv_blocks(width, chunks, per, True)
    return kernel(
        wkv_backward_body, "wkv_backward", (chunks,), here,
        [(a, tokens) for a in (r, k, v, gate, wkv, d_mixed)] + [(states_kept, states)] + list(zip(tables, blocks)),
        [((length, width), BF, tokens)] * 4 + [((8, width), F32, fixed((8, width)))],
        [pltpu.VMEM((width, PAIR), F32)],
    )


def wkv_tables(piece, keep, log_decay, bonus, gain, bias):
    length = piece.shape[0]
    by_chunk = piece.reshape(length // CHUNK, CHUNK)
    before = jnp.concatenate([jnp.full((1,), -1, piece.dtype), by_chunk[:-1, -1]])
    reaches = (by_chunk == before[:, None]).reshape(-1)
    last_same = (by_chunk == by_chunk[:, -1:]).reshape(-1)
    marks = jnp.stack([piece.astype(F32), reaches.astype(F32), last_same.astype(F32), keep], axis=1)
    rows = jnp.pad(marks, ((0, 0), (0, PAIR - 4)))
    columns = jnp.broadcast_to(piece.astype(F32)[None], (8, length))
    offset = jnp.arange(CHUNK).astype(F32)[:, None]
    grow = jnp.exp(offset * log_decay)
    shrink = jnp.exp(-(offset + 1.0) * log_decay)
    tail = jnp.exp((CHUNK - 1.0 - offset) * log_decay)
    zero = jnp.zeros_like(bonus)
    params = jnp.stack([bonus, gain, bias, jnp.exp(CHUNK * log_decay)] + [zero] * 4)
    return rows, columns, grow, shrink, tail, params


def segment_of(lengths, positions):
    rank = jnp.arange(lengths.shape[0])
    starts = jnp.sum(jnp.where(rank[:, None] > rank[None, :], lengths[None, :], 0), axis=1)
    later_flags = (positions[:, None] >= starts[None, 1:]).astype(jnp.int32)
    first_flags = jnp.any(positions[:, None] == starts[None, :], axis=1)
    return (jnp.sum(later_flags, axis=1), first_flags)


def rows_of(vec, *rows):
    return jnp.pad(jnp.stack([vec[i] for i in rows]), ((0, 8 - len(rows)), (0, 0)))


def shards(
    tokens, seq_lengths, out_grad, w_receptance, w_key, w_value, w_gate, w_output,
    ffn_key, ffn_receptance, ffn_value, vectors,
):
    seq, dp = lax.axis_size("seq"), lax.axis_size("dp")
    place = lax.axis_index("seq")
    here = jnp.reshape(place, (1,)).astype(jnp.int32)
    inputs_b, grad_b = tokens[0], out_grad[0]
    own_rows, width = inputs_b.shape
    length, part, unit = own_rows * seq, width // seq, vectors.shape[1]
    per, tile = own_rows // CHUNK, own_rows // 2
    hidden_width = ffn_key.shape[1] // seq
    groups = (seq, dp)
    within = groups if unit == HEAD else None

    vectors_b = jnp.pad(vectors, ((0, 16 - vectors.shape[0]), (0, 0)))

    def stacked_columns(weights, widths, beside=()):
        cut = cut_columns(weights, vectors_b, here, seq)
        *stacked, last = stack_rows(after(trade_seq(cut), beside), widths, vectors_b, here)
        return [w.reshape(-1, w.shape[-1]) for w in stacked] + [last], cut

    def gather_dp(rows):
        return lax.all_gather(rows, "dp", axis=0, tiled=True)

    def scatter_dp(grad):
        return lax.psum_scatter(grad, "dp", scatter_dimension=0, tiled=True)

    def owners_parts(summed):
        rows = summed.shape[0] // seq
        return trade_seq([lax.dynamic_slice_in_dim(summed, (place ^ j) * rows, rows, 0) for j in range(seq)])

    def owners_rows(summed, widths):
        return join_columns(owners_parts(summed), widths, here)

    def turn_pieces(pieces):
        if within is not None:
            return pieces
        return [outside(p, groups, unit) for p in pieces]

    positions = jnp.arange(length, dtype=jnp.int32)
    piece, first_flags = segment_of(seq_lengths[0], positions)

    (columns_in, columns_g, vec_seq), cut = stacked_columns(
        [w_receptance, w_key, w_value, w_gate], [3 * part, part]
    )
    tokens_held = held_back(inputs_b, here, *cut)
    full_in = gather_dp(columns_in)
    vec_parts = gather_small(vec_seq[None, :, : vectors.shape[0]], "dp").astype(F32)
    vec = vec_parts.transpose(2, 1, 0, 3).reshape(-1, width)
    turned = vec_parts.transpose(2, 0, 1, 3).reshape(-1, width)
    vec_own = lax.dynamic_slice_in_dim(vec, place * part, part, 1)
    log_decay = -jnp.exp(vec_own[6])
    tables = wkv_tables(
        piece, 1.0 - first_flags.astype(F32), log_decay, vec_own[7], vec_own[8], vec_own[9]
    )
    marks = tables[0]
    rows_one = rows_of(turned, 0, 1, 2, 3, 4, 5)
    tokens_all = gather_seq(tokens_held, (rows_one, tables))
    full_g = gather_dp(after(columns_g, tokens_all[1:3], rows_one))
    own_o = gather_dp(after(w_output, tokens_all))

    mix_r, mix_k, mix_v, mix_g, step = mixes(
        turn_pieces(tokens_all), marks, rows_one, 4, True, within, here, tile, own_rows // tile
    )
    recept, keyed, valued = (
        dot(m, full_in[:, i * part : (i + 1) * part], NN).astype(BF)
        for i, m in enumerate((mix_r, mix_k, mix_v))
    )
    projected = (recept, keyed, valued)
    ffn_weights = after([ffn_key, ffn_receptance], mix_r)
    if seq == 4:
        pieces_c = trade_seq(cut_with_rider(ffn_weights, grad_b, here))
    else:
        (columns_c, _), _ = stacked_columns(ffn_weights, [hidden_width + part], projected)
        grad_all = gather_seq(after(grad_b, mix_r), projected)
    wkv, states = wkv_forward(recept, keyed, valued, tables, here, per)
    gate_pre, mixed = gated(mix_g, full_g, wkv, tables[5], here, seq)
    if seq == 4:
        pieces_c = after(pieces_c, mixed)
        columns_c = stack_below(pieces_c, here)
    full_c = gather_dp(columns_c)
    full_ck, full_cr = full_c[:, :hidden_width], full_c[:, hidden_width:]
    full_cv = gather_dp(after(ffn_value, columns_c))
    attn = [dot(rows, own_o, NN).astype(BF) for rows in blocks_of(mixed, seq)]
    after_mix, normed_two = after_norm(inputs_b, scatter_seq(attn, here), rows_of(vec, 10, 11), here)

    normed_two = gather_seq(normed_two)
    if seq == 4:
        grad_all = gather_second(grad_b, *after(pieces_c[1:3], normed_two))
    mix_k2, mix_r2, step_two = mixes(
        turn_pieces(normed_two), marks, rows_of(turned, 10, 11, 12, 13), 2, False, within, here, tile,
        own_rows // tile,
    )
    recept_pre = dot(mix_r2, full_cr, NN)
    opened = gather_seq(after(jax.nn.sigmoid(recept_pre).astype(BF), grad_all[3:]))
    key_pre = dot(mix_k2, full_ck, NN)
    smooth = jax.nn.softplus(key_pre)
    hidden = (smooth * smooth).astype(BF)
    slope = (2.0 * smooth * jax.nn.sigmoid(key_pre)).astype(BF)
    hidden, slope = lax.optimization_barrier((hidden, slope))
    later = after(hidden, opened[1:3])
    value_parts = [columns_product(later if j < 2 else hidden, full_cv, part, j, here, seq) for j in reversed(range(seq))]
    value_parts = value_parts[::-1]
    value_relayed = scatter_relay(value_parts, scatter_start(value_parts), here)
    d_value = spread_columns(
        grad_all, by_block(after(opened, value_parts, value_relayed)), here, True, True, tile, own_rows // tile
    )

    grad_cv = dot(hidden, d_value, TN).astype(BF)
    summed_cv = scatter_dp(grad_cv)
    value_terms = scatter_end(value_parts[0], value_relayed)
    d_hidden = dot(after(d_value, grad_cv), full_cv, NT)
    d_key_two = (d_hidden * slope.astype(F32)).astype(BF)
    channel, d_recept_two = channel_out(value_terms, recept_pre, grad_all, here, tile)
    half, first = part // 2, hidden_width // (part // 2)
    grad_ck, grad_cr = [], []

    def beside_two(relayed):
        grad_ck.append(dot(after(mix_k2, relayed), d_key_two, TN).astype(BF))
        grad_cr.append(dot(after(mix_r2, relayed, grad_ck), d_recept_two, TN).astype(BF))
        return grad_ck, grad_cr

    terms_two, sums_two = mixes_back_scatter(
        [(0, d_key_two, 0, full_c, 0, hidden_width)]
        + [(1, d_recept_two, i, full_c, first + i, half) for i in range(2)],
        step_two, marks, rows_of(turned, 12, 13), here, seq, beside_two,
    )
    summed_ck, summed_cr = scatter_dp(grad_ck[0]), scatter_dp(grad_cr[0])
    if within is None:
        terms_two = [outside(t, groups, unit, back=True) for t in terms_two]
    d_after, d_attn, norm_sums_two = norm_back(terms_two, after_mix, grad_b, rows_of(vec, 10), within, here)

    pieces = gather_seq(d_attn)
    *near, far = by_block(pieces)
    near_mixed = [dot(d, own_o, NT).astype(BF) for d in near]
    *near_rows, far_rows = blocks_of(mixed, seq)
    near_wo = sum(dot(m, d, TN) for m, d in zip(near_rows, near))
    far = after(far, near_mixed, near_wo, summed_cv)
    d_mixed = jnp.concatenate([*near_mixed, dot(far, own_o, NT).astype(BF)], axis=0)
    grad_wo = (near_wo + dot(far_rows, far, TN)).astype(BF)
    summed_o = scatter_dp(grad_wo)
    d_mixed = after(d_mixed, summed_ck, grad_wo)
    d_recept, d_keyed, d_valued, d_gate, sums = wkv_backward(
        recept, keyed, valued, gate_pre, wkv, d_mixed, states, tables, here, per
    )
    channel = after(trade_seq(blocks_of(after(channel, d_mixed), seq)), d_recept)
    grads_vg = [
        dot(after(m, channel), d, TN).astype(BF) for m, d in ((mix_v, d_valued), (mix_g, d_gate))
    ]
    summed_vg = scatter_dp(jnp.concatenate(grads_vg, axis=1))
    grads_rk, others = [], []

    def beside(relayed):
        grads_rk.extend(
            dot(after(m, relayed), d, TN).astype(BF) for m, d in ((mix_r, d_recept), (mix_k, d_keyed))
        )
        others.append(spread_columns([after_mix], after(channel, relayed), here, False, False, CHUNK, per))
        others.append(after(summed_cv, relayed).astype(F32))
        return grads_rk, others

    d_recept, d_keyed = after((d_recept, d_keyed), grads_vg, summed_o)
    terms, sums_one = mixes_back_scatter(
        [(i, d, 0, full_in, i, part) for i, d in enumerate((d_recept, d_keyed, d_valued))]
        + [(3, d_gate, 0, full_g, 0, part)],
        step, marks, rows_of(turned, 2, 3, 4, 5), here, seq, beside,
    )
    summed_rk = scatter_dp(jnp.concatenate(grads_rk, axis=1))
    out_rows, sum_cv = others
    if within is None:
        terms = [outside(t, groups, unit, back=True) for t in terms]
    tokens_grad, _, norm_sums = norm_back(terms, inputs_b, d_after, rows_of(vec, 0), within, here)

    summed_c = jnp.concatenate(after([summed_ck, summed_cr], terms), axis=1)
    sum_ck, sum_cr = owners_rows(summed_c, [ffn_key.shape[1], width])
    sum_o = summed_o.astype(F32)
    sum_v, sum_g = owners_rows(summed_vg, [width] * 2)

    def by_device(rows, turn):
        if turn:
            return rows.reshape(-1, dp, seq, unit).transpose(1, 2, 0, 3)
        return rows.reshape(-1, seq, dp, unit).transpose(2, 1, 0, 3)

    own_sums = jnp.stack([sums[0] * log_decay, sums[1], sums[2], sums[3]])
    own_sums = lax.dynamic_update_slice(jnp.zeros((4, width), F32), own_sums, (0, place * part))
    vector_rows = jnp.concatenate(
        [
            by_device(norm_sums[:2], False), by_device(sums_one[:4], True), by_device(own_sums, False),
            by_device(norm_sums_two[:2], False), by_device(sums_two[:2], True),
        ],
        axis=2,
    )
    sum_vec = scatter_small(vector_rows.reshape((-1,) + vector_rows.shape[2:]))
    sum_r, sum_k = owners_rows(after(summed_rk, sum_ck, sum_v, sum_vec), [width] * 2)
    return (
        out_rows[None], tokens_grad[None], sum_r, sum_k, sum_v, sum_g, sum_o,
        sum_ck, sum_cr, sum_cv, sum_vec,
    )


def solution(mesh):
    tokens = P("dp", "seq", None)
    rows = P(("seq", "dp"), None)
    columns = P(None, ("seq", "dp"))
    return jax.shard_map(
        shards,
        mesh=mesh,
        in_specs=(tokens, P("dp", None), tokens) + (rows,) * 8 + (columns,),
        out_specs=(tokens, tokens) + (rows,) * 8 + (columns,),
        check_vma=False,
    )
```

```python
from functools import partial

import jax
import jax.numpy as jnp
from jax import lax
from jax.experimental import pallas as pl
from jax.experimental.pallas import tpu as pltpu
from jax.sharding import PartitionSpec as P

HEAD = 64
PAIR = 128
CHUNK = 128
EPSILON = 1e-05
GROUP_EPSILON = 1.0
BF = jnp.bfloat16
F32 = jnp.float32
NT = (((1,), (1,)), ((), ()))
TN = (((0,), (0,)), ((), ()))
NN = (((1,), (0,)), ((), ()))


def swap(value, axis, distance):
    size = lax.axis_size(axis)
    return lax.ppermute(value, axis, [(i, i ^ distance) for i in range(size)])


def after(value, *others):
    return lax.optimization_barrier((value, others))[0]


def gather_second(part, one, two):
    half = part.shape[0] // 2
    columns = part.shape[1]
    low, high = swap(one[:half, :columns], "seq", 2), swap(two[half : 2 * half, :columns], "seq", 1)
    return [part, one, two, low, high]


def gather_seq(part, first=()):
    size = lax.axis_size("seq")
    if size == 4:
        half = part.shape[0] // 2
        one, two = swap(part, "seq", 1), swap(part, "seq", 2)
        one, two = after((one, two), first)
        low, high = swap(one[:half], "seq", 2), swap(two[half:], "seq", 1)
        return [part, one, two, low, high]
    return [part] + [swap(part, "seq", distance) for distance in range(1, size)]


def by_block(pieces):
    if lax.axis_size("seq") == 4:
        return pieces[:3] + [jnp.concatenate(pieces[3:], axis=0)]
    return pieces


def scatter_start(parts):
    if lax.axis_size("seq") != 4:
        return ()
    low, high = parts[3:] if len(parts) == 5 else blocks_of(parts[3], 2)
    return swap(low, "seq", 1), swap(high, "seq", 2)


def relay_body(here, one_ref, two_ref, low_ref, high_ref, one_out, two_out):
    one, two = one_ref[...], two_ref[...]
    first = pl.program_id(0) == 0
    low, high = low_ref[...].astype(F32), high_ref[...].astype(F32)
    one_out[...] = jnp.where(first, one, (one.astype(F32) + high).astype(BF))
    two_out[...] = jnp.where(first, (two.astype(F32) + low).astype(BF), two)


def scatter_relay(parts, started, here):
    if lax.axis_size("seq") != 4:
        return parts[1:]
    (_, one, two, *_), (low, high) = parts, started
    (rows, width), half = one.shape, block(low.shape, lambda i, h: (i, 0))
    return kernel(
        relay_body, "relay", (2,), here,
        [(one, half), (two, half), (low, fixed(low.shape)), (high, fixed(low.shape))],
        [((rows, width), BF, half)] * 2,
    )


def scatter_end(own, relayed):
    return [own] + [swap(part, "seq", j + 1) for j, part in enumerate(relayed)]


def scatter_seq(parts, here):
    return scatter_end(parts[0], scatter_relay(parts, scatter_start(parts), here))


def trade_seq(parts):
    return [parts[0]] + [swap(part, "seq", j + 1) for j, part in enumerate(parts[1:])]


def blocks_of(values, size):
    rows = values.shape[0] // size
    return [values[j * rows : (j + 1) * rows] for j in range(size)]


def bits_of(size):
    return [1 << b for b in range(size.bit_length() - 1)]


def gather_small(part, axis):
    for bit in bits_of(lax.axis_size(axis)):
        other = swap(part, axis, bit)
        second = (lax.axis_index(axis) & bit) != 0
        part = jnp.concatenate([jnp.where(second, other, part), jnp.where(second, part, other)], axis=0)
    return part


def scatter_small(parts, between):
    for axis in ("dp", "seq"):
        parts = after(parts, between) if axis == "seq" else parts
        for bit in reversed(bits_of(lax.axis_size(axis))):
            half = parts.shape[0] // 2
            second = (lax.axis_index(axis) & bit) != 0
            low, high = parts[:half], parts[half:]
            parts = jnp.where(second, high, low) + swap(jnp.where(second, low, high), axis, bit)
    return parts[0]


def block(shape, index):
    return pl.BlockSpec(shape, lambda *i: index(*i[:-1], i[-1][0]))


def fixed(shape):
    return pl.BlockSpec(shape, lambda *i: (0,) * len(shape))


def relative(tile, per, here):
    return (lax.div(tile, per) ^ here) * per + lax.rem(tile, per)


def kernel(body, name, grid, here, ins, outs, scratch=(), vmem=48):
    return pl.pallas_call(
        body,
        out_shape=[jax.ShapeDtypeStruct(shape, kind) for shape, kind, _ in outs],
        grid_spec=pltpu.PrefetchScalarGridSpec(
            num_scalar_prefetch=1,
            grid=grid,
            in_specs=[spec for _, spec in ins],
            out_specs=[spec for _, _, spec in outs],
            scratch_shapes=list(scratch),
        ),
        compiler_params=pltpu.CompilerParams(vmem_limit_bytes=vmem * 2**20),
        name=name,
    )(here, *[array for array, _ in ins])


def pieced(pieces, tile, columns, column, place):
    ins, start = [], 0
    for piece in pieces:
        count = piece.shape[0] // tile

        def index(i, h, start=start, count=count):
            return jnp.clip(place(i, h) - start, 0, count - 1), column(h)

        ins.append((piece, block((tile, columns), index)))
        start += count
    return ins


def picked(refs, counts, tile, held):
    start = 0
    for ref, count in zip(refs, counts):

        @pl.when((tile >= start) & (tile < start + count))
        def _(ref=ref):
            held[...] = ref[...]

        start += count
    return held[...].astype(F32)


def counts_of(pieces, tile):
    return [piece.shape[0] // tile for piece in pieces]


def row_index(rows):
    return lax.broadcasted_iota(jnp.int32, (rows, 1), 0)


def placed(place, width):
    return pl.ds(pl.multiple_of(place * width, width), width)


def cut_body(count, parts, here, *refs):
    ins, beside, outs = refs[:count], refs[count], refs[count + 1 :]
    rows = ins[0].shape[0]
    for j in range(parts):
        outs[j][rows:, :] = jnp.zeros_like(outs[j][rows:, :])
        outs[j][rows:, : beside.shape[1]] = beside[...]
    at = 0
    for ref in ins:
        width = ref.shape[1] // parts
        for j in range(parts):
            outs[j][:rows, at : at + width] = ref[:, placed(here[0] ^ j, width)]
        at += width


def cut_columns(weights, beside, here, parts):
    rows, width = weights[0].shape[0] + beside.shape[0], sum(w.shape[1] for w in weights) // parts
    return kernel(
        partial(cut_body, len(weights), parts), "cut_columns", (1,), here,
        [(w, fixed(w.shape)) for w in [*weights, beside]],
        [((rows, width), BF, fixed((rows, width)))] * parts,
    )


def stack_body(parts, here, *refs):
    start = 0
    outs, beside = refs[parts:-1], refs[-1]
    for out in outs:
        for j in range(parts):
            out[here[0] ^ j] = refs[j][: out.shape[1], start : start + out.shape[2]]
        start += out.shape[2]
    for j in range(parts):
        beside[here[0] ^ j] = refs[j][out.shape[1] :, : beside.shape[2]]


def stack_rows(pieces, widths, beside, here):
    parts, rows = len(pieces), pieces[0].shape[0] - beside.shape[0]
    shapes = [(parts, rows, width) for width in widths] + [(parts,) + beside.shape]
    return kernel(
        partial(stack_body, parts), "stack_rows", (1,), here,
        [(p, fixed(p.shape)) for p in pieces],
        [(shape, BF, fixed(shape)) for shape in shapes],
    )


def ride_body(count, here, *refs):
    ins, rider, outs = refs[:count], refs[count], refs[count + 1 :]
    for j, out in enumerate(outs):
        top, at = 0, 0
        if j in (1, 2):
            top = rider.shape[0]
            out[:top, : rider.shape[1]] = rider[...]
            out[:top, rider.shape[1] :] = jnp.zeros_like(out[:top, rider.shape[1] :])
        for ref in ins:
            width = ref.shape[1] // 4
            out[top:, at : at + width] = ref[:, placed(here[0] ^ j, width)]
            at += width


def cut_with_rider(weights, rider, here):
    rows, width = weights[0].shape[0], sum(w.shape[1] for w in weights) // 4
    return kernel(
        partial(ride_body, len(weights)), "cut_columns", (1,), here,
        [(w, fixed(w.shape)) for w in [*weights, rider]],
        [((n, width), BF, fixed((n, width))) for n in (rows, rows + rider.shape[0], rows + rider.shape[0], rows)],
    )


def unride_body(here, *refs):
    out = refs[-1]
    rows = out.shape[1]
    for j, ref in enumerate(refs[:-1]):
        out[here[0] ^ j] = ref[ref.shape[0] - rows :, :]


def stack_below(pieces, here):
    shape = (4,) + pieces[0].shape
    (stacked,) = kernel(
        unride_body, "stack_rows", (1,), here,
        [(p, fixed(p.shape)) for p in pieces],
        [(shape, BF, fixed(shape))],
    )
    return stacked.reshape(-1, shape[-1])


def hold_body(here, in_ref, *refs):
    refs[-1][...] = in_ref[...]


def held_back(values, here, *others):
    rows, width = values.shape
    own = block((rows // 2, width), lambda i, h: (i, 0))
    (copy,) = kernel(
        hold_body, "hold", (2,), here,
        [(values, own)] + [(o, pl.BlockSpec(memory_space=pl.ANY)) for o in others],
        [((rows, width), values.dtype, own)],
    )
    return copy


def join_body(parts, count, here, *refs):
    ins, outs = refs[:parts], refs[parts:]
    at = 0
    for ref in outs:
        width = ref.shape[1] // parts
        for j in range(parts):
            ref[:, placed(here[0] ^ j, width)] = ins[j][:, at : at + width].astype(F32)
        at += width


def join_columns(pieces, widths, here):
    parts, rows = len(pieces), pieces[0].shape[0]
    return kernel(
        partial(join_body, parts, len(widths)), "join_columns", (1,), here,
        [(p, fixed(p.shape)) for p in pieces],
        [((rows, width), F32, fixed((rows, width))) for width in widths],
    )


def spread_body(counts, parts, product, here, *refs):
    bases, pieces, out, held = refs[: len(counts)], refs[len(counts) : -2], refs[-2], refs[-1]
    picked(bases, counts, pl.program_id(0), held)
    width = pieces[0].shape[1]
    for j in range(parts):
        at = placed(here[0] ^ j, width)
        piece, base = pieces[j][...].astype(F32), held[:, at].astype(F32)
        out[:, at] = (base * piece if product else base + piece).astype(BF)


def spread_columns(bases, columns, here, product, turn, tile, per):
    rows, width = sum(counts_of(bases, tile)) * tile, bases[0].shape[1]

    def turned(i, j):
        return (lax.div(i, per) ^ j) * per + lax.rem(i, per) if turn else i

    (result,) = kernel(
        partial(spread_body, counts_of(bases, tile), len(columns), product), "spread_columns", (rows // tile,), here,
        pieced(bases, tile, width, lambda h: 0, lambda i, h: i)
        + [(c, block((tile, c.shape[1]), lambda i, h, j=j: (turned(i, j), 0))) for j, c in enumerate(columns)],
        [((rows, width), BF, block((tile, width), lambda i, h: (i, 0)))],
        [pltpu.VMEM((tile, width), bases[0].dtype)],
    )
    return result


def shuffled(values, groups, back=False):
    seq, dp = groups
    if back:
        seq, dp = dp, seq
    lane = lax.broadcasted_iota(jnp.int32, (1, PAIR), 1) < HEAD
    source = [s * dp + d for d in range(dp) for s in range(seq)]
    columns = []
    for one, two in zip(source[::2], source[1::2]):
        low = values[:, one // 2 * PAIR : (one // 2 + 1) * PAIR]
        high = values[:, two // 2 * PAIR : (two // 2 + 1) * PAIR]
        low = pltpu.roll(low, HEAD, 1) if one % 2 else low
        high = high if two % 2 else pltpu.roll(high, HEAD, 1)
        columns.append(jnp.where(lane, low, high))
    return jnp.concatenate(columns, axis=1)


def outside(values, groups, channels, back=False):
    seq, dp = groups[::-1] if back else groups
    return values.reshape(-1, seq, dp, channels).swapaxes(1, 2).reshape(values.shape)


def centre(values):
    centred = values - jnp.mean(values, axis=-1, keepdims=True)
    spread = jnp.mean(centred * centred, axis=-1, keepdims=True)
    return centred, lax.rsqrt(spread + EPSILON)


def mix_body(count, norm, groups, counts, per, here, *refs):
    pieces, (marks_ref, vec_ref) = refs[: len(counts)], refs[len(counts) : len(counts) + 2]
    outs, last, held = refs[len(counts) + 2 : -2], refs[-2], refs[-1]

    @pl.when(pl.program_id(0) == 0)
    def _():
        last[...] = jnp.zeros_like(last)

    values = picked(pieces, counts, relative(pl.program_id(0), per, here[0]), held)
    if norm:
        centred, inverse = centre(values)
        values = centred * inverse
    if groups:
        values = shuffled(values, groups)
    if norm:
        values = values * vec_ref[0:1, :] + vec_ref[1:2, :]
    rows = values.shape[0]
    previous = jnp.where(row_index(rows) == 0, last[0:1, :], pltpu.roll(values, 1, 0)) * marks_ref[:, 3:4]
    last[0:1, :] = values[rows - 1 :, :]
    step = values - previous
    outs[count][...] = step.astype(BF)
    for i in range(count):
        outs[i][...] = (previous + step * vec_ref[2 + i : 3 + i, :]).astype(BF)


def mixes(pieces, marks, vec, count, norm, groups, here, tile, per):
    rows, width = marks.shape[0], pieces[0].shape[1]
    own = block((tile, width), lambda i, h: (relative(i, per, h), 0))
    return kernel(
        partial(mix_body, count, norm, groups, counts_of(pieces, tile), per), "mixes", (rows // tile,), here,
        pieced(pieces, tile, width, lambda h: 0, lambda i, h: relative(i, per, h))
        + [(marks, block((tile, PAIR), lambda i, h: (i, 0))), (vec, fixed(vec.shape))],
        [((rows, width), BF, own)] * (count + 1),
        [pltpu.VMEM((8, width), F32), pltpu.VMEM((tile, width), BF)],
    )


def mixes_back_body(which, first, seq, outs, here, *refs):
    count = len(which)
    grads, nexts, weights = refs[:count], refs[count : 2 * count], refs[2 * count : 3 * count]
    step_ref, marks_ref, next_marks_ref, vec_ref, *out_refs, sums_ref = refs[3 * count :]

    @pl.when(pl.program_id(1) == 0)
    def _():
        sums_ref[...] = jnp.zeros_like(sums_ref)

    step = step_ref[...].astype(F32)
    rows = step.shape[0]
    total = straight = None
    for i in range(which[-1] + 1):
        grad = sum(
            dot(jnp.concatenate([grads[k][...], nexts[k][...]], axis=0), weights[k][...], NT)
            for k in range(count)
            if which[k] == i
        )
        sums_ref[i : i + 1, :] += jnp.sum(grad[:rows] * step, axis=0, keepdims=True)
        part = grad * vec_ref[i : i + 1, :]
        total, straight = (total + grad, straight + part) if i else (grad, part)
    inside = ((first + pl.program_id(1)) ^ here[0]) < seq - 1
    keep = jnp.concatenate([marks_ref[:, 3:4], jnp.where(inside, next_marks_ref[:, 3:4], 0.0)], axis=0)
    kept = (total - straight) * keep
    up = pltpu.roll(kept, kept.shape[0] - 1, 0)
    result = (straight[:rows] + up[:rows]).astype(BF)
    if len(out_refs) == 1:
        out_refs[0][...] = result
        return
    if outs == 1:
        out_refs[0][...] = result[: rows // 2]
        out_refs[1][...] = result[rows // 2 :]
        return
    for k, out_ref in enumerate(out_refs):

        @pl.when(pl.program_id(1) == k)
        def _(out_ref=out_ref):
            out_ref[...] = result


EXTRA = 16


def mixes_back(terms, step, marks, vec, here, seq, first, count, halves=False):
    rows, width = step.shape
    tile, columns = rows // seq, min(512, width)
    extras = tile // EXTRA

    def following(i, h):
        return jnp.minimum(((first + i) ^ h) + 1, seq - 1)

    ins = [(g, block((tile, n), lambda c, i, h, at=at: (first + i, at))) for _, g, at, _, _, n in terms]
    ins += [
        (g, block((EXTRA, n), lambda c, i, h, at=at: ((following(i, h) ^ h) * extras, at)))
        for _, g, at, _, _, n in terms
    ]
    ins += [(w, block((columns, n), lambda c, i, h, at=at: (c, at))) for _, _, _, w, at, n in terms]
    ins += [
        (step, block((tile, columns), lambda c, i, h: (first + i, c))),
        (marks, block((tile, PAIR), lambda c, i, h: ((first + i) ^ h, 0))),
        (marks, block((EXTRA, PAIR), lambda c, i, h: (following(i, h) * extras, 0))),
        (vec, block((8, columns), lambda c, i, h: (0, c))),
    ]
    size = tile // 2 if halves else tile
    *parts, sums = kernel(
        partial(mixes_back_body, [t[0] for t in terms], first, seq, count), "mixes_back", (width // columns, count), here, ins,
        [((size, width), BF, block((size, columns), lambda c, i, h: (0, c)))] * (2 if halves else count)
        + [((8, width), F32, block((8, columns), lambda c, i, h: (0, c)))],
    )
    return parts, sums


def mixes_back_scatter(terms, step, marks, vec, here, seq, beside):
    if seq != 4:
        parts, sums = mixes_back(terms, step, marks, vec, here, seq, 0, seq)
        return after(scatter_seq(parts, here), beside(parts)), sums

    def call(first, count, *before):
        ordered = after([t[1] for t in terms], *before)
        return mixes_back(
            [(t[0], g) + t[2:] for t, g in zip(terms, ordered)], step, marks, vec, here, seq, first, count, first == 3
        )

    far, sums_far = call(3, 1)
    near, sums_near = call(1, 2, far)
    parts = [None, *near, *far]
    started = after(scatter_start(parts), near)
    relayed = scatter_relay(parts, started, here)
    (own,), sums_own = call(0, 1, near, relayed)
    return after(scatter_end(own, relayed), beside(relayed)), sums_far + sums_near + sums_own


def after_body(count, here, x_ref, vec_ref, *refs):
    after_ref, normed_ref = refs[count:]
    after = x_ref[...].astype(F32)
    for ref in refs[:count]:
        after = after + ref[...].astype(F32)
    after_ref[...] = after
    centred, inverse = centre(after)
    normed_ref[...] = (centred * inverse * vec_ref[0:1, :] + vec_ref[1:2, :]).astype(BF)


def after_norm(inputs, terms, vec, here):
    rows, width = inputs.shape
    own = block((CHUNK, width), lambda i, h: (i, 0))
    return kernel(
        partial(after_body, len(terms)), "after_norm", (rows // CHUNK,), here,
        [(inputs, own), (vec, fixed(vec.shape))] + [(t, own) for t in terms],
        [((rows, width), F32, own), ((rows, width), BF, own)],
    )


def norm_back_body(count, groups, here, x_ref, base_ref, vec_ref, *refs):
    wide_ref, narrow_ref, sums_ref = refs[count:]

    @pl.when(pl.program_id(0) == 0)
    def _():
        sums_ref[...] = jnp.zeros_like(sums_ref)

    grad = refs[0][...].astype(F32)
    for ref in refs[1:count]:
        grad = grad + ref[...].astype(F32)
    if groups:
        grad = shuffled(grad, groups, back=True)
    centred, inverse = centre(x_ref[...].astype(F32))
    normed = centred * inverse
    sums_ref[0:1, :] += jnp.sum(grad * normed, axis=0, keepdims=True)
    sums_ref[1:2, :] += jnp.sum(grad, axis=0, keepdims=True)
    grad = grad * vec_ref[0:1, :]
    grad = grad - jnp.mean(grad, axis=-1, keepdims=True) - normed * jnp.mean(grad * normed, axis=-1, keepdims=True)
    result = base_ref[...].astype(F32) + inverse * grad
    wide_ref[...] = result
    narrow_ref[...] = result.astype(BF)


def norm_back(terms, inputs, base, vec, groups, here):
    rows, width = inputs.shape
    own = block((CHUNK, width), lambda i, h: (i, 0))
    return kernel(
        partial(norm_back_body, len(terms), groups), "norm_back", (rows // CHUNK,), here,
        [(inputs, own), (base, own), (vec, fixed(vec.shape))] + [(t, own) for t in terms],
        [((rows, width), F32, own), ((rows, width), BF, own), ((8, width), F32, fixed((8, width)))],
    )


def gate_body(mix_ref, weight_ref, wkv_ref, par_ref, gate_ref, mixed_ref):
    gate = dot(mix_ref[...], weight_ref[...], NN)
    gate_ref[...] = gate
    ones = jnp.where(same_head(), 1.0, 0.0).astype(BF)
    for pair in range(gate.shape[1] // PAIR):
        at = slice(pair * PAIR, (pair + 1) * PAIR)
        wkv = wkv_ref[:, at]
        centred = wkv - head_sum_fine(wkv, ones) * (1.0 / HEAD)
        spread = head_sum(centred * centred, ones) * (1.0 / HEAD)
        normed = centred * lax.rsqrt(spread + GROUP_EPSILON) * par_ref[1:2, at] + par_ref[2:3, at]
        mixed_ref[:, at] = (normed * (gate[:, at] / (1.0 + jnp.exp(-gate[:, at])))).astype(BF)


def gated(mix_g, weights, wkv, params, here, seq):
    rows, width = mix_g.shape
    tile, part = rows // seq, wkv.shape[1]
    own = block((tile, part), lambda i, h: (i, 0))
    return kernel(
        lambda here, *refs: gate_body(*refs), "gate", (seq,), here,
        [
            (mix_g, block((tile, width), lambda i, h: (i, 0))),
            (weights, block((width, part), lambda i, h: (0, 0))),
            (wkv, own),
            (params, fixed(params.shape)),
        ],
        [((rows, part), F32, own), ((rows, part), BF, own)],
    )


def columns_body(here, left_ref, right_ref, out_ref):
    out_ref[...] = dot(left_ref[...], right_ref[...], NN).astype(BF)


def columns_product(left, right, part, relative_to, here, seq):
    rows, depth = left.shape
    tile = rows // seq
    (result,) = kernel(
        columns_body, "value_columns", (seq,), here,
        [
            (left, block((tile, depth), lambda i, h: (i, 0))),
            (right, block((depth, part), lambda i, h: (0, h ^ relative_to))),
        ],
        [((rows, part), BF, block((tile, part), lambda i, h: (i ^ relative_to, 0)))],
    )
    return result


def channel_body(counts, here, pre_ref, *refs):
    grads, terms, (channel_ref, d_recept_ref, held) = refs[: len(counts)], refs[len(counts) : -3], refs[-3:]
    value = sum(ref[...].astype(F32) for ref in terms)
    opened = 1.0 / (1.0 + jnp.exp(-pre_ref[...]))
    channel = opened * value
    channel_ref[...] = channel.astype(BF)
    grad = picked(grads, counts, pl.program_id(0), held)
    d_recept_ref[...] = (grad * channel * (1.0 - opened)).astype(BF)


def channel_out(terms, pre, grads, here, tile):
    rows, part = pre.shape
    own = block((tile, part), lambda i, h: (i, 0))
    return kernel(
        partial(channel_body, counts_of(grads, tile)), "channel", (rows // tile,), here,
        [(pre, own)] + pieced(grads, tile, part, lambda h: h, lambda i, h: i) + [(t, own) for t in terms],
        [((rows, part), BF, own)] * 2,
        [pltpu.VMEM((tile, part), BF)],
    )


def head_masks():
    lane = lax.broadcasted_iota(jnp.int32, (1, PAIR), 1)
    first = (lane < HEAD).astype(F32)
    return first, 1.0 - first


def same_head():
    row = lax.broadcasted_iota(jnp.int32, (PAIR, PAIR), 0) < HEAD
    column = lax.broadcasted_iota(jnp.int32, (PAIR, PAIR), 1) < HEAD
    return row == column


def dot(left, right, dims):
    return lax.dot_general(left, right, dims, preferred_element_type=F32)


def head_sum(values, ones):
    return dot(values.astype(BF), ones, NN)


def head_sum_fine(values, ones):
    coarse = values.astype(BF)
    rest = (values - coarse.astype(F32)).astype(BF)
    return dot(coarse, ones, NN) + dot(rest, ones, NN)


def stacked(values, first, second):
    return jnp.concatenate([(values * first).astype(BF), (values * second).astype(BF)], axis=0)


def masks_of(rows_ref, columns_ref):
    segment = rows_ref[:, 0:1]
    reaches = rows_ref[:, 1:2]
    last_same = rows_ref[:, 2:3]
    reach_last = rows_ref[CHUNK - 1 : CHUNK, 1:2]
    before = lax.broadcasted_iota(jnp.int32, (CHUNK, CHUNK), 1) < lax.broadcasted_iota(
        jnp.int32, (CHUNK, CHUNK), 0
    )
    allowed = jnp.where((segment == columns_ref[0:1, :]) & before, 1.0, 0.0)
    return reaches, last_same, reach_last, jnp.concatenate([allowed, allowed], axis=0)


def wkv_forward_body(
    here, r_ref, k_ref, v_ref, rows_ref, columns_ref, grow_ref, shrink_ref, tail_ref, par_ref,
    wkv_ref, states_ref, state,
):
    @pl.when(pl.program_id(0) == 0)
    def _():
        state[...] = jnp.zeros_like(state)

    first, second = head_masks()
    block = same_head()
    ones = jnp.where(block, 1.0, 0.0).astype(BF)
    reaches, last_same, reach_last, allowed = masks_of(rows_ref, columns_ref)
    for pair in range(r_ref.shape[1] // PAIR):
        at = slice(pair * PAIR, (pair + 1) * PAIR)
        r, k, v = r_ref[:, at].astype(F32), k_ref[:, at].astype(F32), v_ref[:, at].astype(F32)
        bonus, decay = par_ref[0:1, at], par_ref[3:4, at]
        held = state[at, :]
        held_b = held.astype(BF)
        states_ref[0, at, :] = held_b
        grown = r * grow_ref[:, at]
        shrunk = (k * shrink_ref[:, at]).astype(BF)
        scores = (dot(stacked(grown, first, second), shrunk, NT) * allowed).astype(BF)
        both = jnp.concatenate([scores[:CHUNK], scores[CHUNK:]], axis=1)
        wkv = dot(both, stacked(v, first, second), NN)
        wkv = wkv + dot((grown * reaches).astype(BF), held_b, NT)
        wkv = wkv + head_sum(r * bonus * k, ones) * v
        fresh = dot(v_ref[:, at], (k * tail_ref[:, at] * last_same).astype(BF), TN)
        state[at, :] = held * (decay * reach_last) + jnp.where(block, fresh, 0.0)
        wkv_ref[:, at] = wkv


def wkv_backward_body(
    here, r_ref, k_ref, v_ref, d_wkv_ref, states_ref,
    rows_ref, columns_ref, grow_ref, shrink_ref, tail_ref, par_ref,
    d_r_ref, d_k_ref, d_v_ref, sums_ref, d_state,
):
    @pl.when(pl.program_id(0) == 0)
    def _():
        d_state[...] = jnp.zeros_like(d_state)
        sums_ref[...] = jnp.zeros_like(sums_ref)

    first, second = head_masks()
    block = same_head()
    ones = jnp.where(block, 1.0, 0.0).astype(BF)
    reaches, last_same, reach_last, allowed = masks_of(rows_ref, columns_ref)
    offset = lax.broadcasted_iota(jnp.int32, (CHUNK, PAIR), 0).astype(F32)
    for pair in range(r_ref.shape[1] // PAIR):
        at = slice(pair * PAIR, (pair + 1) * PAIR)
        bonus, decay = par_ref[0:1, at], par_ref[3:4, at]
        d_wkv = d_wkv_ref[:, at].astype(F32)
        r, k, v = r_ref[:, at].astype(F32), k_ref[:, at].astype(F32), v_ref[:, at].astype(F32)
        v_b, d_wkv_b = v_ref[:, at], d_wkv_ref[:, at]
        grow, shrink, tail = grow_ref[:, at], shrink_ref[:, at], tail_ref[:, at] * last_same
        held = states_ref[0, at, :]
        later = d_state[at, :]
        later_b = later.astype(BF)
        grown = r * grow
        shrunk = k * shrink
        shrunk_b = shrunk.astype(BF)
        tailed_b = (k * tail).astype(BF)
        grown_two = stacked(grown, first, second)
        d_wkv_two = stacked(d_wkv, first, second)
        scores = (dot(grown_two, shrunk_b, NT) * allowed).astype(BF)
        d_scores = (dot(d_wkv_two, v_b, NT) * allowed).astype(BF)
        d_both = jnp.concatenate([d_scores[:CHUNK], d_scores[CHUNK:]], axis=1)
        d_grown = dot(d_both, stacked(shrunk, first, second), NN)
        d_grown = d_grown + dot((d_wkv * reaches).astype(BF), held, NN)
        d_shrunk = dot(d_scores, grown_two, TN)
        d_tailed = dot(v_b, later_b, NN)
        share = head_sum(r * bonus * k, ones)
        d_share = head_sum(d_wkv * v, ones)
        d_v = dot(scores, d_wkv_two, TN) + dot(tailed_b, later_b, NT) + share * d_wkv
        d_r_ref[:, at] = (d_grown * grow + d_share * bonus * k).astype(BF)
        d_k_ref[:, at] = (d_shrunk * shrink + d_tailed * tail + d_share * bonus * r).astype(BF)
        d_v_ref[:, at] = d_v.astype(BF)
        carried = decay * reach_last
        d_fresh = dot(d_wkv_b, (grown * reaches).astype(BF), TN)
        d_state[at, :] = later * carried + jnp.where(block, d_fresh, 0.0)
        grown_b = grown.astype(BF).astype(F32)
        d_log = (
            offset * grown_b * d_grown
            - (offset + 1.0) * shrunk_b.astype(F32) * d_shrunk
            + (CHUNK - 1.0 - offset) * tailed_b.astype(F32) * d_tailed
        )
        kept = CHUNK * carried * jnp.sum(held.astype(F32) * later, axis=0, keepdims=True)
        sums_ref[0:1, at] += jnp.sum(d_log, axis=0, keepdims=True) + kept
        sums_ref[1:2, at] += jnp.sum(d_share * r * k, axis=0, keepdims=True)


def gate_backward_body(here, wkv_ref, g_ref, d_mixed_ref, par_ref, d_wkv_ref, d_g_ref, sums_ref):
    @pl.when(pl.program_id(0) == 0)
    def _():
        sums_ref[...] = jnp.zeros_like(sums_ref)

    ones = jnp.where(same_head(), 1.0, 0.0).astype(BF)
    for pair in range(wkv_ref.shape[1] // PAIR):
        at = slice(pair * PAIR, (pair + 1) * PAIR)
        gain, bias = par_ref[1:2, at], par_ref[2:3, at]
        wkv, gate, d_mixed = wkv_ref[:, at], g_ref[:, at], d_mixed_ref[:, at].astype(F32)
        centred = wkv - head_sum_fine(wkv, ones) * (1.0 / HEAD)
        spread = head_sum(centred * centred, ones) * (1.0 / HEAD)
        inverse = lax.rsqrt(spread + GROUP_EPSILON)
        normed = centred * inverse
        opened = 1.0 / (1.0 + jnp.exp(-gate))
        d_scaled = d_mixed * gate * opened
        d_g = d_mixed * (normed * gain + bias) * opened * (1.0 + gate * (1.0 - opened))
        d_g_ref[:, at] = d_g.astype(BF)
        d_normed = d_scaled * gain
        mean_one = head_sum(d_normed, ones) * (1.0 / HEAD)
        mean_two = head_sum(d_normed * normed, ones) * (1.0 / HEAD)
        d_wkv_ref[:, at] = (inverse * (d_normed - mean_one - normed * mean_two)).astype(BF)
        sums_ref[0:1, at] += jnp.sum(d_scaled * normed, axis=0, keepdims=True)
        sums_ref[1:2, at] += jnp.sum(d_scaled, axis=0, keepdims=True)


def gate_backward(wkv, gate, d_mixed, params, here):
    rows, part = wkv.shape
    own = block((2 * CHUNK, part), lambda i, h: (i, 0))
    return kernel(
        gate_backward_body, "gate_backward", (rows // (2 * CHUNK),), here,
        [(a, own) for a in (wkv, gate, d_mixed)] + [(params, fixed(params.shape))],
        [((rows, part), BF, own)] * 2 + [((8, part), F32, fixed((8, part)))],
    )


def wkv_blocks(width, chunks, per, backward):
    def chunk(i):
        return chunks - 1 - i if backward else i

    tokens = block((CHUNK, width), lambda i, h: (relative(chunk(i), per, h), 0))
    states = block((1, width, PAIR), lambda i, h: (chunk(i), 0, 0))
    tables = [
        block((CHUNK, PAIR), lambda i, h: (chunk(i), 0)),
        block((8, CHUNK), lambda i, h: (0, chunk(i))),
    ]
    return tokens, states, tables + [fixed((CHUNK, width))] * 3 + [fixed((8, width))]


def wkv_forward(r, k, v, tables, here, per):
    length, width = r.shape
    chunks = length // CHUNK
    tokens, states, blocks = wkv_blocks(width, chunks, per, False)
    return kernel(
        wkv_forward_body, "wkv_forward", (chunks,), here,
        [(a, tokens) for a in (r, k, v)] + list(zip(tables, blocks)),
        [((length, width), F32, tokens), ((chunks, width, PAIR), BF, states)],
        [pltpu.VMEM((width, PAIR), F32)],
    )


def wkv_backward(r, k, v, d_wkv, states_kept, tables, here, per):
    length, width = r.shape
    chunks = length // CHUNK
    tokens, states, blocks = wkv_blocks(width, chunks, per, True)
    return kernel(
        wkv_backward_body, "wkv_backward", (chunks,), here,
        [(a, tokens) for a in (r, k, v, d_wkv)] + [(states_kept, states)] + list(zip(tables, blocks)),
        [((length, width), BF, tokens)] * 3 + [((8, width), F32, fixed((8, width)))],
        [pltpu.VMEM((width, PAIR), F32)],
    )


def wkv_tables(piece, keep, log_decay, bonus, gain, bias):
    length = piece.shape[0]
    by_chunk = piece.reshape(length // CHUNK, CHUNK)
    before = jnp.concatenate([jnp.full((1,), -1, piece.dtype), by_chunk[:-1, -1]])
    reaches = (by_chunk == before[:, None]).reshape(-1)
    last_same = (by_chunk == by_chunk[:, -1:]).reshape(-1)
    marks = jnp.stack([piece.astype(F32), reaches.astype(F32), last_same.astype(F32), keep], axis=1)
    rows = jnp.pad(marks, ((0, 0), (0, PAIR - 4)))
    columns = jnp.broadcast_to(piece.astype(F32)[None], (8, length))
    offset = jnp.arange(CHUNK).astype(F32)[:, None]
    grow = jnp.exp(offset * log_decay)
    shrink = jnp.exp(-(offset + 1.0) * log_decay)
    tail = jnp.exp((CHUNK - 1.0 - offset) * log_decay)
    zero = jnp.zeros_like(bonus)
    params = jnp.stack([bonus, gain, bias, jnp.exp(CHUNK * log_decay)] + [zero] * 4)
    return rows, columns, grow, shrink, tail, params


def segment_of(lengths, positions):
    rank = jnp.arange(lengths.shape[0])
    starts = jnp.sum(jnp.where(rank[:, None] > rank[None, :], lengths[None, :], 0), axis=1)
    later_flags = (positions[:, None] >= starts[None, 1:]).astype(jnp.int32)
    first_flags = jnp.any(positions[:, None] == starts[None, :], axis=1)
    return (jnp.sum(later_flags, axis=1), first_flags)


def rows_of(vec, *rows):
    return jnp.pad(jnp.stack([vec[i] for i in rows]), ((0, 8 - len(rows)), (0, 0)))


def shards(
    tokens, seq_lengths, out_grad, w_receptance, w_key, w_value, w_gate, w_output,
    ffn_key, ffn_receptance, ffn_value, vectors,
):
    seq, dp = lax.axis_size("seq"), lax.axis_size("dp")
    place = lax.axis_index("seq")
    here = jnp.reshape(place, (1,)).astype(jnp.int32)
    inputs_b, grad_b = tokens[0], out_grad[0]
    own_rows, width = inputs_b.shape
    length, part, unit = own_rows * seq, width // seq, vectors.shape[1]
    per, tile = own_rows // CHUNK, own_rows // 2
    hidden_width = ffn_key.shape[1] // seq
    groups = (seq, dp)
    within = groups if unit == HEAD else None

    vectors_b = jnp.pad(vectors, ((0, 16 - vectors.shape[0]), (0, 0)))

    def stacked_columns(weights, widths, beside=()):
        cut = cut_columns(weights, vectors_b, here, seq)
        *stacked, last = stack_rows(after(trade_seq(cut), beside), widths, vectors_b, here)
        return [w.reshape(-1, w.shape[-1]) for w in stacked] + [last], cut

    def gather_dp(rows):
        return lax.all_gather(rows, "dp", axis=0, tiled=True)

    def scatter_dp(grad):
        return lax.psum_scatter(grad, "dp", scatter_dimension=0, tiled=True)

    def owners_parts(summed):
        rows = summed.shape[0] // seq
        return trade_seq([lax.dynamic_slice_in_dim(summed, (place ^ j) * rows, rows, 0) for j in range(seq)])

    def owners_rows(summed, widths):
        return join_columns(owners_parts(summed), widths, here)

    def turn_pieces(pieces):
        if within is not None:
            return pieces
        return [outside(p, groups, unit) for p in pieces]

    positions = jnp.arange(length, dtype=jnp.int32)
    piece, first_flags = segment_of(seq_lengths[0], positions)

    (columns_in, columns_g, vec_seq), cut = stacked_columns(
        [w_receptance, w_key, w_value, w_gate], [3 * part, part]
    )
    tokens_held = held_back(inputs_b, here, *cut)
    full_in = gather_dp(columns_in)
    vec_parts = gather_small(vec_seq[None, :, : vectors.shape[0]], "dp").astype(F32)
    vec = vec_parts.transpose(2, 1, 0, 3).reshape(-1, width)
    turned = vec_parts.transpose(2, 0, 1, 3).reshape(-1, width)
    vec_own = lax.dynamic_slice_in_dim(vec, place * part, part, 1)
    log_decay = -jnp.exp(vec_own[6])
    tables = wkv_tables(
        piece, 1.0 - first_flags.astype(F32), log_decay, vec_own[7], vec_own[8], vec_own[9]
    )
    marks = tables[0]
    rows_one = rows_of(turned, 0, 1, 2, 3, 4, 5)
    tokens_all = gather_seq(tokens_held, (rows_one, tables))
    full_g = gather_dp(after(columns_g, tokens_all[1:3], rows_one))
    own_o = gather_dp(after(w_output, tokens_all))

    mix_r, mix_k, mix_v, mix_g, step = mixes(
        turn_pieces(tokens_all), marks, rows_one, 4, True, within, here, tile, own_rows // tile
    )
    recept, keyed, valued = (
        dot(m, full_in[:, i * part : (i + 1) * part], NN).astype(BF)
        for i, m in enumerate((mix_r, mix_k, mix_v))
    )
    projected = (recept, keyed, valued)
    ffn_weights = after([ffn_key, ffn_receptance], mix_r)
    if seq == 4:
        pieces_c = trade_seq(cut_with_rider(ffn_weights, grad_b, here))
    else:
        (columns_c, _), _ = stacked_columns(ffn_weights, [hidden_width + part], projected)
        grad_all = gather_seq(after(grad_b, mix_r), projected)
    wkv, states = wkv_forward(recept, keyed, valued, tables, here, per)
    gate_pre, mixed = gated(mix_g, full_g, wkv, tables[5], here, seq)
    if seq == 4:
        pieces_c = after(pieces_c, mixed)
        columns_c = stack_below(pieces_c, here)
    full_c = gather_dp(columns_c)
    full_ck, full_cr = full_c[:, :hidden_width], full_c[:, hidden_width:]
    full_cv = gather_dp(after(ffn_value, columns_c))
    attn = [dot(rows, own_o, NN).astype(BF) for rows in blocks_of(mixed, seq)]
    after_mix, normed_two = after_norm(inputs_b, scatter_seq(attn, here), rows_of(vec, 10, 11), here)

    normed_two = gather_seq(normed_two)
    if seq == 4:
        grad_all = gather_second(grad_b, *after(pieces_c[1:3], normed_two))
    mix_k2, mix_r2, step_two = mixes(
        turn_pieces(normed_two), marks, rows_of(turned, 10, 11, 12, 13), 2, False, within, here, tile,
        own_rows // tile,
    )
    recept_pre = dot(mix_r2, full_cr, NN)
    opened = gather_seq(after(jax.nn.sigmoid(recept_pre).astype(BF), grad_all[3:]))
    key_pre = dot(mix_k2, full_ck, NN)
    smooth = jax.nn.softplus(key_pre)
    hidden = (smooth * smooth).astype(BF)
    slope = (2.0 * smooth * jax.nn.sigmoid(key_pre)).astype(BF)
    hidden, slope = lax.optimization_barrier((hidden, slope))
    later = after(hidden, opened[1:3])
    value_parts = [columns_product(later if j < 2 else hidden, full_cv, part, j, here, seq) for j in reversed(range(seq))]
    value_parts = value_parts[::-1]
    value_relayed = scatter_relay(value_parts, scatter_start(value_parts), here)
    d_value = spread_columns(
        grad_all, by_block(after(opened, value_parts, value_relayed)), here, True, True, tile, own_rows // tile
    )

    grad_cv = dot(hidden, d_value, TN).astype(BF)
    summed_cv = scatter_dp(grad_cv)
    value_terms = scatter_end(value_parts[0], value_relayed)
    d_hidden = dot(after(d_value, grad_cv), full_cv, NT)
    d_key_two = (d_hidden * slope.astype(F32)).astype(BF)
    channel, d_recept_two = channel_out(value_terms, recept_pre, grad_all, here, tile)
    half, first = part // 2, hidden_width // (part // 2)
    grad_ck, grad_cr = [], []

    def beside_two(relayed):
        grad_ck.append(dot(after(mix_k2, relayed), d_key_two, TN).astype(BF))
        grad_cr.append(dot(after(mix_r2, relayed, grad_ck), d_recept_two, TN).astype(BF))
        return grad_ck, grad_cr

    terms_two, sums_two = mixes_back_scatter(
        [(0, d_key_two, 0, full_c, 0, hidden_width)]
        + [(1, d_recept_two, i, full_c, first + i, half) for i in range(2)],
        step_two, marks, rows_of(turned, 12, 13), here, seq, beside_two,
    )
    summed_ck, summed_cr = scatter_dp(grad_ck[0]), scatter_dp(grad_cr[0])
    if within is None:
        terms_two = [outside(t, groups, unit, back=True) for t in terms_two]
    d_after, d_attn, norm_sums_two = norm_back(terms_two, after_mix, grad_b, rows_of(vec, 10), within, here)

    pieces = gather_seq(d_attn)
    *near, far = by_block(pieces)
    near_mixed = [dot(d, own_o, NT).astype(BF) for d in near]
    *near_rows, far_rows = blocks_of(mixed, seq)
    near_wo = sum(dot(m, d, TN) for m, d in zip(near_rows, near))
    far = after(far, near_mixed, near_wo, summed_cv)
    d_mixed = jnp.concatenate([*near_mixed, dot(far, own_o, NT).astype(BF)], axis=0)
    grad_wo = (near_wo + dot(far_rows, far, TN)).astype(BF)
    summed_o = scatter_dp(grad_wo)
    d_mixed = after(d_mixed, summed_ck, grad_wo)
    d_wkv, d_gate, gate_sums = gate_backward(wkv, gate_pre, d_mixed, tables[5], here)
    grad_g = dot(mix_g, d_gate, TN).astype(BF)
    summed_g = scatter_dp(grad_g)
    d_recept, d_keyed, d_valued, sums = wkv_backward(
        recept, keyed, valued, after(d_wkv, grad_g), states, tables, here, per
    )
    channel = after(trade_seq(blocks_of(after(channel, d_mixed), seq)), d_recept)
    grads_in = [
        dot(after(m, channel), d, TN).astype(BF)
        for m, d in ((mix_r, d_recept), (mix_k, d_keyed), (mix_v, d_valued))
    ]
    summed_in = scatter_dp(jnp.concatenate(grads_in, axis=1))
    others = []

    def beside(relayed):
        others.append(spread_columns([after_mix], after(channel, relayed), here, False, False, CHUNK, per))
        others.append(after(summed_cv, relayed).astype(F32))
        return others

    d_recept, d_keyed = after((d_recept, d_keyed), grads_in, summed_o, summed_cr)
    terms, sums_one = mixes_back_scatter(
        [(i, d, 0, full_in, i, part) for i, d in enumerate((d_recept, d_keyed, d_valued))]
        + [(3, d_gate, 0, full_g, 0, part)],
        step, marks, rows_of(turned, 2, 3, 4, 5), here, seq, beside,
    )
    out_rows, sum_cv = others
    if within is None:
        terms = [outside(t, groups, unit, back=True) for t in terms]
    tokens_grad, _, norm_sums = norm_back(terms, inputs_b, d_after, rows_of(vec, 0), within, here)

    summed_c = jnp.concatenate(after([summed_ck, summed_cr, summed_g], terms), axis=1)
    sum_ck, sum_cr, sum_g = owners_rows(summed_c, [ffn_key.shape[1], width, width])
    sum_o = summed_o.astype(F32)

    def by_device(rows, turn):
        if turn:
            return rows.reshape(-1, dp, seq, unit).transpose(1, 2, 0, 3)
        return rows.reshape(-1, seq, dp, unit).transpose(2, 1, 0, 3)

    own_sums = jnp.stack([sums[0] * log_decay, sums[1], gate_sums[0], gate_sums[1]])
    own_sums = lax.dynamic_update_slice(jnp.zeros((4, width), F32), own_sums, (0, place * part))
    vector_rows = jnp.concatenate(
        [
            by_device(norm_sums[:2], False), by_device(sums_one[:4], True), by_device(own_sums, False),
            by_device(norm_sums_two[:2], False), by_device(sums_two[:2], True),
        ],
        axis=2,
    )
    sum_vec = scatter_small(vector_rows.reshape((-1,) + vector_rows.shape[2:]), sum_ck)
    sum_r, sum_k, sum_v = owners_rows(after(summed_in, sum_vec), [width] * 3)
    return (
        out_rows[None], tokens_grad[None], sum_r, sum_k, sum_v, sum_g, sum_o,
        sum_ck, sum_cr, sum_cv, sum_vec,
    )


def solution(mesh):
    tokens = P("dp", "seq", None)
    rows = P(("seq", "dp"), None)
    columns = P(None, ("seq", "dp"))
    return jax.shard_map(
        shards,
        mesh=mesh,
        in_specs=(tokens, P("dp", None), tokens) + (rows,) * 8 + (columns,),
        out_specs=(tokens, tokens) + (rows,) * 8 + (columns,),
        check_vma=False,
    )
```

```python
from functools import partial

import jax
import jax.numpy as jnp
from jax import lax
from jax.experimental import pallas as pl
from jax.experimental.pallas import tpu as pltpu
from jax.sharding import PartitionSpec as P

HEAD = 64
PAIR = 128
CHUNK = 128
EPSILON = 1e-05
GROUP_EPSILON = 1.0
BF = jnp.bfloat16
F32 = jnp.float32
NT = (((1,), (1,)), ((), ()))
TN = (((0,), (0,)), ((), ()))
NN = (((1,), (0,)), ((), ()))


def swap(value, axis, distance):
    size = lax.axis_size(axis)
    return lax.ppermute(value, axis, [(i, i ^ distance) for i in range(size)])


def after(value, *others):
    return lax.optimization_barrier((value, others))[0]


def gather_second(part, one, two):
    half = part.shape[0] // 2
    columns = part.shape[1]
    low, high = swap(one[:half, :columns], "seq", 2), swap(two[half : 2 * half, :columns], "seq", 1)
    return [part, one, two, low, high]


def gather_seq(part, first=()):
    size = lax.axis_size("seq")
    if size == 4:
        half = part.shape[0] // 2
        one, two = swap(part, "seq", 1), swap(part, "seq", 2)
        one, two = after((one, two), first)
        low, high = swap(one[:half], "seq", 2), swap(two[half:], "seq", 1)
        return [part, one, two, low, high]
    return [part] + [swap(part, "seq", distance) for distance in range(1, size)]


def by_block(pieces):
    if lax.axis_size("seq") == 4:
        return pieces[:3] + [jnp.concatenate(pieces[3:], axis=0)]
    return pieces


def scatter_start(parts):
    if lax.axis_size("seq") != 4:
        return ()
    low, high = parts[3:] if len(parts) == 5 else blocks_of(parts[3], 2)
    return swap(low, "seq", 1), swap(high, "seq", 2)


def relay_body(here, one_ref, two_ref, low_ref, high_ref, one_out, two_out):
    one, two = one_ref[...], two_ref[...]
    first = pl.program_id(0) == 0
    low, high = low_ref[...].astype(F32), high_ref[...].astype(F32)
    one_out[...] = jnp.where(first, one, (one.astype(F32) + high).astype(BF))
    two_out[...] = jnp.where(first, (two.astype(F32) + low).astype(BF), two)


def scatter_relay(parts, started, here):
    if lax.axis_size("seq") != 4:
        return parts[1:]
    (_, one, two, *_), (low, high) = parts, started
    (rows, width), half = one.shape, block(low.shape, lambda i, h: (i, 0))
    return kernel(
        relay_body, "relay", (2,), here,
        [(one, half), (two, half), (low, fixed(low.shape)), (high, fixed(low.shape))],
        [((rows, width), BF, half)] * 2,
    )


def scatter_end(own, relayed):
    return [own] + [swap(part, "seq", j + 1) for j, part in enumerate(relayed)]


def scatter_seq(parts, here):
    return scatter_end(parts[0], scatter_relay(parts, scatter_start(parts), here))


def trade_seq(parts):
    return [parts[0]] + [swap(part, "seq", j + 1) for j, part in enumerate(parts[1:])]


def blocks_of(values, size):
    rows = values.shape[0] // size
    return [values[j * rows : (j + 1) * rows] for j in range(size)]


def bits_of(size):
    return [1 << b for b in range(size.bit_length() - 1)]


def gather_small(part, axis):
    for bit in bits_of(lax.axis_size(axis)):
        other = swap(part, axis, bit)
        second = (lax.axis_index(axis) & bit) != 0
        part = jnp.concatenate([jnp.where(second, other, part), jnp.where(second, part, other)], axis=0)
    return part


def scatter_small(parts, between):
    for axis in ("dp", "seq"):
        parts = after(parts, between) if axis == "seq" else parts
        for bit in reversed(bits_of(lax.axis_size(axis))):
            half = parts.shape[0] // 2
            second = (lax.axis_index(axis) & bit) != 0
            low, high = parts[:half], parts[half:]
            parts = jnp.where(second, high, low) + swap(jnp.where(second, low, high), axis, bit)
    return parts[0]


def block(shape, index):
    return pl.BlockSpec(shape, lambda *i: index(*i[:-1], i[-1][0]))


def fixed(shape):
    return pl.BlockSpec(shape, lambda *i: (0,) * len(shape))


def relative(tile, per, here):
    return (lax.div(tile, per) ^ here) * per + lax.rem(tile, per)


def kernel(body, name, grid, here, ins, outs, scratch=(), vmem=48):
    return pl.pallas_call(
        body,
        out_shape=[jax.ShapeDtypeStruct(shape, kind) for shape, kind, _ in outs],
        grid_spec=pltpu.PrefetchScalarGridSpec(
            num_scalar_prefetch=1,
            grid=grid,
            in_specs=[spec for _, spec in ins],
            out_specs=[spec for _, _, spec in outs],
            scratch_shapes=list(scratch),
        ),
        compiler_params=pltpu.CompilerParams(vmem_limit_bytes=vmem * 2**20),
        name=name,
    )(here, *[array for array, _ in ins])


def pieced(pieces, tile, columns, column, place):
    ins, start = [], 0
    for piece in pieces:
        count = piece.shape[0] // tile

        def index(i, h, start=start, count=count):
            return jnp.clip(place(i, h) - start, 0, count - 1), column(h)

        ins.append((piece, block((tile, columns), index)))
        start += count
    return ins


def picked(refs, counts, tile, held):
    start = 0
    for ref, count in zip(refs, counts):

        @pl.when((tile >= start) & (tile < start + count))
        def _(ref=ref):
            held[...] = ref[...]

        start += count
    return held[...].astype(F32)


def counts_of(pieces, tile):
    return [piece.shape[0] // tile for piece in pieces]


def row_index(rows):
    return lax.broadcasted_iota(jnp.int32, (rows, 1), 0)


def placed(place, width):
    return pl.ds(pl.multiple_of(place * width, width), width)


def cut_body(count, parts, here, *refs):
    ins, beside, outs = refs[:count], refs[count], refs[count + 1 :]
    rows = ins[0].shape[0]
    for j in range(parts):
        outs[j][rows:, :] = jnp.zeros_like(outs[j][rows:, :])
        outs[j][rows:, : beside.shape[1]] = beside[...]
    at = 0
    for ref in ins:
        width = ref.shape[1] // parts
        for j in range(parts):
            outs[j][:rows, at : at + width] = ref[:, placed(here[0] ^ j, width)]
        at += width


def cut_columns(weights, beside, here, parts):
    rows, width = weights[0].shape[0] + beside.shape[0], sum(w.shape[1] for w in weights) // parts
    return kernel(
        partial(cut_body, len(weights), parts), "cut_columns", (1,), here,
        [(w, fixed(w.shape)) for w in [*weights, beside]],
        [((rows, width), BF, fixed((rows, width)))] * parts,
    )


def stack_body(parts, here, *refs):
    start = 0
    outs, beside = refs[parts:-1], refs[-1]
    for out in outs:
        for j in range(parts):
            out[here[0] ^ j] = refs[j][: out.shape[1], start : start + out.shape[2]]
        start += out.shape[2]
    for j in range(parts):
        beside[here[0] ^ j] = refs[j][out.shape[1] :, : beside.shape[2]]


def stack_rows(pieces, widths, beside, here):
    parts, rows = len(pieces), pieces[0].shape[0] - beside.shape[0]
    shapes = [(parts, rows, width) for width in widths] + [(parts,) + beside.shape]
    return kernel(
        partial(stack_body, parts), "stack_rows", (1,), here,
        [(p, fixed(p.shape)) for p in pieces],
        [(shape, BF, fixed(shape)) for shape in shapes],
    )


def ride_body(count, here, *refs):
    ins, rider, outs = refs[:count], refs[count], refs[count + 1 :]
    for j, out in enumerate(outs):
        top, at = 0, 0
        if j in (1, 2):
            top = rider.shape[0]
            out[:top, : rider.shape[1]] = rider[...]
            out[:top, rider.shape[1] :] = jnp.zeros_like(out[:top, rider.shape[1] :])
        for ref in ins:
            width = ref.shape[1] // 4
            out[top:, at : at + width] = ref[:, placed(here[0] ^ j, width)]
            at += width


def cut_with_rider(weights, rider, here):
    rows, width = weights[0].shape[0], sum(w.shape[1] for w in weights) // 4
    return kernel(
        partial(ride_body, len(weights)), "cut_columns", (1,), here,
        [(w, fixed(w.shape)) for w in [*weights, rider]],
        [((n, width), BF, fixed((n, width))) for n in (rows, rows + rider.shape[0], rows + rider.shape[0], rows)],
    )


def unride_body(here, *refs):
    out = refs[-1]
    rows = out.shape[1]
    for j, ref in enumerate(refs[:-1]):
        out[here[0] ^ j] = ref[ref.shape[0] - rows :, :]


def stack_below(pieces, here):
    shape = (4,) + pieces[0].shape
    (stacked,) = kernel(
        unride_body, "stack_rows", (1,), here,
        [(p, fixed(p.shape)) for p in pieces],
        [(shape, BF, fixed(shape))],
    )
    return stacked.reshape(-1, shape[-1])


def hold_body(here, in_ref, *refs):
    refs[-1][...] = in_ref[...]


def held_back(values, here, *others):
    rows, width = values.shape
    own = block((rows // 2, width), lambda i, h: (i, 0))
    (copy,) = kernel(
        hold_body, "hold", (2,), here,
        [(values, own)] + [(o, pl.BlockSpec(memory_space=pl.ANY)) for o in others],
        [((rows, width), values.dtype, own)],
    )
    return copy


def join_body(parts, count, here, *refs):
    ins, outs = refs[:parts], refs[parts:]
    at = 0
    for ref in outs:
        width = ref.shape[1] // parts
        for j in range(parts):
            ref[:, placed(here[0] ^ j, width)] = ins[j][:, at : at + width].astype(F32)
        at += width


def join_columns(pieces, widths, here):
    parts, rows = len(pieces), pieces[0].shape[0]
    return kernel(
        partial(join_body, parts, len(widths)), "join_columns", (1,), here,
        [(p, fixed(p.shape)) for p in pieces],
        [((rows, width), F32, fixed((rows, width))) for width in widths],
    )


def spread_body(counts, parts, product, here, *refs):
    bases, pieces, out, held = refs[: len(counts)], refs[len(counts) : -2], refs[-2], refs[-1]
    picked(bases, counts, pl.program_id(0), held)
    width = pieces[0].shape[1]
    for j in range(parts):
        at = placed(here[0] ^ j, width)
        piece, base = pieces[j][...].astype(F32), held[:, at].astype(F32)
        out[:, at] = (base * piece if product else base + piece).astype(BF)


def spread_columns(bases, columns, here, product, turn, tile, per):
    rows, width = sum(counts_of(bases, tile)) * tile, bases[0].shape[1]

    def turned(i, j):
        return (lax.div(i, per) ^ j) * per + lax.rem(i, per) if turn else i

    (result,) = kernel(
        partial(spread_body, counts_of(bases, tile), len(columns), product), "spread_columns", (rows // tile,), here,
        pieced(bases, tile, width, lambda h: 0, lambda i, h: i)
        + [(c, block((tile, c.shape[1]), lambda i, h, j=j: (turned(i, j), 0))) for j, c in enumerate(columns)],
        [((rows, width), BF, block((tile, width), lambda i, h: (i, 0)))],
        [pltpu.VMEM((tile, width), bases[0].dtype)],
    )
    return result


def shuffled(values, groups, back=False):
    seq, dp = groups
    if back:
        seq, dp = dp, seq
    lane = lax.broadcasted_iota(jnp.int32, (1, PAIR), 1) < HEAD
    source = [s * dp + d for d in range(dp) for s in range(seq)]
    columns = []
    for one, two in zip(source[::2], source[1::2]):
        low = values[:, one // 2 * PAIR : (one // 2 + 1) * PAIR]
        high = values[:, two // 2 * PAIR : (two // 2 + 1) * PAIR]
        low = pltpu.roll(low, HEAD, 1) if one % 2 else low
        high = high if two % 2 else pltpu.roll(high, HEAD, 1)
        columns.append(jnp.where(lane, low, high))
    return jnp.concatenate(columns, axis=1)


def outside(values, groups, channels, back=False):
    seq, dp = groups[::-1] if back else groups
    return values.reshape(-1, seq, dp, channels).swapaxes(1, 2).reshape(values.shape)


def centre(values):
    centred = values - jnp.mean(values, axis=-1, keepdims=True)
    spread = jnp.mean(centred * centred, axis=-1, keepdims=True)
    return centred, lax.rsqrt(spread + EPSILON)


def mix_body(count, norm, groups, counts, per, mixed, open_up, here, *refs):
    pieces, (marks_ref, vec_ref) = refs[: len(counts)], refs[len(counts) : len(counts) + 2]
    weights = refs[len(counts) + 2 : len(counts) + 2 + len(mixed)]
    outs, last, held = refs[len(counts) + 2 + len(mixed) : -2], refs[-2], refs[-1]
    products = outs[count + 1 :]

    @pl.when(pl.program_id(0) == 0)
    def _():
        last[...] = jnp.zeros_like(last)

    values = picked(pieces, counts, relative(pl.program_id(0), per, here[0]), held)
    if norm:
        centred, inverse = centre(values)
        values = centred * inverse
    if groups:
        values = shuffled(values, groups)
    if norm:
        values = values * vec_ref[0:1, :] + vec_ref[1:2, :]
    rows = values.shape[0]
    previous = jnp.where(row_index(rows) == 0, last[0:1, :], pltpu.roll(values, 1, 0)) * marks_ref[:, 3:4]
    last[0:1, :] = values[rows - 1 :, :]
    step = values - previous
    outs[count][...] = step.astype(BF)
    for i in range(count):
        mix = (previous + step * vec_ref[2 + i : 3 + i, :]).astype(BF)
        outs[i][...] = mix
        if i in mixed:
            k = mixed.index(i)
            product = dot(mix, weights[k][...], NN)
            if open_up:
                products[0][...] = product
                products[1][...] = (1.0 / (1.0 + jnp.exp(-product))).astype(BF)
            else:
                products[k][...] = product.astype(BF)


def mixes(pieces, marks, vec, count, norm, groups, here, tile, per, weights, open_up):
    rows, width = marks.shape[0], pieces[0].shape[1]
    own = block((tile, width), lambda i, h: (relative(i, per, h), 0))
    outs = [((rows, width), BF, own)] * (count + 1)
    for _, _, _, part in weights:
        narrow = block((tile, part), lambda i, h: (relative(i, per, h), 0))
        outs += [((rows, part), F32 if open_up else BF, narrow)] + [((rows, part), BF, narrow)] * open_up
    return kernel(
        partial(mix_body, count, norm, groups, counts_of(pieces, tile), per, [w[0] for w in weights], open_up),
        "mixes", (rows // tile,), here,
        pieced(pieces, tile, width, lambda h: 0, lambda i, h: relative(i, per, h))
        + [(marks, block((tile, PAIR), lambda i, h: (i, 0))), (vec, fixed(vec.shape))]
        + [(w, pl.BlockSpec((width, part), lambda *_, at=at: (0, at))) for _, w, at, part in weights],
        outs,
        [pltpu.VMEM((8, width), F32), pltpu.VMEM((tile, width), BF)],
        vmem=58,
    )


def mixes_back_body(which, first, seq, outs, here, *refs):
    count = len(which)
    grads, nexts, weights = refs[:count], refs[count : 2 * count], refs[2 * count : 3 * count]
    step_ref, marks_ref, next_marks_ref, vec_ref, *out_refs, sums_ref = refs[3 * count :]

    @pl.when(pl.program_id(1) == 0)
    def _():
        sums_ref[...] = jnp.zeros_like(sums_ref)

    step = step_ref[...].astype(F32)
    rows = step.shape[0]
    total = straight = None
    for i in range(which[-1] + 1):
        grad = sum(
            dot(jnp.concatenate([grads[k][...], nexts[k][...]], axis=0), weights[k][...], NT)
            for k in range(count)
            if which[k] == i
        )
        sums_ref[i : i + 1, :] += jnp.sum(grad[:rows] * step, axis=0, keepdims=True)
        part = grad * vec_ref[i : i + 1, :]
        total, straight = (total + grad, straight + part) if i else (grad, part)
    inside = ((first + pl.program_id(1)) ^ here[0]) < seq - 1
    keep = jnp.concatenate([marks_ref[:, 3:4], jnp.where(inside, next_marks_ref[:, 3:4], 0.0)], axis=0)
    kept = (total - straight) * keep
    up = pltpu.roll(kept, kept.shape[0] - 1, 0)
    result = (straight[:rows] + up[:rows]).astype(BF)
    if len(out_refs) == 1:
        out_refs[0][...] = result
        return
    if outs == 1:
        out_refs[0][...] = result[: rows // 2]
        out_refs[1][...] = result[rows // 2 :]
        return
    for k, out_ref in enumerate(out_refs):

        @pl.when(pl.program_id(1) == k)
        def _(out_ref=out_ref):
            out_ref[...] = result


EXTRA = 16


def mixes_back(terms, step, marks, vec, here, seq, first, count, halves=False):
    rows, width = step.shape
    tile, columns = rows // seq, min(512, width)
    extras = tile // EXTRA

    def following(i, h):
        return jnp.minimum(((first + i) ^ h) + 1, seq - 1)

    ins = [(g, block((tile, n), lambda c, i, h, at=at: (first + i, at))) for _, g, at, _, _, n in terms]
    ins += [
        (g, block((EXTRA, n), lambda c, i, h, at=at: ((following(i, h) ^ h) * extras, at)))
        for _, g, at, _, _, n in terms
    ]
    ins += [(w, block((columns, n), lambda c, i, h, at=at: (c, at))) for _, _, _, w, at, n in terms]
    ins += [
        (step, block((tile, columns), lambda c, i, h: (first + i, c))),
        (marks, block((tile, PAIR), lambda c, i, h: ((first + i) ^ h, 0))),
        (marks, block((EXTRA, PAIR), lambda c, i, h: (following(i, h) * extras, 0))),
        (vec, block((8, columns), lambda c, i, h: (0, c))),
    ]
    size = tile // 2 if halves else tile
    *parts, sums = kernel(
        partial(mixes_back_body, [t[0] for t in terms], first, seq, count), "mixes_back", (width // columns, count), here, ins,
        [((size, width), BF, block((size, columns), lambda c, i, h: (0, c)))] * (2 if halves else count)
        + [((8, width), F32, block((8, columns), lambda c, i, h: (0, c)))],
    )
    return parts, sums


def mixes_back_scatter(terms, step, marks, vec, here, seq, beside):
    if seq != 4:
        parts, sums = mixes_back(terms, step, marks, vec, here, seq, 0, seq)
        return after(scatter_seq(parts, here), beside(parts)), sums

    def call(first, count, *before):
        ordered = after([t[1] for t in terms], *before)
        return mixes_back(
            [(t[0], g) + t[2:] for t, g in zip(terms, ordered)], step, marks, vec, here, seq, first, count, first == 3
        )

    far, sums_far = call(3, 1)
    near, sums_near = call(1, 2, far)
    parts = [None, *near, *far]
    started = after(scatter_start(parts), near)
    relayed = scatter_relay(parts, started, here)
    (own,), sums_own = call(0, 1, near, relayed)
    return after(scatter_end(own, relayed), beside(relayed)), sums_far + sums_near + sums_own


def after_body(count, here, x_ref, vec_ref, *refs):
    after_ref, normed_ref = refs[count:]
    after = x_ref[...].astype(F32)
    for ref in refs[:count]:
        after = after + ref[...].astype(F32)
    after_ref[...] = after
    centred, inverse = centre(after)
    normed_ref[...] = (centred * inverse * vec_ref[0:1, :] + vec_ref[1:2, :]).astype(BF)


def after_norm(inputs, terms, vec, here):
    rows, width = inputs.shape
    own = block((CHUNK, width), lambda i, h: (i, 0))
    return kernel(
        partial(after_body, len(terms)), "after_norm", (rows // CHUNK,), here,
        [(inputs, own), (vec, fixed(vec.shape))] + [(t, own) for t in terms],
        [((rows, width), F32, own), ((rows, width), BF, own)],
    )


def norm_back_body(count, groups, here, x_ref, base_ref, vec_ref, *refs):
    wide_ref, narrow_ref, sums_ref = refs[count:]

    @pl.when(pl.program_id(0) == 0)
    def _():
        sums_ref[...] = jnp.zeros_like(sums_ref)

    grad = refs[0][...].astype(F32)
    for ref in refs[1:count]:
        grad = grad + ref[...].astype(F32)
    if groups:
        grad = shuffled(grad, groups, back=True)
    centred, inverse = centre(x_ref[...].astype(F32))
    normed = centred * inverse
    sums_ref[0:1, :] += jnp.sum(grad * normed, axis=0, keepdims=True)
    sums_ref[1:2, :] += jnp.sum(grad, axis=0, keepdims=True)
    grad = grad * vec_ref[0:1, :]
    grad = grad - jnp.mean(grad, axis=-1, keepdims=True) - normed * jnp.mean(grad * normed, axis=-1, keepdims=True)
    result = base_ref[...].astype(F32) + inverse * grad
    wide_ref[...] = result
    narrow_ref[...] = result.astype(BF)


def norm_back(terms, inputs, base, vec, groups, here):
    rows, width = inputs.shape
    own = block((CHUNK, width), lambda i, h: (i, 0))
    return kernel(
        partial(norm_back_body, len(terms), groups), "norm_back", (rows // CHUNK,), here,
        [(inputs, own), (base, own), (vec, fixed(vec.shape))] + [(t, own) for t in terms],
        [((rows, width), F32, own), ((rows, width), BF, own), ((8, width), F32, fixed((8, width)))],
    )


def gate_body(mix_ref, weight_ref, wkv_ref, par_ref, gate_ref, mixed_ref):
    gate = dot(mix_ref[...], weight_ref[...], NN)
    gate_ref[...] = gate
    ones = jnp.where(same_head(), 1.0, 0.0).astype(BF)
    for pair in range(gate.shape[1] // PAIR):
        at = slice(pair * PAIR, (pair + 1) * PAIR)
        wkv = wkv_ref[:, at]
        centred = wkv - head_sum_fine(wkv, ones) * (1.0 / HEAD)
        spread = head_sum(centred * centred, ones) * (1.0 / HEAD)
        normed = centred * lax.rsqrt(spread + GROUP_EPSILON) * par_ref[1:2, at] + par_ref[2:3, at]
        mixed_ref[:, at] = (normed * (gate[:, at] / (1.0 + jnp.exp(-gate[:, at])))).astype(BF)


def gated(mix_g, weights, wkv, params, here, seq):
    rows, width = mix_g.shape
    tile, part = rows // seq, wkv.shape[1]
    own = block((tile, part), lambda i, h: (i, 0))
    return kernel(
        lambda here, *refs: gate_body(*refs), "gate", (seq,), here,
        [
            (mix_g, block((tile, width), lambda i, h: (i, 0))),
            (weights, block((width, part), lambda i, h: (0, 0))),
            (wkv, own),
            (params, fixed(params.shape)),
        ],
        [((rows, part), F32, own), ((rows, part), BF, own)],
    )


def columns_body(here, left_ref, right_ref, out_ref):
    out_ref[...] = dot(left_ref[...], right_ref[...], NN).astype(BF)


def columns_product(left, right, part, relative_to, here, seq):
    rows, depth = left.shape
    tile = rows // seq
    (result,) = kernel(
        columns_body, "value_columns", (seq,), here,
        [
            (left, block((tile, depth), lambda i, h: (i, 0))),
            (right, block((depth, part), lambda i, h: (0, h ^ relative_to))),
        ],
        [((rows, part), BF, block((tile, part), lambda i, h: (i ^ relative_to, 0)))],
    )
    return result


def channel_body(counts, here, pre_ref, *refs):
    grads, terms, (channel_ref, d_recept_ref, held) = refs[: len(counts)], refs[len(counts) : -3], refs[-3:]
    value = sum(ref[...].astype(F32) for ref in terms)
    opened = 1.0 / (1.0 + jnp.exp(-pre_ref[...]))
    channel = opened * value
    channel_ref[...] = channel.astype(BF)
    grad = picked(grads, counts, pl.program_id(0), held)
    d_recept_ref[...] = (grad * channel * (1.0 - opened)).astype(BF)


def channel_out(terms, pre, grads, here, tile):
    rows, part = pre.shape
    own = block((tile, part), lambda i, h: (i, 0))
    return kernel(
        partial(channel_body, counts_of(grads, tile)), "channel", (rows // tile,), here,
        [(pre, own)] + pieced(grads, tile, part, lambda h: h, lambda i, h: i) + [(t, own) for t in terms],
        [((rows, part), BF, own)] * 2,
        [pltpu.VMEM((tile, part), BF)],
    )


def head_masks():
    lane = lax.broadcasted_iota(jnp.int32, (1, PAIR), 1)
    first = (lane < HEAD).astype(F32)
    return first, 1.0 - first


def same_head():
    row = lax.broadcasted_iota(jnp.int32, (PAIR, PAIR), 0) < HEAD
    column = lax.broadcasted_iota(jnp.int32, (PAIR, PAIR), 1) < HEAD
    return row == column


def dot(left, right, dims):
    return lax.dot_general(left, right, dims, preferred_element_type=F32)


def head_sum(values, ones):
    return dot(values.astype(BF), ones, NN)


def head_sum_fine(values, ones):
    coarse = values.astype(BF)
    rest = (values - coarse.astype(F32)).astype(BF)
    return dot(coarse, ones, NN) + dot(rest, ones, NN)


def stacked(values, first, second):
    return jnp.concatenate([(values * first).astype(BF), (values * second).astype(BF)], axis=0)


def masks_of(rows_ref, columns_ref):
    segment = rows_ref[:, 0:1]
    reaches = rows_ref[:, 1:2]
    last_same = rows_ref[:, 2:3]
    reach_last = rows_ref[CHUNK - 1 : CHUNK, 1:2]
    before = lax.broadcasted_iota(jnp.int32, (CHUNK, CHUNK), 1) < lax.broadcasted_iota(
        jnp.int32, (CHUNK, CHUNK), 0
    )
    allowed = jnp.where((segment == columns_ref[0:1, :]) & before, 1.0, 0.0)
    return reaches, last_same, reach_last, jnp.concatenate([allowed, allowed], axis=0)


def wkv_forward_body(
    here, r_ref, k_ref, v_ref, rows_ref, columns_ref, grow_ref, shrink_ref, tail_ref, par_ref,
    wkv_ref, states_ref, state,
):
    @pl.when(pl.program_id(0) == 0)
    def _():
        state[...] = jnp.zeros_like(state)

    first, second = head_masks()
    block = same_head()
    ones = jnp.where(block, 1.0, 0.0).astype(BF)
    reaches, last_same, reach_last, allowed = masks_of(rows_ref, columns_ref)
    for pair in range(r_ref.shape[1] // PAIR):
        at = slice(pair * PAIR, (pair + 1) * PAIR)
        r, k, v = r_ref[:, at].astype(F32), k_ref[:, at].astype(F32), v_ref[:, at].astype(F32)
        bonus, decay = par_ref[0:1, at], par_ref[3:4, at]
        held = state[at, :]
        held_b = held.astype(BF)
        states_ref[0, at, :] = held_b
        grown = r * grow_ref[:, at]
        shrunk = (k * shrink_ref[:, at]).astype(BF)
        scores = (dot(stacked(grown, first, second), shrunk, NT) * allowed).astype(BF)
        both = jnp.concatenate([scores[:CHUNK], scores[CHUNK:]], axis=1)
        wkv = dot(both, stacked(v, first, second), NN)
        wkv = wkv + dot((grown * reaches).astype(BF), held_b, NT)
        wkv = wkv + head_sum(r * bonus * k, ones) * v
        fresh = dot(v_ref[:, at], (k * tail_ref[:, at] * last_same).astype(BF), TN)
        state[at, :] = held * (decay * reach_last) + jnp.where(block, fresh, 0.0)
        wkv_ref[:, at] = wkv


def wkv_backward_body(
    here, r_ref, k_ref, v_ref, d_wkv_ref, states_ref,
    rows_ref, columns_ref, grow_ref, shrink_ref, tail_ref, par_ref,
    d_r_ref, d_k_ref, d_v_ref, sums_ref, d_state,
):
    @pl.when(pl.program_id(0) == 0)
    def _():
        d_state[...] = jnp.zeros_like(d_state)
        sums_ref[...] = jnp.zeros_like(sums_ref)

    first, second = head_masks()
    block = same_head()
    ones = jnp.where(block, 1.0, 0.0).astype(BF)
    reaches, last_same, reach_last, allowed = masks_of(rows_ref, columns_ref)
    offset = lax.broadcasted_iota(jnp.int32, (CHUNK, PAIR), 0).astype(F32)
    for pair in range(r_ref.shape[1] // PAIR):
        at = slice(pair * PAIR, (pair + 1) * PAIR)
        bonus, decay = par_ref[0:1, at], par_ref[3:4, at]
        d_wkv = d_wkv_ref[:, at].astype(F32)
        r, k, v = r_ref[:, at].astype(F32), k_ref[:, at].astype(F32), v_ref[:, at].astype(F32)
        v_b, d_wkv_b = v_ref[:, at], d_wkv_ref[:, at]
        grow, shrink, tail = grow_ref[:, at], shrink_ref[:, at], tail_ref[:, at] * last_same
        held = states_ref[0, at, :]
        later = d_state[at, :]
        later_b = later.astype(BF)
        grown = r * grow
        shrunk = k * shrink
        shrunk_b = shrunk.astype(BF)
        tailed_b = (k * tail).astype(BF)
        grown_two = stacked(grown, first, second)
        d_wkv_two = stacked(d_wkv, first, second)
        scores = (dot(grown_two, shrunk_b, NT) * allowed).astype(BF)
        d_scores = (dot(d_wkv_two, v_b, NT) * allowed).astype(BF)
        d_both = jnp.concatenate([d_scores[:CHUNK], d_scores[CHUNK:]], axis=1)
        d_grown = dot(d_both, stacked(shrunk, first, second), NN)
        d_grown = d_grown + dot((d_wkv * reaches).astype(BF), held, NN)
        d_shrunk = dot(d_scores, grown_two, TN)
        d_tailed = dot(v_b, later_b, NN)
        share = head_sum(r * bonus * k, ones)
        d_share = head_sum(d_wkv * v, ones)
        d_v = dot(scores, d_wkv_two, TN) + dot(tailed_b, later_b, NT) + share * d_wkv
        d_r_ref[:, at] = (d_grown * grow + d_share * bonus * k).astype(BF)
        d_k_ref[:, at] = (d_shrunk * shrink + d_tailed * tail + d_share * bonus * r).astype(BF)
        d_v_ref[:, at] = d_v.astype(BF)
        carried = decay * reach_last
        d_fresh = dot(d_wkv_b, (grown * reaches).astype(BF), TN)
        d_state[at, :] = later * carried + jnp.where(block, d_fresh, 0.0)
        grown_b = grown.astype(BF).astype(F32)
        d_log = (
            offset * grown_b * d_grown
            - (offset + 1.0) * shrunk_b.astype(F32) * d_shrunk
            + (CHUNK - 1.0 - offset) * tailed_b.astype(F32) * d_tailed
        )
        kept = CHUNK * carried * jnp.sum(held.astype(F32) * later, axis=0, keepdims=True)
        sums_ref[0:1, at] += jnp.sum(d_log, axis=0, keepdims=True) + kept
        sums_ref[1:2, at] += jnp.sum(d_share * r * k, axis=0, keepdims=True)


def gate_backward_body(here, wkv_ref, g_ref, d_mixed_ref, par_ref, d_wkv_ref, d_g_ref, sums_ref):
    @pl.when(pl.program_id(0) == 0)
    def _():
        sums_ref[...] = jnp.zeros_like(sums_ref)

    ones = jnp.where(same_head(), 1.0, 0.0).astype(BF)
    for pair in range(wkv_ref.shape[1] // PAIR):
        at = slice(pair * PAIR, (pair + 1) * PAIR)
        gain, bias = par_ref[1:2, at], par_ref[2:3, at]
        wkv, gate, d_mixed = wkv_ref[:, at], g_ref[:, at], d_mixed_ref[:, at].astype(F32)
        centred = wkv - head_sum_fine(wkv, ones) * (1.0 / HEAD)
        spread = head_sum(centred * centred, ones) * (1.0 / HEAD)
        inverse = lax.rsqrt(spread + GROUP_EPSILON)
        normed = centred * inverse
        opened = 1.0 / (1.0 + jnp.exp(-gate))
        d_scaled = d_mixed * gate * opened
        d_g = d_mixed * (normed * gain + bias) * opened * (1.0 + gate * (1.0 - opened))
        d_g_ref[:, at] = d_g.astype(BF)
        d_normed = d_scaled * gain
        mean_one = head_sum(d_normed, ones) * (1.0 / HEAD)
        mean_two = head_sum(d_normed * normed, ones) * (1.0 / HEAD)
        d_wkv_ref[:, at] = (inverse * (d_normed - mean_one - normed * mean_two)).astype(BF)
        sums_ref[0:1, at] += jnp.sum(d_scaled * normed, axis=0, keepdims=True)
        sums_ref[1:2, at] += jnp.sum(d_scaled, axis=0, keepdims=True)


def gate_backward(wkv, gate, d_mixed, params, here):
    rows, part = wkv.shape
    own = block((2 * CHUNK, part), lambda i, h: (i, 0))
    return kernel(
        gate_backward_body, "gate_backward", (rows // (2 * CHUNK),), here,
        [(a, own) for a in (wkv, gate, d_mixed)] + [(params, fixed(params.shape))],
        [((rows, part), BF, own)] * 2 + [((8, part), F32, fixed((8, part)))],
    )


def wkv_blocks(width, chunks, per, backward):
    def chunk(i):
        return chunks - 1 - i if backward else i

    tokens = block((CHUNK, width), lambda i, h: (relative(chunk(i), per, h), 0))
    states = block((1, width, PAIR), lambda i, h: (chunk(i), 0, 0))
    tables = [
        block((CHUNK, PAIR), lambda i, h: (chunk(i), 0)),
        block((8, CHUNK), lambda i, h: (0, chunk(i))),
    ]
    return tokens, states, tables + [fixed((CHUNK, width))] * 3 + [fixed((8, width))]


def wkv_forward(r, k, v, tables, here, per):
    length, width = r.shape
    chunks = length // CHUNK
    tokens, states, blocks = wkv_blocks(width, chunks, per, False)
    return kernel(
        wkv_forward_body, "wkv_forward", (chunks,), here,
        [(a, tokens) for a in (r, k, v)] + list(zip(tables, blocks)),
        [((length, width), F32, tokens), ((chunks, width, PAIR), BF, states)],
        [pltpu.VMEM((width, PAIR), F32)],
    )


def wkv_backward(r, k, v, d_wkv, states_kept, tables, here, per):
    length, width = r.shape
    chunks = length // CHUNK
    tokens, states, blocks = wkv_blocks(width, chunks, per, True)
    return kernel(
        wkv_backward_body, "wkv_backward", (chunks,), here,
        [(a, tokens) for a in (r, k, v, d_wkv)] + [(states_kept, states)] + list(zip(tables, blocks)),
        [((length, width), BF, tokens)] * 3 + [((8, width), F32, fixed((8, width)))],
        [pltpu.VMEM((width, PAIR), F32)],
    )


def wkv_tables(piece, keep, log_decay, bonus, gain, bias):
    length = piece.shape[0]
    by_chunk = piece.reshape(length // CHUNK, CHUNK)
    before = jnp.concatenate([jnp.full((1,), -1, piece.dtype), by_chunk[:-1, -1]])
    reaches = (by_chunk == before[:, None]).reshape(-1)
    last_same = (by_chunk == by_chunk[:, -1:]).reshape(-1)
    marks = jnp.stack([piece.astype(F32), reaches.astype(F32), last_same.astype(F32), keep], axis=1)
    rows = jnp.pad(marks, ((0, 0), (0, PAIR - 4)))
    columns = jnp.broadcast_to(piece.astype(F32)[None], (8, length))
    offset = jnp.arange(CHUNK).astype(F32)[:, None]
    grow = jnp.exp(offset * log_decay)
    shrink = jnp.exp(-(offset + 1.0) * log_decay)
    tail = jnp.exp((CHUNK - 1.0 - offset) * log_decay)
    zero = jnp.zeros_like(bonus)
    params = jnp.stack([bonus, gain, bias, jnp.exp(CHUNK * log_decay)] + [zero] * 4)
    return rows, columns, grow, shrink, tail, params


def segment_of(lengths, positions):
    rank = jnp.arange(lengths.shape[0])
    starts = jnp.sum(jnp.where(rank[:, None] > rank[None, :], lengths[None, :], 0), axis=1)
    later_flags = (positions[:, None] >= starts[None, 1:]).astype(jnp.int32)
    first_flags = jnp.any(positions[:, None] == starts[None, :], axis=1)
    return (jnp.sum(later_flags, axis=1), first_flags)


def rows_of(vec, *rows):
    return jnp.pad(jnp.stack([vec[i] for i in rows]), ((0, 8 - len(rows)), (0, 0)))


def shards(
    tokens, seq_lengths, out_grad, w_receptance, w_key, w_value, w_gate, w_output,
    ffn_key, ffn_receptance, ffn_value, vectors,
):
    seq, dp = lax.axis_size("seq"), lax.axis_size("dp")
    place = lax.axis_index("seq")
    here = jnp.reshape(place, (1,)).astype(jnp.int32)
    inputs_b, grad_b = tokens[0], out_grad[0]
    own_rows, width = inputs_b.shape
    length, part, unit = own_rows * seq, width // seq, vectors.shape[1]
    per, tile = own_rows // CHUNK, own_rows // 2
    hidden_width = ffn_key.shape[1] // seq
    groups = (seq, dp)
    within = groups if unit == HEAD else None

    vectors_b = jnp.pad(vectors, ((0, 16 - vectors.shape[0]), (0, 0)))

    def stacked_columns(weights, widths, beside=()):
        cut = cut_columns(weights, vectors_b, here, seq)
        *stacked, last = stack_rows(after(trade_seq(cut), beside), widths, vectors_b, here)
        return [w.reshape(-1, w.shape[-1]) for w in stacked] + [last], cut

    def gather_dp(rows):
        return lax.all_gather(rows, "dp", axis=0, tiled=True)

    def scatter_dp(grad):
        return lax.psum_scatter(grad, "dp", scatter_dimension=0, tiled=True)

    def owners_parts(summed):
        rows = summed.shape[0] // seq
        return trade_seq([lax.dynamic_slice_in_dim(summed, (place ^ j) * rows, rows, 0) for j in range(seq)])

    def owners_rows(summed, widths):
        return join_columns(owners_parts(summed), widths, here)

    def turn_pieces(pieces):
        if within is not None:
            return pieces
        return [outside(p, groups, unit) for p in pieces]

    positions = jnp.arange(length, dtype=jnp.int32)
    piece, first_flags = segment_of(seq_lengths[0], positions)

    (columns_in, columns_g, vec_seq), cut = stacked_columns(
        [w_receptance, w_key, w_value, w_gate], [3 * part, part]
    )
    tokens_held = held_back(inputs_b, here, *cut)
    full_in = gather_dp(columns_in)
    vec_parts = gather_small(vec_seq[None, :, : vectors.shape[0]], "dp").astype(F32)
    vec = vec_parts.transpose(2, 1, 0, 3).reshape(-1, width)
    turned = vec_parts.transpose(2, 0, 1, 3).reshape(-1, width)
    vec_own = lax.dynamic_slice_in_dim(vec, place * part, part, 1)
    log_decay = -jnp.exp(vec_own[6])
    tables = wkv_tables(
        piece, 1.0 - first_flags.astype(F32), log_decay, vec_own[7], vec_own[8], vec_own[9]
    )
    marks = tables[0]
    rows_one = rows_of(turned, 0, 1, 2, 3, 4, 5)
    tokens_all = gather_seq(tokens_held, (rows_one, tables))
    full_g = gather_dp(after(columns_g, tokens_all[1:3], rows_one))
    own_o = gather_dp(after(w_output, tokens_all))

    mix_r, mix_k, mix_v, mix_g, step, recept, keyed, valued = mixes(
        turn_pieces(tokens_all), marks, rows_one, 4, True, within, here, tile, own_rows // tile,
        [(i, full_in, i, part) for i in range(3)], False,
    )
    projected = (recept, keyed, valued)
    ffn_weights = after([ffn_key, ffn_receptance], tokens_all)
    if seq == 4:
        pieces_c = trade_seq(cut_with_rider(ffn_weights, grad_b, here))
    else:
        (columns_c, _), _ = stacked_columns(ffn_weights, [hidden_width + part], projected)
        grad_all = gather_seq(after(grad_b, mix_r), projected)
    wkv, states = wkv_forward(recept, keyed, valued, tables, here, per)
    gate_pre, mixed = gated(mix_g, full_g, wkv, tables[5], here, seq)
    if seq == 4:
        pieces_c = after(pieces_c, mixed)
        columns_c = stack_below(pieces_c, here)
    full_c = gather_dp(columns_c)
    full_ck, full_cr = full_c[:, :hidden_width], full_c[:, hidden_width:]
    full_cv = gather_dp(after(ffn_value, columns_c))
    attn = [dot(rows, own_o, NN).astype(BF) for rows in blocks_of(mixed, seq)]
    after_mix, normed_two = after_norm(inputs_b, scatter_seq(attn, here), rows_of(vec, 10, 11), here)

    normed_two = gather_seq(normed_two)
    if seq == 4:
        grad_all = gather_second(grad_b, *after(pieces_c[1:3], normed_two))
    mix_k2, mix_r2, step_two, recept_pre, opened = mixes(
        turn_pieces(normed_two), marks, rows_of(turned, 10, 11, 12, 13), 2, False, within, here, tile,
        own_rows // tile, [(1, full_cr, 0, part)], True,
    )
    opened = gather_seq(after(opened, grad_all[3:]))
    key_pre = dot(mix_k2, full_ck, NN)
    smooth = jax.nn.softplus(key_pre)
    hidden = (smooth * smooth).astype(BF)
    slope = (2.0 * smooth * jax.nn.sigmoid(key_pre)).astype(BF)
    hidden, slope = lax.optimization_barrier((hidden, slope))
    later = after(hidden, opened[1:3])
    value_parts = [columns_product(later if j < 2 else hidden, full_cv, part, j, here, seq) for j in reversed(range(seq))]
    value_parts = value_parts[::-1]
    value_relayed = scatter_relay(value_parts, scatter_start(value_parts), here)
    d_value = spread_columns(
        grad_all, by_block(after(opened, value_parts, value_relayed)), here, True, True, tile, own_rows // tile
    )

    grad_cv = dot(hidden, d_value, TN).astype(BF)
    summed_cv = scatter_dp(grad_cv)
    value_terms = scatter_end(value_parts[0], value_relayed)
    d_hidden = dot(after(d_value, grad_cv), full_cv, NT)
    d_key_two = (d_hidden * slope.astype(F32)).astype(BF)
    channel, d_recept_two = channel_out(value_terms, recept_pre, grad_all, here, tile)
    grad_ck, grad_cr = [], []

    def beside_two(relayed):
        grad_ck.append(dot(after(mix_k2, relayed), d_key_two, TN).astype(BF))
        grad_cr.append(dot(after(mix_r2, relayed, grad_ck), d_recept_two, TN).astype(BF))
        return grad_ck, grad_cr

    terms_two, sums_two = mixes_back_scatter(
        [(0, d_key_two, 0, full_c, 0, hidden_width), (1, d_recept_two, 0, full_cr, 0, part)],
        step_two, marks, rows_of(turned, 12, 13), here, seq, beside_two,
    )
    summed_ck = scatter_dp(grad_ck[0])
    if within is None:
        terms_two = [outside(t, groups, unit, back=True) for t in terms_two]
    d_after, d_attn, norm_sums_two = norm_back(terms_two, after_mix, grad_b, rows_of(vec, 10), within, here)

    pieces = gather_seq(d_attn)
    *near, far = by_block(pieces)
    near_mixed = [dot(d, own_o, NT).astype(BF) for d in near]
    *near_rows, far_rows = blocks_of(mixed, seq)
    near_wo = sum(dot(m, d, TN) for m, d in zip(near_rows, near))
    far = after(far, near_mixed, near_wo, summed_cv)
    d_mixed = jnp.concatenate([*near_mixed, dot(far, own_o, NT).astype(BF)], axis=0)
    grad_wo = (near_wo + dot(far_rows, far, TN)).astype(BF)
    summed_o = scatter_dp(grad_wo)
    d_mixed = after(d_mixed, summed_ck, grad_wo)
    d_wkv, d_gate, gate_sums = gate_backward(wkv, gate_pre, d_mixed, tables[5], here)
    grad_g = dot(mix_g, d_gate, TN).astype(BF)
    summed_crg = scatter_dp(jnp.concatenate([grad_cr[0], grad_g], axis=1))
    d_recept, d_keyed, d_valued, sums = wkv_backward(
        recept, keyed, valued, after(d_wkv, grad_g), states, tables, here, per
    )
    channel = after(trade_seq(blocks_of(after(channel, d_mixed), seq)), d_recept)
    grads_in = [
        dot(after(m, channel), d, TN).astype(BF)
        for m, d in ((mix_r, d_recept), (mix_k, d_keyed), (mix_v, d_valued))
    ]
    summed_in = scatter_dp(jnp.concatenate(grads_in, axis=1))
    others = []

    def beside(relayed):
        others.append(spread_columns([after_mix], after(channel, relayed), here, False, False, CHUNK, per))
        others.append(after(summed_cv, relayed).astype(F32))
        return others

    d_recept, d_keyed = after((d_recept, d_keyed), grads_in, summed_o)
    terms, sums_one = mixes_back_scatter(
        [(i, d, 0, full_in, i, part) for i, d in enumerate((d_recept, d_keyed, d_valued))]
        + [(3, d_gate, 0, full_g, 0, part)],
        step, marks, rows_of(turned, 2, 3, 4, 5), here, seq, beside,
    )
    out_rows, sum_cv = others
    if within is None:
        terms = [outside(t, groups, unit, back=True) for t in terms]
    tokens_grad, _, norm_sums = norm_back(terms, inputs_b, d_after, rows_of(vec, 0), within, here)

    summed_c = jnp.concatenate(after([summed_ck, summed_crg], terms), axis=1)
    sum_ck, sum_cr, sum_g = owners_rows(summed_c, [ffn_key.shape[1], width, width])
    sum_o = summed_o.astype(F32)

    def by_device(rows, turn):
        if turn:
            return rows.reshape(-1, dp, seq, unit).transpose(1, 2, 0, 3)
        return rows.reshape(-1, seq, dp, unit).transpose(2, 1, 0, 3)

    own_sums = jnp.stack([sums[0] * log_decay, sums[1], gate_sums[0], gate_sums[1]])
    own_sums = lax.dynamic_update_slice(jnp.zeros((4, width), F32), own_sums, (0, place * part))
    vector_rows = jnp.concatenate(
        [
            by_device(norm_sums[:2], False), by_device(sums_one[:4], True), by_device(own_sums, False),
            by_device(norm_sums_two[:2], False), by_device(sums_two[:2], True),
        ],
        axis=2,
    )
    sum_vec = scatter_small(vector_rows.reshape((-1,) + vector_rows.shape[2:]), sum_ck)
    sum_r, sum_k, sum_v = owners_rows(after(summed_in, sum_vec), [width] * 3)
    return (
        out_rows[None], tokens_grad[None], sum_r, sum_k, sum_v, sum_g, sum_o,
        sum_ck, sum_cr, sum_cv, sum_vec,
    )


def solution(mesh):
    tokens = P("dp", "seq", None)
    rows = P(("seq", "dp"), None)
    columns = P(None, ("seq", "dp"))
    return jax.shard_map(
        shards,
        mesh=mesh,
        in_specs=(tokens, P("dp", None), tokens) + (rows,) * 8 + (columns,),
        out_specs=(tokens, tokens) + (rows,) * 8 + (columns,),
        check_vma=False,
    )
```

```python
from functools import partial

import jax
import jax.numpy as jnp
from jax import lax
from jax.experimental import pallas as pl
from jax.experimental.pallas import tpu as pltpu
from jax.sharding import PartitionSpec as P

HEAD = 64
PAIR = 128
CHUNK = 128
EPSILON = 1e-05
GROUP_EPSILON = 1.0
BF = jnp.bfloat16
F32 = jnp.float32
NT = (((1,), (1,)), ((), ()))
TN = (((0,), (0,)), ((), ()))
NN = (((1,), (0,)), ((), ()))


def swap(value, axis, distance):
    size = lax.axis_size(axis)
    return lax.ppermute(value, axis, [(i, i ^ distance) for i in range(size)])


def after(value, *others):
    return lax.optimization_barrier((value, others))[0]


def gather_second(part, one, two):
    half = part.shape[0] // 2
    columns = part.shape[1]
    low, high = swap(one[:half, :columns], "seq", 2), swap(two[half : 2 * half, :columns], "seq", 1)
    return [part, one, two, low, high]


def gather_seq(part, first=()):
    size = lax.axis_size("seq")
    if size == 4:
        half = part.shape[0] // 2
        one, two = swap(part, "seq", 1), swap(part, "seq", 2)
        one, two = after((one, two), first)
        low, high = swap(one[:half], "seq", 2), swap(two[half:], "seq", 1)
        return [part, one, two, low, high]
    return [part] + [swap(part, "seq", distance) for distance in range(1, size)]


def by_block(pieces):
    if lax.axis_size("seq") == 4:
        return pieces[:3] + [jnp.concatenate(pieces[3:], axis=0)]
    return pieces


def scatter_start(parts):
    if lax.axis_size("seq") != 4:
        return ()
    low, high = parts[3:] if len(parts) == 5 else blocks_of(parts[3], 2)
    return swap(low, "seq", 1), swap(high, "seq", 2)


def relay_body(here, one_ref, two_ref, low_ref, high_ref, one_out, two_out):
    one, two = one_ref[...], two_ref[...]
    first = pl.program_id(0) == 0
    low, high = low_ref[...].astype(F32), high_ref[...].astype(F32)
    one_out[...] = jnp.where(first, one, (one.astype(F32) + high).astype(BF))
    two_out[...] = jnp.where(first, (two.astype(F32) + low).astype(BF), two)


def scatter_relay(parts, started, here):
    if lax.axis_size("seq") != 4:
        return parts[1:]
    (_, one, two, *_), (low, high) = parts, started
    (rows, width), half = one.shape, block(low.shape, lambda i, h: (i, 0))
    return kernel(
        relay_body, "relay", (2,), here,
        [(one, half), (two, half), (low, fixed(low.shape)), (high, fixed(low.shape))],
        [((rows, width), BF, half)] * 2,
    )


def scatter_end(own, relayed):
    return [own] + [swap(part, "seq", j + 1) for j, part in enumerate(relayed)]


def scatter_seq(parts, here):
    return scatter_end(parts[0], scatter_relay(parts, scatter_start(parts), here))


def trade_seq(parts):
    return [parts[0]] + [swap(part, "seq", j + 1) for j, part in enumerate(parts[1:])]


def blocks_of(values, size):
    rows = values.shape[0] // size
    return [values[j * rows : (j + 1) * rows] for j in range(size)]


def bits_of(size):
    return [1 << b for b in range(size.bit_length() - 1)]


def gather_small(part, axis):
    for bit in bits_of(lax.axis_size(axis)):
        other = swap(part, axis, bit)
        second = (lax.axis_index(axis) & bit) != 0
        part = jnp.concatenate([jnp.where(second, other, part), jnp.where(second, part, other)], axis=0)
    return part


def scatter_small(parts, axis, before_last=()):
    for bit in reversed(bits_of(lax.axis_size(axis))):
        parts = after(parts, before_last) if bit == 1 else parts
        half = parts.shape[0] // 2
        second = (lax.axis_index(axis) & bit) != 0
        low, high = parts[:half], parts[half:]
        parts = jnp.where(second, high, low) + swap(jnp.where(second, low, high), axis, bit)
    return parts


def block(shape, index):
    return pl.BlockSpec(shape, lambda *i: index(*i[:-1], i[-1][0]))


def fixed(shape):
    return pl.BlockSpec(shape, lambda *i: (0,) * len(shape))


def relative(tile, per, here):
    return (lax.div(tile, per) ^ here) * per + lax.rem(tile, per)


def kernel(body, name, grid, here, ins, outs, scratch=(), vmem=48):
    return pl.pallas_call(
        body,
        out_shape=[jax.ShapeDtypeStruct(shape, kind) for shape, kind, _ in outs],
        grid_spec=pltpu.PrefetchScalarGridSpec(
            num_scalar_prefetch=1,
            grid=grid,
            in_specs=[spec for _, spec in ins],
            out_specs=[spec for _, _, spec in outs],
            scratch_shapes=list(scratch),
        ),
        compiler_params=pltpu.CompilerParams(vmem_limit_bytes=vmem * 2**20),
        name=name,
    )(here, *[array for array, _ in ins])


def pieced(pieces, tile, columns, column, place):
    ins, start = [], 0
    for piece in pieces:
        count = piece.shape[0] // tile

        def index(i, h, start=start, count=count):
            return jnp.clip(place(i, h) - start, 0, count - 1), column(h)

        ins.append((piece, block((tile, columns), index)))
        start += count
    return ins


def picked(refs, counts, tile, held):
    start = 0
    for ref, count in zip(refs, counts):

        @pl.when((tile >= start) & (tile < start + count))
        def _(ref=ref):
            held[...] = ref[...]

        start += count
    return held[...].astype(F32)


def counts_of(pieces, tile):
    return [piece.shape[0] // tile for piece in pieces]


def row_index(rows):
    return lax.broadcasted_iota(jnp.int32, (rows, 1), 0)


def placed(place, width):
    return pl.ds(pl.multiple_of(place * width, width), width)


def cut_body(count, parts, here, *refs):
    ins, beside, outs = refs[:count], refs[count], refs[count + 1 :]
    rows = ins[0].shape[0]
    for j in range(parts):
        outs[j][rows:, :] = jnp.zeros_like(outs[j][rows:, :])
        outs[j][rows:, : beside.shape[1]] = beside[...]
    at = 0
    for ref in ins:
        width = ref.shape[1] // parts
        for j in range(parts):
            outs[j][:rows, at : at + width] = ref[:, placed(here[0] ^ j, width)]
        at += width


def cut_columns(weights, beside, here, parts):
    rows, width = weights[0].shape[0] + beside.shape[0], sum(w.shape[1] for w in weights) // parts
    return kernel(
        partial(cut_body, len(weights), parts), "cut_columns", (1,), here,
        [(w, fixed(w.shape)) for w in [*weights, beside]],
        [((rows, width), BF, fixed((rows, width)))] * parts,
    )


def stack_body(parts, here, *refs):
    start = 0
    outs, beside = refs[parts:-1], refs[-1]
    for out in outs:
        for j in range(parts):
            out[here[0] ^ j] = refs[j][: out.shape[1], start : start + out.shape[2]]
        start += out.shape[2]
    for j in range(parts):
        beside[here[0] ^ j] = refs[j][out.shape[1] :, : beside.shape[2]]


def stack_rows(pieces, widths, beside, here):
    parts, rows = len(pieces), pieces[0].shape[0] - beside.shape[0]
    shapes = [(parts, rows, width) for width in widths] + [(parts,) + beside.shape]
    return kernel(
        partial(stack_body, parts), "stack_rows", (1,), here,
        [(p, fixed(p.shape)) for p in pieces],
        [(shape, BF, fixed(shape)) for shape in shapes],
    )


def ride_body(count, here, *refs):
    ins, rider, outs = refs[:count], refs[count], refs[count + 1 :]
    for j, out in enumerate(outs):
        top, at = 0, 0
        if j in (1, 2):
            top = rider.shape[0]
            out[:top, : rider.shape[1]] = rider[...]
            out[:top, rider.shape[1] :] = jnp.zeros_like(out[:top, rider.shape[1] :])
        for ref in ins:
            width = ref.shape[1] // 4
            out[top:, at : at + width] = ref[:, placed(here[0] ^ j, width)]
            at += width


def cut_with_rider(weights, rider, here):
    rows, width = weights[0].shape[0], sum(w.shape[1] for w in weights) // 4
    return kernel(
        partial(ride_body, len(weights)), "cut_columns", (1,), here,
        [(w, fixed(w.shape)) for w in [*weights, rider]],
        [((n, width), BF, fixed((n, width))) for n in (rows, rows + rider.shape[0], rows + rider.shape[0], rows)],
    )


def unride_body(here, *refs):
    out = refs[-1]
    rows = out.shape[1]
    for j, ref in enumerate(refs[:-1]):
        out[here[0] ^ j] = ref[ref.shape[0] - rows :, :]


def stack_below(pieces, here):
    shape = (4,) + pieces[0].shape
    (stacked,) = kernel(
        unride_body, "stack_rows", (1,), here,
        [(p, fixed(p.shape)) for p in pieces],
        [(shape, BF, fixed(shape))],
    )
    return stacked.reshape(-1, shape[-1])


def hold_body(here, in_ref, *refs):
    refs[-1][...] = in_ref[...]


def held_back(values, here, *others):
    rows, width = values.shape
    own = block((rows // 2, width), lambda i, h: (i, 0))
    (copy,) = kernel(
        hold_body, "hold", (2,), here,
        [(values, own)] + [(o, pl.BlockSpec(memory_space=pl.ANY)) for o in others],
        [((rows, width), values.dtype, own)],
    )
    return copy


def join_body(parts, count, here, *refs):
    ins, outs = refs[:parts], refs[parts:]
    at = 0
    for ref in outs:
        width = ref.shape[1] // parts
        for j in range(parts):
            ref[:, placed(here[0] ^ j, width)] = ins[j][:, at : at + width].astype(F32)
        at += width


def join_columns(pieces, widths, here):
    parts, rows = len(pieces), pieces[0].shape[0]
    return kernel(
        partial(join_body, parts, len(widths)), "join_columns", (1,), here,
        [(p, fixed(p.shape)) for p in pieces],
        [((rows, width), F32, fixed((rows, width))) for width in widths],
    )


def spread_body(counts, parts, product, here, *refs):
    bases, pieces, out, held = refs[: len(counts)], refs[len(counts) : -2], refs[-2], refs[-1]
    picked(bases, counts, pl.program_id(0), held)
    width = pieces[0].shape[1]
    for j in range(parts):
        at = placed(here[0] ^ j, width)
        piece, base = pieces[j][...].astype(F32), held[:, at].astype(F32)
        out[:, at] = (base * piece if product else base + piece).astype(BF)


def spread_columns(bases, columns, here, product, turn, tile, per):
    rows, width = sum(counts_of(bases, tile)) * tile, bases[0].shape[1]

    def turned(i, j):
        return (lax.div(i, per) ^ j) * per + lax.rem(i, per) if turn else i

    (result,) = kernel(
        partial(spread_body, counts_of(bases, tile), len(columns), product), "spread_columns", (rows // tile,), here,
        pieced(bases, tile, width, lambda h: 0, lambda i, h: i)
        + [(c, block((tile, c.shape[1]), lambda i, h, j=j: (turned(i, j), 0))) for j, c in enumerate(columns)],
        [((rows, width), BF, block((tile, width), lambda i, h: (i, 0)))],
        [pltpu.VMEM((tile, width), bases[0].dtype)],
    )
    return result


def shuffled(values, groups, back=False):
    seq, dp = groups
    if back:
        seq, dp = dp, seq
    lane = lax.broadcasted_iota(jnp.int32, (1, PAIR), 1) < HEAD
    source = [s * dp + d for d in range(dp) for s in range(seq)]
    columns = []
    for one, two in zip(source[::2], source[1::2]):
        low = values[:, one // 2 * PAIR : (one // 2 + 1) * PAIR]
        high = values[:, two // 2 * PAIR : (two // 2 + 1) * PAIR]
        low = pltpu.roll(low, HEAD, 1) if one % 2 else low
        high = high if two % 2 else pltpu.roll(high, HEAD, 1)
        columns.append(jnp.where(lane, low, high))
    return jnp.concatenate(columns, axis=1)


def outside(values, groups, channels, back=False):
    seq, dp = groups[::-1] if back else groups
    return values.reshape(-1, seq, dp, channels).swapaxes(1, 2).reshape(values.shape)


def centre(values):
    centred = values - jnp.mean(values, axis=-1, keepdims=True)
    spread = jnp.mean(centred * centred, axis=-1, keepdims=True)
    return centred, lax.rsqrt(spread + EPSILON)


def mix_body(count, norm, groups, counts, per, mixed, open_up, here, *refs):
    pieces, (marks_ref, vec_ref) = refs[: len(counts)], refs[len(counts) : len(counts) + 2]
    weights = refs[len(counts) + 2 : len(counts) + 2 + len(mixed)]
    outs, last, held = refs[len(counts) + 2 + len(mixed) : -2], refs[-2], refs[-1]
    products = outs[count + 1 :]

    @pl.when(pl.program_id(0) == 0)
    def _():
        last[...] = jnp.zeros_like(last)

    values = picked(pieces, counts, relative(pl.program_id(0), per, here[0]), held)
    if norm:
        centred, inverse = centre(values)
        values = centred * inverse
    if groups:
        values = shuffled(values, groups)
    if norm:
        values = values * vec_ref[0:1, :] + vec_ref[1:2, :]
    rows = values.shape[0]
    previous = jnp.where(row_index(rows) == 0, last[0:1, :], pltpu.roll(values, 1, 0)) * marks_ref[:, 3:4]
    last[0:1, :] = values[rows - 1 :, :]
    step = values - previous
    outs[count][...] = step.astype(BF)
    for i in range(count):
        mix = (previous + step * vec_ref[2 + i : 3 + i, :]).astype(BF)
        outs[i][...] = mix
        if i in mixed:
            k = mixed.index(i)
            product = dot(mix, weights[k][...], NN)
            if open_up:
                products[0][...] = product
                products[1][...] = (1.0 / (1.0 + jnp.exp(-product))).astype(BF)
            else:
                products[k][...] = product.astype(BF)


def mixes(pieces, marks, vec, count, norm, groups, here, tile, per, weights, open_up):
    rows, width = marks.shape[0], pieces[0].shape[1]
    own = block((tile, width), lambda i, h: (relative(i, per, h), 0))
    outs = [((rows, width), BF, own)] * (count + 1)
    for _, _, _, part in weights:
        narrow = block((tile, part), lambda i, h: (relative(i, per, h), 0))
        outs += [((rows, part), F32 if open_up else BF, narrow)] + [((rows, part), BF, narrow)] * open_up
    return kernel(
        partial(mix_body, count, norm, groups, counts_of(pieces, tile), per, [w[0] for w in weights], open_up),
        "mixes", (rows // tile,), here,
        pieced(pieces, tile, width, lambda h: 0, lambda i, h: relative(i, per, h))
        + [(marks, block((tile, PAIR), lambda i, h: (i, 0))), (vec, fixed(vec.shape))]
        + [(w, pl.BlockSpec((width, part), lambda *_, at=at: (0, at))) for _, w, at, part in weights],
        outs,
        [pltpu.VMEM((8, width), F32), pltpu.VMEM((tile, width), BF)],
        vmem=58,
    )


def mixes_back_body(which, first, seq, outs, here, *refs):
    count = len(which)
    grads, nexts, weights = refs[:count], refs[count : 2 * count], refs[2 * count : 3 * count]
    step_ref, marks_ref, next_marks_ref, vec_ref, *out_refs, sums_ref = refs[3 * count :]

    @pl.when(pl.program_id(1) == 0)
    def _():
        sums_ref[...] = jnp.zeros_like(sums_ref)

    step = step_ref[...].astype(F32)
    rows = step.shape[0]
    total = straight = None
    for i in range(which[-1] + 1):
        grad = sum(
            dot(jnp.concatenate([grads[k][...], nexts[k][...]], axis=0), weights[k][...], NT)
            for k in range(count)
            if which[k] == i
        )
        sums_ref[i : i + 1, :] += jnp.sum(grad[:rows] * step, axis=0, keepdims=True)
        part = grad * vec_ref[i : i + 1, :]
        total, straight = (total + grad, straight + part) if i else (grad, part)
    inside = ((first + pl.program_id(1)) ^ here[0]) < seq - 1
    keep = jnp.concatenate([marks_ref[:, 3:4], jnp.where(inside, next_marks_ref[:, 3:4], 0.0)], axis=0)
    kept = (total - straight) * keep
    up = pltpu.roll(kept, kept.shape[0] - 1, 0)
    result = (straight[:rows] + up[:rows]).astype(BF)
    if len(out_refs) == 1:
        out_refs[0][...] = result
        return
    if outs == 1:
        out_refs[0][...] = result[: rows // 2]
        out_refs[1][...] = result[rows // 2 :]
        return
    for k, out_ref in enumerate(out_refs):

        @pl.when(pl.program_id(1) == k)
        def _(out_ref=out_ref):
            out_ref[...] = result


EXTRA = 16


def mixes_back(terms, step, marks, vec, here, seq, first, count, halves=False):
    rows, width = step.shape
    tile, columns = rows // seq, min(512, width)
    extras = tile // EXTRA

    def following(i, h):
        return jnp.minimum(((first + i) ^ h) + 1, seq - 1)

    ins = [(g, block((tile, n), lambda c, i, h, at=at: (first + i, at))) for _, g, at, _, _, n in terms]
    ins += [
        (g, block((EXTRA, n), lambda c, i, h, at=at: ((following(i, h) ^ h) * extras, at)))
        for _, g, at, _, _, n in terms
    ]
    ins += [(w, block((columns, n), lambda c, i, h, at=at: (c, at))) for _, _, _, w, at, n in terms]
    ins += [
        (step, block((tile, columns), lambda c, i, h: (first + i, c))),
        (marks, block((tile, PAIR), lambda c, i, h: ((first + i) ^ h, 0))),
        (marks, block((EXTRA, PAIR), lambda c, i, h: (following(i, h) * extras, 0))),
        (vec, block((8, columns), lambda c, i, h: (0, c))),
    ]
    size = tile // 2 if halves else tile
    *parts, sums = kernel(
        partial(mixes_back_body, [t[0] for t in terms], first, seq, count), "mixes_back", (width // columns, count), here, ins,
        [((size, width), BF, block((size, columns), lambda c, i, h: (0, c)))] * (2 if halves else count)
        + [((8, width), F32, block((8, columns), lambda c, i, h: (0, c)))],
    )
    return parts, sums


def mixes_back_scatter(terms, step, marks, vec, here, seq, beside):
    if seq != 4:
        parts, sums = mixes_back(terms, step, marks, vec, here, seq, 0, seq)
        return after(scatter_seq(parts, here), beside(parts)), sums

    def call(first, count, *before):
        ordered = after([t[1] for t in terms], *before)
        return mixes_back(
            [(t[0], g) + t[2:] for t, g in zip(terms, ordered)], step, marks, vec, here, seq, first, count, first == 3
        )

    far, sums_far = call(3, 1)
    near, sums_near = call(1, 2, far)
    parts = [None, *near, *far]
    started = after(scatter_start(parts), near)
    relayed = scatter_relay(parts, started, here)
    (own,), sums_own = call(0, 1, near, relayed)
    return after(scatter_end(own, relayed), beside(relayed)), sums_far + sums_near + sums_own


def after_body(count, here, x_ref, vec_ref, *refs):
    after_ref, normed_ref = refs[count:]
    after = x_ref[...].astype(F32)
    for ref in refs[:count]:
        after = after + ref[...].astype(F32)
    after_ref[...] = after
    centred, inverse = centre(after)
    normed_ref[...] = (centred * inverse * vec_ref[0:1, :] + vec_ref[1:2, :]).astype(BF)


def after_norm(inputs, terms, vec, here):
    rows, width = inputs.shape
    own = block((CHUNK, width), lambda i, h: (i, 0))
    return kernel(
        partial(after_body, len(terms)), "after_norm", (rows // CHUNK,), here,
        [(inputs, own), (vec, fixed(vec.shape))] + [(t, own) for t in terms],
        [((rows, width), F32, own), ((rows, width), BF, own)],
    )


def norm_back_body(count, groups, here, x_ref, base_ref, vec_ref, *refs):
    wide_ref, narrow_ref, sums_ref = refs[count:]

    @pl.when(pl.program_id(0) == 0)
    def _():
        sums_ref[...] = jnp.zeros_like(sums_ref)

    grad = refs[0][...].astype(F32)
    for ref in refs[1:count]:
        grad = grad + ref[...].astype(F32)
    if groups:
        grad = shuffled(grad, groups, back=True)
    centred, inverse = centre(x_ref[...].astype(F32))
    normed = centred * inverse
    sums_ref[0:1, :] += jnp.sum(grad * normed, axis=0, keepdims=True)
    sums_ref[1:2, :] += jnp.sum(grad, axis=0, keepdims=True)
    grad = grad * vec_ref[0:1, :]
    grad = grad - jnp.mean(grad, axis=-1, keepdims=True) - normed * jnp.mean(grad * normed, axis=-1, keepdims=True)
    result = base_ref[...].astype(F32) + inverse * grad
    wide_ref[...] = result
    narrow_ref[...] = result.astype(BF)


def norm_back(terms, inputs, base, vec, groups, here):
    rows, width = inputs.shape
    own = block((CHUNK, width), lambda i, h: (i, 0))
    return kernel(
        partial(norm_back_body, len(terms), groups), "norm_back", (rows // CHUNK,), here,
        [(inputs, own), (base, own), (vec, fixed(vec.shape))] + [(t, own) for t in terms],
        [((rows, width), F32, own), ((rows, width), BF, own), ((8, width), F32, fixed((8, width)))],
    )


def gate_body(mix_ref, weight_ref, wkv_ref, par_ref, gate_ref, mixed_ref):
    gate = dot(mix_ref[...], weight_ref[...], NN)
    gate_ref[...] = gate
    ones = jnp.where(same_head(), 1.0, 0.0).astype(BF)
    for pair in range(gate.shape[1] // PAIR):
        at = slice(pair * PAIR, (pair + 1) * PAIR)
        wkv = wkv_ref[:, at]
        centred = wkv - head_sum_fine(wkv, ones) * (1.0 / HEAD)
        spread = head_sum(centred * centred, ones) * (1.0 / HEAD)
        normed = centred * lax.rsqrt(spread + GROUP_EPSILON) * par_ref[1:2, at] + par_ref[2:3, at]
        mixed_ref[:, at] = (normed * (gate[:, at] / (1.0 + jnp.exp(-gate[:, at])))).astype(BF)


def gated(mix_g, weights, wkv, params, here, seq):
    rows, width = mix_g.shape
    tile, part = rows // seq, wkv.shape[1]
    own = block((tile, part), lambda i, h: (i, 0))
    return kernel(
        lambda here, *refs: gate_body(*refs), "gate", (seq,), here,
        [
            (mix_g, block((tile, width), lambda i, h: (i, 0))),
            (weights, block((width, part), lambda i, h: (0, 0))),
            (wkv, own),
            (params, fixed(params.shape)),
        ],
        [((rows, part), F32, own), ((rows, part), BF, own)],
    )


def columns_body(here, left_ref, right_ref, out_ref):
    out_ref[...] = dot(left_ref[...], right_ref[...], NN).astype(BF)


def columns_product(left, right, part, relative_to, here, seq):
    rows, depth = left.shape
    tile = rows // seq
    (result,) = kernel(
        columns_body, "value_columns", (seq,), here,
        [
            (left, block((tile, depth), lambda i, h: (i, 0))),
            (right, block((depth, part), lambda i, h: (0, h ^ relative_to))),
        ],
        [((rows, part), BF, block((tile, part), lambda i, h: (i ^ relative_to, 0)))],
    )
    return result


def channel_body(counts, here, pre_ref, *refs):
    grads, terms, (channel_ref, d_recept_ref, held) = refs[: len(counts)], refs[len(counts) : -3], refs[-3:]
    value = sum(ref[...].astype(F32) for ref in terms)
    opened = 1.0 / (1.0 + jnp.exp(-pre_ref[...]))
    channel = opened * value
    channel_ref[...] = channel.astype(BF)
    grad = picked(grads, counts, pl.program_id(0), held)
    d_recept_ref[...] = (grad * channel * (1.0 - opened)).astype(BF)


def channel_out(terms, pre, grads, here, tile):
    rows, part = pre.shape
    own = block((tile, part), lambda i, h: (i, 0))
    return kernel(
        partial(channel_body, counts_of(grads, tile)), "channel", (rows // tile,), here,
        [(pre, own)] + pieced(grads, tile, part, lambda h: h, lambda i, h: i) + [(t, own) for t in terms],
        [((rows, part), BF, own)] * 2,
        [pltpu.VMEM((tile, part), BF)],
    )


def head_masks():
    lane = lax.broadcasted_iota(jnp.int32, (1, PAIR), 1)
    first = (lane < HEAD).astype(F32)
    return first, 1.0 - first


def same_head():
    row = lax.broadcasted_iota(jnp.int32, (PAIR, PAIR), 0) < HEAD
    column = lax.broadcasted_iota(jnp.int32, (PAIR, PAIR), 1) < HEAD
    return row == column


def dot(left, right, dims):
    return lax.dot_general(left, right, dims, preferred_element_type=F32)


def head_sum(values, ones):
    return dot(values.astype(BF), ones, NN)


def head_sum_fine(values, ones):
    coarse = values.astype(BF)
    rest = (values - coarse.astype(F32)).astype(BF)
    return dot(coarse, ones, NN) + dot(rest, ones, NN)


def stacked(values, first, second):
    return jnp.concatenate([(values * first).astype(BF), (values * second).astype(BF)], axis=0)


def masks_of(rows_ref, columns_ref):
    segment = rows_ref[:, 0:1]
    reaches = rows_ref[:, 1:2]
    last_same = rows_ref[:, 2:3]
    reach_last = rows_ref[CHUNK - 1 : CHUNK, 1:2]
    before = lax.broadcasted_iota(jnp.int32, (CHUNK, CHUNK), 1) < lax.broadcasted_iota(
        jnp.int32, (CHUNK, CHUNK), 0
    )
    allowed = jnp.where((segment == columns_ref[0:1, :]) & before, 1.0, 0.0)
    return reaches, last_same, reach_last, jnp.concatenate([allowed, allowed], axis=0)


def wkv_forward_body(
    here, r_ref, k_ref, v_ref, rows_ref, columns_ref, grow_ref, shrink_ref, tail_ref, par_ref,
    wkv_ref, states_ref, state,
):
    @pl.when(pl.program_id(0) == 0)
    def _():
        state[...] = jnp.zeros_like(state)

    first, second = head_masks()
    block = same_head()
    ones = jnp.where(block, 1.0, 0.0).astype(BF)
    reaches, last_same, reach_last, allowed = masks_of(rows_ref, columns_ref)
    for pair in range(r_ref.shape[1] // PAIR):
        at = slice(pair * PAIR, (pair + 1) * PAIR)
        r, k, v = r_ref[:, at].astype(F32), k_ref[:, at].astype(F32), v_ref[:, at].astype(F32)
        bonus, decay = par_ref[0:1, at], par_ref[3:4, at]
        held = state[at, :]
        held_b = held.astype(BF)
        states_ref[0, at, :] = held_b
        grown = r * grow_ref[:, at]
        shrunk = (k * shrink_ref[:, at]).astype(BF)
        scores = (dot(stacked(grown, first, second), shrunk, NT) * allowed).astype(BF)
        both = jnp.concatenate([scores[:CHUNK], scores[CHUNK:]], axis=1)
        wkv = dot(both, stacked(v, first, second), NN)
        wkv = wkv + dot((grown * reaches).astype(BF), held_b, NT)
        wkv = wkv + head_sum(r * bonus * k, ones) * v
        fresh = dot(v_ref[:, at], (k * tail_ref[:, at] * last_same).astype(BF), TN)
        state[at, :] = held * (decay * reach_last) + jnp.where(block, fresh, 0.0)
        wkv_ref[:, at] = wkv


def wkv_backward_body(
    here, r_ref, k_ref, v_ref, d_wkv_ref, states_ref,
    rows_ref, columns_ref, grow_ref, shrink_ref, tail_ref, par_ref,
    d_r_ref, d_k_ref, d_v_ref, sums_ref, d_state,
):
    @pl.when(pl.program_id(0) == 0)
    def _():
        d_state[...] = jnp.zeros_like(d_state)
        sums_ref[...] = jnp.zeros_like(sums_ref)

    first, second = head_masks()
    block = same_head()
    ones = jnp.where(block, 1.0, 0.0).astype(BF)
    reaches, last_same, reach_last, allowed = masks_of(rows_ref, columns_ref)
    offset = lax.broadcasted_iota(jnp.int32, (CHUNK, PAIR), 0).astype(F32)
    for pair in range(r_ref.shape[1] // PAIR):
        at = slice(pair * PAIR, (pair + 1) * PAIR)
        bonus, decay = par_ref[0:1, at], par_ref[3:4, at]
        d_wkv = d_wkv_ref[:, at].astype(F32)
        r, k, v = r_ref[:, at].astype(F32), k_ref[:, at].astype(F32), v_ref[:, at].astype(F32)
        v_b, d_wkv_b = v_ref[:, at], d_wkv_ref[:, at]
        grow, shrink, tail = grow_ref[:, at], shrink_ref[:, at], tail_ref[:, at] * last_same
        held = states_ref[0, at, :]
        later = d_state[at, :]
        later_b = later.astype(BF)
        grown = r * grow
        shrunk = k * shrink
        shrunk_b = shrunk.astype(BF)
        tailed_b = (k * tail).astype(BF)
        grown_two = stacked(grown, first, second)
        d_wkv_two = stacked(d_wkv, first, second)
        scores = (dot(grown_two, shrunk_b, NT) * allowed).astype(BF)
        d_scores = (dot(d_wkv_two, v_b, NT) * allowed).astype(BF)
        d_both = jnp.concatenate([d_scores[:CHUNK], d_scores[CHUNK:]], axis=1)
        d_grown = dot(d_both, stacked(shrunk, first, second), NN)
        d_grown = d_grown + dot((d_wkv * reaches).astype(BF), held, NN)
        d_shrunk = dot(d_scores, grown_two, TN)
        d_tailed = dot(v_b, later_b, NN)
        share = head_sum(r * bonus * k, ones)
        d_share = head_sum(d_wkv * v, ones)
        d_v = dot(scores, d_wkv_two, TN) + dot(tailed_b, later_b, NT) + share * d_wkv
        d_r_ref[:, at] = (d_grown * grow + d_share * bonus * k).astype(BF)
        d_k_ref[:, at] = (d_shrunk * shrink + d_tailed * tail + d_share * bonus * r).astype(BF)
        d_v_ref[:, at] = d_v.astype(BF)
        carried = decay * reach_last
        d_fresh = dot(d_wkv_b, (grown * reaches).astype(BF), TN)
        d_state[at, :] = later * carried + jnp.where(block, d_fresh, 0.0)
        grown_b = grown.astype(BF).astype(F32)
        d_log = (
            offset * grown_b * d_grown
            - (offset + 1.0) * shrunk_b.astype(F32) * d_shrunk
            + (CHUNK - 1.0 - offset) * tailed_b.astype(F32) * d_tailed
        )
        kept = CHUNK * carried * jnp.sum(held.astype(F32) * later, axis=0, keepdims=True)
        sums_ref[0:1, at] += jnp.sum(d_log, axis=0, keepdims=True) + kept
        sums_ref[1:2, at] += jnp.sum(d_share * r * k, axis=0, keepdims=True)


def gate_backward_body(here, wkv_ref, g_ref, d_mixed_ref, par_ref, d_wkv_ref, d_g_ref, sums_ref):
    @pl.when(pl.program_id(0) == 0)
    def _():
        sums_ref[...] = jnp.zeros_like(sums_ref)

    ones = jnp.where(same_head(), 1.0, 0.0).astype(BF)
    for pair in range(wkv_ref.shape[1] // PAIR):
        at = slice(pair * PAIR, (pair + 1) * PAIR)
        gain, bias = par_ref[1:2, at], par_ref[2:3, at]
        wkv, gate, d_mixed = wkv_ref[:, at], g_ref[:, at], d_mixed_ref[:, at].astype(F32)
        centred = wkv - head_sum_fine(wkv, ones) * (1.0 / HEAD)
        spread = head_sum(centred * centred, ones) * (1.0 / HEAD)
        inverse = lax.rsqrt(spread + GROUP_EPSILON)
        normed = centred * inverse
        opened = 1.0 / (1.0 + jnp.exp(-gate))
        d_scaled = d_mixed * gate * opened
        d_g = d_mixed * (normed * gain + bias) * opened * (1.0 + gate * (1.0 - opened))
        d_g_ref[:, at] = d_g.astype(BF)
        d_normed = d_scaled * gain
        mean_one = head_sum(d_normed, ones) * (1.0 / HEAD)
        mean_two = head_sum(d_normed * normed, ones) * (1.0 / HEAD)
        d_wkv_ref[:, at] = (inverse * (d_normed - mean_one - normed * mean_two)).astype(BF)
        sums_ref[0:1, at] += jnp.sum(d_scaled * normed, axis=0, keepdims=True)
        sums_ref[1:2, at] += jnp.sum(d_scaled, axis=0, keepdims=True)


def gate_backward(wkv, gate, d_mixed, params, here):
    rows, part = wkv.shape
    own = block((2 * CHUNK, part), lambda i, h: (i, 0))
    return kernel(
        gate_backward_body, "gate_backward", (rows // (2 * CHUNK),), here,
        [(a, own) for a in (wkv, gate, d_mixed)] + [(params, fixed(params.shape))],
        [((rows, part), BF, own)] * 2 + [((8, part), F32, fixed((8, part)))],
    )


def wkv_blocks(width, chunks, per, backward):
    def chunk(i):
        return chunks - 1 - i if backward else i

    tokens = block((CHUNK, width), lambda i, h: (relative(chunk(i), per, h), 0))
    states = block((1, width, PAIR), lambda i, h: (chunk(i), 0, 0))
    tables = [
        block((CHUNK, PAIR), lambda i, h: (chunk(i), 0)),
        block((8, CHUNK), lambda i, h: (0, chunk(i))),
    ]
    return tokens, states, tables + [fixed((CHUNK, width))] * 3 + [fixed((8, width))]


def wkv_forward(r, k, v, tables, here, per):
    length, width = r.shape
    chunks = length // CHUNK
    tokens, states, blocks = wkv_blocks(width, chunks, per, False)
    return kernel(
        wkv_forward_body, "wkv_forward", (chunks,), here,
        [(a, tokens) for a in (r, k, v)] + list(zip(tables, blocks)),
        [((length, width), F32, tokens), ((chunks, width, PAIR), BF, states)],
        [pltpu.VMEM((width, PAIR), F32)],
    )


def wkv_backward(r, k, v, d_wkv, states_kept, tables, here, per):
    length, width = r.shape
    chunks = length // CHUNK
    tokens, states, blocks = wkv_blocks(width, chunks, per, True)
    return kernel(
        wkv_backward_body, "wkv_backward", (chunks,), here,
        [(a, tokens) for a in (r, k, v, d_wkv)] + [(states_kept, states)] + list(zip(tables, blocks)),
        [((length, width), BF, tokens)] * 3 + [((8, width), F32, fixed((8, width)))],
        [pltpu.VMEM((width, PAIR), F32)],
    )


def wkv_tables(piece, keep, log_decay, bonus, gain, bias):
    length = piece.shape[0]
    by_chunk = piece.reshape(length // CHUNK, CHUNK)
    before = jnp.concatenate([jnp.full((1,), -1, piece.dtype), by_chunk[:-1, -1]])
    reaches = (by_chunk == before[:, None]).reshape(-1)
    last_same = (by_chunk == by_chunk[:, -1:]).reshape(-1)
    marks = jnp.stack([piece.astype(F32), reaches.astype(F32), last_same.astype(F32), keep], axis=1)
    rows = jnp.pad(marks, ((0, 0), (0, PAIR - 4)))
    columns = jnp.broadcast_to(piece.astype(F32)[None], (8, length))
    offset = jnp.arange(CHUNK).astype(F32)[:, None]
    grow = jnp.exp(offset * log_decay)
    shrink = jnp.exp(-(offset + 1.0) * log_decay)
    tail = jnp.exp((CHUNK - 1.0 - offset) * log_decay)
    zero = jnp.zeros_like(bonus)
    params = jnp.stack([bonus, gain, bias, jnp.exp(CHUNK * log_decay)] + [zero] * 4)
    return rows, columns, grow, shrink, tail, params


def segment_of(lengths, positions):
    rank = jnp.arange(lengths.shape[0])
    starts = jnp.sum(jnp.where(rank[:, None] > rank[None, :], lengths[None, :], 0), axis=1)
    later_flags = (positions[:, None] >= starts[None, 1:]).astype(jnp.int32)
    first_flags = jnp.any(positions[:, None] == starts[None, :], axis=1)
    return (jnp.sum(later_flags, axis=1), first_flags)


def rows_of(vec, *rows):
    return jnp.pad(jnp.stack([vec[i] for i in rows]), ((0, 8 - len(rows)), (0, 0)))


def shards(
    tokens, seq_lengths, out_grad, w_receptance, w_key, w_value, w_gate, w_output,
    ffn_key, ffn_receptance, ffn_value, vectors,
):
    seq, dp = lax.axis_size("seq"), lax.axis_size("dp")
    place = lax.axis_index("seq")
    here = jnp.reshape(place, (1,)).astype(jnp.int32)
    inputs_b, grad_b = tokens[0], out_grad[0]
    own_rows, width = inputs_b.shape
    length, part, unit = own_rows * seq, width // seq, vectors.shape[1]
    per, tile = own_rows // CHUNK, own_rows // 2
    hidden_width = ffn_key.shape[1] // seq
    groups = (seq, dp)
    within = groups if unit == HEAD else None

    vectors_b = jnp.pad(vectors, ((0, 16 - vectors.shape[0]), (0, 0)))

    def stacked_columns(weights, widths, beside=()):
        cut = cut_columns(weights, vectors_b, here, seq)
        *stacked, last = stack_rows(after(trade_seq(cut), beside), widths, vectors_b, here)
        return [w.reshape(-1, w.shape[-1]) for w in stacked] + [last], cut

    def gather_dp(rows):
        return lax.all_gather(rows, "dp", axis=0, tiled=True)

    def scatter_dp(grad):
        return lax.psum_scatter(grad, "dp", scatter_dimension=0, tiled=True)

    def owners_parts(summed):
        rows = summed.shape[0] // seq
        return trade_seq([lax.dynamic_slice_in_dim(summed, (place ^ j) * rows, rows, 0) for j in range(seq)])

    def owners_rows(summed, widths):
        return join_columns(owners_parts(summed), widths, here)

    def turn_pieces(pieces):
        if within is not None:
            return pieces
        return [outside(p, groups, unit) for p in pieces]

    positions = jnp.arange(length, dtype=jnp.int32)
    piece, first_flags = segment_of(seq_lengths[0], positions)

    (columns_in, columns_g, vec_seq), cut = stacked_columns(
        [w_receptance, w_key, w_value, w_gate], [3 * part, part]
    )
    tokens_held = held_back(inputs_b, here, *cut)
    full_in = gather_dp(columns_in)
    vec_parts = gather_small(vec_seq[None, :, : vectors.shape[0]], "dp").astype(F32)
    vec = vec_parts.transpose(2, 1, 0, 3).reshape(-1, width)
    turned = vec_parts.transpose(2, 0, 1, 3).reshape(-1, width)
    vec_own = lax.dynamic_slice_in_dim(vec, place * part, part, 1)
    log_decay = -jnp.exp(vec_own[6])
    tables = wkv_tables(
        piece, 1.0 - first_flags.astype(F32), log_decay, vec_own[7], vec_own[8], vec_own[9]
    )
    marks = tables[0]
    rows_one = rows_of(turned, 0, 1, 2, 3, 4, 5)
    tokens_all = gather_seq(tokens_held, (rows_one, tables))
    full_g = gather_dp(after(columns_g, tokens_all[1:3], rows_one))
    own_o = gather_dp(after(w_output, tokens_all))

    mix_r, mix_k, mix_v, mix_g, step, recept, keyed, valued = mixes(
        turn_pieces(tokens_all), marks, rows_one, 4, True, within, here, tile, own_rows // tile,
        [(i, full_in, i, part) for i in range(3)], False,
    )
    projected = (recept, keyed, valued)
    ffn_weights = after([ffn_key, ffn_receptance], tokens_all)
    if seq == 4:
        pieces_c = trade_seq(cut_with_rider(ffn_weights, grad_b, here))
    else:
        (columns_c, _), _ = stacked_columns(ffn_weights, [hidden_width + part], projected)
        grad_all = gather_seq(after(grad_b, mix_r), projected)
    wkv, states = wkv_forward(recept, keyed, valued, tables, here, per)
    gate_pre, mixed = gated(mix_g, full_g, wkv, tables[5], here, seq)
    if seq == 4:
        pieces_c = after(pieces_c, mixed)
        columns_c = stack_below(pieces_c, here)
    full_c = gather_dp(columns_c)
    full_ck, full_cr = full_c[:, :hidden_width], full_c[:, hidden_width:]
    full_cv = gather_dp(after(ffn_value, columns_c))
    attn = [dot(rows, own_o, NN).astype(BF) for rows in blocks_of(mixed, seq)]
    after_mix, normed_two = after_norm(inputs_b, scatter_seq(attn, here), rows_of(vec, 10, 11), here)

    normed_two = gather_seq(normed_two)
    if seq == 4:
        grad_all = gather_second(grad_b, *after(pieces_c[1:3], normed_two))
    mix_k2, mix_r2, step_two, recept_pre, opened = mixes(
        turn_pieces(normed_two), marks, rows_of(turned, 10, 11, 12, 13), 2, False, within, here, tile,
        own_rows // tile, [(1, full_cr, 0, part)], True,
    )
    opened = gather_seq(after(opened, grad_all[3:]))
    key_pre = dot(mix_k2, full_ck, NN)
    smooth = jax.nn.softplus(key_pre)
    hidden = (smooth * smooth).astype(BF)
    slope = (2.0 * smooth * jax.nn.sigmoid(key_pre)).astype(BF)
    hidden, slope = lax.optimization_barrier((hidden, slope))
    later = after(hidden, opened[1:3])
    value_parts = [columns_product(later if j < 2 else hidden, full_cv, part, j, here, seq) for j in reversed(range(seq))]
    value_parts = value_parts[::-1]
    value_relayed = scatter_relay(value_parts, scatter_start(value_parts), here)
    d_value = spread_columns(
        grad_all, by_block(after(opened, value_parts, value_relayed)), here, True, True, tile, own_rows // tile
    )

    grad_cv = dot(hidden, d_value, TN).astype(BF)
    summed_cv = scatter_dp(grad_cv)
    value_terms = scatter_end(value_parts[0], value_relayed)
    d_hidden = dot(after(d_value, grad_cv), full_cv, NT)
    d_key_two = (d_hidden * slope.astype(F32)).astype(BF)
    channel, d_recept_two = channel_out(value_terms, recept_pre, grad_all, here, tile)
    grad_ck, grad_cr = [], []

    def beside_two(relayed):
        grad_ck.append(dot(after(mix_k2, relayed), d_key_two, TN).astype(BF))
        grad_cr.append(dot(after(mix_r2, relayed, grad_ck), d_recept_two, TN).astype(BF))
        return grad_ck, grad_cr

    terms_two, sums_two = mixes_back_scatter(
        [(0, d_key_two, 0, full_c, 0, hidden_width), (1, d_recept_two, 0, full_cr, 0, part)],
        step_two, marks, rows_of(turned, 12, 13), here, seq, beside_two,
    )
    summed_ck = scatter_dp(grad_ck[0])
    if within is None:
        terms_two = [outside(t, groups, unit, back=True) for t in terms_two]
    d_after, d_attn, norm_sums_two = norm_back(terms_two, after_mix, grad_b, rows_of(vec, 10), within, here)

    pieces = gather_seq(d_attn)
    *near, far = by_block(pieces)
    near_mixed = [dot(d, own_o, NT).astype(BF) for d in near]
    *near_rows, far_rows = blocks_of(mixed, seq)
    near_wo = sum(dot(m, d, TN) for m, d in zip(near_rows, near))
    far = after(far, near_mixed, near_wo, summed_cv)
    d_mixed = jnp.concatenate([*near_mixed, dot(far, own_o, NT).astype(BF)], axis=0)
    grad_wo = (near_wo + dot(far_rows, far, TN)).astype(BF)
    summed_o = scatter_dp(grad_wo)
    d_mixed = after(d_mixed, summed_ck, grad_wo)
    d_wkv, d_gate, gate_sums = gate_backward(wkv, gate_pre, d_mixed, tables[5], here)
    grad_g = dot(mix_g, d_gate, TN).astype(BF)
    summed_crg = scatter_dp(jnp.concatenate([grad_cr[0], grad_g], axis=1))
    d_recept, d_keyed, d_valued, sums = wkv_backward(
        recept, keyed, valued, after(d_wkv, grad_g), states, tables, here, per
    )
    channel = after(trade_seq(blocks_of(after(channel, d_mixed), seq)), d_recept)
    grads_in = [
        dot(after(m, channel), d, TN).astype(BF)
        for m, d in ((mix_r, d_recept), (mix_k, d_keyed), (mix_v, d_valued))
    ]
    summed_in = scatter_dp(jnp.concatenate(grads_in, axis=1))
    others = []

    def beside(relayed):
        others.append(spread_columns([after_mix], after(channel, relayed), here, False, False, CHUNK, per))
        others.append(after(summed_cv, relayed).astype(F32))
        return others

    d_recept, d_keyed = after((d_recept, d_keyed), grads_in, summed_o)
    terms, sums_one = mixes_back_scatter(
        [(i, d, 0, full_in, i, part) for i, d in enumerate((d_recept, d_keyed, d_valued))]
        + [(3, d_gate, 0, full_g, 0, part)],
        step, marks, rows_of(turned, 2, 3, 4, 5), here, seq, beside,
    )
    out_rows, sum_cv = others
    if within is None:
        terms = [outside(t, groups, unit, back=True) for t in terms]
    tokens_grad, _, norm_sums = norm_back(terms, inputs_b, d_after, rows_of(vec, 0), within, here)

    sum_o = summed_o.astype(F32)

    def by_device(rows, turn):
        if turn:
            return rows.reshape(-1, dp, seq, unit).transpose(2, 1, 0, 3)
        return rows.reshape(-1, seq, dp, unit).transpose(1, 2, 0, 3)

    own_sums = jnp.stack([sums[0] * log_decay, sums[1], gate_sums[0], gate_sums[1]])
    own_sums = lax.dynamic_update_slice(jnp.zeros((4, width), F32), own_sums, (0, place * part))
    vector_rows = jnp.concatenate(
        [
            by_device(norm_sums[:2], False), by_device(sums_one[:4], True), by_device(own_sums, False),
            by_device(norm_sums_two[:2], False), by_device(sums_two[:2], True),
        ],
        axis=2,
    )
    sums_seq = scatter_small(vector_rows.reshape((-1,) + vector_rows.shape[2:]), "seq")
    summed_c = jnp.concatenate(after([summed_ck, summed_crg], sums_seq), axis=1)
    sum_ck, sum_cr, sum_g = owners_rows(summed_c, [ffn_key.shape[1], width, width])
    sum_vec = scatter_small(sums_seq, "dp", sum_ck)[0]
    sum_r, sum_k, sum_v = owners_rows(after(summed_in, sum_ck), [width] * 3)
    return (
        out_rows[None], tokens_grad[None], sum_r, sum_k, sum_v, sum_g, sum_o,
        sum_ck, sum_cr, sum_cv, sum_vec,
    )


def solution(mesh):
    tokens = P("dp", "seq", None)
    rows = P(("seq", "dp"), None)
    columns = P(None, ("seq", "dp"))
    return jax.shard_map(
        shards,
        mesh=mesh,
        in_specs=(tokens, P("dp", None), tokens) + (rows,) * 8 + (columns,),
        out_specs=(tokens, tokens) + (rows,) * 8 + (columns,),
        check_vma=False,
    )
```

```python
from functools import partial

import jax
import jax.numpy as jnp
from jax import lax
from jax.experimental import pallas as pl
from jax.experimental.pallas import tpu as pltpu
from jax.sharding import PartitionSpec as P

HEAD = 64
PAIR = 128
CHUNK = 128
EPSILON = 1e-05
GROUP_EPSILON = 1.0
BF = jnp.bfloat16
F32 = jnp.float32
NT = (((1,), (1,)), ((), ()))
TN = (((0,), (0,)), ((), ()))
NN = (((1,), (0,)), ((), ()))


def swap(value, axis, distance):
    size = lax.axis_size(axis)
    return lax.ppermute(value, axis, [(i, i ^ distance) for i in range(size)])


def after(value, *others):
    return lax.optimization_barrier((value, others))[0]


def gather_second(part, one, two):
    half = part.shape[0] // 2
    columns = part.shape[1]
    low, high = swap(one[:half, :columns], "seq", 2), swap(two[half : 2 * half, :columns], "seq", 1)
    return [part, one, two, low, high]


def gather_seq(part, first=()):
    size = lax.axis_size("seq")
    if size == 4:
        half = part.shape[0] // 2
        one, two = swap(part, "seq", 1), swap(part, "seq", 2)
        one, two = after((one, two), first)
        low, high = swap(one[:half], "seq", 2), swap(two[half:], "seq", 1)
        return [part, one, two, low, high]
    return [part] + [swap(part, "seq", distance) for distance in range(1, size)]


def by_block(pieces):
    if lax.axis_size("seq") == 4:
        return pieces[:3] + [jnp.concatenate(pieces[3:], axis=0)]
    return pieces


def scatter_start(parts):
    if lax.axis_size("seq") != 4:
        return ()
    low, high = parts[3:] if len(parts) == 5 else blocks_of(parts[3], 2)
    return swap(low, "seq", 1), swap(high, "seq", 2)


def relay_body(here, one_ref, two_ref, low_ref, high_ref, one_out, two_out):
    one, two = one_ref[...], two_ref[...]
    first = pl.program_id(0) == 0
    low, high = low_ref[...].astype(F32), high_ref[...].astype(F32)
    one_out[...] = jnp.where(first, one, (one.astype(F32) + high).astype(BF))
    two_out[...] = jnp.where(first, (two.astype(F32) + low).astype(BF), two)


def scatter_relay(parts, started, here):
    if lax.axis_size("seq") != 4:
        return parts[1:]
    (_, one, two, *_), (low, high) = parts, started
    (rows, width), half = one.shape, block(low.shape, lambda i, h: (i, 0))
    return kernel(
        relay_body, "relay", (2,), here,
        [(one, half), (two, half), (low, fixed(low.shape)), (high, fixed(low.shape))],
        [((rows, width), BF, half)] * 2,
    )


def scatter_end(own, relayed):
    return [own] + [swap(part, "seq", j + 1) for j, part in enumerate(relayed)]


def scatter_seq(parts, here):
    return scatter_end(parts[0], scatter_relay(parts, scatter_start(parts), here))


def trade_seq(parts):
    return [parts[0]] + [swap(part, "seq", j + 1) for j, part in enumerate(parts[1:])]


def blocks_of(values, size):
    rows = values.shape[0] // size
    return [values[j * rows : (j + 1) * rows] for j in range(size)]


def bits_of(size):
    return [1 << b for b in range(size.bit_length() - 1)]


def gather_small(part, axis):
    for bit in bits_of(lax.axis_size(axis)):
        other = swap(part, axis, bit)
        second = (lax.axis_index(axis) & bit) != 0
        part = jnp.concatenate([jnp.where(second, other, part), jnp.where(second, part, other)], axis=0)
    return part


def scatter_small(parts, axis):
    for bit in reversed(bits_of(lax.axis_size(axis))):
        half = parts.shape[0] // 2
        second = (lax.axis_index(axis) & bit) != 0
        low, high = parts[:half], parts[half:]
        parts = jnp.where(second, high, low) + swap(jnp.where(second, low, high), axis, bit)
    return parts


def block(shape, index):
    return pl.BlockSpec(shape, lambda *i: index(*i[:-1], i[-1][0]))


def fixed(shape):
    return pl.BlockSpec(shape, lambda *i: (0,) * len(shape))


def relative(tile, per, here):
    return (lax.div(tile, per) ^ here) * per + lax.rem(tile, per)


def kernel(body, name, grid, here, ins, outs, scratch=(), vmem=48):
    return pl.pallas_call(
        body,
        out_shape=[jax.ShapeDtypeStruct(shape, kind) for shape, kind, _ in outs],
        grid_spec=pltpu.PrefetchScalarGridSpec(
            num_scalar_prefetch=1,
            grid=grid,
            in_specs=[spec for _, spec in ins],
            out_specs=[spec for _, _, spec in outs],
            scratch_shapes=list(scratch),
        ),
        compiler_params=pltpu.CompilerParams(vmem_limit_bytes=vmem * 2**20),
        name=name,
    )(here, *[array for array, _ in ins])


def pieced(pieces, tile, columns, column, place):
    ins, start = [], 0
    for piece in pieces:
        count = piece.shape[0] // tile

        def index(i, h, start=start, count=count):
            return jnp.clip(place(i, h) - start, 0, count - 1), column(h)

        ins.append((piece, block((tile, columns), index)))
        start += count
    return ins


def picked(refs, counts, tile, held):
    start = 0
    for ref, count in zip(refs, counts):

        @pl.when((tile >= start) & (tile < start + count))
        def _(ref=ref):
            held[...] = ref[...]

        start += count
    return held[...].astype(F32)


def counts_of(pieces, tile):
    return [piece.shape[0] // tile for piece in pieces]


def row_index(rows):
    return lax.broadcasted_iota(jnp.int32, (rows, 1), 0)


def placed(place, width):
    return pl.ds(pl.multiple_of(place * width, width), width)


def cut_body(count, parts, here, *refs):
    ins, beside, outs = refs[:count], refs[count], refs[count + 1 :]
    rows = ins[0].shape[0]
    for j in range(parts):
        outs[j][rows:, :] = jnp.zeros_like(outs[j][rows:, :])
        outs[j][rows:, : beside.shape[1]] = beside[...]
    at = 0
    for ref in ins:
        width = ref.shape[1] // parts
        for j in range(parts):
            outs[j][:rows, at : at + width] = ref[:, placed(here[0] ^ j, width)]
        at += width


def cut_columns(weights, beside, here, parts):
    rows, width = weights[0].shape[0] + beside.shape[0], sum(w.shape[1] for w in weights) // parts
    return kernel(
        partial(cut_body, len(weights), parts), "cut_columns", (1,), here,
        [(w, fixed(w.shape)) for w in [*weights, beside]],
        [((rows, width), BF, fixed((rows, width)))] * parts,
    )


def stack_body(parts, here, *refs):
    start = 0
    outs, beside = refs[parts:-1], refs[-1]
    for out in outs:
        for j in range(parts):
            out[here[0] ^ j] = refs[j][: out.shape[1], start : start + out.shape[2]]
        start += out.shape[2]
    for j in range(parts):
        beside[here[0] ^ j] = refs[j][out.shape[1] :, : beside.shape[2]]


def stack_rows(pieces, widths, beside, here):
    parts, rows = len(pieces), pieces[0].shape[0] - beside.shape[0]
    shapes = [(parts, rows, width) for width in widths] + [(parts,) + beside.shape]
    return kernel(
        partial(stack_body, parts), "stack_rows", (1,), here,
        [(p, fixed(p.shape)) for p in pieces],
        [(shape, BF, fixed(shape)) for shape in shapes],
    )


def ride_body(count, here, *refs):
    ins, rider, outs = refs[:count], refs[count], refs[count + 1 :]
    for j, out in enumerate(outs):
        top, at = 0, 0
        if j in (1, 2):
            top = rider.shape[0]
            out[:top, : rider.shape[1]] = rider[...]
            out[:top, rider.shape[1] :] = jnp.zeros_like(out[:top, rider.shape[1] :])
        for ref in ins:
            width = ref.shape[1] // 4
            out[top:, at : at + width] = ref[:, placed(here[0] ^ j, width)]
            at += width


def cut_with_rider(weights, rider, here):
    rows, width = weights[0].shape[0], sum(w.shape[1] for w in weights) // 4
    return kernel(
        partial(ride_body, len(weights)), "cut_columns", (1,), here,
        [(w, fixed(w.shape)) for w in [*weights, rider]],
        [((n, width), BF, fixed((n, width))) for n in (rows, rows + rider.shape[0], rows + rider.shape[0], rows)],
    )


def unride_body(here, *refs):
    out = refs[-1]
    rows = out.shape[1]
    for j, ref in enumerate(refs[:-1]):
        out[here[0] ^ j] = ref[ref.shape[0] - rows :, :]


def stack_below(pieces, here):
    shape = (4,) + pieces[0].shape
    (stacked,) = kernel(
        unride_body, "stack_rows", (1,), here,
        [(p, fixed(p.shape)) for p in pieces],
        [(shape, BF, fixed(shape))],
    )
    return stacked.reshape(-1, shape[-1])


def hold_body(here, in_ref, *refs):
    refs[-1][...] = in_ref[...]


def held_back(values, here, *others):
    rows, width = values.shape
    own = block((rows // 2, width), lambda i, h: (i, 0))
    (copy,) = kernel(
        hold_body, "hold", (2,), here,
        [(values, own)] + [(o, pl.BlockSpec(memory_space=pl.ANY)) for o in others],
        [((rows, width), values.dtype, own)],
    )
    return copy


def join_body(parts, count, here, *refs):
    ins, outs = refs[:parts], refs[parts:]
    at = 0
    for ref in outs:
        width = ref.shape[1] // parts
        for j in range(parts):
            ref[:, placed(here[0] ^ j, width)] = ins[j][:, at : at + width].astype(F32)
        at += width


def join_columns(pieces, widths, here):
    parts, rows = len(pieces), pieces[0].shape[0]
    return kernel(
        partial(join_body, parts, len(widths)), "join_columns", (1,), here,
        [(p, fixed(p.shape)) for p in pieces],
        [((rows, width), F32, fixed((rows, width))) for width in widths],
    )


def spread_body(counts, parts, product, here, *refs):
    bases, pieces, out, held = refs[: len(counts)], refs[len(counts) : -2], refs[-2], refs[-1]
    picked(bases, counts, pl.program_id(0), held)
    width = pieces[0].shape[1]
    for j in range(parts):
        at = placed(here[0] ^ j, width)
        piece, base = pieces[j][...].astype(F32), held[:, at].astype(F32)
        out[:, at] = (base * piece if product else base + piece).astype(BF)


def spread_columns(bases, columns, here, product, turn, tile, per):
    rows, width = sum(counts_of(bases, tile)) * tile, bases[0].shape[1]

    def turned(i, j):
        return (lax.div(i, per) ^ j) * per + lax.rem(i, per) if turn else i

    (result,) = kernel(
        partial(spread_body, counts_of(bases, tile), len(columns), product), "spread_columns", (rows // tile,), here,
        pieced(bases, tile, width, lambda h: 0, lambda i, h: i)
        + [(c, block((tile, c.shape[1]), lambda i, h, j=j: (turned(i, j), 0))) for j, c in enumerate(columns)],
        [((rows, width), BF, block((tile, width), lambda i, h: (i, 0)))],
        [pltpu.VMEM((tile, width), bases[0].dtype)],
    )
    return result


def shuffled(values, groups, back=False):
    seq, dp = groups
    if back:
        seq, dp = dp, seq
    lane = lax.broadcasted_iota(jnp.int32, (1, PAIR), 1) < HEAD
    source = [s * dp + d for d in range(dp) for s in range(seq)]
    columns = []
    for one, two in zip(source[::2], source[1::2]):
        low = values[:, one // 2 * PAIR : (one // 2 + 1) * PAIR]
        high = values[:, two // 2 * PAIR : (two // 2 + 1) * PAIR]
        low = pltpu.roll(low, HEAD, 1) if one % 2 else low
        high = high if two % 2 else pltpu.roll(high, HEAD, 1)
        columns.append(jnp.where(lane, low, high))
    return jnp.concatenate(columns, axis=1)


def outside(values, groups, channels, back=False):
    seq, dp = groups[::-1] if back else groups
    return values.reshape(-1, seq, dp, channels).swapaxes(1, 2).reshape(values.shape)


def centre(values):
    centred = values - jnp.mean(values, axis=-1, keepdims=True)
    spread = jnp.mean(centred * centred, axis=-1, keepdims=True)
    return centred, lax.rsqrt(spread + EPSILON)


def mix_body(count, norm, groups, counts, per, mixed, open_up, here, *refs):
    pieces, (marks_ref, vec_ref) = refs[: len(counts)], refs[len(counts) : len(counts) + 2]
    weights = refs[len(counts) + 2 : len(counts) + 2 + len(mixed)]
    outs, last, held = refs[len(counts) + 2 + len(mixed) : -2], refs[-2], refs[-1]
    products = outs[count + 1 :]

    @pl.when(pl.program_id(0) == 0)
    def _():
        last[...] = jnp.zeros_like(last)

    values = picked(pieces, counts, relative(pl.program_id(0), per, here[0]), held)
    if norm:
        centred, inverse = centre(values)
        values = centred * inverse
    if groups:
        values = shuffled(values, groups)
    if norm:
        values = values * vec_ref[0:1, :] + vec_ref[1:2, :]
    rows = values.shape[0]
    previous = jnp.where(row_index(rows) == 0, last[0:1, :], pltpu.roll(values, 1, 0)) * marks_ref[:, 3:4]
    last[0:1, :] = values[rows - 1 :, :]
    step = values - previous
    outs[count][...] = step.astype(BF)
    for i in range(count):
        mix = (previous + step * vec_ref[2 + i : 3 + i, :]).astype(BF)
        outs[i][...] = mix
        if i in mixed:
            k = mixed.index(i)
            product = dot(mix, weights[k][...], NN)
            if open_up:
                products[0][...] = product
                products[1][...] = (1.0 / (1.0 + jnp.exp(-product))).astype(BF)
            else:
                products[k][...] = product.astype(BF)


def mixes(pieces, marks, vec, count, norm, groups, here, tile, per, weights, open_up):
    rows, width = marks.shape[0], pieces[0].shape[1]
    own = block((tile, width), lambda i, h: (relative(i, per, h), 0))
    outs = [((rows, width), BF, own)] * (count + 1)
    for _, _, _, part in weights:
        narrow = block((tile, part), lambda i, h: (relative(i, per, h), 0))
        outs += [((rows, part), F32 if open_up else BF, narrow)] + [((rows, part), BF, narrow)] * open_up
    return kernel(
        partial(mix_body, count, norm, groups, counts_of(pieces, tile), per, [w[0] for w in weights], open_up),
        "mixes", (rows // tile,), here,
        pieced(pieces, tile, width, lambda h: 0, lambda i, h: relative(i, per, h))
        + [(marks, block((tile, PAIR), lambda i, h: (i, 0))), (vec, fixed(vec.shape))]
        + [(w, pl.BlockSpec((width, part), lambda *_, at=at: (0, at))) for _, w, at, part in weights],
        outs,
        [pltpu.VMEM((8, width), F32), pltpu.VMEM((tile, width), BF)],
        vmem=58,
    )


def mixes_back_body(which, first, seq, outs, here, *refs):
    count = len(which)
    grads, nexts, weights = refs[:count], refs[count : 2 * count], refs[2 * count : 3 * count]
    step_ref, marks_ref, next_marks_ref, vec_ref, *out_refs, sums_ref = refs[3 * count :]

    @pl.when(pl.program_id(1) == 0)
    def _():
        sums_ref[...] = jnp.zeros_like(sums_ref)

    step = step_ref[...].astype(F32)
    rows = step.shape[0]
    total = straight = None
    for i in range(which[-1] + 1):
        grad = sum(
            dot(jnp.concatenate([grads[k][...], nexts[k][...]], axis=0), weights[k][...], NT)
            for k in range(count)
            if which[k] == i
        )
        sums_ref[i : i + 1, :] += jnp.sum(grad[:rows] * step, axis=0, keepdims=True)
        part = grad * vec_ref[i : i + 1, :]
        total, straight = (total + grad, straight + part) if i else (grad, part)
    inside = ((first + pl.program_id(1)) ^ here[0]) < seq - 1
    keep = jnp.concatenate([marks_ref[:, 3:4], jnp.where(inside, next_marks_ref[:, 3:4], 0.0)], axis=0)
    kept = (total - straight) * keep
    up = pltpu.roll(kept, kept.shape[0] - 1, 0)
    result = (straight[:rows] + up[:rows]).astype(BF)
    if len(out_refs) == 1:
        out_refs[0][...] = result
        return
    if outs == 1:
        out_refs[0][...] = result[: rows // 2]
        out_refs[1][...] = result[rows // 2 :]
        return
    for k, out_ref in enumerate(out_refs):

        @pl.when(pl.program_id(1) == k)
        def _(out_ref=out_ref):
            out_ref[...] = result


EXTRA = 16


def mixes_back(terms, step, marks, vec, here, seq, first, count, halves=False):
    rows, width = step.shape
    tile, columns = rows // seq, min(512, width)
    extras = tile // EXTRA

    def following(i, h):
        return jnp.minimum(((first + i) ^ h) + 1, seq - 1)

    ins = [(g, block((tile, n), lambda c, i, h, at=at: (first + i, at))) for _, g, at, _, _, n in terms]
    ins += [
        (g, block((EXTRA, n), lambda c, i, h, at=at: ((following(i, h) ^ h) * extras, at)))
        for _, g, at, _, _, n in terms
    ]
    ins += [(w, block((columns, n), lambda c, i, h, at=at: (c, at))) for _, _, _, w, at, n in terms]
    ins += [
        (step, block((tile, columns), lambda c, i, h: (first + i, c))),
        (marks, block((tile, PAIR), lambda c, i, h: ((first + i) ^ h, 0))),
        (marks, block((EXTRA, PAIR), lambda c, i, h: (following(i, h) * extras, 0))),
        (vec, block((8, columns), lambda c, i, h: (0, c))),
    ]
    size = tile // 2 if halves else tile
    *parts, sums = kernel(
        partial(mixes_back_body, [t[0] for t in terms], first, seq, count), "mixes_back", (width // columns, count), here, ins,
        [((size, width), BF, block((size, columns), lambda c, i, h: (0, c)))] * (2 if halves else count)
        + [((8, width), F32, block((8, columns), lambda c, i, h: (0, c)))],
    )
    return parts, sums


def mixes_back_scatter(terms, step, marks, vec, here, seq, beside):
    if seq != 4:
        parts, sums = mixes_back(terms, step, marks, vec, here, seq, 0, seq)
        return after(scatter_seq(parts, here), beside(parts)), sums

    def call(first, count, *before):
        ordered = after([t[1] for t in terms], *before)
        return mixes_back(
            [(t[0], g) + t[2:] for t, g in zip(terms, ordered)], step, marks, vec, here, seq, first, count, first == 3
        )

    far, sums_far = call(3, 1)
    near, sums_near = call(1, 2, far)
    parts = [None, *near, *far]
    started = after(scatter_start(parts), near)
    relayed = scatter_relay(parts, started, here)
    (own,), sums_own = call(0, 1, near, relayed)
    return after(scatter_end(own, relayed), beside(relayed)), sums_far + sums_near + sums_own


def after_body(count, here, x_ref, vec_ref, *refs):
    after_ref, normed_ref = refs[count:]
    after = x_ref[...].astype(F32)
    for ref in refs[:count]:
        after = after + ref[...].astype(F32)
    after_ref[...] = after
    centred, inverse = centre(after)
    normed_ref[...] = (centred * inverse * vec_ref[0:1, :] + vec_ref[1:2, :]).astype(BF)


def after_norm(inputs, terms, vec, here):
    rows, width = inputs.shape
    own = block((CHUNK, width), lambda i, h: (i, 0))
    return kernel(
        partial(after_body, len(terms)), "after_norm", (rows // CHUNK,), here,
        [(inputs, own), (vec, fixed(vec.shape))] + [(t, own) for t in terms],
        [((rows, width), F32, own), ((rows, width), BF, own)],
    )


def norm_back_body(count, groups, here, x_ref, base_ref, vec_ref, *refs):
    wide_ref, narrow_ref, sums_ref = refs[count:]

    @pl.when(pl.program_id(0) == 0)
    def _():
        sums_ref[...] = jnp.zeros_like(sums_ref)

    grad = refs[0][...].astype(F32)
    for ref in refs[1:count]:
        grad = grad + ref[...].astype(F32)
    if groups:
        grad = shuffled(grad, groups, back=True)
    centred, inverse = centre(x_ref[...].astype(F32))
    normed = centred * inverse
    sums_ref[0:1, :] += jnp.sum(grad * normed, axis=0, keepdims=True)
    sums_ref[1:2, :] += jnp.sum(grad, axis=0, keepdims=True)
    grad = grad * vec_ref[0:1, :]
    grad = grad - jnp.mean(grad, axis=-1, keepdims=True) - normed * jnp.mean(grad * normed, axis=-1, keepdims=True)
    result = base_ref[...].astype(F32) + inverse * grad
    wide_ref[...] = result
    narrow_ref[...] = result.astype(BF)


def norm_back(terms, inputs, base, vec, groups, here):
    rows, width = inputs.shape
    own = block((CHUNK, width), lambda i, h: (i, 0))
    return kernel(
        partial(norm_back_body, len(terms), groups), "norm_back", (rows // CHUNK,), here,
        [(inputs, own), (base, own), (vec, fixed(vec.shape))] + [(t, own) for t in terms],
        [((rows, width), F32, own), ((rows, width), BF, own), ((8, width), F32, fixed((8, width)))],
    )


def gate_body(mix_ref, weight_ref, wkv_ref, par_ref, gate_ref, mixed_ref):
    gate = dot(mix_ref[...], weight_ref[...], NN)
    gate_ref[...] = gate
    ones = jnp.where(same_head(), 1.0, 0.0).astype(BF)
    for pair in range(gate.shape[1] // PAIR):
        at = slice(pair * PAIR, (pair + 1) * PAIR)
        wkv = wkv_ref[:, at]
        centred = wkv - head_sum_fine(wkv, ones) * (1.0 / HEAD)
        spread = head_sum(centred * centred, ones) * (1.0 / HEAD)
        normed = centred * lax.rsqrt(spread + GROUP_EPSILON) * par_ref[1:2, at] + par_ref[2:3, at]
        mixed_ref[:, at] = (normed * (gate[:, at] / (1.0 + jnp.exp(-gate[:, at])))).astype(BF)


def gated(mix_g, weights, wkv, params, here, seq):
    rows, width = mix_g.shape
    tile, part = rows // seq, wkv.shape[1]
    own = block((tile, part), lambda i, h: (i, 0))
    return kernel(
        lambda here, *refs: gate_body(*refs), "gate", (seq,), here,
        [
            (mix_g, block((tile, width), lambda i, h: (i, 0))),
            (weights, block((width, part), lambda i, h: (0, 0))),
            (wkv, own),
            (params, fixed(params.shape)),
        ],
        [((rows, part), F32, own), ((rows, part), BF, own)],
    )


def columns_body(here, left_ref, right_ref, out_ref):
    out_ref[...] = dot(left_ref[...], right_ref[...], NN).astype(BF)


def columns_product(left, right, part, relative_to, here, seq):
    rows, depth = left.shape
    tile = rows // seq
    (result,) = kernel(
        columns_body, "value_columns", (seq,), here,
        [
            (left, block((tile, depth), lambda i, h: (i, 0))),
            (right, block((depth, part), lambda i, h: (0, h ^ relative_to))),
        ],
        [((rows, part), BF, block((tile, part), lambda i, h: (i ^ relative_to, 0)))],
    )
    return result


def channel_body(counts, here, pre_ref, *refs):
    grads, terms, (channel_ref, d_recept_ref, held) = refs[: len(counts)], refs[len(counts) : -3], refs[-3:]
    value = sum(ref[...].astype(F32) for ref in terms)
    opened = 1.0 / (1.0 + jnp.exp(-pre_ref[...]))
    channel = opened * value
    channel_ref[...] = channel.astype(BF)
    grad = picked(grads, counts, pl.program_id(0), held)
    d_recept_ref[...] = (grad * channel * (1.0 - opened)).astype(BF)


def channel_out(terms, pre, grads, here, tile):
    rows, part = pre.shape
    own = block((tile, part), lambda i, h: (i, 0))
    return kernel(
        partial(channel_body, counts_of(grads, tile)), "channel", (rows // tile,), here,
        [(pre, own)] + pieced(grads, tile, part, lambda h: h, lambda i, h: i) + [(t, own) for t in terms],
        [((rows, part), BF, own)] * 2,
        [pltpu.VMEM((tile, part), BF)],
    )


def head_masks():
    lane = lax.broadcasted_iota(jnp.int32, (1, PAIR), 1)
    first = (lane < HEAD).astype(F32)
    return first, 1.0 - first


def same_head():
    row = lax.broadcasted_iota(jnp.int32, (PAIR, PAIR), 0) < HEAD
    column = lax.broadcasted_iota(jnp.int32, (PAIR, PAIR), 1) < HEAD
    return row == column


def dot(left, right, dims):
    return lax.dot_general(left, right, dims, preferred_element_type=F32)


def head_sum(values, ones):
    return dot(values.astype(BF), ones, NN)


def head_sum_fine(values, ones):
    coarse = values.astype(BF)
    rest = (values - coarse.astype(F32)).astype(BF)
    return dot(coarse, ones, NN) + dot(rest, ones, NN)


def stacked(values, first, second):
    return jnp.concatenate([(values * first).astype(BF), (values * second).astype(BF)], axis=0)


def masks_of(rows_ref, columns_ref):
    segment = rows_ref[:, 0:1]
    reaches = rows_ref[:, 1:2]
    last_same = rows_ref[:, 2:3]
    reach_last = rows_ref[CHUNK - 1 : CHUNK, 1:2]
    before = lax.broadcasted_iota(jnp.int32, (CHUNK, CHUNK), 1) < lax.broadcasted_iota(
        jnp.int32, (CHUNK, CHUNK), 0
    )
    allowed = jnp.where((segment == columns_ref[0:1, :]) & before, 1.0, 0.0)
    return reaches, last_same, reach_last, jnp.concatenate([allowed, allowed], axis=0)


def wkv_forward_body(
    here, r_ref, k_ref, v_ref, rows_ref, columns_ref, grow_ref, shrink_ref, tail_ref, par_ref,
    wkv_ref, states_ref, state,
):
    @pl.when(pl.program_id(0) == 0)
    def _():
        state[...] = jnp.zeros_like(state)

    first, second = head_masks()
    block = same_head()
    ones = jnp.where(block, 1.0, 0.0).astype(BF)
    reaches, last_same, reach_last, allowed = masks_of(rows_ref, columns_ref)
    for pair in range(r_ref.shape[1] // PAIR):
        at = slice(pair * PAIR, (pair + 1) * PAIR)
        r, k, v = r_ref[:, at].astype(F32), k_ref[:, at].astype(F32), v_ref[:, at].astype(F32)
        bonus, decay = par_ref[0:1, at], par_ref[3:4, at]
        held = state[at, :]
        held_b = held.astype(BF)
        states_ref[0, at, :] = held_b
        grown = r * grow_ref[:, at]
        shrunk = (k * shrink_ref[:, at]).astype(BF)
        scores = (dot(stacked(grown, first, second), shrunk, NT) * allowed).astype(BF)
        both = jnp.concatenate([scores[:CHUNK], scores[CHUNK:]], axis=1)
        wkv = dot(both, stacked(v, first, second), NN)
        wkv = wkv + dot((grown * reaches).astype(BF), held_b, NT)
        wkv = wkv + head_sum(r * bonus * k, ones) * v
        fresh = dot(v_ref[:, at], (k * tail_ref[:, at] * last_same).astype(BF), TN)
        state[at, :] = held * (decay * reach_last) + jnp.where(block, fresh, 0.0)
        wkv_ref[:, at] = wkv


def wkv_backward_body(
    here, r_ref, k_ref, v_ref, d_wkv_ref, states_ref,
    rows_ref, columns_ref, grow_ref, shrink_ref, tail_ref, par_ref,
    d_r_ref, d_k_ref, d_v_ref, sums_ref, d_state,
):
    @pl.when(pl.program_id(0) == 0)
    def _():
        d_state[...] = jnp.zeros_like(d_state)
        sums_ref[...] = jnp.zeros_like(sums_ref)

    first, second = head_masks()
    block = same_head()
    ones = jnp.where(block, 1.0, 0.0).astype(BF)
    reaches, last_same, reach_last, allowed = masks_of(rows_ref, columns_ref)
    offset = lax.broadcasted_iota(jnp.int32, (CHUNK, PAIR), 0).astype(F32)
    for pair in range(r_ref.shape[1] // PAIR):
        at = slice(pair * PAIR, (pair + 1) * PAIR)
        bonus, decay = par_ref[0:1, at], par_ref[3:4, at]
        d_wkv = d_wkv_ref[:, at].astype(F32)
        r, k, v = r_ref[:, at].astype(F32), k_ref[:, at].astype(F32), v_ref[:, at].astype(F32)
        v_b, d_wkv_b = v_ref[:, at], d_wkv_ref[:, at]
        grow, shrink, tail = grow_ref[:, at], shrink_ref[:, at], tail_ref[:, at] * last_same
        held = states_ref[0, at, :]
        later = d_state[at, :]
        later_b = later.astype(BF)
        grown = r * grow
        shrunk = k * shrink
        shrunk_b = shrunk.astype(BF)
        tailed_b = (k * tail).astype(BF)
        grown_two = stacked(grown, first, second)
        d_wkv_two = stacked(d_wkv, first, second)
        scores = (dot(grown_two, shrunk_b, NT) * allowed).astype(BF)
        d_scores = (dot(d_wkv_two, v_b, NT) * allowed).astype(BF)
        d_both = jnp.concatenate([d_scores[:CHUNK], d_scores[CHUNK:]], axis=1)
        d_grown = dot(d_both, stacked(shrunk, first, second), NN)
        d_grown = d_grown + dot((d_wkv * reaches).astype(BF), held, NN)
        d_shrunk = dot(d_scores, grown_two, TN)
        d_tailed = dot(v_b, later_b, NN)
        share = head_sum(r * bonus * k, ones)
        d_share = head_sum(d_wkv * v, ones)
        d_v = dot(scores, d_wkv_two, TN) + dot(tailed_b, later_b, NT) + share * d_wkv
        d_r_ref[:, at] = (d_grown * grow + d_share * bonus * k).astype(BF)
        d_k_ref[:, at] = (d_shrunk * shrink + d_tailed * tail + d_share * bonus * r).astype(BF)
        d_v_ref[:, at] = d_v.astype(BF)
        carried = decay * reach_last
        d_fresh = dot(d_wkv_b, (grown * reaches).astype(BF), TN)
        d_state[at, :] = later * carried + jnp.where(block, d_fresh, 0.0)
        grown_b = grown.astype(BF).astype(F32)
        d_log = (
            offset * grown_b * d_grown
            - (offset + 1.0) * shrunk_b.astype(F32) * d_shrunk
            + (CHUNK - 1.0 - offset) * tailed_b.astype(F32) * d_tailed
        )
        kept = CHUNK * carried * jnp.sum(held.astype(F32) * later, axis=0, keepdims=True)
        sums_ref[0:1, at] += jnp.sum(d_log, axis=0, keepdims=True) + kept
        sums_ref[1:2, at] += jnp.sum(d_share * r * k, axis=0, keepdims=True)


def gate_backward_body(here, wkv_ref, g_ref, d_mixed_ref, par_ref, d_wkv_ref, d_g_ref, sums_ref):
    @pl.when(pl.program_id(0) == 0)
    def _():
        sums_ref[...] = jnp.zeros_like(sums_ref)

    ones = jnp.where(same_head(), 1.0, 0.0).astype(BF)
    for pair in range(wkv_ref.shape[1] // PAIR):
        at = slice(pair * PAIR, (pair + 1) * PAIR)
        gain, bias = par_ref[1:2, at], par_ref[2:3, at]
        wkv, gate, d_mixed = wkv_ref[:, at], g_ref[:, at], d_mixed_ref[:, at].astype(F32)
        centred = wkv - head_sum_fine(wkv, ones) * (1.0 / HEAD)
        spread = head_sum(centred * centred, ones) * (1.0 / HEAD)
        inverse = lax.rsqrt(spread + GROUP_EPSILON)
        normed = centred * inverse
        opened = 1.0 / (1.0 + jnp.exp(-gate))
        d_scaled = d_mixed * gate * opened
        d_g = d_mixed * (normed * gain + bias) * opened * (1.0 + gate * (1.0 - opened))
        d_g_ref[:, at] = d_g.astype(BF)
        d_normed = d_scaled * gain
        mean_one = head_sum(d_normed, ones) * (1.0 / HEAD)
        mean_two = head_sum(d_normed * normed, ones) * (1.0 / HEAD)
        d_wkv_ref[:, at] = (inverse * (d_normed - mean_one - normed * mean_two)).astype(BF)
        sums_ref[0:1, at] += jnp.sum(d_scaled * normed, axis=0, keepdims=True)
        sums_ref[1:2, at] += jnp.sum(d_scaled, axis=0, keepdims=True)


def gate_backward(wkv, gate, d_mixed, params, here):
    rows, part = wkv.shape
    own = block((2 * CHUNK, part), lambda i, h: (i, 0))
    return kernel(
        gate_backward_body, "gate_backward", (rows // (2 * CHUNK),), here,
        [(a, own) for a in (wkv, gate, d_mixed)] + [(params, fixed(params.shape))],
        [((rows, part), BF, own)] * 2 + [((8, part), F32, fixed((8, part)))],
    )


def wkv_blocks(width, chunks, per, backward):
    def chunk(i):
        return chunks - 1 - i if backward else i

    tokens = block((CHUNK, width), lambda i, h: (relative(chunk(i), per, h), 0))
    states = block((1, width, PAIR), lambda i, h: (chunk(i), 0, 0))
    tables = [
        block((CHUNK, PAIR), lambda i, h: (chunk(i), 0)),
        block((8, CHUNK), lambda i, h: (0, chunk(i))),
    ]
    return tokens, states, tables + [fixed((CHUNK, width))] * 3 + [fixed((8, width))]


def wkv_forward(r, k, v, tables, here, per):
    length, width = r.shape
    chunks = length // CHUNK
    tokens, states, blocks = wkv_blocks(width, chunks, per, False)
    return kernel(
        wkv_forward_body, "wkv_forward", (chunks,), here,
        [(a, tokens) for a in (r, k, v)] + list(zip(tables, blocks)),
        [((length, width), F32, tokens), ((chunks, width, PAIR), BF, states)],
        [pltpu.VMEM((width, PAIR), F32)],
    )


def wkv_backward(r, k, v, d_wkv, states_kept, tables, here, per):
    length, width = r.shape
    chunks = length // CHUNK
    tokens, states, blocks = wkv_blocks(width, chunks, per, True)
    return kernel(
        wkv_backward_body, "wkv_backward", (chunks,), here,
        [(a, tokens) for a in (r, k, v, d_wkv)] + [(states_kept, states)] + list(zip(tables, blocks)),
        [((length, width), BF, tokens)] * 3 + [((8, width), F32, fixed((8, width)))],
        [pltpu.VMEM((width, PAIR), F32)],
    )


def wkv_tables(piece, keep, log_decay, bonus, gain, bias):
    length = piece.shape[0]
    by_chunk = piece.reshape(length // CHUNK, CHUNK)
    before = jnp.concatenate([jnp.full((1,), -1, piece.dtype), by_chunk[:-1, -1]])
    reaches = (by_chunk == before[:, None]).reshape(-1)
    last_same = (by_chunk == by_chunk[:, -1:]).reshape(-1)
    marks = jnp.stack([piece.astype(F32), reaches.astype(F32), last_same.astype(F32), keep], axis=1)
    rows = jnp.pad(marks, ((0, 0), (0, PAIR - 4)))
    columns = jnp.broadcast_to(piece.astype(F32)[None], (8, length))
    offset = jnp.arange(CHUNK).astype(F32)[:, None]
    grow = jnp.exp(offset * log_decay)
    shrink = jnp.exp(-(offset + 1.0) * log_decay)
    tail = jnp.exp((CHUNK - 1.0 - offset) * log_decay)
    zero = jnp.zeros_like(bonus)
    params = jnp.stack([bonus, gain, bias, jnp.exp(CHUNK * log_decay)] + [zero] * 4)
    return rows, columns, grow, shrink, tail, params


def segment_of(lengths, positions):
    rank = jnp.arange(lengths.shape[0])
    starts = jnp.sum(jnp.where(rank[:, None] > rank[None, :], lengths[None, :], 0), axis=1)
    later_flags = (positions[:, None] >= starts[None, 1:]).astype(jnp.int32)
    first_flags = jnp.any(positions[:, None] == starts[None, :], axis=1)
    return (jnp.sum(later_flags, axis=1), first_flags)


def rows_of(vec, *rows):
    return jnp.pad(jnp.stack([vec[i] for i in rows]), ((0, 8 - len(rows)), (0, 0)))


def shards(
    tokens, seq_lengths, out_grad, w_receptance, w_key, w_value, w_gate, w_output,
    ffn_key, ffn_receptance, ffn_value, vectors,
):
    seq, dp = lax.axis_size("seq"), lax.axis_size("dp")
    place = lax.axis_index("seq")
    here = jnp.reshape(place, (1,)).astype(jnp.int32)
    inputs_b, grad_b = tokens[0], out_grad[0]
    own_rows, width = inputs_b.shape
    length, part, unit = own_rows * seq, width // seq, vectors.shape[1]
    per, tile = own_rows // CHUNK, own_rows // 2
    hidden_width = ffn_key.shape[1] // seq
    groups = (seq, dp)
    within = groups if unit == HEAD else None

    vectors_b = jnp.pad(vectors, ((0, 16 - vectors.shape[0]), (0, 0)))

    def stacked_columns(weights, widths, beside=()):
        cut = cut_columns(weights, vectors_b, here, seq)
        *stacked, last = stack_rows(after(trade_seq(cut), beside), widths, vectors_b, here)
        return [w.reshape(-1, w.shape[-1]) for w in stacked] + [last], cut

    def gather_dp(rows):
        return lax.all_gather(rows, "dp", axis=0, tiled=True)

    def scatter_dp(grad):
        return lax.psum_scatter(grad, "dp", scatter_dimension=0, tiled=True)

    def owners_parts(summed):
        rows = summed.shape[0] // seq
        return trade_seq([lax.dynamic_slice_in_dim(summed, (place ^ j) * rows, rows, 0) for j in range(seq)])

    def owners_rows(summed, widths):
        return join_columns(owners_parts(summed), widths, here)

    def turn_pieces(pieces):
        if within is not None:
            return pieces
        return [outside(p, groups, unit) for p in pieces]

    positions = jnp.arange(length, dtype=jnp.int32)
    piece, first_flags = segment_of(seq_lengths[0], positions)

    (columns_in, columns_g, vec_seq), cut = stacked_columns(
        [w_receptance, w_key, w_value, w_gate], [3 * part, part]
    )
    tokens_held = held_back(inputs_b, here, *cut)
    full_in = gather_dp(columns_in)
    vec_parts = gather_small(vec_seq[None, :, : vectors.shape[0]], "dp").astype(F32)
    vec = vec_parts.transpose(2, 1, 0, 3).reshape(-1, width)
    turned = vec_parts.transpose(2, 0, 1, 3).reshape(-1, width)
    vec_own = lax.dynamic_slice_in_dim(vec, place * part, part, 1)
    log_decay = -jnp.exp(vec_own[6])
    tables = wkv_tables(
        piece, 1.0 - first_flags.astype(F32), log_decay, vec_own[7], vec_own[8], vec_own[9]
    )
    marks = tables[0]
    rows_one = rows_of(turned, 0, 1, 2, 3, 4, 5)
    tokens_all = gather_seq(tokens_held, (rows_one, tables))
    full_g = gather_dp(after(columns_g, tokens_all[1:3], rows_one))
    own_o = gather_dp(after(w_output, tokens_all))

    mix_r, mix_k, mix_v, mix_g, step, recept, keyed, valued = mixes(
        turn_pieces(tokens_all), marks, rows_one, 4, True, within, here, tile, own_rows // tile,
        [(i, full_in, i, part) for i in range(3)], False,
    )
    projected = (recept, keyed, valued)
    ffn_weights = after([ffn_key, ffn_receptance], tokens_all)
    if seq == 4:
        pieces_c = trade_seq(cut_with_rider(ffn_weights, grad_b, here))
    else:
        (columns_c, _), _ = stacked_columns(ffn_weights, [hidden_width + part], projected)
        grad_all = gather_seq(after(grad_b, mix_r), projected)
    wkv, states = wkv_forward(recept, keyed, valued, tables, here, per)
    gate_pre, mixed = gated(mix_g, full_g, wkv, tables[5], here, seq)
    if seq == 4:
        pieces_c = after(pieces_c, mixed)
        columns_c = stack_below(pieces_c, here)
    full_c = gather_dp(columns_c)
    full_ck, full_cr = full_c[:, :hidden_width], full_c[:, hidden_width:]
    full_cv = gather_dp(after(ffn_value, columns_c))
    attn = [dot(rows, own_o, NN).astype(BF) for rows in blocks_of(mixed, seq)]
    after_mix, normed_two = after_norm(inputs_b, scatter_seq(attn, here), rows_of(vec, 10, 11), here)

    normed_two = gather_seq(normed_two)
    if seq == 4:
        grad_all = gather_second(grad_b, *after(pieces_c[1:3], normed_two))
    mix_k2, mix_r2, step_two, recept_pre, opened = mixes(
        turn_pieces(normed_two), marks, rows_of(turned, 10, 11, 12, 13), 2, False, within, here, tile,
        own_rows // tile, [(1, full_cr, 0, part)], True,
    )
    opened = gather_seq(after(opened, grad_all[3:]))
    key_pre = dot(mix_k2, full_ck, NN)
    smooth = jax.nn.softplus(key_pre)
    hidden = (smooth * smooth).astype(BF)
    slope = (2.0 * smooth * jax.nn.sigmoid(key_pre)).astype(BF)
    hidden, slope = lax.optimization_barrier((hidden, slope))
    later = after(hidden, opened[1:3])
    value_parts = [columns_product(later if j < 2 else hidden, full_cv, part, j, here, seq) for j in reversed(range(seq))]
    value_parts = value_parts[::-1]
    value_relayed = scatter_relay(value_parts, scatter_start(value_parts), here)
    d_value = spread_columns(
        grad_all, by_block(after(opened, value_parts, value_relayed)), here, True, True, tile, own_rows // tile
    )

    grad_cv = dot(hidden, d_value, TN).astype(BF)
    summed_cv = scatter_dp(grad_cv)
    value_terms = scatter_end(value_parts[0], value_relayed)
    d_hidden = dot(after(d_value, grad_cv), full_cv, NT)
    d_key_two = (d_hidden * slope.astype(F32)).astype(BF)
    channel, d_recept_two = channel_out(value_terms, recept_pre, grad_all, here, tile)
    grad_ck, grad_cr = [], []

    def beside_two(relayed):
        grad_ck.append(dot(after(mix_k2, relayed), d_key_two, TN).astype(BF))
        grad_cr.append(dot(after(mix_r2, relayed, grad_ck), d_recept_two, TN).astype(BF))
        return grad_ck, grad_cr

    terms_two, sums_two = mixes_back_scatter(
        [(0, d_key_two, 0, full_c, 0, hidden_width), (1, d_recept_two, 0, full_cr, 0, part)],
        step_two, marks, rows_of(turned, 12, 13), here, seq, beside_two,
    )
    summed_ck = scatter_dp(grad_ck[0])
    if within is None:
        terms_two = [outside(t, groups, unit, back=True) for t in terms_two]
    d_after, d_attn, norm_sums_two = norm_back(terms_two, after_mix, grad_b, rows_of(vec, 10), within, here)

    pieces = gather_seq(d_attn)
    *near, far = by_block(pieces)
    near_mixed = [dot(d, own_o, NT).astype(BF) for d in near]
    *near_rows, far_rows = blocks_of(mixed, seq)
    near_wo = sum(dot(m, d, TN) for m, d in zip(near_rows, near))
    far = after(far, near_mixed, near_wo, summed_cv)
    d_mixed = jnp.concatenate([*near_mixed, dot(far, own_o, NT).astype(BF)], axis=0)
    grad_wo = (near_wo + dot(far_rows, far, TN)).astype(BF)
    summed_o = scatter_dp(grad_wo)
    d_mixed = after(d_mixed, summed_ck, grad_wo)
    d_wkv, d_gate, gate_sums = gate_backward(wkv, gate_pre, d_mixed, tables[5], here)
    grad_g = dot(mix_g, d_gate, TN).astype(BF)
    summed_crg = scatter_dp(jnp.concatenate([grad_cr[0], grad_g], axis=1))
    d_recept, d_keyed, d_valued, sums = wkv_backward(
        recept, keyed, valued, after(d_wkv, grad_g), states, tables, here, per
    )
    channel = after(trade_seq(blocks_of(after(channel, d_mixed), seq)), d_recept)
    grads_in = [
        dot(after(m, channel), d, TN).astype(BF)
        for m, d in ((mix_r, d_recept), (mix_k, d_keyed), (mix_v, d_valued))
    ]
    summed_in = scatter_dp(jnp.concatenate(grads_in, axis=1))
    others = []

    def beside(relayed):
        others.append(spread_columns([after_mix], after(channel, relayed), here, False, False, CHUNK, per))
        others.append(after(summed_cv, relayed).astype(F32))
        return others

    d_recept, d_keyed = after((d_recept, d_keyed), grads_in, summed_o)
    terms, sums_one = mixes_back_scatter(
        [(i, d, 0, full_in, i, part) for i, d in enumerate((d_recept, d_keyed, d_valued))]
        + [(3, d_gate, 0, full_g, 0, part)],
        step, marks, rows_of(turned, 2, 3, 4, 5), here, seq, beside,
    )
    out_rows, sum_cv = others
    summed_c = jnp.concatenate(after([summed_ck, summed_crg], sums_one), axis=1)
    sent_c = owners_parts(summed_c)
    terms = after(terms, summed_c, sent_c[0])
    if within is None:
        terms = [outside(t, groups, unit, back=True) for t in terms]
    tokens_grad, _, norm_sums = norm_back(terms, inputs_b, d_after, rows_of(vec, 0), within, here)

    sum_o = summed_o.astype(F32)

    def by_device(rows, turn):
        if turn:
            return rows.reshape(-1, dp, seq, unit).transpose(2, 1, 0, 3)
        return rows.reshape(-1, seq, dp, unit).transpose(1, 2, 0, 3)

    own_sums = jnp.stack([sums[0] * log_decay, sums[1], gate_sums[0], gate_sums[1]])
    own_sums = lax.dynamic_update_slice(jnp.zeros((4, width), F32), own_sums, (0, place * part))
    vector_rows = jnp.concatenate(
        [
            by_device(norm_sums[:2], False), by_device(sums_one[:4], True), by_device(own_sums, False),
            by_device(norm_sums_two[:2], False), by_device(sums_two[:2], True),
        ],
        axis=2,
    )
    parts_c = after(sent_c, tokens_grad)
    sum_ck, sum_cr, sum_g = join_columns(parts_c, [ffn_key.shape[1], width, width], here)
    vector_rows = after(vector_rows, sum_ck)
    sums_seq = scatter_small(vector_rows.reshape((-1,) + vector_rows.shape[2:]), "seq")
    sum_vec = scatter_small(sums_seq, "dp")[0]
    sum_r, sum_k, sum_v = owners_rows(after(summed_in, sums_seq), [width] * 3)
    return (
        out_rows[None], tokens_grad[None], sum_r, sum_k, sum_v, sum_g, sum_o,
        sum_ck, sum_cr, sum_cv, sum_vec,
    )


def solution(mesh):
    tokens = P("dp", "seq", None)
    rows = P(("seq", "dp"), None)
    columns = P(None, ("seq", "dp"))
    return jax.shard_map(
        shards,
        mesh=mesh,
        in_specs=(tokens, P("dp", None), tokens) + (rows,) * 8 + (columns,),
        out_specs=(tokens, tokens) + (rows,) * 8 + (columns,),
        check_vma=False,
    )
```

```python
from functools import partial

import jax
import jax.numpy as jnp
from jax import lax
from jax.experimental import pallas as pl
from jax.experimental.pallas import tpu as pltpu
from jax.sharding import PartitionSpec as P

HEAD = 64
PAIR = 128
CHUNK = 128
EPSILON = 1e-05
GROUP_EPSILON = 1.0
BF = jnp.bfloat16
F32 = jnp.float32
NT = (((1,), (1,)), ((), ()))
TN = (((0,), (0,)), ((), ()))
NN = (((1,), (0,)), ((), ()))


def swap(value, axis, distance):
    size = lax.axis_size(axis)
    return lax.ppermute(value, axis, [(i, i ^ distance) for i in range(size)])


def after(value, *others):
    return lax.optimization_barrier((value, others))[0]


def gather_second(part, one, two):
    half = part.shape[0] // 2
    columns = part.shape[1]
    low, high = swap(one[:half, :columns], "seq", 2), swap(two[half : 2 * half, :columns], "seq", 1)
    return [part, one, two, low, high]


def gather_seq(part, first=()):
    size = lax.axis_size("seq")
    if size == 4:
        half = part.shape[0] // 2
        one, two = swap(part, "seq", 1), swap(part, "seq", 2)
        one, two = after((one, two), first)
        low, high = swap(one[:half], "seq", 2), swap(two[half:], "seq", 1)
        return [part, one, two, low, high]
    return [part] + [swap(part, "seq", distance) for distance in range(1, size)]


def by_block(pieces):
    if lax.axis_size("seq") == 4:
        return pieces[:3] + [jnp.concatenate(pieces[3:], axis=0)]
    return pieces


def scatter_start(parts):
    if lax.axis_size("seq") != 4:
        return ()
    low, high = parts[3:] if len(parts) == 5 else blocks_of(parts[3], 2)
    return swap(low, "seq", 1), swap(high, "seq", 2)


def relay_body(here, one_ref, two_ref, low_ref, high_ref, one_out, two_out):
    one, two = one_ref[...], two_ref[...]
    first = pl.program_id(0) == 0
    low, high = low_ref[...].astype(F32), high_ref[...].astype(F32)
    one_out[...] = jnp.where(first, one, (one.astype(F32) + high).astype(BF))
    two_out[...] = jnp.where(first, (two.astype(F32) + low).astype(BF), two)


def scatter_relay(parts, started, here):
    if lax.axis_size("seq") != 4:
        return parts[1:]
    (_, one, two, *_), (low, high) = parts, started
    (rows, width), half = one.shape, block(low.shape, lambda i, h: (i, 0))
    return kernel(
        relay_body, "relay", (2,), here,
        [(one, half), (two, half), (low, fixed(low.shape)), (high, fixed(low.shape))],
        [((rows, width), BF, half)] * 2,
    )


def scatter_end(own, relayed):
    return [own] + [swap(part, "seq", j + 1) for j, part in enumerate(relayed)]


def scatter_seq(parts, here):
    return scatter_end(parts[0], scatter_relay(parts, scatter_start(parts), here))


def trade_seq(parts):
    return [parts[0]] + [swap(part, "seq", j + 1) for j, part in enumerate(parts[1:])]


def blocks_of(values, size):
    rows = values.shape[0] // size
    return [values[j * rows : (j + 1) * rows] for j in range(size)]


def bits_of(size):
    return [1 << b for b in range(size.bit_length() - 1)]


def gather_small(part, axis):
    for bit in bits_of(lax.axis_size(axis)):
        other = swap(part, axis, bit)
        second = (lax.axis_index(axis) & bit) != 0
        part = jnp.concatenate([jnp.where(second, other, part), jnp.where(second, part, other)], axis=0)
    return part


def scatter_small(parts, axis, before_last=()):
    for bit in reversed(bits_of(lax.axis_size(axis))):
        parts = after(parts, before_last) if bit == 1 else parts
        half = parts.shape[0] // 2
        second = (lax.axis_index(axis) & bit) != 0
        low, high = parts[:half], parts[half:]
        parts = jnp.where(second, high, low) + swap(jnp.where(second, low, high), axis, bit)
    return parts


def block(shape, index):
    return pl.BlockSpec(shape, lambda *i: index(*i[:-1], i[-1][0]))


def fixed(shape):
    return pl.BlockSpec(shape, lambda *i: (0,) * len(shape))


def relative(tile, per, here):
    return (lax.div(tile, per) ^ here) * per + lax.rem(tile, per)


def kernel(body, name, grid, here, ins, outs, scratch=(), vmem=48):
    return pl.pallas_call(
        body,
        out_shape=[jax.ShapeDtypeStruct(shape, kind) for shape, kind, _ in outs],
        grid_spec=pltpu.PrefetchScalarGridSpec(
            num_scalar_prefetch=1,
            grid=grid,
            in_specs=[spec for _, spec in ins],
            out_specs=[spec for _, _, spec in outs],
            scratch_shapes=list(scratch),
        ),
        compiler_params=pltpu.CompilerParams(vmem_limit_bytes=vmem * 2**20),
        name=name,
    )(here, *[array for array, _ in ins])


def pieced(pieces, tile, columns, column, place):
    ins, start = [], 0
    for piece in pieces:
        count = piece.shape[0] // tile

        def index(i, h, start=start, count=count):
            return jnp.clip(place(i, h) - start, 0, count - 1), column(h)

        ins.append((piece, block((tile, columns), index)))
        start += count
    return ins


def picked(refs, counts, tile, held):
    start = 0
    for ref, count in zip(refs, counts):

        @pl.when((tile >= start) & (tile < start + count))
        def _(ref=ref):
            held[...] = ref[...]

        start += count
    return held[...].astype(F32)


def counts_of(pieces, tile):
    return [piece.shape[0] // tile for piece in pieces]


def row_index(rows):
    return lax.broadcasted_iota(jnp.int32, (rows, 1), 0)


def placed(place, width):
    return pl.ds(pl.multiple_of(place * width, width), width)


def cut_body(count, parts, here, *refs):
    ins, beside, outs = refs[:count], refs[count], refs[count + 1 :]
    rows = ins[0].shape[0]
    for j in range(parts):
        outs[j][rows:, :] = jnp.zeros_like(outs[j][rows:, :])
        outs[j][rows:, : beside.shape[1]] = beside[...]
    at = 0
    for ref in ins:
        width = ref.shape[1] // parts
        for j in range(parts):
            outs[j][:rows, at : at + width] = ref[:, placed(here[0] ^ j, width)]
        at += width


def cut_columns(weights, beside, here, parts):
    rows, width = weights[0].shape[0] + beside.shape[0], sum(w.shape[1] for w in weights) // parts
    return kernel(
        partial(cut_body, len(weights), parts), "cut_columns", (1,), here,
        [(w, fixed(w.shape)) for w in [*weights, beside]],
        [((rows, width), BF, fixed((rows, width)))] * parts,
    )


def stack_body(parts, here, *refs):
    start = 0
    outs, beside = refs[parts:-1], refs[-1]
    for out in outs:
        for j in range(parts):
            out[here[0] ^ j] = refs[j][: out.shape[1], start : start + out.shape[2]]
        start += out.shape[2]
    for j in range(parts):
        beside[here[0] ^ j] = refs[j][out.shape[1] :, : beside.shape[2]]


def stack_rows(pieces, widths, beside, here):
    parts, rows = len(pieces), pieces[0].shape[0] - beside.shape[0]
    shapes = [(parts, rows, width) for width in widths] + [(parts,) + beside.shape]
    return kernel(
        partial(stack_body, parts), "stack_rows", (1,), here,
        [(p, fixed(p.shape)) for p in pieces],
        [(shape, BF, fixed(shape)) for shape in shapes],
    )


def ride_body(count, here, *refs):
    ins, rider, outs = refs[:count], refs[count], refs[count + 1 :]
    for j, out in enumerate(outs):
        top, at = 0, 0
        if j in (1, 2):
            top = rider.shape[0]
            out[:top, : rider.shape[1]] = rider[...]
            out[:top, rider.shape[1] :] = jnp.zeros_like(out[:top, rider.shape[1] :])
        for ref in ins:
            width = ref.shape[1] // 4
            out[top:, at : at + width] = ref[:, placed(here[0] ^ j, width)]
            at += width


def cut_with_rider(weights, rider, here):
    rows, width = weights[0].shape[0], sum(w.shape[1] for w in weights) // 4
    return kernel(
        partial(ride_body, len(weights)), "cut_columns", (1,), here,
        [(w, fixed(w.shape)) for w in [*weights, rider]],
        [((n, width), BF, fixed((n, width))) for n in (rows, rows + rider.shape[0], rows + rider.shape[0], rows)],
    )


def unride_body(here, *refs):
    out = refs[-1]
    rows = out.shape[1]
    for j, ref in enumerate(refs[:-1]):
        out[here[0] ^ j] = ref[ref.shape[0] - rows :, :]


def stack_below(pieces, here):
    shape = (4,) + pieces[0].shape
    (stacked,) = kernel(
        unride_body, "stack_rows", (1,), here,
        [(p, fixed(p.shape)) for p in pieces],
        [(shape, BF, fixed(shape))],
    )
    return stacked.reshape(-1, shape[-1])


def hold_body(here, in_ref, *refs):
    refs[-1][...] = in_ref[...]


def held_back(values, here, *others):
    rows, width = values.shape
    own = block((rows // 2, width), lambda i, h: (i, 0))
    (copy,) = kernel(
        hold_body, "hold", (2,), here,
        [(values, own)] + [(o, pl.BlockSpec(memory_space=pl.ANY)) for o in others],
        [((rows, width), values.dtype, own)],
    )
    return copy


def join_body(parts, count, here, *refs):
    ins, outs = refs[:parts], refs[parts:]
    at = 0
    for ref in outs:
        width = ref.shape[1] // parts
        for j in range(parts):
            ref[:, placed(here[0] ^ j, width)] = ins[j][:, at : at + width].astype(F32)
        at += width


def join_columns(pieces, widths, here):
    parts, rows = len(pieces), pieces[0].shape[0]
    return kernel(
        partial(join_body, parts, len(widths)), "join_columns", (1,), here,
        [(p, fixed(p.shape)) for p in pieces],
        [((rows, width), F32, fixed((rows, width))) for width in widths],
    )


def spread_body(counts, parts, product, here, *refs):
    bases, pieces, out, held = refs[: len(counts)], refs[len(counts) : -2], refs[-2], refs[-1]
    picked(bases, counts, pl.program_id(0), held)
    width = pieces[0].shape[1]
    for j in range(parts):
        at = placed(here[0] ^ j, width)
        piece, base = pieces[j][...].astype(F32), held[:, at].astype(F32)
        out[:, at] = (base * piece if product else base + piece).astype(BF)


def spread_columns(bases, columns, here, product, turn, tile, per):
    rows, width = sum(counts_of(bases, tile)) * tile, bases[0].shape[1]

    def turned(i, j):
        return (lax.div(i, per) ^ j) * per + lax.rem(i, per) if turn else i

    (result,) = kernel(
        partial(spread_body, counts_of(bases, tile), len(columns), product), "spread_columns", (rows // tile,), here,
        pieced(bases, tile, width, lambda h: 0, lambda i, h: i)
        + [(c, block((tile, c.shape[1]), lambda i, h, j=j: (turned(i, j), 0))) for j, c in enumerate(columns)],
        [((rows, width), BF, block((tile, width), lambda i, h: (i, 0)))],
        [pltpu.VMEM((tile, width), bases[0].dtype)],
    )
    return result


def shuffled(values, groups, back=False):
    seq, dp = groups
    if back:
        seq, dp = dp, seq
    lane = lax.broadcasted_iota(jnp.int32, (1, PAIR), 1) < HEAD
    source = [s * dp + d for d in range(dp) for s in range(seq)]
    columns = []
    for one, two in zip(source[::2], source[1::2]):
        low = values[:, one // 2 * PAIR : (one // 2 + 1) * PAIR]
        high = values[:, two // 2 * PAIR : (two // 2 + 1) * PAIR]
        low = pltpu.roll(low, HEAD, 1) if one % 2 else low
        high = high if two % 2 else pltpu.roll(high, HEAD, 1)
        columns.append(jnp.where(lane, low, high))
    return jnp.concatenate(columns, axis=1)


def outside(values, groups, channels, back=False):
    seq, dp = groups[::-1] if back else groups
    return values.reshape(-1, seq, dp, channels).swapaxes(1, 2).reshape(values.shape)


def centre(values):
    centred = values - jnp.mean(values, axis=-1, keepdims=True)
    spread = jnp.mean(centred * centred, axis=-1, keepdims=True)
    return centred, lax.rsqrt(spread + EPSILON)


def mix_body(count, norm, groups, counts, per, mixed, open_up, here, *refs):
    pieces, (marks_ref, vec_ref) = refs[: len(counts)], refs[len(counts) : len(counts) + 2]
    weights = refs[len(counts) + 2 : len(counts) + 2 + len(mixed)]
    outs, last, held = refs[len(counts) + 2 + len(mixed) : -2], refs[-2], refs[-1]
    products = outs[count + 1 :]

    @pl.when(pl.program_id(0) == 0)
    def _():
        last[...] = jnp.zeros_like(last)

    values = picked(pieces, counts, relative(pl.program_id(0), per, here[0]), held)
    if norm:
        centred, inverse = centre(values)
        values = centred * inverse
    if groups:
        values = shuffled(values, groups)
    if norm:
        values = values * vec_ref[0:1, :] + vec_ref[1:2, :]
    rows = values.shape[0]
    previous = jnp.where(row_index(rows) == 0, last[0:1, :], pltpu.roll(values, 1, 0)) * marks_ref[:, 3:4]
    last[0:1, :] = values[rows - 1 :, :]
    step = values - previous
    outs[count][...] = step.astype(BF)
    for i in range(count):
        mix = (previous + step * vec_ref[2 + i : 3 + i, :]).astype(BF)
        outs[i][...] = mix
        if i in mixed:
            k = mixed.index(i)
            product = dot(mix, weights[k][...], NN)
            if open_up:
                products[0][...] = product
                products[1][...] = (1.0 / (1.0 + jnp.exp(-product))).astype(BF)
            else:
                products[k][...] = product.astype(BF)


def mixes(pieces, marks, vec, count, norm, groups, here, tile, per, weights, open_up):
    rows, width = marks.shape[0], pieces[0].shape[1]
    own = block((tile, width), lambda i, h: (relative(i, per, h), 0))
    outs = [((rows, width), BF, own)] * (count + 1)
    for _, _, _, part in weights:
        narrow = block((tile, part), lambda i, h: (relative(i, per, h), 0))
        outs += [((rows, part), F32 if open_up else BF, narrow)] + [((rows, part), BF, narrow)] * open_up
    return kernel(
        partial(mix_body, count, norm, groups, counts_of(pieces, tile), per, [w[0] for w in weights], open_up),
        "mixes", (rows // tile,), here,
        pieced(pieces, tile, width, lambda h: 0, lambda i, h: relative(i, per, h))
        + [(marks, block((tile, PAIR), lambda i, h: (i, 0))), (vec, fixed(vec.shape))]
        + [(w, pl.BlockSpec((width, part), lambda *_, at=at: (0, at))) for _, w, at, part in weights],
        outs,
        [pltpu.VMEM((8, width), F32), pltpu.VMEM((tile, width), BF)],
        vmem=58,
    )


def mixes_back_body(which, first, seq, outs, here, *refs):
    count = len(which)
    grads, nexts, weights = refs[:count], refs[count : 2 * count], refs[2 * count : 3 * count]
    step_ref, marks_ref, next_marks_ref, vec_ref, *out_refs, sums_ref = refs[3 * count :]

    @pl.when(pl.program_id(1) == 0)
    def _():
        sums_ref[...] = jnp.zeros_like(sums_ref)

    step = step_ref[...].astype(F32)
    rows = step.shape[0]
    total = straight = None
    for i in range(which[-1] + 1):
        grad = sum(
            dot(jnp.concatenate([grads[k][...], nexts[k][...]], axis=0), weights[k][...], NT)
            for k in range(count)
            if which[k] == i
        )
        sums_ref[i : i + 1, :] += jnp.sum(grad[:rows] * step, axis=0, keepdims=True)
        part = grad * vec_ref[i : i + 1, :]
        total, straight = (total + grad, straight + part) if i else (grad, part)
    inside = ((first + pl.program_id(1)) ^ here[0]) < seq - 1
    keep = jnp.concatenate([marks_ref[:, 3:4], jnp.where(inside, next_marks_ref[:, 3:4], 0.0)], axis=0)
    kept = (total - straight) * keep
    up = pltpu.roll(kept, kept.shape[0] - 1, 0)
    result = (straight[:rows] + up[:rows]).astype(BF)
    if len(out_refs) == 1:
        out_refs[0][...] = result
        return
    if outs == 1:
        out_refs[0][...] = result[: rows // 2]
        out_refs[1][...] = result[rows // 2 :]
        return
    for k, out_ref in enumerate(out_refs):

        @pl.when(pl.program_id(1) == k)
        def _(out_ref=out_ref):
            out_ref[...] = result


EXTRA = 16


def mixes_back(terms, step, marks, vec, here, seq, first, count, halves=False):
    rows, width = step.shape
    tile, columns = rows // seq, min(512, width)
    extras = tile // EXTRA

    def following(i, h):
        return jnp.minimum(((first + i) ^ h) + 1, seq - 1)

    ins = [(g, block((tile, n), lambda c, i, h, at=at: (first + i, at))) for _, g, at, _, _, n in terms]
    ins += [
        (g, block((EXTRA, n), lambda c, i, h, at=at: ((following(i, h) ^ h) * extras, at)))
        for _, g, at, _, _, n in terms
    ]
    ins += [(w, block((columns, n), lambda c, i, h, at=at: (c, at))) for _, _, _, w, at, n in terms]
    ins += [
        (step, block((tile, columns), lambda c, i, h: (first + i, c))),
        (marks, block((tile, PAIR), lambda c, i, h: ((first + i) ^ h, 0))),
        (marks, block((EXTRA, PAIR), lambda c, i, h: (following(i, h) * extras, 0))),
        (vec, block((8, columns), lambda c, i, h: (0, c))),
    ]
    size = tile // 2 if halves else tile
    *parts, sums = kernel(
        partial(mixes_back_body, [t[0] for t in terms], first, seq, count), "mixes_back", (width // columns, count), here, ins,
        [((size, width), BF, block((size, columns), lambda c, i, h: (0, c)))] * (2 if halves else count)
        + [((8, width), F32, block((8, columns), lambda c, i, h: (0, c)))],
    )
    return parts, sums


def mixes_back_scatter(terms, step, marks, vec, here, seq, beside):
    if seq != 4:
        parts, sums = mixes_back(terms, step, marks, vec, here, seq, 0, seq)
        return after(scatter_seq(parts, here), beside(parts)), sums

    def call(first, count, *before):
        ordered = after([t[1] for t in terms], *before)
        return mixes_back(
            [(t[0], g) + t[2:] for t, g in zip(terms, ordered)], step, marks, vec, here, seq, first, count, first == 3
        )

    far, sums_far = call(3, 1)
    near, sums_near = call(1, 2, far)
    parts = [None, *near, *far]
    started = after(scatter_start(parts), near)
    relayed = scatter_relay(parts, started, here)
    (own,), sums_own = call(0, 1, near, relayed)
    return after(scatter_end(own, relayed), beside(relayed)), sums_far + sums_near + sums_own


def after_body(count, here, x_ref, vec_ref, *refs):
    after_ref, normed_ref = refs[count:]
    after = x_ref[...].astype(F32)
    for ref in refs[:count]:
        after = after + ref[...].astype(F32)
    after_ref[...] = after
    centred, inverse = centre(after)
    normed_ref[...] = (centred * inverse * vec_ref[0:1, :] + vec_ref[1:2, :]).astype(BF)


def after_norm(inputs, terms, vec, here):
    rows, width = inputs.shape
    own = block((CHUNK, width), lambda i, h: (i, 0))
    return kernel(
        partial(after_body, len(terms)), "after_norm", (rows // CHUNK,), here,
        [(inputs, own), (vec, fixed(vec.shape))] + [(t, own) for t in terms],
        [((rows, width), F32, own), ((rows, width), BF, own)],
    )


def norm_back_body(count, groups, here, x_ref, base_ref, vec_ref, *refs):
    wide_ref, narrow_ref, sums_ref = refs[count:]

    @pl.when(pl.program_id(0) == 0)
    def _():
        sums_ref[...] = jnp.zeros_like(sums_ref)

    grad = refs[0][...].astype(F32)
    for ref in refs[1:count]:
        grad = grad + ref[...].astype(F32)
    if groups:
        grad = shuffled(grad, groups, back=True)
    centred, inverse = centre(x_ref[...].astype(F32))
    normed = centred * inverse
    sums_ref[0:1, :] += jnp.sum(grad * normed, axis=0, keepdims=True)
    sums_ref[1:2, :] += jnp.sum(grad, axis=0, keepdims=True)
    grad = grad * vec_ref[0:1, :]
    grad = grad - jnp.mean(grad, axis=-1, keepdims=True) - normed * jnp.mean(grad * normed, axis=-1, keepdims=True)
    result = base_ref[...].astype(F32) + inverse * grad
    wide_ref[...] = result
    narrow_ref[...] = result.astype(BF)


def norm_back(terms, inputs, base, vec, groups, here):
    rows, width = inputs.shape
    own = block((CHUNK, width), lambda i, h: (i, 0))
    return kernel(
        partial(norm_back_body, len(terms), groups), "norm_back", (rows // CHUNK,), here,
        [(inputs, own), (base, own), (vec, fixed(vec.shape))] + [(t, own) for t in terms],
        [((rows, width), F32, own), ((rows, width), BF, own), ((8, width), F32, fixed((8, width)))],
    )


def gate_body(mix_ref, weight_ref, wkv_ref, par_ref, gate_ref, mixed_ref):
    gate = dot(mix_ref[...], weight_ref[...], NN)
    gate_ref[...] = gate
    ones = jnp.where(same_head(), 1.0, 0.0).astype(BF)
    for pair in range(gate.shape[1] // PAIR):
        at = slice(pair * PAIR, (pair + 1) * PAIR)
        wkv = wkv_ref[:, at]
        centred = wkv - head_sum_fine(wkv, ones) * (1.0 / HEAD)
        spread = head_sum(centred * centred, ones) * (1.0 / HEAD)
        normed = centred * lax.rsqrt(spread + GROUP_EPSILON) * par_ref[1:2, at] + par_ref[2:3, at]
        mixed_ref[:, at] = (normed * (gate[:, at] / (1.0 + jnp.exp(-gate[:, at])))).astype(BF)


def gated(mix_g, weights, wkv, params, here, seq):
    rows, width = mix_g.shape
    tile, part = rows // seq, wkv.shape[1]
    own = block((tile, part), lambda i, h: (i, 0))
    return kernel(
        lambda here, *refs: gate_body(*refs), "gate", (seq,), here,
        [
            (mix_g, block((tile, width), lambda i, h: (i, 0))),
            (weights, block((width, part), lambda i, h: (0, 0))),
            (wkv, own),
            (params, fixed(params.shape)),
        ],
        [((rows, part), F32, own), ((rows, part), BF, own)],
    )


def columns_body(here, left_ref, right_ref, out_ref):
    out_ref[...] = dot(left_ref[...], right_ref[...], NN).astype(BF)


def columns_product(left, right, part, relative_to, here, seq):
    rows, depth = left.shape
    tile = rows // seq
    (result,) = kernel(
        columns_body, "value_columns", (seq,), here,
        [
            (left, block((tile, depth), lambda i, h: (i, 0))),
            (right, block((depth, part), lambda i, h: (0, h ^ relative_to))),
        ],
        [((rows, part), BF, block((tile, part), lambda i, h: (i ^ relative_to, 0)))],
    )
    return result


def channel_body(counts, here, pre_ref, *refs):
    grads, terms, (channel_ref, d_recept_ref, held) = refs[: len(counts)], refs[len(counts) : -3], refs[-3:]
    value = sum(ref[...].astype(F32) for ref in terms)
    opened = 1.0 / (1.0 + jnp.exp(-pre_ref[...]))
    channel = opened * value
    channel_ref[...] = channel.astype(BF)
    grad = picked(grads, counts, pl.program_id(0), held)
    d_recept_ref[...] = (grad * channel * (1.0 - opened)).astype(BF)


def channel_out(terms, pre, grads, here, tile):
    rows, part = pre.shape
    own = block((tile, part), lambda i, h: (i, 0))
    return kernel(
        partial(channel_body, counts_of(grads, tile)), "channel", (rows // tile,), here,
        [(pre, own)] + pieced(grads, tile, part, lambda h: h, lambda i, h: i) + [(t, own) for t in terms],
        [((rows, part), BF, own)] * 2,
        [pltpu.VMEM((tile, part), BF)],
    )


def head_masks():
    lane = lax.broadcasted_iota(jnp.int32, (1, PAIR), 1)
    first = (lane < HEAD).astype(F32)
    return first, 1.0 - first


def same_head():
    row = lax.broadcasted_iota(jnp.int32, (PAIR, PAIR), 0) < HEAD
    column = lax.broadcasted_iota(jnp.int32, (PAIR, PAIR), 1) < HEAD
    return row == column


def dot(left, right, dims):
    return lax.dot_general(left, right, dims, preferred_element_type=F32)


def head_sum(values, ones):
    return dot(values.astype(BF), ones, NN)


def head_sum_fine(values, ones):
    coarse = values.astype(BF)
    rest = (values - coarse.astype(F32)).astype(BF)
    return dot(coarse, ones, NN) + dot(rest, ones, NN)


def stacked(values, first, second):
    return jnp.concatenate([(values * first).astype(BF), (values * second).astype(BF)], axis=0)


def masks_of(rows_ref, columns_ref):
    segment = rows_ref[:, 0:1]
    reaches = rows_ref[:, 1:2]
    last_same = rows_ref[:, 2:3]
    reach_last = rows_ref[CHUNK - 1 : CHUNK, 1:2]
    before = lax.broadcasted_iota(jnp.int32, (CHUNK, CHUNK), 1) < lax.broadcasted_iota(
        jnp.int32, (CHUNK, CHUNK), 0
    )
    allowed = jnp.where((segment == columns_ref[0:1, :]) & before, 1.0, 0.0)
    return reaches, last_same, reach_last, jnp.concatenate([allowed, allowed], axis=0)


def wkv_forward_body(
    here, r_ref, k_ref, v_ref, rows_ref, columns_ref, grow_ref, shrink_ref, tail_ref, par_ref,
    wkv_ref, states_ref, state,
):
    @pl.when(pl.program_id(0) == 0)
    def _():
        state[...] = jnp.zeros_like(state)

    first, second = head_masks()
    block = same_head()
    ones = jnp.where(block, 1.0, 0.0).astype(BF)
    reaches, last_same, reach_last, allowed = masks_of(rows_ref, columns_ref)
    for pair in range(r_ref.shape[1] // PAIR):
        at = slice(pair * PAIR, (pair + 1) * PAIR)
        r, k, v = r_ref[:, at].astype(F32), k_ref[:, at].astype(F32), v_ref[:, at].astype(F32)
        bonus, decay = par_ref[0:1, at], par_ref[3:4, at]
        held = state[at, :]
        held_b = held.astype(BF)
        states_ref[0, at, :] = held_b
        grown = r * grow_ref[:, at]
        shrunk = (k * shrink_ref[:, at]).astype(BF)
        scores = (dot(stacked(grown, first, second), shrunk, NT) * allowed).astype(BF)
        both = jnp.concatenate([scores[:CHUNK], scores[CHUNK:]], axis=1)
        wkv = dot(both, stacked(v, first, second), NN)
        wkv = wkv + dot((grown * reaches).astype(BF), held_b, NT)
        wkv = wkv + head_sum(r * bonus * k, ones) * v
        fresh = dot(v_ref[:, at], (k * tail_ref[:, at] * last_same).astype(BF), TN)
        state[at, :] = held * (decay * reach_last) + jnp.where(block, fresh, 0.0)
        wkv_ref[:, at] = wkv


def wkv_backward_body(
    here, r_ref, k_ref, v_ref, d_wkv_ref, states_ref,
    rows_ref, columns_ref, grow_ref, shrink_ref, tail_ref, par_ref,
    d_r_ref, d_k_ref, d_v_ref, sums_ref, d_state,
):
    @pl.when(pl.program_id(0) == 0)
    def _():
        d_state[...] = jnp.zeros_like(d_state)
        sums_ref[...] = jnp.zeros_like(sums_ref)

    first, second = head_masks()
    block = same_head()
    ones = jnp.where(block, 1.0, 0.0).astype(BF)
    reaches, last_same, reach_last, allowed = masks_of(rows_ref, columns_ref)
    offset = lax.broadcasted_iota(jnp.int32, (CHUNK, PAIR), 0).astype(F32)
    for pair in range(r_ref.shape[1] // PAIR):
        at = slice(pair * PAIR, (pair + 1) * PAIR)
        bonus, decay = par_ref[0:1, at], par_ref[3:4, at]
        d_wkv = d_wkv_ref[:, at].astype(F32)
        r, k, v = r_ref[:, at].astype(F32), k_ref[:, at].astype(F32), v_ref[:, at].astype(F32)
        v_b, d_wkv_b = v_ref[:, at], d_wkv_ref[:, at]
        grow, shrink, tail = grow_ref[:, at], shrink_ref[:, at], tail_ref[:, at] * last_same
        held = states_ref[0, at, :]
        later = d_state[at, :]
        later_b = later.astype(BF)
        grown = r * grow
        shrunk = k * shrink
        shrunk_b = shrunk.astype(BF)
        tailed_b = (k * tail).astype(BF)
        grown_two = stacked(grown, first, second)
        d_wkv_two = stacked(d_wkv, first, second)
        scores = (dot(grown_two, shrunk_b, NT) * allowed).astype(BF)
        d_scores = (dot(d_wkv_two, v_b, NT) * allowed).astype(BF)
        d_both = jnp.concatenate([d_scores[:CHUNK], d_scores[CHUNK:]], axis=1)
        d_grown = dot(d_both, stacked(shrunk, first, second), NN)
        d_grown = d_grown + dot((d_wkv * reaches).astype(BF), held, NN)
        d_shrunk = dot(d_scores, grown_two, TN)
        d_tailed = dot(v_b, later_b, NN)
        share = head_sum(r * bonus * k, ones)
        d_share = head_sum(d_wkv * v, ones)
        d_v = dot(scores, d_wkv_two, TN) + dot(tailed_b, later_b, NT) + share * d_wkv
        d_r_ref[:, at] = (d_grown * grow + d_share * bonus * k).astype(BF)
        d_k_ref[:, at] = (d_shrunk * shrink + d_tailed * tail + d_share * bonus * r).astype(BF)
        d_v_ref[:, at] = d_v.astype(BF)
        carried = decay * reach_last
        d_fresh = dot(d_wkv_b, (grown * reaches).astype(BF), TN)
        d_state[at, :] = later * carried + jnp.where(block, d_fresh, 0.0)
        grown_b = grown.astype(BF).astype(F32)
        d_log = (
            offset * grown_b * d_grown
            - (offset + 1.0) * shrunk_b.astype(F32) * d_shrunk
            + (CHUNK - 1.0 - offset) * tailed_b.astype(F32) * d_tailed
        )
        kept = CHUNK * carried * jnp.sum(held.astype(F32) * later, axis=0, keepdims=True)
        sums_ref[0:1, at] += jnp.sum(d_log, axis=0, keepdims=True) + kept
        sums_ref[1:2, at] += jnp.sum(d_share * r * k, axis=0, keepdims=True)


def gate_backward_body(here, wkv_ref, g_ref, d_mixed_ref, par_ref, d_wkv_ref, d_g_ref, sums_ref):
    @pl.when(pl.program_id(0) == 0)
    def _():
        sums_ref[...] = jnp.zeros_like(sums_ref)

    ones = jnp.where(same_head(), 1.0, 0.0).astype(BF)
    for pair in range(wkv_ref.shape[1] // PAIR):
        at = slice(pair * PAIR, (pair + 1) * PAIR)
        gain, bias = par_ref[1:2, at], par_ref[2:3, at]
        wkv, gate, d_mixed = wkv_ref[:, at], g_ref[:, at], d_mixed_ref[:, at].astype(F32)
        centred = wkv - head_sum_fine(wkv, ones) * (1.0 / HEAD)
        spread = head_sum(centred * centred, ones) * (1.0 / HEAD)
        inverse = lax.rsqrt(spread + GROUP_EPSILON)
        normed = centred * inverse
        opened = 1.0 / (1.0 + jnp.exp(-gate))
        d_scaled = d_mixed * gate * opened
        d_g = d_mixed * (normed * gain + bias) * opened * (1.0 + gate * (1.0 - opened))
        d_g_ref[:, at] = d_g.astype(BF)
        d_normed = d_scaled * gain
        mean_one = head_sum(d_normed, ones) * (1.0 / HEAD)
        mean_two = head_sum(d_normed * normed, ones) * (1.0 / HEAD)
        d_wkv_ref[:, at] = (inverse * (d_normed - mean_one - normed * mean_two)).astype(BF)
        sums_ref[0:1, at] += jnp.sum(d_scaled * normed, axis=0, keepdims=True)
        sums_ref[1:2, at] += jnp.sum(d_scaled, axis=0, keepdims=True)


def gate_backward(wkv, gate, d_mixed, params, here):
    rows, part = wkv.shape
    own = block((2 * CHUNK, part), lambda i, h: (i, 0))
    return kernel(
        gate_backward_body, "gate_backward", (rows // (2 * CHUNK),), here,
        [(a, own) for a in (wkv, gate, d_mixed)] + [(params, fixed(params.shape))],
        [((rows, part), BF, own)] * 2 + [((8, part), F32, fixed((8, part)))],
    )


def wkv_blocks(width, chunks, per, backward):
    def chunk(i):
        return chunks - 1 - i if backward else i

    tokens = block((CHUNK, width), lambda i, h: (relative(chunk(i), per, h), 0))
    states = block((1, width, PAIR), lambda i, h: (chunk(i), 0, 0))
    tables = [
        block((CHUNK, PAIR), lambda i, h: (chunk(i), 0)),
        block((8, CHUNK), lambda i, h: (0, chunk(i))),
    ]
    return tokens, states, tables + [fixed((CHUNK, width))] * 3 + [fixed((8, width))]


def wkv_forward(r, k, v, tables, here, per):
    length, width = r.shape
    chunks = length // CHUNK
    tokens, states, blocks = wkv_blocks(width, chunks, per, False)
    return kernel(
        wkv_forward_body, "wkv_forward", (chunks,), here,
        [(a, tokens) for a in (r, k, v)] + list(zip(tables, blocks)),
        [((length, width), F32, tokens), ((chunks, width, PAIR), BF, states)],
        [pltpu.VMEM((width, PAIR), F32)],
    )


def wkv_backward(r, k, v, d_wkv, states_kept, tables, here, per):
    length, width = r.shape
    chunks = length // CHUNK
    tokens, states, blocks = wkv_blocks(width, chunks, per, True)
    return kernel(
        wkv_backward_body, "wkv_backward", (chunks,), here,
        [(a, tokens) for a in (r, k, v, d_wkv)] + [(states_kept, states)] + list(zip(tables, blocks)),
        [((length, width), BF, tokens)] * 3 + [((8, width), F32, fixed((8, width)))],
        [pltpu.VMEM((width, PAIR), F32)],
    )


def wkv_tables(piece, keep, log_decay, bonus, gain, bias):
    length = piece.shape[0]
    by_chunk = piece.reshape(length // CHUNK, CHUNK)
    before = jnp.concatenate([jnp.full((1,), -1, piece.dtype), by_chunk[:-1, -1]])
    reaches = (by_chunk == before[:, None]).reshape(-1)
    last_same = (by_chunk == by_chunk[:, -1:]).reshape(-1)
    marks = jnp.stack([piece.astype(F32), reaches.astype(F32), last_same.astype(F32), keep], axis=1)
    rows = jnp.pad(marks, ((0, 0), (0, PAIR - 4)))
    columns = jnp.broadcast_to(piece.astype(F32)[None], (8, length))
    offset = jnp.arange(CHUNK).astype(F32)[:, None]
    grow = jnp.exp(offset * log_decay)
    shrink = jnp.exp(-(offset + 1.0) * log_decay)
    tail = jnp.exp((CHUNK - 1.0 - offset) * log_decay)
    zero = jnp.zeros_like(bonus)
    params = jnp.stack([bonus, gain, bias, jnp.exp(CHUNK * log_decay)] + [zero] * 4)
    return rows, columns, grow, shrink, tail, params


def segment_of(lengths, positions):
    rank = jnp.arange(lengths.shape[0])
    starts = jnp.sum(jnp.where(rank[:, None] > rank[None, :], lengths[None, :], 0), axis=1)
    later_flags = (positions[:, None] >= starts[None, 1:]).astype(jnp.int32)
    first_flags = jnp.any(positions[:, None] == starts[None, :], axis=1)
    return (jnp.sum(later_flags, axis=1), first_flags)


def rows_of(vec, *rows):
    return jnp.pad(jnp.stack([vec[i] for i in rows]), ((0, 8 - len(rows)), (0, 0)))


def shards(
    tokens, seq_lengths, out_grad, w_receptance, w_key, w_value, w_gate, w_output,
    ffn_key, ffn_receptance, ffn_value, vectors,
):
    seq, dp = lax.axis_size("seq"), lax.axis_size("dp")
    place = lax.axis_index("seq")
    here = jnp.reshape(place, (1,)).astype(jnp.int32)
    inputs_b, grad_b = tokens[0], out_grad[0]
    own_rows, width = inputs_b.shape
    length, part, unit = own_rows * seq, width // seq, vectors.shape[1]
    per, tile = own_rows // CHUNK, own_rows // 2
    hidden_width = ffn_key.shape[1] // seq
    groups = (seq, dp)
    within = groups if unit == HEAD else None

    vectors_b = jnp.pad(vectors, ((0, 16 - vectors.shape[0]), (0, 0)))

    def stacked_columns(weights, widths, beside=()):
        cut = cut_columns(weights, vectors_b, here, seq)
        *stacked, last = stack_rows(after(trade_seq(cut), beside), widths, vectors_b, here)
        return [w.reshape(-1, w.shape[-1]) for w in stacked] + [last], cut

    def gather_dp(rows):
        return lax.all_gather(rows, "dp", axis=0, tiled=True)

    def scatter_dp(grad):
        return lax.psum_scatter(grad, "dp", scatter_dimension=0, tiled=True)

    def owners_parts(summed):
        rows = summed.shape[0] // seq
        return trade_seq([lax.dynamic_slice_in_dim(summed, (place ^ j) * rows, rows, 0) for j in range(seq)])

    def owners_rows(summed, widths):
        return join_columns(owners_parts(summed), widths, here)

    def turn_pieces(pieces):
        if within is not None:
            return pieces
        return [outside(p, groups, unit) for p in pieces]

    positions = jnp.arange(length, dtype=jnp.int32)
    piece, first_flags = segment_of(seq_lengths[0], positions)

    (columns_in, columns_g, vec_seq), cut = stacked_columns(
        [w_receptance, w_key, w_value, w_gate], [3 * part, part]
    )
    tokens_held = held_back(inputs_b, here, *cut)
    full_in = gather_dp(columns_in)
    vec_parts = gather_small(vec_seq[None, :, : vectors.shape[0]], "dp").astype(F32)
    vec = vec_parts.transpose(2, 1, 0, 3).reshape(-1, width)
    turned = vec_parts.transpose(2, 0, 1, 3).reshape(-1, width)
    vec_own = lax.dynamic_slice_in_dim(vec, place * part, part, 1)
    log_decay = -jnp.exp(vec_own[6])
    tables = wkv_tables(
        piece, 1.0 - first_flags.astype(F32), log_decay, vec_own[7], vec_own[8], vec_own[9]
    )
    marks = tables[0]
    rows_one = rows_of(turned, 0, 1, 2, 3, 4, 5)
    tokens_all = gather_seq(tokens_held, (rows_one, tables))
    full_g = gather_dp(after(columns_g, tokens_all[1:3], rows_one))
    own_o = gather_dp(after(w_output, tokens_all))

    mix_r, mix_k, mix_v, mix_g, step, recept, keyed, valued = mixes(
        turn_pieces(tokens_all), marks, rows_one, 4, True, within, here, tile, own_rows // tile,
        [(i, full_in, i, part) for i in range(3)], False,
    )
    projected = (recept, keyed, valued)
    ffn_weights = after([ffn_key, ffn_receptance], tokens_all)
    if seq == 4:
        pieces_c = trade_seq(cut_with_rider(ffn_weights, grad_b, here))
    else:
        (columns_c, _), _ = stacked_columns(ffn_weights, [hidden_width + part], projected)
        grad_all = gather_seq(after(grad_b, mix_r), projected)
    wkv, states = wkv_forward(recept, keyed, valued, tables, here, per)
    gate_pre, mixed = gated(mix_g, full_g, wkv, tables[5], here, seq)
    if seq == 4:
        pieces_c = after(pieces_c, mixed)
        columns_c = stack_below(pieces_c, here)
    full_c = gather_dp(columns_c)
    full_ck, full_cr = full_c[:, :hidden_width], full_c[:, hidden_width:]
    full_cv = gather_dp(after(ffn_value, columns_c))
    attn = [dot(rows, own_o, NN).astype(BF) for rows in blocks_of(mixed, seq)]
    after_mix, normed_two = after_norm(inputs_b, scatter_seq(attn, here), rows_of(vec, 10, 11), here)

    normed_two = gather_seq(normed_two)
    if seq == 4:
        grad_all = gather_second(grad_b, *after(pieces_c[1:3], normed_two))
    mix_k2, mix_r2, step_two, recept_pre, opened = mixes(
        turn_pieces(normed_two), marks, rows_of(turned, 10, 11, 12, 13), 2, False, within, here, tile,
        own_rows // tile, [(1, full_cr, 0, part)], True,
    )
    opened = gather_seq(after(opened, grad_all[3:]))
    key_pre = dot(mix_k2, full_ck, NN)
    smooth = jax.nn.softplus(key_pre)
    hidden = (smooth * smooth).astype(BF)
    slope = (2.0 * smooth * jax.nn.sigmoid(key_pre)).astype(BF)
    hidden, slope = lax.optimization_barrier((hidden, slope))
    later = after(hidden, opened[1:3])
    value_parts = [columns_product(later if j < 2 else hidden, full_cv, part, j, here, seq) for j in reversed(range(seq))]
    value_parts = value_parts[::-1]
    value_relayed = scatter_relay(value_parts, scatter_start(value_parts), here)
    d_value = spread_columns(
        grad_all, by_block(after(opened, value_parts, value_relayed)), here, True, True, tile, own_rows // tile
    )

    grad_cv = dot(hidden, d_value, TN).astype(BF)
    summed_cv = scatter_dp(grad_cv)
    value_terms = scatter_end(value_parts[0], value_relayed)
    d_hidden = dot(after(d_value, grad_cv), full_cv, NT)
    d_key_two = (d_hidden * slope.astype(F32)).astype(BF)
    channel, d_recept_two = channel_out(value_terms, recept_pre, grad_all, here, tile)
    grad_ck, grad_cr = [], []

    def beside_two(relayed):
        grad_ck.append(dot(after(mix_k2, relayed), d_key_two, TN).astype(BF))
        grad_cr.append(dot(after(mix_r2, relayed, grad_ck), d_recept_two, TN).astype(BF))
        return grad_ck, grad_cr

    terms_two, sums_two = mixes_back_scatter(
        [(0, d_key_two, 0, full_c, 0, hidden_width), (1, d_recept_two, 0, full_cr, 0, part)],
        step_two, marks, rows_of(turned, 12, 13), here, seq, beside_two,
    )
    summed_ck = scatter_dp(grad_ck[0])
    if within is None:
        terms_two = [outside(t, groups, unit, back=True) for t in terms_two]
    d_after, d_attn, norm_sums_two = norm_back(terms_two, after_mix, grad_b, rows_of(vec, 10), within, here)

    pieces = gather_seq(d_attn)
    *near, far = by_block(pieces)
    near_mixed = [dot(d, own_o, NT).astype(BF) for d in near]
    *near_rows, far_rows = blocks_of(mixed, seq)
    near_wo = sum(dot(m, d, TN) for m, d in zip(near_rows, near))
    far = after(far, near_mixed, near_wo, summed_cv)
    d_mixed = jnp.concatenate([*near_mixed, dot(far, own_o, NT).astype(BF)], axis=0)
    grad_wo = (near_wo + dot(far_rows, far, TN)).astype(BF)
    summed_o = scatter_dp(grad_wo)
    d_mixed = after(d_mixed, summed_ck, grad_wo)
    d_wkv, d_gate, gate_sums = gate_backward(wkv, gate_pre, d_mixed, tables[5], here)
    grad_g = dot(mix_g, d_gate, TN).astype(BF)
    summed_crg = scatter_dp(jnp.concatenate([grad_cr[0], grad_g], axis=1))
    d_recept, d_keyed, d_valued, sums = wkv_backward(
        recept, keyed, valued, after(d_wkv, grad_g), states, tables, here, per
    )
    channel = after(trade_seq(blocks_of(after(channel, d_mixed), seq)), d_recept)
    grads_in = [
        dot(after(m, channel), d, TN).astype(BF)
        for m, d in ((mix_r, d_recept), (mix_k, d_keyed), (mix_v, d_valued))
    ]
    summed_in = scatter_dp(jnp.concatenate(grads_in, axis=1))
    others = []

    def beside(relayed):
        others.append(spread_columns([after_mix], after(channel, relayed), here, False, False, CHUNK, per))
        others.append(after(summed_cv, relayed).astype(F32))
        return others

    d_recept, d_keyed = after((d_recept, d_keyed), grads_in, summed_o)
    terms, sums_one = mixes_back_scatter(
        [(i, d, 0, full_in, i, part) for i, d in enumerate((d_recept, d_keyed, d_valued))]
        + [(3, d_gate, 0, full_g, 0, part)],
        step, marks, rows_of(turned, 2, 3, 4, 5), here, seq, beside,
    )
    out_rows, sum_cv = others
    if within is None:
        terms = [outside(t, groups, unit, back=True) for t in terms]
    tokens_grad, _, norm_sums = norm_back(terms, inputs_b, d_after, rows_of(vec, 0), within, here)

    sum_o = summed_o.astype(F32)

    def by_device(rows, turn):
        if turn:
            return rows.reshape(-1, dp, seq, unit).transpose(2, 1, 0, 3)
        return rows.reshape(-1, seq, dp, unit).transpose(1, 2, 0, 3)

    own_sums = jnp.stack([sums[0] * log_decay, sums[1], gate_sums[0], gate_sums[1]])
    own_sums = lax.dynamic_update_slice(jnp.zeros((4, width), F32), own_sums, (0, place * part))
    vector_rows = jnp.concatenate(
        [
            by_device(norm_sums[:2], False), by_device(sums_one[:4], True), by_device(own_sums, False),
            by_device(norm_sums_two[:2], False), by_device(sums_two[:2], True),
        ],
        axis=2,
    )
    sums_seq = scatter_small(vector_rows.reshape((-1,) + vector_rows.shape[2:]), "seq")
    summed_c = jnp.concatenate(after([summed_ck, summed_crg], sums_seq), axis=1)
    sum_ck, sum_cr, sum_g = owners_rows(summed_c, [ffn_key.shape[1], width, width])
    sum_vec = scatter_small(sums_seq, "dp", sum_ck)[0]
    sum_r, sum_k, sum_v = owners_rows(after(summed_in, sums_seq), [width] * 3)
    return (
        out_rows[None], tokens_grad[None], sum_r, sum_k, sum_v, sum_g, sum_o,
        sum_ck, sum_cr, sum_cv, sum_vec,
    )


def solution(mesh):
    tokens = P("dp", "seq", None)
    rows = P(("seq", "dp"), None)
    columns = P(None, ("seq", "dp"))
    return jax.shard_map(
        shards,
        mesh=mesh,
        in_specs=(tokens, P("dp", None), tokens) + (rows,) * 8 + (columns,),
        out_specs=(tokens, tokens) + (rows,) * 8 + (columns,),
        check_vma=False,
    )
```
